32 devices in a mesh: row: 8 (over y, x, core), col: 4 (over z).
Axes of the slice: x: 2, y: 2, z: 4, core: 2. Of those that a mesh axis runs over, the one named last changes fastest.
Arguments:
- nodes: bfloat16 [32768, 256], P(('row', 'col')), may hold values from -6 to 6
- tiles: bfloat16 [256, 4, 4, 128, 128], P('row', 'col'), may hold values from -0.12988281 to 0.12988281
- tile_col: int32 [256, 4, 4], P('row', 'col'), may hold values from 0 to 63, as said below
- tile_count: int32 [256, 4], P('row', 'col'), may hold values from 0 to 4, as said below
- w_in: bfloat16 [512, 256], replicated, may hold values from -0.25 to 0.25
- bias_in: float32 [256], replicated, may hold values from -3 to 3
- w_out: bfloat16 [256, 256], replicated, may hold values from -0.375 to 0.375
- ln_gain: float32 [256], replicated, may hold values from 0.1 to 1.9
- ln_shift: float32 [256], replicated, may hold values from -3 to 3
- cotangent: bfloat16 [32768, 256], P(('row', 'col')), may hold values from -6 to 6
Outputs:
- updated: bfloat16 [32768, 256], P(('row', 'col'))
- grad_nodes: bfloat16 [32768, 256], P(('row', 'col'))
- grad_tiles: bfloat16 [256, 4, 4, 128, 128], P('row', 'col')
- grad_w_in: float32 [512, 256], replicated
- grad_w_out: float32 [256, 256], replicated
- grad_vectors: float32 [3, 256], replicated
The draws below stay inside these ranges and needn't reach their ends.
Inputs may be any that keep to these rules, and one draw needn't show every extreme that they name: `tile_col`: index within the column group; slots at or past the block row's tile_count are ignored. `tile_count`: loads differ between devices; 4 is reached in every draw.
All inputs are finite; a program needn't handle non-finite values.
Results may differ from the reference program's by a relative error of at most 0.02.
Values may be sent and summed in bfloat16 or wider, within the bound.
No kernel may reach another device: no remote copies, remote signals or barrier semaphores. Data moves between devices by JAX's collectives and lax.ppermute only.
A program may use at most 256 MiB of HBM per device.

```python
import jax
import jax.numpy as jnp
from jax import lax

D = 256
BS = 128
KS = 4
BPD = 8
NODES = 32768
NB = 256
RB = 32
CB = 64
N_ROW = 8
N_COL = 4


def draw_tile_col(key, part):
    key = jax.random.fold_in(key, 11)
    return jax.random.randint(key, (NB, N_COL, KS), 0, CB).astype(jnp.int32)


def draw_tile_count(key, part):
    key = jax.random.fold_in(key, 23)
    level_key, count_key = jax.random.split(key)
    groups = NB // RB
    levels = jax.random.randint(level_key, (groups, 1, N_COL), 1, KS + 1)
    counts = jax.random.randint(count_key, (groups, RB, N_COL), 0, KS + 1)
    counts = jnp.minimum(counts, levels).reshape(NB, N_COL)
    return counts.at[0, 0].set(KS).astype(jnp.int32)


def steps_of(own_key, extent, cuts, least, high):
    def one(dim, blocks):
        steps = jax.random.uniform(jax.random.fold_in(jax.random.fold_in(own_key, 6), dim), (blocks,), jnp.float32, least / len(cuts), high / len(cuts))
        return jnp.repeat(jnp.exp(steps), extent[dim] // blocks).reshape((-1,) + (1,) * (len(extent) - dim - 1))

    level = one(*cuts[0])
    for cut in cuts[1:]:
        level = level * one(*cut)
    return level


def normal_values(stream_key, shape, width, limit, shards=(), held_as=jnp.bfloat16):
    gain = steps_of(stream_key, shape, shards, -0.22, 0.18) if shards else 1.0
    entries = jax.random.normal(stream_key, shape, jnp.float32) * width * gain
    return jnp.minimum(jnp.maximum(entries, -limit), limit).astype(held_as)


def setup_inputs(seed: int = 0) -> dict:
    arg_keys = jax.random.split(jax.random.key(seed), 11)
    return {
        "nodes": normal_values(arg_keys[0], (NODES, D), 1.0, 6.0, ((0, 32),)),
        "tiles": normal_values(arg_keys[1], (NB, N_COL, KS, BS, BS), 0.022, 0.12988281, ((0, 8), (1, 4))),
        "tile_col": draw_tile_col(jax.random.fold_in(arg_keys[10], 71), 0),
        "tile_count": draw_tile_count(jax.random.fold_in(arg_keys[10], 71), 0),
        "w_in": normal_values(arg_keys[4], (2 * D, D), (2 * D) ** -0.5, 0.25),
        "bias_in": normal_values(arg_keys[5], (D,), 0.5, 3.0, (), jnp.float32),
        "w_out": normal_values(arg_keys[6], (D, D), D ** -0.5, 0.375),
        "ln_gain": jnp.clip(1.0 + 0.18 * jax.random.normal(arg_keys[7], (D,), jnp.float32), 0.1, 1.9),
        "ln_shift": normal_values(arg_keys[8], (D,), 0.5, 3.0, (), jnp.float32),
        "cotangent": normal_values(arg_keys[9], (NODES, D), 1.0, 6.0, ((0, 32),)),
    }


def source_blocks(tile_col):
    column = lax.broadcasted_iota(jnp.int32, tile_col.shape, 1)
    return ((tile_col // BPD * N_COL + column) * BPD + tile_col % BPD).astype(jnp.int32)

def live_mask(tile_count):
    slot = lax.broadcasted_iota(jnp.int32, (NB, N_COL, KS), 2)
    return slot < tile_count[:, :, None]

def reference(nodes, tiles, tile_col, tile_count, w_in, bias_in, w_out, ln_gain, ln_shift, cotangent):
    live = live_mask(tile_count)
    live_tiles = jnp.where(live[:, :, :, None, None], tiles, jnp.zeros((), tiles.dtype))
    source = source_blocks(tile_col)
    node_blocks = nodes.reshape(NB, BS, D)
    group_tiles = live_tiles.reshape(N_ROW, RB, N_COL, KS, BS, BS)
    group_source = source.reshape(N_ROW, RB, N_COL, KS)

    def forward_group(args):
        tile_group, src_group = args
        picked = node_blocks[src_group].astype(jnp.float32)
        parts = jnp.einsum('rckij,rckjd->rcid', tile_group.astype(jnp.float32), picked)
        rounded = parts.astype(jnp.bfloat16).astype(jnp.float32)
        return lax.optimization_barrier(jnp.sum(rounded, axis=1))
    message = lax.map(forward_group, (group_tiles, group_source)).reshape(NODES, D).astype(jnp.bfloat16)
    pre = jnp.dot(nodes, w_in[:D], preferred_element_type=jnp.float32) + jnp.dot(message, w_in[D:], preferred_element_type=jnp.float32) + bias_in
    act = (pre * jax.nn.sigmoid(pre)).astype(jnp.bfloat16)
    proj = jnp.dot(act, w_out, preferred_element_type=jnp.float32)
    mean = lax.optimization_barrier(jnp.mean(proj, axis=-1, keepdims=True))
    var = lax.optimization_barrier(jnp.mean((proj - mean) ** 2, axis=-1, keepdims=True))
    rstd = 1.0 / jnp.sqrt(var + 1e-05)
    normed = (proj - mean) * rstd
    updated = (nodes.astype(jnp.float32) + normed * ln_gain + ln_shift).astype(jnp.bfloat16)
    grad_out = cotangent.astype(jnp.float32)
    gscaled = grad_out * ln_gain
    gproj = ((gscaled - lax.optimization_barrier(jnp.mean(gscaled, axis=-1, keepdims=True)) - normed * lax.optimization_barrier(jnp.mean(gscaled * normed, axis=-1, keepdims=True))) * rstd).astype(jnp.bfloat16)
    gact = jnp.dot(gproj, w_out.T, preferred_element_type=jnp.float32)
    sig = jax.nn.sigmoid(pre)
    gpre = gact * sig * (1.0 + pre * (1.0 - sig))
    gpre_b = gpre.astype(jnp.bfloat16)
    gmsg = jnp.dot(gpre_b, w_in[D:].T, preferred_element_type=jnp.float32).astype(jnp.bfloat16)
    direct = grad_out + jnp.dot(gpre_b, w_in[:D].T, preferred_element_type=jnp.float32)
    gmsg_groups = gmsg.reshape(N_ROW, RB, BS, D)

    def backward_group(total, args):
        tile_group, src_group, grad_group = args
        back = jnp.einsum('rckij,rid->rckjd', tile_group.astype(jnp.float32), grad_group.astype(jnp.float32))
        seg = (lax.broadcasted_iota(jnp.int32, (RB, N_COL, KS), 1) * NB + src_group).reshape(-1)
        summed = jax.ops.segment_sum(back.reshape(RB * N_COL * KS, BS, D), seg, num_segments=N_COL * NB)
        rounded = summed.astype(jnp.bfloat16).astype(jnp.float32)
        return (total + lax.optimization_barrier(jnp.sum(rounded.reshape(N_COL, NB, BS, D), axis=0)), None)
    agg, _ = lax.scan(backward_group, jnp.zeros((NB, BS, D), jnp.float32), (group_tiles, group_source, gmsg_groups))
    grad_nodes = (direct + agg.reshape(NODES, D)).astype(jnp.bfloat16)

    def tile_group_grad(args):
        src_group, grad_group = args
        picked = node_blocks[src_group].astype(jnp.float32)
        return jnp.einsum('rid,rckjd->rckij', grad_group.astype(jnp.float32), picked)
    tile_grads = lax.map(tile_group_grad, (group_source, gmsg_groups)).reshape(NB, N_COL, KS, BS, BS)
    tile_grads = jnp.where(live[:, :, :, None, None], tile_grads * jnp.float32(D) ** (-0.5), jnp.float32(0.0)).astype(jnp.bfloat16)
    factor = jnp.float32(NODES) ** (-0.5)
    grad_w_in = jnp.concatenate([jnp.dot(nodes.T, gpre_b, preferred_element_type=jnp.float32), jnp.dot(message.T, gpre_b, preferred_element_type=jnp.float32)], axis=0) * factor
    grad_w_out = jnp.dot(act.T, gproj, preferred_element_type=jnp.float32) * factor
    grad_vectors = jnp.stack([lax.optimization_barrier(jnp.sum(gpre, axis=0)), lax.optimization_barrier(jnp.sum(grad_out * normed, axis=0)), lax.optimization_barrier(jnp.sum(grad_out, axis=0))]) * factor
    return (updated, grad_nodes, tile_grads, grad_w_in, grad_w_out, grad_vectors)
```

```python
import functools

import jax
import jax.numpy as jnp
from jax import lax
from jax.experimental import pallas as pl
from jax.experimental.pallas import tpu as pltpu
from jax.sharding import PartitionSpec as P

F32 = jnp.float32
BF16 = jnp.bfloat16
ANY = pl.BlockSpec(memory_space=pl.ANY)
SMEM = pl.BlockSpec(memory_space=pltpu.SMEM)
VMEM = pl.BlockSpec(memory_space=pltpu.VMEM)
MIB = 1 << 20
TN = (((0,), (0,)), ((), ()))
NT = (((1,), (1,)), ((), ()))


def mm(a, b, dims=(((1,), (0,)), ((), ()))):
    return lax.dot_general(a, b, dims, preferred_element_type=F32)


def load_pieces(pieces, dst, sem, first):
    copies = []
    offset = 0
    for index, piece in enumerate(pieces):
        copy = pltpu.make_async_copy(
            piece, dst.at[pl.ds(offset, piece.shape[0])], sem.at[first + index]
        )
        copy.start()
        copies.append(copy)
        offset += piece.shape[0]
    return copies


def masked_tile(tiles, row, slot, count):
    tile = tiles[row, slot]
    return jnp.where(slot < count, tile, jnp.zeros_like(tile))


def forward_kernel(groups, total, n_pieces, cols, counts, off, *refs):
    pieces, tiles = refs[:n_pieces], refs[n_pieces]
    outs = refs[n_pieces + 1 : n_pieces + 1 + len(groups)]
    nodes_v, tiles_v, sem, tile_sem = refs[n_pieces + 1 + len(groups) :]
    rows, width = outs[0].shape
    slots, block = tiles.shape[1], tiles.shape[2]
    blocks = rows // block
    copies = load_pieces(pieces, nodes_v, sem, 0)
    tile_copies = []
    for index, group in enumerate(groups):
        actual = lax.rem(off[0] + group, total)
        copy = pltpu.make_async_copy(
            tiles.at[pl.ds(actual * blocks, blocks)],
            tiles_v.at[pl.ds(index * blocks, blocks)],
            tile_sem.at[index],
        )
        copy.start()
        tile_copies.append(copy)
    for copy in copies:
        copy.wait()
    for index, group in enumerate(groups):
        tile_copies[index].wait()
        first = lax.rem(off[0] + group, total) * blocks
        out = outs[index]

        def step(i, carry, first=first, out=out, index=index):
            row = first + i
            count = counts[row]
            parts = []
            for pair in range(slots // 2):
                left, right = 2 * pair, 2 * pair + 1
                tile = jnp.concatenate(
                    [
                        masked_tile(tiles_v, index * blocks + i, slot, count)
                        for slot in (left, right)
                    ],
                    axis=1,
                )
                node = jnp.concatenate(
                    [
                        nodes_v[pl.ds(pl.multiple_of(cols[row * slots + slot] * block, block), block)]
                        for slot in (left, right)
                    ],
                    axis=0,
                )
                parts.append(mm(tile, node))
            value = parts[0]
            for part in parts[1:]:
                value = value + part
            out[pl.ds(pl.multiple_of(i * block, block), block)] = value.astype(BF16)
            return carry

        lax.fori_loop(0, blocks, step, 0, unroll=4)


def forward_call(cols, counts, off, pieces, tiles, groups, total, rows):
    width = pieces[0].shape[1]
    gathered = sum(piece.shape[0] for piece in pieces)
    slots, block = tiles.shape[1], tiles.shape[2]
    blocks = rows // block
    flops = len(groups) * blocks * slots * 2 * block * block * width
    return pl.pallas_call(
        functools.partial(forward_kernel, groups, total, len(pieces)),
        out_shape=[jax.ShapeDtypeStruct((rows, width), BF16) for _ in groups],
        in_specs=[SMEM, SMEM, SMEM] + [ANY] * (len(pieces) + 1),
        out_specs=[VMEM] * len(groups),
        scratch_shapes=[
            pltpu.VMEM((gathered, width), BF16),
            pltpu.VMEM((len(groups) * blocks,) + tiles.shape[1:], BF16),
            pltpu.SemaphoreType.DMA((len(pieces),)),
            pltpu.SemaphoreType.DMA((len(groups),)),
        ],
        compiler_params=pltpu.CompilerParams(vmem_limit_bytes=40 * MIB),
        cost_estimate=pl.CostEstimate(
            flops=flops, bytes_accessed=2 * gathered * width + 2 * len(groups) * rows * (width + slots * block), transcendentals=0
        ),
        name="partial_messages",
    )(cols, counts, off, *pieces, tiles)


def mlp_kernel(
    n_parts, nodes, cot, *refs
):
    parts = refs[:n_parts]
    w_in, bias, w_out, gain, shift, updated, gmsg, gpre_o, act_o, gproj_o, msg_o, vec = refs[n_parts:]
    width = nodes.shape[1]
    message = parts[0][...].astype(F32)
    for part in parts[1:]:
        message = message + part[...].astype(F32)
    message = message.astype(BF16)
    node = nodes[...]
    pre = mm(node, w_in[:width]) + mm(message, w_in[width:]) + bias[...]
    sig = jax.nn.sigmoid(pre)
    act = (pre * sig).astype(BF16)
    proj = mm(act, w_out[...])
    mean = jnp.mean(proj, axis=-1, keepdims=True)
    var = jnp.mean((proj - mean) ** 2, axis=-1, keepdims=True)
    rstd = 1.0 / jnp.sqrt(var + 1e-05)
    normed = (proj - mean) * rstd
    updated[...] = (node.astype(F32) + normed * gain[...] + shift[...]).astype(BF16)
    grad_out = cot[...].astype(F32)
    gscaled = grad_out * gain[...]
    gproj = (
        (
            gscaled
            - jnp.mean(gscaled, axis=-1, keepdims=True)
            - normed * jnp.mean(gscaled * normed, axis=-1, keepdims=True)
        )
        * rstd
    ).astype(BF16)
    gact = mm(gproj, w_out[...], NT)
    gpre = gact * sig * (1.0 + pre * (1.0 - sig))
    gpre_b = gpre.astype(BF16)
    gmsg[...] = mm(gpre_b, w_in[width:], NT).astype(BF16)
    gpre_o[...] = gpre_b
    act_o[...] = act
    gproj_o[...] = gproj
    msg_o[...] = message

    @pl.when(pl.program_id(0) == 0)
    def _():
        vec[...] = jnp.zeros_like(vec)

    vec[0:1] += jnp.sum(gpre, axis=0, keepdims=True)
    vec[1:2] += jnp.sum(grad_out * normed, axis=0, keepdims=True)
    vec[2:3] += jnp.sum(grad_out, axis=0, keepdims=True)


def mlp_call(nodes, cot, parts, w_in, bias, w_out, gain, shift):
    rows, width = nodes.shape
    step = min(rows, 256)
    blocked = pl.BlockSpec((step, width), lambda i: (i, 0))

    def whole(array):
        return pl.BlockSpec(array.shape, lambda i: (0, 0))

    row_like = jax.ShapeDtypeStruct((rows, width), BF16)
    return pl.pallas_call(
        functools.partial(mlp_kernel, len(parts)),
        grid=(rows // step,),
        out_shape=[row_like] * 6 + [jax.ShapeDtypeStruct((8, width), F32)],
        in_specs=[blocked] * (2 + len(parts)) + [whole(a) for a in (w_in, bias, w_out, gain, shift)],
        out_specs=[blocked] * 6 + [pl.BlockSpec((8, width), lambda i: (0, 0))],
        compiler_params=pltpu.CompilerParams(vmem_limit_bytes=40 * MIB),
        cost_estimate=pl.CostEstimate(
            flops=2 * rows * width * width * 5, bytes_accessed=2 * rows * width * 11, transcendentals=rows * width
        ),
        name="mlp",
    )(nodes, cot, *parts, w_in, bias, w_out, gain, shift)


def weight_kernel(factor, nodes, msg, act, gpre, gproj, cot, w_in, vec, grads, direct):
    width = nodes.shape[1]

    @pl.when(pl.program_id(0) == 0)
    def _():
        grads[: 3 * width] = jnp.zeros((3 * width, width), F32)
        grads[3 * width :] = vec[...] * factor

    gpre_b = gpre[...]
    grads[:width] += mm(nodes[...], gpre_b, TN) * factor
    grads[width : 2 * width] += mm(msg[...], gpre_b, TN) * factor
    grads[2 * width : 3 * width] += mm(act[...], gproj[...], TN) * factor
    direct[...] = cot[...].astype(F32) + mm(gpre_b, w_in[:width], NT)


def weight_call(factor, nodes, msg, act, gpre, gproj, cot, w_in, vec):
    rows, width = nodes.shape
    step = min(rows, 256)
    blocked = pl.BlockSpec((step, width), lambda i: (i, 0))

    def whole(shape):
        return pl.BlockSpec(shape, lambda i: (0, 0))

    grads = (3 * width + 8, width)
    return pl.pallas_call(
        functools.partial(weight_kernel, factor),
        grid=(rows // step,),
        out_shape=[jax.ShapeDtypeStruct(grads, F32), jax.ShapeDtypeStruct((rows, width), F32)],
        in_specs=[blocked] * 6 + [whole(w_in.shape), whole(vec.shape)],
        out_specs=[whole(grads), blocked],
        compiler_params=pltpu.CompilerParams(vmem_limit_bytes=40 * MIB),
        cost_estimate=pl.CostEstimate(
            flops=2 * rows * width * width * 4, bytes_accessed=2 * rows * width * 10, transcendentals=0
        ),
        name="weight_grads",
    )(nodes, msg, act, gpre, gproj, cot, w_in, vec)


def grad_copies(total, rows, refs, dst, sem, off):
    if len(refs) == 1:
        return [(None, pltpu.make_async_copy(refs[0], dst, sem.at[0]))]
    own = off[0]
    jobs = [(None, pltpu.make_async_copy(refs[0], dst.at[pl.ds(own * rows, rows)], sem.at[0]))]
    for distance in range(1, total):
        lower = jnp.maximum(own - distance, 0)
        upper = jnp.minimum(own + distance, total - 1)
        jobs.append(
            (
                own >= distance,
                pltpu.make_async_copy(
                    refs[distance], dst.at[pl.ds(lower * rows, rows)], sem.at[distance]
                ),
            )
        )
        jobs.append(
            (
                own + distance < total,
                pltpu.make_async_copy(
                    refs[total - 1 + distance],
                    dst.at[pl.ds(upper * rows, rows)],
                    sem.at[total - 1 + distance],
                ),
            )
        )
    return jobs


def run_jobs(jobs, verb):
    for condition, copy in jobs:
        if condition is None:
            getattr(copy, verb)()
        else:
            pl.when(condition)(getattr(copy, verb))


def back_kernel(total, rows, n_grads, out_pieces, cols, counts, off, *refs):
    grads, tiles = refs[:n_grads], refs[n_grads]
    outs = refs[n_grads + 1 : n_grads + 1 + len(out_pieces)]
    grad_v, tiles_v, acc, sem, tile_sem = refs[n_grads + 1 + len(out_pieces) :]
    row_blocks, slots, block = tiles.shape[:3]
    jobs = grad_copies(total, rows, grads, grad_v, sem, off)
    run_jobs(jobs, "start")
    tile_copy = pltpu.make_async_copy(tiles, tiles_v, tile_sem.at[0])
    tile_copy.start()
    acc[...] = jnp.zeros_like(acc)
    run_jobs(jobs, "wait")
    tile_copy.wait()

    def step(row, carry):
        count = counts[row]
        grad = grad_v[pl.ds(pl.multiple_of(row * block, block), block)]
        for slot in range(slots):
            part = mm(masked_tile(tiles_v, row, slot, count), grad, TN)
            where = pl.ds(pl.multiple_of(cols[row * slots + slot] * block, block), block)
            acc[where] += part
        return carry

    lax.fori_loop(0, row_blocks, step, 0, unroll=2)
    piece = acc.shape[0] // sum(len(members) for members in out_pieces)
    for out, members in zip(outs, out_pieces):
        for index, member in enumerate(members):
            out[pl.ds(index * piece, piece)] = acc[pl.ds(member * piece, piece)].astype(BF16)


def back_call(cols, counts, off, grads, tiles, total, rows, gathered, out_pieces):
    width = grads[0].shape[1]
    row_blocks, slots, block = tiles.shape[:3]
    n_pieces = sum(len(members) for members in out_pieces)
    piece = gathered // n_pieces
    return pl.pallas_call(
        functools.partial(back_kernel, total, rows, len(grads), out_pieces),
        out_shape=[jax.ShapeDtypeStruct((len(m) * piece, width), BF16) for m in out_pieces],
        in_specs=[SMEM, SMEM, SMEM] + [ANY] * (len(grads) + 1),
        out_specs=[VMEM] * len(out_pieces),
        scratch_shapes=[
            pltpu.VMEM((total * rows, width), BF16),
            pltpu.VMEM(tiles.shape, BF16),
            pltpu.VMEM((gathered, width), F32),
            pltpu.SemaphoreType.DMA((2 * total,)),
            pltpu.SemaphoreType.DMA((1,)),
        ],
        compiler_params=pltpu.CompilerParams(vmem_limit_bytes=56 * MIB),
        cost_estimate=pl.CostEstimate(
            flops=row_blocks * slots * 2 * block * block * width,
            bytes_accessed=2 * width * (gathered + total * rows) + 2 * tiles.size,
            transcendentals=0,
        ),
        name="back_terms",
    )(cols, counts, off, *grads, tiles)


def tile_grad_kernel(total, rows, n_grads, n_pieces, chunk, cols, counts, off, *refs):
    grads = refs[:n_grads]
    pieces = refs[n_grads : n_grads + n_pieces]
    out = refs[n_grads + n_pieces]
    grad_v, nodes_v, sem, piece_sem = refs[n_grads + n_pieces + 1 :]
    slots, block = out.shape[1], out.shape[2]
    width = nodes_v.shape[1]
    scale = float(width) ** -0.5

    @pl.when(pl.program_id(0) == 0)
    def _():
        jobs = grad_copies(total, rows, grads, grad_v, sem, off)
        run_jobs(jobs, "start")
        copies = load_pieces(pieces, nodes_v, piece_sem, 0)
        run_jobs(jobs, "wait")
        for copy in copies:
            copy.wait()

    def step(i, carry):
        row = pl.program_id(0) * chunk + i
        count = counts[row]
        grad = grad_v[pl.ds(pl.multiple_of(row * block, block), block)]
        for slot in range(slots):
            node = nodes_v[pl.ds(pl.multiple_of(cols[row * slots + slot] * block, block), block)]
            value = mm(grad, node, NT) * scale
            out[i, slot] = jnp.where(slot < count, value, 0.0).astype(BF16)
        return carry

    lax.fori_loop(0, chunk, step, 0, unroll=2)


def tile_grad_call(cols, counts, off, grads, pieces, shape, total, rows):
    row_blocks, slots, block = shape[:3]
    width = pieces[0].shape[1]
    gathered = sum(piece.shape[0] for piece in pieces)
    chunk = min(row_blocks, 8)
    return pl.pallas_call(
        functools.partial(tile_grad_kernel, total, rows, len(grads), len(pieces), chunk),
        grid=(row_blocks // chunk,),
        out_shape=jax.ShapeDtypeStruct(shape, BF16),
        in_specs=[SMEM, SMEM, SMEM] + [ANY] * (len(grads) + len(pieces)),
        out_specs=pl.BlockSpec((chunk, slots, block, block), lambda i: (i, 0, 0, 0)),
        scratch_shapes=[
            pltpu.VMEM((total * rows, width), BF16),
            pltpu.VMEM((gathered, width), BF16),
            pltpu.SemaphoreType.DMA((2 * total,)),
            pltpu.SemaphoreType.DMA((len(pieces),)),
        ],
        compiler_params=pltpu.CompilerParams(vmem_limit_bytes=40 * MIB),
        cost_estimate=pl.CostEstimate(
            flops=row_blocks * slots * 2 * block * block * width,
            bytes_accessed=2 * width * (gathered + total * rows) + 2 * row_blocks * slots * block * block,
            transcendentals=0,
        ),
        name="tile_grads",
    )(cols, counts, off, *grads, *pieces)


def add(*terms):
    value = terms[0].astype(F32)
    for term in terms[1:]:
        value = value + term.astype(F32)
    return value.astype(BF16)


def swap(value, bit, size):
    return lax.ppermute(value, "row", [(i, i ^ bit) for i in range(size)])


def shift_line(value, by, size):
    return lax.ppermute(value, "col", [(i, i + by) for i in range(size) if 0 <= i + by < size])


def gather_square(nodes):
    half = nodes.shape[0] // 2
    own = (nodes[:half], nodes[half:])
    y_first = swap(own[0], 4, 8)
    x_second = swap(own[1], 2, 8)
    x_first = swap(own[0], 2, 8)
    y_second = swap(own[1], 4, 8)
    diag = (swap(y_first, 2, 8), swap(x_second, 4, 8))
    even = [own, (x_first, x_second), (y_first, y_second), diag]
    pieces = [nodes, swap(nodes, 1, 8)]
    for pair in even[1:]:
        pieces += list(pair) + [swap(value, 1, 8) for value in pair]
    return pieces


def reduce_square(even, odd, rows):
    half = rows // 2
    other = swap(odd, 1, 8)

    def both(place, part):
        where = slice(place * rows + part * half, place * rows + (part + 1) * half)
        return even[where], other[where]

    diag_first = swap(add(*both(3, 0)), 2, 8)
    diag_second = swap(add(*both(3, 1)), 4, 8)
    x_first = swap(add(*both(1, 0)), 2, 8)
    y_second = swap(add(*both(2, 1)), 4, 8)
    y_first = swap(add(*both(2, 0), diag_first), 4, 8)
    x_second = swap(add(*both(1, 1), diag_second), 2, 8)
    first = sum(term.astype(F32) for term in (*both(0, 0), x_first, y_first))
    second = sum(term.astype(F32) for term in (*both(0, 1), x_second, y_second))
    return jnp.concatenate([first, second], axis=0)


def body(n_row, n_col, nodes, tiles, tile_col, tile_count, w_in, bias_in, w_out, ln_gain, ln_shift, cotangent):
    rows, width = nodes.shape
    row_blocks, _, slots, block = tiles.shape[:4]
    tile_local = tiles.reshape(row_blocks, slots, block, block)
    cols = tile_col.reshape(row_blocks * slots)
    counts = tile_count.reshape(row_blocks)
    blocks = rows // block
    square = n_row == 8
    line = n_col == 4
    if square:
        mine = lax.axis_index("row").astype(jnp.int32)
        cols = ((cols // blocks) ^ mine) * blocks + cols % blocks
        pieces = gather_square(nodes)
    else:
        pieces = [lax.all_gather(nodes, "row", axis=0, tiled=True)]
    gathered = n_row * rows
    zero = jnp.zeros((1,), jnp.int32)
    if line:
        off = lax.axis_index("col").astype(jnp.int32).reshape(1)
        part1, part3 = forward_call(cols, counts, off, pieces, tile_local, (1, 3), n_col, rows)
        part2, part0 = forward_call(cols, counts, off, pieces, tile_local, (2, 0), n_col, rows)
        right = shift_line(part3, 1, n_col)
        left = shift_line(part1, -1, n_col)
        right = shift_line(add(part2, right), 1, n_col)
        left = shift_line(add(part2, left), -1, n_col)
        right = shift_line(add(part1, right), 1, n_col)
        left = shift_line(add(part3, left), -1, n_col)
        parts = [part0, right, left]
    else:
        off = zero
        partial = forward_call(
            cols, counts, off, pieces, tile_local, tuple(range(n_col)), n_col, rows
        )
        parts = [
            lax.psum_scatter(
                jnp.concatenate(partial, axis=0), "col", scatter_dimension=0, tiled=True
            )
        ]
    vectors = [v.reshape(1, width) for v in (bias_in, ln_gain, ln_shift)]
    updated, gmsg, gpre_b, act, gproj, message, vec = mlp_call(
        nodes, cotangent, parts, w_in, vectors[0], w_out, vectors[1], vectors[2]
    )
    if line:
        rights, lefts = [gmsg], [gmsg]
        for _ in range(n_col - 1):
            rights.append(shift_line(rights[-1], 1, n_col))
            lefts.append(shift_line(lefts[-1], -1, n_col))
        grads = rights + lefts[1:]
    else:
        grads = [lax.all_gather(gmsg, "col", axis=0, tiled=True)]
    factor = float(rows * n_row * n_col) ** -0.5
    weight_terms, direct = weight_call(
        factor, nodes, message, act, gpre_b, gproj, cotangent, w_in, vec
    )
    weight_sums = lax.psum(weight_terms, ("row", "col"))
    if square:
        odd, even = back_call(
            cols, counts, off, grads, tile_local, n_col, rows, gathered, ((1, 3, 5, 7), (0, 2, 4, 6))
        )
        back = reduce_square(even, odd, rows)
    else:
        (terms,) = back_call(
            cols, counts, off, grads, tile_local, n_col, rows, gathered, (tuple(range(n_row)),)
        )
        back = lax.psum_scatter(terms, "row", scatter_dimension=0, tiled=True).astype(F32)
    grad_nodes = (direct + back).astype(BF16)
    grad_tiles = tile_grad_call(
        cols, counts, off, grads, pieces, tile_local.shape, n_col, rows
    ).reshape(tiles.shape)
    return (
        updated,
        grad_nodes,
        grad_tiles,
        weight_sums[: 2 * width],
        weight_sums[2 * width : 3 * width],
        weight_sums[3 * width : 3 * width + 3],
    )


def solution(mesh):
    placed = (
        P(("row", "col"), None),
        P("row", "col", None, None, None),
        P("row", "col", None),
        P("row", "col"),
        P(),
        P(),
        P(),
        P(),
        P(),
        P(("row", "col"), None),
    )
    return jax.shard_map(
        functools.partial(body, mesh.shape["row"], mesh.shape["col"]),
        mesh=mesh,
        in_specs=placed,
        out_specs=(
            P(("row", "col"), None),
            P(("row", "col"), None),
            P("row", "col", None, None, None),
            P(),
            P(),
            P(),
        ),
        check_vma=False,
    )
```

```python
import functools

import jax
import jax.numpy as jnp
from jax import lax
from jax.experimental import pallas as pl
from jax.experimental.pallas import tpu as pltpu
from jax.sharding import PartitionSpec as P

F32 = jnp.float32
BF16 = jnp.bfloat16
ANY = pl.BlockSpec(memory_space=pl.ANY)
SMEM = pl.BlockSpec(memory_space=pltpu.SMEM)
VMEM = pl.BlockSpec(memory_space=pltpu.VMEM)
MIB = 1 << 20
TN = (((0,), (0,)), ((), ()))
NT = (((1,), (1,)), ((), ()))
PARAMS = pltpu.CompilerParams(vmem_limit_bytes=60 * MIB)


def mm(a, b, dims=(((1,), (0,)), ((), ()))):
    return lax.dot_general(a, b, dims, preferred_element_type=F32)


def block_at(index, block):
    return pl.ds(pl.multiple_of(index * block, block), block)


def load_pieces(pieces, dst, sem, first):
    copies = []
    offset = 0
    for index, piece in enumerate(pieces):
        copy = pltpu.make_async_copy(
            piece, dst.at[pl.ds(offset, piece.shape[0])], sem.at[first + index]
        )
        copy.start()
        copies.append(copy)
        offset += piece.shape[0]
    return copies


def masked_tile(tiles, row, slot, count):
    tile = tiles[row, slot]
    return jnp.where(slot < count, tile, jnp.zeros_like(tile))


def forward_kernel(picks, n_pieces, cols, counts, order, *refs):
    pieces, tiles = refs[:n_pieces], refs[n_pieces]
    outs = refs[n_pieces + 1 : n_pieces + 1 + len(picks)]
    nodes_v, tiles_v, sem, tile_sem = refs[n_pieces + 1 + len(picks) :]
    rows, width = outs[0].shape
    slots, block = tiles.shape[1], tiles.shape[2]
    blocks = rows // block
    copies = load_pieces(pieces, nodes_v, sem, 0)
    tile_copies = []
    for index, pick in enumerate(picks):
        copy = pltpu.make_async_copy(
            tiles.at[pl.ds(order[pick] * blocks, blocks)],
            tiles_v.at[pl.ds(index * blocks, blocks)],
            tile_sem.at[index],
        )
        copy.start()
        tile_copies.append(copy)
    for copy in copies:
        copy.wait()
    for index, pick in enumerate(picks):
        tile_copies[index].wait()
        first = order[pick] * blocks
        out = outs[index]

        def step(i, carry, first=first, out=out, index=index):
            row = first + i
            count = counts[row]
            parts = []
            for pair in range(slots // 2):
                both = (2 * pair, 2 * pair + 1)
                tile = jnp.concatenate(
                    [masked_tile(tiles_v, index * blocks + i, slot, count) for slot in both], axis=1
                )
                node = jnp.concatenate(
                    [nodes_v[block_at(cols[row * slots + slot], block)] for slot in both], axis=0
                )
                parts.append(mm(tile, node))
            value = parts[0]
            for part in parts[1:]:
                value = value + part
            out[block_at(i, block)] = value.astype(BF16)
            return carry

        lax.fori_loop(0, blocks, step, 0, unroll=4)


def forward_call(cols, counts, order, pieces, tiles, picks, rows, after=()):
    width = pieces[0].shape[1]
    gathered = sum(piece.shape[0] for piece in pieces)
    slots, block = tiles.shape[1], tiles.shape[2]
    blocks = rows // block
    count = len(picks) * blocks * slots
    return pl.pallas_call(
        functools.partial(forward_kernel, picks, len(pieces)),
        out_shape=[jax.ShapeDtypeStruct((rows, width), BF16) for _ in picks],
        in_specs=[SMEM, SMEM, SMEM] + [ANY] * (len(pieces) + 1),
        out_specs=[VMEM] * len(picks),
        scratch_shapes=[
            pltpu.VMEM((gathered, width), BF16),
            pltpu.VMEM((len(picks) * blocks,) + tiles.shape[1:], BF16),
            pltpu.SemaphoreType.DMA((len(pieces),)),
            pltpu.SemaphoreType.DMA((len(picks),)),
        ],
        compiler_params=PARAMS,
        cost_estimate=pl.CostEstimate(
            flops=count * 2 * block * block * width,
            bytes_accessed=2 * (gathered + len(picks) * rows) * width + 2 * count * block * block,
            transcendentals=0,
        ),
        name="partial_messages",
    )(cols, counts, order, *pieces, tiles)


def mlp_kernel(kinds, middle, nodes, cot, *refs):
    n_parts = sum(len(chunk) for chunk in kinds)
    parts = refs[:n_parts]
    w_in, bias, w_out, gain, shift, updated, gpre_o, act_o, gproj_o, msg_o, vec = refs[
        n_parts : n_parts + 11
    ]
    gmsgs = refs[n_parts + 11 :]
    width = nodes.shape[1]
    inner = middle[0] > 0
    messages = []
    place = 0
    for chunk in kinds:
        total = None
        for kind in chunk:
            term = parts[place][...].astype(F32)
            place += 1
            if kind == "inner":
                term = jnp.where(inner, term, 0.0)
            total = term if total is None else total + term
        messages.append(total.astype(BF16))
    message = jnp.concatenate(messages, axis=1) if len(messages) > 1 else messages[0]
    node = nodes[...]
    pre = mm(node, w_in[:width]) + mm(message, w_in[width:]) + bias[...]
    sig = jax.nn.sigmoid(pre)
    act = (pre * sig).astype(BF16)
    proj = mm(act, w_out[...])
    mean = jnp.mean(proj, axis=-1, keepdims=True)
    var = jnp.mean((proj - mean) ** 2, axis=-1, keepdims=True)
    rstd = 1.0 / jnp.sqrt(var + 1e-05)
    normed = (proj - mean) * rstd
    updated[...] = (node.astype(F32) + normed * gain[...] + shift[...]).astype(BF16)
    grad_out = cot[...].astype(F32)
    gscaled = grad_out * gain[...]
    gproj = (
        (
            gscaled
            - jnp.mean(gscaled, axis=-1, keepdims=True)
            - normed * jnp.mean(gscaled * normed, axis=-1, keepdims=True)
        )
        * rstd
    ).astype(BF16)
    gact = mm(gproj, w_out[...], NT)
    gpre = gact * sig * (1.0 + pre * (1.0 - sig))
    gpre_b = gpre.astype(BF16)
    gmsg = mm(gpre_b, w_in[width:], NT).astype(BF16)
    part = width // len(gmsgs)
    for index, out in enumerate(gmsgs):
        out[...] = gmsg[:, index * part : (index + 1) * part]
    gpre_o[...] = gpre_b
    act_o[...] = act
    gproj_o[...] = gproj
    msg_o[...] = message

    @pl.when(pl.program_id(0) == 0)
    def _():
        vec[...] = jnp.zeros_like(vec)

    vec[0:1] += jnp.sum(gpre, axis=0, keepdims=True)
    vec[1:2] += jnp.sum(grad_out * normed, axis=0, keepdims=True)
    vec[2:3] += jnp.sum(grad_out, axis=0, keepdims=True)


def mlp_call(middle, nodes, cot, parts, kinds, w_in, bias, w_out, gain, shift):
    rows, width = nodes.shape
    step = min(rows, 256)

    def blocked(array):
        return pl.BlockSpec((step, array.shape[1]), lambda i: (i, 0))

    def whole(array):
        return pl.BlockSpec(array.shape, lambda i: (0, 0))

    flat = [term for chunk in parts for term in chunk]
    row_like = jax.ShapeDtypeStruct((rows, width), BF16)
    chunk_like = jax.ShapeDtypeStruct((rows, width // len(parts)), BF16)
    outs = [row_like] * 5 + [jax.ShapeDtypeStruct((8, width), F32)] + [chunk_like] * len(parts)
    weights = (w_in, bias, w_out, gain, shift)
    result = pl.pallas_call(
        functools.partial(mlp_kernel, kinds),
        grid=(rows // step,),
        out_shape=outs,
        in_specs=[SMEM] + [blocked(a) for a in (nodes, cot, *flat)] + [whole(a) for a in weights],
        out_specs=[blocked(a) for a in outs[:5]] + [whole(outs[5])] + [blocked(a) for a in outs[6:]],
        compiler_params=PARAMS,
        cost_estimate=pl.CostEstimate(
            flops=2 * rows * width * width * 5, bytes_accessed=2 * rows * width * 11, transcendentals=rows * width
        ),
        name="mlp",
    )(middle, nodes, cot, *flat, *weights)
    return result[:6], result[6:]


def weight_kernel(factor, nodes, msg, act, gpre, gproj, cot, w_in, vec, grads, direct):
    width = nodes.shape[1]

    @pl.when(pl.program_id(0) == 0)
    def _():
        grads[: 3 * width] = jnp.zeros((3 * width, width), F32)
        grads[3 * width :] = vec[...] * factor

    gpre_b = gpre[...]
    grads[:width] += mm(nodes[...], gpre_b, TN) * factor
    grads[width : 2 * width] += mm(msg[...], gpre_b, TN) * factor
    grads[2 * width : 3 * width] += mm(act[...], gproj[...], TN) * factor
    direct[...] = cot[...].astype(F32) + mm(gpre_b, w_in[:width], NT)


def weight_call(factor, nodes, msg, act, gpre, gproj, cot, w_in, vec):
    rows, width = nodes.shape
    step = min(rows, 256)
    blocked = pl.BlockSpec((step, width), lambda i: (i, 0))

    def whole(shape):
        return pl.BlockSpec(shape, lambda i: (0, 0))

    grads = (3 * width + 8, width)
    return pl.pallas_call(
        functools.partial(weight_kernel, factor),
        grid=(rows // step,),
        out_shape=[jax.ShapeDtypeStruct(grads, F32), jax.ShapeDtypeStruct((rows, width), F32)],
        in_specs=[blocked] * 6 + [whole(w_in.shape), whole(vec.shape)],
        out_specs=[whole(grads), blocked],
        compiler_params=PARAMS,
        cost_estimate=pl.CostEstimate(
            flops=2 * rows * width * width * 4, bytes_accessed=2 * rows * width * 10, transcendentals=0
        ),
        name="weight_grads",
    )(nodes, msg, act, gpre, gproj, cot, w_in, vec)


def grad_jobs(rows, refs, dst, sem, order, middle):
    if len(refs) == 1:
        return [(None, pltpu.make_async_copy(refs[0], dst, sem.at[0]))]
    inner = middle[0] > 0
    outer = middle[0] == 0
    plan = ((3, None), (2, None), (1, inner), (1, outer), (0, inner), (0, outer))
    return [
        (
            condition,
            pltpu.make_async_copy(refs[index], dst.at[block_at(order[group], rows)], sem.at[index]),
        )
        for index, (group, condition) in enumerate(plan)
    ]


def run_jobs(jobs, verb):
    for condition, copy in jobs:
        if condition is None:
            getattr(copy, verb)()
        else:
            pl.when(condition)(getattr(copy, verb))


def back_kernel(rows, n_grads, n_after, out_pieces, cols, counts, order, middle, *refs):
    grads, tiles = refs[:n_grads], refs[n_grads]
    refs = refs[n_grads + 1 + n_after :]
    outs = refs[: len(out_pieces)]
    grad_v, tiles_v, acc, sem, tile_sem = refs[len(out_pieces) :]
    row_blocks, slots, block = tiles.shape[:3]
    jobs = grad_jobs(rows, grads, grad_v, sem, order, middle)
    run_jobs(jobs, "start")
    tile_copy = pltpu.make_async_copy(tiles, tiles_v, tile_sem.at[0])
    tile_copy.start()
    acc[...] = jnp.zeros_like(acc)
    run_jobs(jobs, "wait")
    tile_copy.wait()

    def step(row, carry):
        count = counts[row]
        grad = grad_v[block_at(row, block)]
        for slot in range(slots):
            part = mm(masked_tile(tiles_v, row, slot, count), grad, TN)
            acc[block_at(cols[row * slots + slot], block)] += part
        return carry

    lax.fori_loop(0, row_blocks, step, 0, unroll=2)
    piece = acc.shape[0] // sum(len(members) for members in out_pieces)
    for out, members in zip(outs, out_pieces):
        for index, member in enumerate(members):
            out[pl.ds(index * piece, piece)] = acc[pl.ds(member * piece, piece)].astype(BF16)


def back_call(cols, counts, order, middle, grads, tiles, total, gathered, out_pieces, after=()):
    rows, width = grads[0].shape
    rows = total if len(grads) == 1 else rows
    row_blocks, slots, block = tiles.shape[:3]
    piece = gathered // sum(len(members) for members in out_pieces)
    return pl.pallas_call(
        functools.partial(back_kernel, rows, len(grads), len(after), out_pieces),
        out_shape=[jax.ShapeDtypeStruct((len(m) * piece, width), BF16) for m in out_pieces],
        in_specs=[SMEM] * 4 + [ANY] * (len(grads) + 1 + len(after)),
        out_specs=[VMEM] * len(out_pieces),
        scratch_shapes=[
            pltpu.VMEM((total, width), BF16),
            pltpu.VMEM(tiles.shape, BF16),
            pltpu.VMEM((gathered, width), F32),
            pltpu.SemaphoreType.DMA((len(grads),)),
            pltpu.SemaphoreType.DMA((1,)),
        ],
        compiler_params=PARAMS,
        cost_estimate=pl.CostEstimate(
            flops=row_blocks * slots * 2 * block * block * width,
            bytes_accessed=2 * width * (gathered + total) + 2 * tiles.size,
            transcendentals=0,
        ),
        name="back_terms",
    )(cols, counts, order, middle, *grads, tiles, *after)


def tile_grad_kernel(rows, n_grads, n_pieces, n_chunks, n_after, step_rows, cols, counts, order, middle, *refs):
    grads = refs[: n_grads * n_chunks]
    refs = refs[n_grads * n_chunks :]
    pieces = refs[: n_pieces * n_chunks]
    out, grad_v, nodes_v, sem, piece_sem = refs[n_pieces * n_chunks + n_after :]
    slots, block = out.shape[1], out.shape[2]
    width = nodes_v.shape[1]
    part = width // n_chunks
    scale = float(width) ** -0.5

    @pl.when(pl.program_id(0) == 0)
    def _():
        jobs, copies = [], []
        for chunk in range(n_chunks):
            columns = pl.ds(chunk * part, part)
            jobs += grad_jobs(
                rows,
                grads[chunk * n_grads : (chunk + 1) * n_grads],
                grad_v.at[:, columns],
                sem.at[chunk],
                order,
                middle,
            )
            copies += load_pieces(
                pieces[chunk * n_pieces : (chunk + 1) * n_pieces],
                nodes_v.at[:, columns],
                piece_sem.at[chunk],
                0,
            )
        run_jobs(jobs, "start")
        run_jobs(jobs, "wait")
        for copy in copies:
            copy.wait()

    def step(i, carry):
        row = pl.program_id(0) * step_rows + i
        count = counts[row]
        grad = grad_v[block_at(row, block)]
        for slot in range(slots):
            node = nodes_v[block_at(cols[row * slots + slot], block)]
            value = mm(grad, node, NT) * scale
            out[i, slot] = jnp.where(slot < count, value, 0.0).astype(BF16)
        return carry

    lax.fori_loop(0, step_rows, step, 0, unroll=2)


def tile_grad_call(cols, counts, order, middle, grads, pieces, shape, total, after=()):
    row_blocks, slots, block = shape[:3]
    chunks = len(grads)
    rows, width = grads[0][0].shape
    rows = total if len(grads[0]) == 1 else rows
    width = width * chunks
    gathered = sum(piece.shape[0] for piece in pieces[0])
    step_rows = min(row_blocks, 8)
    flat = [a for chunk in grads for a in chunk] + [a for chunk in pieces for a in chunk]
    return pl.pallas_call(
        functools.partial(
            tile_grad_kernel, rows, len(grads[0]), len(pieces[0]), chunks, len(after), step_rows
        ),
        grid=(row_blocks // step_rows,),
        out_shape=jax.ShapeDtypeStruct(shape, BF16),
        in_specs=[SMEM] * 4 + [ANY] * (len(flat) + len(after)),
        out_specs=pl.BlockSpec((step_rows, slots, block, block), lambda i: (i, 0, 0, 0)),
        scratch_shapes=[
            pltpu.VMEM((total, width), BF16),
            pltpu.VMEM((gathered, width), BF16),
            pltpu.SemaphoreType.DMA((chunks, len(grads[0]))),
            pltpu.SemaphoreType.DMA((chunks, len(pieces[0]))),
        ],
        compiler_params=PARAMS,
        cost_estimate=pl.CostEstimate(
            flops=row_blocks * slots * 2 * block * block * width,
            bytes_accessed=2 * width * (gathered + total) + 2 * row_blocks * slots * block * block,
            transcendentals=0,
        ),
        name="tile_grads",
    )(cols, counts, order, middle, *flat, *after)


def add(*terms):
    value = terms[0].astype(F32)
    for term in terms[1:]:
        value = value + term.astype(F32)
    return value.astype(BF16)


def swap(value, bit):
    return lax.ppermute(value, "row", [(i, i ^ bit) for i in range(8)])


def outer_swap(value):
    return lax.ppermute(value, "col", [(0, 1), (1, 0), (2, 3), (3, 2)])


def inner_swap(value):
    return lax.ppermute(value, "col", [(0, 0), (1, 2), (2, 1), (3, 3)])


def gather_square(nodes, by_x):
    x_side, y_side = swap(nodes, 2), swap(nodes, 4)
    diag = swap(y_side, 2) if by_x else swap(x_side, 4)
    pieces = []
    for piece in (nodes, x_side, y_side, diag):
        pieces += [piece, swap(piece, 1)]
    return pieces


def reduce_square(even, odd, rows, by_x):
    other = swap(odd, 1)

    def both(place):
        where = slice(place * rows, (place + 1) * rows)
        return even[where], other[where]

    if by_x:
        diag = swap(add(*both(3)), 2)
        x_side = swap(add(*both(1)), 2)
        y_side = swap(add(*both(2), diag), 4)
    else:
        diag = swap(add(*both(3)), 4)
        y_side = swap(add(*both(2)), 4)
        x_side = swap(add(*both(1), diag), 2)
    return (*both(0), x_side, y_side)


def reduce_line(far, near, pair, own, inner):
    far_in = outer_swap(far)
    near_in = outer_swap(near)
    far_sum = inner_swap(add(far, far_in))
    near_sum = inner_swap(add(near, near_in))
    pair_in = outer_swap(add(pair, jnp.where(inner, far_sum, jnp.zeros_like(far_sum))))
    return own, pair_in, near_sum


def gather_line(own):
    pair = outer_swap(own)
    near_inner = inner_swap(own)
    far_inner = inner_swap(pair)
    near_outer = outer_swap(near_inner)
    far_outer = outer_swap(far_inner)
    return [own, pair, near_inner, near_outer, far_inner, far_outer]


def body(n_row, n_col, nodes, tiles, tile_col, tile_count, w_in, bias_in, w_out, ln_gain, ln_shift, cotangent):
    rows, width = nodes.shape
    row_blocks, _, slots, block = tiles.shape[:4]
    tile_local = tiles.reshape(row_blocks, slots, block, block)
    cols = tile_col.reshape(row_blocks * slots)
    counts = tile_count.reshape(row_blocks)
    blocks = rows // block
    gathered, total = n_row * rows, n_col * rows
    square_line = n_row == 8 and n_col == 4
    if square_line:
        mine = lax.axis_index("row").astype(jnp.int32)
        cols = ((cols // blocks) ^ mine) * blocks + cols % blocks
        level = lax.axis_index("col").astype(jnp.int32)
        low = level < 2
        order = jnp.stack([jnp.where(low, 3, 0), jnp.where(low, 2, 1), level ^ 1, level]).astype(jnp.int32)
        inner = (level == 1) | (level == 2)
        middle = inner.astype(jnp.int32).reshape(1)
        chunks = 2
        part = width // chunks
        pieces, parts, kinds = [], [], []
        for chunk in range(chunks):
            pieces.append(gather_square(nodes[:, chunk * part : (chunk + 1) * part], chunk == 0))
            far, near = forward_call(cols, counts, order, pieces[-1], tile_local, (0, 1), rows)
            pair, own = forward_call(cols, counts, order, pieces[-1], tile_local, (2, 3), rows)
            parts.append(reduce_line(far, near, pair, own, inner))
            kinds.append(("all", "all", "inner"))
    else:
        order = jnp.arange(n_col, dtype=jnp.int32)
        middle = jnp.zeros((1,), jnp.int32)
        pieces = [[lax.all_gather(nodes, "row", axis=0, tiled=True)]]
        partial = forward_call(
            cols, counts, order, pieces[0], tile_local, tuple(range(n_col)), rows
        )
        partial = jnp.concatenate(partial, axis=0)
        parts = [[lax.psum_scatter(partial, "col", scatter_dimension=0, tiled=True)]]
        kinds = [("all",)]
    vectors = [v.reshape(1, width) for v in (bias_in, ln_gain, ln_shift)]
    (updated, gpre_b, act, gproj, message, vec), gmsgs = mlp_call(
        middle, nodes, cotangent, parts, kinds, w_in, vectors[0], w_out, vectors[1], vectors[2]
    )
    if square_line:
        grads = [gather_line(gmsg) for gmsg in gmsgs]
    else:
        grads = [[lax.all_gather(gmsgs[0], "col", axis=0, tiled=True)]]
    factor = float(rows * n_row * n_col) ** -0.5
    weight_terms, direct = weight_call(
        factor, nodes, message, act, gpre_b, gproj, cotangent, w_in, vec
    )
    weight_sums = lax.psum(lax.psum(weight_terms, "row"), "col")
    if square_line:
        sums = []
        for chunk in range(chunks):
            odd, even = back_call(
                cols, counts, order, middle, grads[chunk], tile_local, total, gathered,
                ((1, 3, 5, 7), (0, 2, 4, 6)),
            )
            terms = reduce_square(even, odd, rows, chunk == 0)
            sums.append(sum(term.astype(F32) for term in terms))
        after = (odd,)
        back = jnp.concatenate(sums, axis=1)
    else:
        (terms,) = back_call(
            cols, counts, order, middle, grads[0], tile_local, total, gathered, (tuple(range(n_row)),)
        )
        back = lax.psum_scatter(terms, "row", scatter_dimension=0, tiled=True).astype(F32)
        after = (terms,)
    grad_nodes = (direct + back).astype(BF16)
    grad_tiles = tile_grad_call(
        cols, counts, order, middle, grads, pieces, tile_local.shape, total, after
    ).reshape(tiles.shape)
    return (
        updated,
        grad_nodes,
        grad_tiles,
        weight_sums[: 2 * width],
        weight_sums[2 * width : 3 * width],
        weight_sums[3 * width : 3 * width + 3],
    )


def solution(mesh):
    placed = (
        P(("row", "col"), None),
        P("row", "col", None, None, None),
        P("row", "col", None),
        P("row", "col"),
        P(),
        P(),
        P(),
        P(),
        P(),
        P(("row", "col"), None),
    )
    return jax.shard_map(
        functools.partial(body, mesh.shape["row"], mesh.shape["col"]),
        mesh=mesh,
        in_specs=placed,
        out_specs=(
            P(("row", "col"), None),
            P(("row", "col"), None),
            P("row", "col", None, None, None),
            P(),
            P(),
            P(),
        ),
        check_vma=False,
    )
```

```python
import functools

import jax
import jax.numpy as jnp
from jax import lax
from jax.experimental import pallas as pl
from jax.experimental.pallas import tpu as pltpu
from jax.sharding import PartitionSpec as P

F32 = jnp.float32
BF16 = jnp.bfloat16
ANY = pl.BlockSpec(memory_space=pl.ANY)
SMEM = pl.BlockSpec(memory_space=pltpu.SMEM)
VMEM = pl.BlockSpec(memory_space=pltpu.VMEM)
MIB = 1 << 20
TN = (((0,), (0,)), ((), ()))
NT = (((1,), (1,)), ((), ()))
PEAK_FLOPS_PER_US = 1153.5e6


LIVE_STEP = 4
SWAP_ORDER = (0, 4, 2, 6, 1, 5, 3, 7)


def params(mib):
    return pltpu.CompilerParams(vmem_limit_bytes=mib * MIB)


def cost(microseconds):
    return pl.CostEstimate(flops=int(microseconds * PEAK_FLOPS_PER_US), bytes_accessed=MIB, transcendentals=0)


def mm(a, b, dims=(((1,), (0,)), ((), ()))):
    return lax.dot_general(a, b, dims, preferred_element_type=F32)


def block_at(index, block):
    return pl.ds(pl.multiple_of(index * block, block), block)


def load_pieces(pieces, dst, sem, first):
    copies = []
    offset = 0
    for index, piece in enumerate(pieces):
        copy = pltpu.make_async_copy(
            piece, dst.at[pl.ds(offset, piece.shape[0])], sem.at[first + index]
        )
        copy.start()
        copies.append(copy)
        offset += piece.shape[0]
    return copies


def masked_tile(tiles, row, slot, count):
    tile = tiles[row, slot]
    return jnp.where(slot < count, tile, jnp.zeros_like(tile))


def forward_kernel(picks, n_pieces, cols, counts, order, *refs):
    pieces, tiles = refs[:n_pieces], refs[n_pieces]
    outs = refs[n_pieces + 1 : n_pieces + 1 + len(picks)]
    nodes_v, tiles_v, sem, tile_sem = refs[n_pieces + 1 + len(picks) :]
    rows, width = outs[0].shape
    slots, block = tiles.shape[1], tiles.shape[2]
    blocks = rows // block
    copies = load_pieces(pieces, nodes_v, sem, 0)
    tile_copies = []
    for index, pick in enumerate(picks):
        copy = pltpu.make_async_copy(
            tiles.at[pl.ds(order[pick] * blocks, blocks)],
            tiles_v.at[pl.ds(index * blocks, blocks)],
            tile_sem.at[index],
        )
        copy.start()
        tile_copies.append(copy)
    for copy in copies:
        copy.wait()
    for index, pick in enumerate(picks):
        tile_copies[index].wait()
        first = order[pick] * blocks
        out = outs[index]

        def step(i, carry, first=first, out=out, index=index):
            row = first + i
            count = counts[row]
            parts = []
            for pair in range(slots // 2):
                both = (2 * pair, 2 * pair + 1)
                tile = jnp.concatenate(
                    [masked_tile(tiles_v, index * blocks + i, slot, count) for slot in both], axis=1
                )
                node = jnp.concatenate(
                    [nodes_v[block_at(cols[row * slots + slot], block)] for slot in both], axis=0
                )
                parts.append(mm(tile, node))
            value = parts[0]
            for part in parts[1:]:
                value = value + part
            out[block_at(i, block)] = value.astype(BF16)
            return carry

        lax.fori_loop(0, blocks, step, 0, unroll=4)


def forward_call(cols, counts, order, pieces, tiles, picks, rows, after=()):
    width = pieces[0].shape[1]
    gathered = sum(piece.shape[0] for piece in pieces)
    slots, block = tiles.shape[1], tiles.shape[2]
    blocks = rows // block
    return pl.pallas_call(
        functools.partial(forward_kernel, picks, len(pieces)),
        out_shape=[jax.ShapeDtypeStruct((rows, width), BF16) for _ in picks],
        in_specs=[SMEM, SMEM, SMEM] + [ANY] * (len(pieces) + 1),
        out_specs=[VMEM] * len(picks),
        scratch_shapes=[
            pltpu.VMEM((gathered, width), BF16),
            pltpu.VMEM((len(picks) * blocks,) + tiles.shape[1:], BF16),
            pltpu.SemaphoreType.DMA((len(pieces),)),
            pltpu.SemaphoreType.DMA((len(picks),)),
        ],
        compiler_params=params(16 if gathered <= 8192 else 40),
        cost_estimate=cost(4.0),
        name="partial_messages",
    )(cols, counts, order, *pieces, tiles)


def mlp_kernel(kinds, middle, nodes, cot, *refs):
    n_parts = sum(len(chunk) for chunk in kinds)
    parts = refs[:n_parts]
    w_in, bias, w_out, gain, shift, updated, gpre_o, act_o, gproj_o, msg_o, vec = refs[
        n_parts : n_parts + 11
    ]
    gmsgs = refs[n_parts + 11 :]
    width = nodes.shape[1]
    inner = middle[0] > 0
    messages = []
    place = 0
    for chunk in kinds:
        total = None
        for kind in chunk:
            term = parts[place][...].astype(F32)
            place += 1
            if kind == "inner":
                term = jnp.where(inner, term, 0.0)
            total = term if total is None else total + term
        messages.append(total.astype(BF16))
    message = jnp.concatenate(messages, axis=1) if len(messages) > 1 else messages[0]
    node = nodes[...]
    pre = mm(node, w_in[:width]) + mm(message, w_in[width:]) + bias[...]
    sig = jax.nn.sigmoid(pre)
    act = (pre * sig).astype(BF16)
    proj = mm(act, w_out[...])
    mean = jnp.mean(proj, axis=-1, keepdims=True)
    var = jnp.mean((proj - mean) ** 2, axis=-1, keepdims=True)
    rstd = 1.0 / jnp.sqrt(var + 1e-05)
    normed = (proj - mean) * rstd
    updated[...] = (node.astype(F32) + normed * gain[...] + shift[...]).astype(BF16)
    grad_out = cot[...].astype(F32)
    gscaled = grad_out * gain[...]
    gproj = (
        (
            gscaled
            - jnp.mean(gscaled, axis=-1, keepdims=True)
            - normed * jnp.mean(gscaled * normed, axis=-1, keepdims=True)
        )
        * rstd
    ).astype(BF16)
    gact = mm(gproj, w_out[...], NT)
    gpre = gact * sig * (1.0 + pre * (1.0 - sig))
    gpre_b = gpre.astype(BF16)
    gmsg = mm(gpre_b, w_in[width:], NT).astype(BF16)
    part = width // len(gmsgs)
    for index, out in enumerate(gmsgs):
        out[...] = gmsg[:, index * part : (index + 1) * part]
    gpre_o[...] = gpre_b
    act_o[...] = act
    gproj_o[...] = gproj
    msg_o[...] = message

    @pl.when(pl.program_id(0) == 0)
    def _():
        vec[...] = jnp.zeros_like(vec)

    vec[0:1] += jnp.sum(gpre, axis=0, keepdims=True)
    vec[1:2] += jnp.sum(grad_out * normed, axis=0, keepdims=True)
    vec[2:3] += jnp.sum(grad_out, axis=0, keepdims=True)


def mlp_call(middle, nodes, cot, parts, kinds, w_in, bias, w_out, gain, shift):
    rows, width = nodes.shape
    step = min(rows, 256)

    def blocked(array):
        return pl.BlockSpec((step, array.shape[1]), lambda i: (i, 0))

    def whole(array):
        return pl.BlockSpec(array.shape, lambda i: (0, 0))

    flat = [term for chunk in parts for term in chunk]
    row_like = jax.ShapeDtypeStruct((rows, width), BF16)
    chunk_like = jax.ShapeDtypeStruct((rows, width // len(parts)), BF16)
    outs = [row_like] * 5 + [jax.ShapeDtypeStruct((8, width), F32)] + [chunk_like] * len(parts)
    weights = (w_in, bias, w_out, gain, shift)
    result = pl.pallas_call(
        functools.partial(mlp_kernel, kinds),
        grid=(rows // step,),
        out_shape=outs,
        in_specs=[SMEM] + [blocked(a) for a in (nodes, cot, *flat)] + [whole(a) for a in weights],
        out_specs=[blocked(a) for a in outs[:5]] + [whole(outs[5])] + [blocked(a) for a in outs[6:]],
        compiler_params=params(20),
        cost_estimate=cost(5.0),
        name="mlp",
    )(middle, nodes, cot, *flat, *weights)
    return result[:6], result[6:]


def weight_kernel(factor, pieces, mine, nodes, msg, act, gpre, gproj, cot, w_in, vec, out, direct, grads):
    width = nodes.shape[1]

    @pl.when(pl.program_id(0) == 0)
    def _():
        grads[...] = jnp.zeros_like(grads)
        grads[3 * width : 3 * width + 8] = vec[...] * factor

    gpre_b = gpre[...]
    grads[:width] += mm(nodes[...], gpre_b, TN) * factor
    grads[width : 2 * width] += mm(msg[...], gpre_b, TN) * factor
    grads[2 * width : 3 * width] += mm(act[...], gproj[...], TN) * factor
    direct[...] = cot[...].astype(F32) + mm(gpre_b, w_in[:width], NT)

    @pl.when(pl.program_id(0) == pl.num_programs(0) - 1)
    def _():
        if pieces == 1:
            out[...] = grads[: out.shape[0]]
        else:
            rows, part = grads.shape[0] // pieces, out.shape[1]
            folds = width // part
            for place in range(pieces):
                where = pl.ds(pl.multiple_of((mine[0] ^ place) * rows, 8), rows)
                for fold in range(folds):
                    first = (place * folds + fold) * rows
                    out[first : first + rows] = grads[where, fold * part : (fold + 1) * part].astype(BF16)


def weight_call(factor, pieces, mine, nodes, msg, act, gpre, gproj, cot, w_in, vec):
    rows, width = nodes.shape
    step = min(rows, 256)
    blocked = pl.BlockSpec((step, width), lambda i: (i, 0))

    def whole(shape):
        return pl.BlockSpec(shape, lambda i: (0, 0))

    padded = (3 * width + width // 2, width)
    if pieces == 1:
        out = jax.ShapeDtypeStruct((3 * width + 8, width), F32)
    else:
        out = jax.ShapeDtypeStruct((2 * padded[0], width // 2), BF16)
    return pl.pallas_call(
        functools.partial(weight_kernel, factor, pieces),
        grid=(rows // step,),
        out_shape=[out, jax.ShapeDtypeStruct((rows, width), F32)],
        in_specs=[SMEM] + [blocked] * 6 + [whole(w_in.shape), whole(vec.shape)],
        out_specs=[whole(out.shape), blocked],
        scratch_shapes=[pltpu.VMEM(padded, F32)],
        compiler_params=params(16),
        cost_estimate=cost(3.0),
        name="weight_grads",
    )(mine, nodes, msg, act, gpre, gproj, cot, w_in, vec)


def unpack_kernel(mine, parts, w_in, w_out, vectors, grads):
    width = w_in.shape[1]
    rows = grads.shape[0] // len(SWAP_ORDER)
    part = parts.shape[1]
    for place, member in enumerate(SWAP_ORDER):
        where = pl.ds(pl.multiple_of((mine[0] ^ member) * rows, 8), rows)
        for fold in range(width // part):
            first = (place * (width // part) + fold) * rows
            grads[where, fold * part : (fold + 1) * part] = parts[first : first + rows].astype(F32)
    w_in[...] = grads[: 2 * width]
    w_out[...] = grads[2 * width : 3 * width]
    vectors[...] = grads[3 * width : 3 * width + 3]


def unpack_call(mine, parts, width):
    shapes = ((2 * width, width), (width, width), (3, width))
    return pl.pallas_call(
        unpack_kernel,
        out_shape=[jax.ShapeDtypeStruct(shape, F32) for shape in shapes],
        in_specs=[SMEM, VMEM],
        out_specs=[VMEM] * 3,
        scratch_shapes=[pltpu.VMEM((3 * width + width // 2, width), F32)],
        compiler_params=params(16),
        cost_estimate=cost(2.0),
        name="weight_unpack",
    )(mine, parts)


def grad_jobs(rows, refs, dst, sem, order, middle):
    if len(refs) == 1:
        return [(None, pltpu.make_async_copy(refs[0], dst, sem.at[0]))]
    inner = middle[0] > 0
    outer = middle[0] == 0
    plan = ((3, None), (2, None), (1, inner), (1, outer), (0, inner), (0, outer))
    return [
        (
            condition,
            pltpu.make_async_copy(refs[index], dst.at[block_at(order[group], rows)], sem.at[index]),
        )
        for index, (group, condition) in enumerate(plan)
    ]


def run_jobs(jobs, verb):
    for condition, copy in jobs:
        if condition is None:
            getattr(copy, verb)()
        else:
            pl.when(condition)(getattr(copy, verb))


def back_kernel(rows, slots, n_grads, n_extra, out_pieces, cols, counts, order, middle, *refs):
    grads, tiles = refs[:n_grads], refs[n_grads]
    extras = refs[n_grads + 1 : n_grads + 1 + n_extra]
    refs = refs[n_grads + 1 + n_extra :]
    outs = refs[: len(out_pieces)]
    grad_v, tiles_v, acc, live, sem, tile_sem, extra_sem = refs[len(out_pieces) :]
    n_tiles, block = tiles.shape[:2]
    n_pieces = sum(len(members) for members in out_pieces)
    piece = acc.shape[0] // n_pieces
    jobs = grad_jobs(rows, grads, grad_v, sem, order, middle)
    run_jobs(jobs, "start")
    tile_copy = pltpu.make_async_copy(tiles, tiles_v, tile_sem.at[0])
    tile_copy.start()
    stride = piece
    extra_copies = []
    if extras:
        extra = extras[0].shape[0] // n_pieces
        stride = piece + extra
        for out, members in zip(outs, out_pieces):
            for index, member in enumerate(members):
                copy = pltpu.make_async_copy(
                    extras[0].at[pl.ds(member * extra, extra)],
                    out.at[pl.ds(index * stride + piece, extra)],
                    extra_sem.at[member],
                )
                copy.start()
                extra_copies.append(copy)
    acc[...] = jnp.zeros_like(acc)

    def collect(row, found):
        count = counts[row]
        for slot in range(slots):
            live[found] = row * slots + slot
            found = found + (slot < count).astype(jnp.int32)
        return found

    found = lax.fori_loop(0, n_tiles // slots, collect, jnp.int32(0))
    for index in range(LIVE_STEP):
        live[found + index] = 0
    run_jobs(jobs, "wait")
    tile_copy.wait()

    def step(i, carry):
        for index in range(LIVE_STEP):
            place = i * LIVE_STEP + index
            tile_index = live[place]
            tile = tiles_v[tile_index]
            tile = jnp.where(place < found, tile, jnp.zeros_like(tile))
            part = mm(tile, grad_v[block_at(tile_index // slots, block)], TN)
            acc[block_at(cols[tile_index], block)] += part
        return carry

    lax.fori_loop(0, (found + LIVE_STEP - 1) // LIVE_STEP, step, 0)
    for out, members in zip(outs, out_pieces):
        for index, member in enumerate(members):
            out[pl.ds(index * stride, piece)] = acc[pl.ds(member * piece, piece)].astype(BF16)
    for copy in extra_copies:
        copy.wait()


def back_call(cols, counts, order, middle, grads, tiles, total, gathered, out_pieces, extras=()):
    rows, width = grads[0].shape
    rows = total if len(grads) == 1 else rows
    row_blocks, slots, block = tiles.shape[:3]
    n_pieces = sum(len(members) for members in out_pieces)
    piece = (gathered + sum(extra.shape[0] for extra in extras)) // n_pieces
    return pl.pallas_call(
        functools.partial(back_kernel, rows, slots, len(grads), len(extras), out_pieces),
        out_shape=[jax.ShapeDtypeStruct((len(m) * piece, width), BF16) for m in out_pieces],
        in_specs=[SMEM] * 4 + [ANY] * (len(grads) + 1 + len(extras)),
        out_specs=[VMEM] * len(out_pieces),
        scratch_shapes=[
            pltpu.VMEM((total, width), BF16),
            pltpu.VMEM((row_blocks * slots, block, block), BF16),
            pltpu.VMEM((gathered, width), F32),
            pltpu.SMEM((row_blocks * slots + 2 * LIVE_STEP,), jnp.int32),
            pltpu.SemaphoreType.DMA((len(grads),)),
            pltpu.SemaphoreType.DMA((1,)),
            pltpu.SemaphoreType.DMA((n_pieces,)),
        ],
        compiler_params=params(24 if gathered <= 8192 else 56),
        cost_estimate=cost(6.0),
        name="back_terms",
    )(cols, counts, order, middle, *grads, tiles.reshape(row_blocks * slots, block, block), *extras)


def tile_grad_kernel(rows, n_grads, n_pieces, n_chunks, n_after, step_rows, cols, counts, order, middle, *refs):
    grads = refs[: n_grads * n_chunks]
    refs = refs[n_grads * n_chunks :]
    pieces = refs[: n_pieces * n_chunks]
    out, grad_v, nodes_v, sem, piece_sem = refs[n_pieces * n_chunks + n_after :]
    slots, block = out.shape[1], out.shape[2]
    width = nodes_v.shape[1]
    part = width // n_chunks
    scale = float(width) ** -0.5

    @pl.when(pl.program_id(0) == 0)
    def _():
        jobs, copies = [], []
        for chunk in range(n_chunks):
            columns = pl.ds(chunk * part, part)
            jobs += grad_jobs(
                rows,
                grads[chunk * n_grads : (chunk + 1) * n_grads],
                grad_v.at[:, columns],
                sem.at[chunk],
                order,
                middle,
            )
            copies += load_pieces(
                pieces[chunk * n_pieces : (chunk + 1) * n_pieces],
                nodes_v.at[:, columns],
                piece_sem.at[chunk],
                0,
            )
        run_jobs(jobs, "start")
        run_jobs(jobs, "wait")
        for copy in copies:
            copy.wait()

    def step(i, carry):
        row = pl.program_id(0) * step_rows + i
        count = counts[row]
        grad = grad_v[block_at(row, block)]
        for pair in range(slots // 2):
            both = (2 * pair, 2 * pair + 1)
            node = jnp.concatenate(
                [nodes_v[block_at(cols[row * slots + slot], block)] for slot in both], axis=0
            )
            value = mm(grad, node, NT) * scale
            for index, slot in enumerate(both):
                half = value[:, index * block : (index + 1) * block]
                out[i, slot] = jnp.where(slot < count, half, 0.0).astype(BF16)
        return carry

    lax.fori_loop(0, step_rows, step, 0, unroll=2)


def tile_grad_call(cols, counts, order, middle, grads, pieces, shape, total, after=()):
    row_blocks, slots, block = shape[:3]
    chunks = len(grads)
    rows, width = grads[0][0].shape
    rows = total if len(grads[0]) == 1 else rows
    width = width * chunks
    gathered = sum(piece.shape[0] for piece in pieces[0])
    step_rows = min(row_blocks, 8)
    flat = [a for chunk in grads for a in chunk] + [a for chunk in pieces for a in chunk]
    return pl.pallas_call(
        functools.partial(
            tile_grad_kernel, rows, len(grads[0]), len(pieces[0]), chunks, len(after), step_rows
        ),
        grid=(row_blocks // step_rows,),
        out_shape=jax.ShapeDtypeStruct(shape, BF16),
        in_specs=[SMEM] * 4 + [ANY] * (len(flat) + len(after)),
        out_specs=pl.BlockSpec((step_rows, slots, block, block), lambda i: (i, 0, 0, 0)),
        scratch_shapes=[
            pltpu.VMEM((total, width), BF16),
            pltpu.VMEM((gathered, width), BF16),
            pltpu.SemaphoreType.DMA((chunks, len(grads[0]))),
            pltpu.SemaphoreType.DMA((chunks, len(pieces[0]))),
        ],
        compiler_params=params(16 if gathered <= 8192 else 40),
        cost_estimate=cost(8.0),
        name="tile_grads",
    )(cols, counts, order, middle, *flat, *after)


def add(*terms):
    value = terms[0].astype(F32)
    for term in terms[1:]:
        value = value + term.astype(F32)
    return value.astype(BF16)


def swap(value, bit):
    return lax.ppermute(value, "row", [(i, i ^ bit) for i in range(8)])


def outer_swap(value):
    return lax.ppermute(value, "col", [(0, 1), (1, 0), (2, 3), (3, 2)])


def mirror_swap(value):
    return lax.ppermute(value, "col", [(0, 3), (3, 0), (1, 2), (2, 1)])


def inner_swap(value):
    return lax.ppermute(value, "col", [(0, 0), (1, 2), (2, 1), (3, 3)])


def gather_square(nodes, by_x, hold=None):
    y_side = swap(nodes, 4)
    if hold is None:
        x_side = swap(nodes, 2)
    else:
        x_side = swap(lax.optimization_barrier((nodes, hold))[0], 2)
    diag = swap(y_side, 2) if by_x else swap(x_side, 4)
    pieces = []
    for piece in (nodes, x_side, y_side, diag):
        pieces += [piece, swap(piece, 1)]
    return pieces


def reduce_square(even, odd, rows, by_x):
    other = swap(odd, 1)

    def both(place):
        where = slice(place * rows, (place + 1) * rows)
        return even[where], other[where]

    if by_x:
        diag = swap(add(*both(3)), 2)
        x_side = swap(add(*both(1)), 2)
        y_side = swap(add(*both(2), diag), 4)
    else:
        diag = swap(add(*both(3)), 4)
        y_side = swap(add(*both(2)), 4)
        x_side = swap(add(*both(1), diag), 2)
    return (*both(0), x_side, y_side)


def sum_weights(terms, width, mine):
    value = add(*terms)
    value = add(value, outer_swap(value))
    value = add(value, mirror_swap(value))
    for bit in (4, 2, 1):
        value = jnp.concatenate([value, swap(value, bit)], axis=0)
    return unpack_call(mine, value, width)


def reduce_line(far, near, pair, own, inner):
    far_in = outer_swap(far)
    near_in = outer_swap(near)
    far_sum = inner_swap(add(far, far_in))
    near_sum = inner_swap(add(near, near_in))
    pair_in = outer_swap(add(pair, jnp.where(inner, far_sum, jnp.zeros_like(far_sum))))
    return own, pair_in, near_sum


def gather_line(own):
    pair = outer_swap(own)
    near_inner = inner_swap(own)
    far_inner = inner_swap(pair)
    near_outer = outer_swap(near_inner)
    far_outer = outer_swap(far_inner)
    return [own, pair, near_inner, near_outer, far_inner, far_outer]


def body(n_row, n_col, nodes, tiles, tile_col, tile_count, w_in, bias_in, w_out, ln_gain, ln_shift, cotangent):
    rows, width = nodes.shape
    row_blocks, _, slots, block = tiles.shape[:4]
    tile_local = tiles.reshape(row_blocks, slots, block, block)
    cols = tile_col.reshape(row_blocks * slots)
    counts = tile_count.reshape(row_blocks)
    blocks = rows // block
    gathered, total = n_row * rows, n_col * rows
    square_line = n_row == 8 and n_col == 4
    if square_line:
        mine = lax.axis_index("row").astype(jnp.int32)
        cols = ((cols // blocks) ^ mine) * blocks + cols % blocks
        level = lax.axis_index("col").astype(jnp.int32)
        low = level < 2
        order = jnp.stack([jnp.where(low, 3, 0), jnp.where(low, 2, 1), level ^ 1, level]).astype(jnp.int32)
        inner = (level == 1) | (level == 2)
        middle = inner.astype(jnp.int32).reshape(1)
        chunks = 2
        part = width // chunks
        pieces, parts, kinds = [], [], []
        for chunk in range(chunks):
            hold = pieces[0][6] if chunk else None
            pieces.append(gather_square(nodes[:, chunk * part : (chunk + 1) * part], chunk == 0, hold))
            far, near = forward_call(cols, counts, order, pieces[-1], tile_local, (0, 1), rows)
            pair, own = forward_call(cols, counts, order, pieces[-1], tile_local, (2, 3), rows)
            parts.append(reduce_line(far, near, pair, own, inner))
            kinds.append(("all", "all", "inner"))
    else:
        order = jnp.arange(n_col, dtype=jnp.int32)
        middle = jnp.zeros((1,), jnp.int32)
        pieces = [[lax.all_gather(nodes, "row", axis=0, tiled=True)]]
        partial = forward_call(
            cols, counts, order, pieces[0], tile_local, tuple(range(n_col)), rows
        )
        partial = jnp.concatenate(partial, axis=0)
        parts = [[lax.psum_scatter(partial, "col", scatter_dimension=0, tiled=True)]]
        kinds = [("all",)]
    vectors = [v.reshape(1, width) for v in (bias_in, ln_gain, ln_shift)]
    (updated, gpre_b, act, gproj, message, vec), gmsgs = mlp_call(
        middle, nodes, cotangent, parts, kinds, w_in, vectors[0], w_out, vectors[1], vectors[2]
    )
    if square_line:
        grads = [gather_line(gmsg) for gmsg in gmsgs]
    else:
        grads = [[lax.all_gather(gmsgs[0], "col", axis=0, tiled=True)]]
    factor = float(rows * n_row * n_col) ** -0.5
    mine = lax.axis_index("row").astype(jnp.int32).reshape(1)
    weight_terms, direct = weight_call(
        factor, n_row if square_line else 1, mine, nodes, message, act, gpre_b, gproj, cotangent, w_in, vec
    )
    if square_line:
        sums = []
        for chunk in range(chunks):
            odd, even = back_call(
                cols, counts, order, middle, grads[chunk], tile_local, total, gathered,
                ((1, 3, 5, 7), (0, 2, 4, 6)), (weight_terms,) if chunk == 0 else (),
            )
            terms = reduce_square(even, odd, odd.shape[0] // 4, chunk == 0)
            if chunk == 0:
                weights = sum_weights([term[rows:] for term in terms], width, mine)
            sums.append(sum(term[:rows].astype(F32) for term in terms))
        after = (odd,)
        back = jnp.concatenate(sums, axis=1)
    else:
        weight_sums = lax.psum(weight_terms, ("row", "col"))
        weights = (
            weight_sums[: 2 * width],
            weight_sums[2 * width : 3 * width],
            weight_sums[3 * width : 3 * width + 3],
        )
        (terms,) = back_call(
            cols, counts, order, middle, grads[0], tile_local, total, gathered, (tuple(range(n_row)),)
        )
        back = lax.psum_scatter(terms, "row", scatter_dimension=0, tiled=True).astype(F32)
        after = (terms,)
    grad_nodes = (direct + back).astype(BF16)
    grad_tiles = tile_grad_call(
        cols, counts, order, middle, grads, pieces, tile_local.shape, total, after
    ).reshape(tiles.shape)
    return (updated, grad_nodes, grad_tiles, *weights)


def solution(mesh):
    placed = (
        P(("row", "col"), None),
        P("row", "col", None, None, None),
        P("row", "col", None),
        P("row", "col"),
        P(),
        P(),
        P(),
        P(),
        P(),
        P(("row", "col"), None),
    )
    return jax.shard_map(
        functools.partial(body, mesh.shape["row"], mesh.shape["col"]),
        mesh=mesh,
        in_specs=placed,
        out_specs=(
            P(("row", "col"), None),
            P(("row", "col"), None),
            P("row", "col", None, None, None),
            P(),
            P(),
            P(),
        ),
        check_vma=False,
    )
```

```python
import functools

import jax
import jax.numpy as jnp
from jax import lax
from jax.experimental import pallas as pl
from jax.experimental.pallas import tpu as pltpu
from jax.sharding import PartitionSpec as P

F32 = jnp.float32
BF16 = jnp.bfloat16
ANY = pl.BlockSpec(memory_space=pl.ANY)
SMEM = pl.BlockSpec(memory_space=pltpu.SMEM)
VMEM = pl.BlockSpec(memory_space=pltpu.VMEM)
MIB = 1 << 20
TN = (((0,), (0,)), ((), ()))
NT = (((1,), (1,)), ((), ()))
PEAK_FLOPS_PER_US = 1153.5e6


LIVE_STEP = 4
GRAD_PLAN = ((3, 0, None), (2, 1, None), (1, 2, "inner"), (1, 3, "outer"), (0, 4, "inner"), (0, 5, "outer"))
SWAP_ORDER = (0, 4, 2, 6, 1, 5, 3, 7)


def params(mib):
    return pltpu.CompilerParams(vmem_limit_bytes=mib * MIB)


def cost(microseconds):
    return pl.CostEstimate(flops=int(microseconds * PEAK_FLOPS_PER_US), bytes_accessed=MIB, transcendentals=0)


def mm(a, b, dims=(((1,), (0,)), ((), ()))):
    return lax.dot_general(a, b, dims, preferred_element_type=F32)


def block_at(index, block):
    return pl.ds(pl.multiple_of(index * block, block), block)


def load_pieces(pieces, dst, sem, first):
    copies = []
    offset = 0
    for index, piece in enumerate(pieces):
        copy = pltpu.make_async_copy(
            piece, dst.at[pl.ds(offset, piece.shape[0])], sem.at[first + index]
        )
        copy.start()
        copies.append(copy)
        offset += piece.shape[0]
    return copies


def forward_kernel(outputs, n_pieces, cols, order, *refs):
    pieces, tiles = refs[:n_pieces], refs[n_pieces]
    outs = refs[n_pieces + 1 : n_pieces + 1 + len(outputs)]
    nodes_v, tiles_v, sem, tile_sem = refs[n_pieces + 1 + len(outputs) :]
    rows = outs[0].shape[0] // len(outputs[0])
    slots, block = tiles.shape[1], tiles.shape[2]
    blocks = rows // block
    copies = load_pieces(pieces, nodes_v, sem, 0)
    places = [(pick, out, index) for out, picks in zip(outs, outputs) for index, pick in enumerate(picks)]
    tile_copies = []
    for place, (pick, _, _) in enumerate(places):
        copy = pltpu.make_async_copy(
            tiles.at[pl.ds(order[pick] * blocks, blocks)],
            tiles_v.at[pl.ds(place * blocks, blocks)],
            tile_sem.at[place],
        )
        copy.start()
        tile_copies.append(copy)
    for copy in copies:
        copy.wait()
    for place, (pick, out, index) in enumerate(places):
        tile_copies[place].wait()
        first = order[pick] * blocks

        def step(i, carry, first=first, out=out, index=index, place=place):
            row = first + i
            parts = []
            for pair in range(slots // 2):
                both = (2 * pair, 2 * pair + 1)
                tile = jnp.concatenate([tiles_v[place * blocks + i, slot] for slot in both], axis=1)
                node = jnp.concatenate(
                    [nodes_v[block_at(cols[row * slots + slot], block)] for slot in both], axis=0
                )
                parts.append(mm(tile, node))
            value = parts[0]
            for part in parts[1:]:
                value = value + part
            out[block_at(index * blocks + i, block)] = value.astype(BF16)
            return carry

        lax.fori_loop(0, blocks, step, 0, unroll=4)


def forward_call(cols, order, pieces, tiles, outputs, rows):
    width = pieces[0].shape[1]
    gathered = sum(piece.shape[0] for piece in pieces)
    slots, block = tiles.shape[1], tiles.shape[2]
    n_picks = sum(len(picks) for picks in outputs)
    return pl.pallas_call(
        functools.partial(forward_kernel, outputs, len(pieces)),
        out_shape=[jax.ShapeDtypeStruct((len(picks) * rows, width), BF16) for picks in outputs],
        in_specs=[SMEM, SMEM] + [ANY] * (len(pieces) + 1),
        out_specs=[VMEM] * len(outputs),
        scratch_shapes=[
            pltpu.VMEM((gathered, width), BF16),
            pltpu.VMEM((n_picks * (rows // block),) + tiles.shape[1:], BF16),
            pltpu.SemaphoreType.DMA((len(pieces),)),
            pltpu.SemaphoreType.DMA((n_picks,)),
        ],
        compiler_params=params(16 if gathered <= 8192 else 40),
        cost_estimate=cost(2.0),
        name="partial_messages",
    )(cols, order, *pieces, tiles)


def mlp_kernel(kinds, middle, nodes, cot, *refs):
    n_parts = sum(len(chunk) for chunk in kinds)
    parts = refs[:n_parts]
    w_in, bias, w_out, gain, shift, updated, gpre_o, act_o, gproj_o, msg_o, vec = refs[
        n_parts : n_parts + 11
    ]
    gmsgs = refs[n_parts + 11 :]
    width = nodes.shape[1]
    inner = middle[0] > 0
    messages = []
    place = 0
    for chunk in kinds:
        total = None
        for kind in chunk:
            term = parts[place][...].astype(F32)
            place += 1
            if kind == "inner":
                term = jnp.where(inner, term, 0.0)
            total = term if total is None else total + term
        messages.append(total.astype(BF16))
    message = jnp.concatenate(messages, axis=1) if len(messages) > 1 else messages[0]
    node = nodes[...]
    pre = mm(node, w_in[:width]) + mm(message, w_in[width:]) + bias[...]
    sig = jax.nn.sigmoid(pre)
    act = (pre * sig).astype(BF16)
    proj = mm(act, w_out[...])
    mean = jnp.mean(proj, axis=-1, keepdims=True)
    var = jnp.mean((proj - mean) ** 2, axis=-1, keepdims=True)
    rstd = 1.0 / jnp.sqrt(var + 1e-05)
    normed = (proj - mean) * rstd
    updated[...] = (node.astype(F32) + normed * gain[...] + shift[...]).astype(BF16)
    grad_out = cot[...].astype(F32)
    gscaled = grad_out * gain[...]
    gproj = (
        (
            gscaled
            - jnp.mean(gscaled, axis=-1, keepdims=True)
            - normed * jnp.mean(gscaled * normed, axis=-1, keepdims=True)
        )
        * rstd
    ).astype(BF16)
    gact = mm(gproj, w_out[...], NT)
    gpre = gact * sig * (1.0 + pre * (1.0 - sig))
    gpre_b = gpre.astype(BF16)
    gmsg = mm(gpre_b, w_in[width:], NT).astype(BF16)
    part = width // len(gmsgs)
    for index, out in enumerate(gmsgs):
        out[...] = gmsg[:, index * part : (index + 1) * part]
    gpre_o[...] = gpre_b
    act_o[...] = act
    gproj_o[...] = gproj
    msg_o[...] = message

    @pl.when(pl.program_id(0) == 0)
    def _():
        vec[...] = jnp.zeros_like(vec)

    vec[0:1] += jnp.sum(gpre, axis=0, keepdims=True)
    vec[1:2] += jnp.sum(grad_out * normed, axis=0, keepdims=True)
    vec[2:3] += jnp.sum(grad_out, axis=0, keepdims=True)


def mlp_call(middle, nodes, cot, parts, kinds, w_in, bias, w_out, gain, shift):
    rows, width = nodes.shape
    step = min(rows, 256)

    def blocked(array):
        return pl.BlockSpec((step, array.shape[1]), lambda i: (i, 0))

    def whole(array):
        return pl.BlockSpec(array.shape, lambda i: (0, 0))

    flat = [term for chunk in parts for term in chunk]
    row_like = jax.ShapeDtypeStruct((rows, width), BF16)
    chunk_like = jax.ShapeDtypeStruct((rows, width // len(parts)), BF16)
    outs = [row_like] * 5 + [jax.ShapeDtypeStruct((8, width), F32)] + [chunk_like] * len(parts)
    weights = (w_in, bias, w_out, gain, shift)
    result = pl.pallas_call(
        functools.partial(mlp_kernel, kinds),
        grid=(rows // step,),
        out_shape=outs,
        in_specs=[SMEM] + [blocked(a) for a in (nodes, cot, *flat)] + [whole(a) for a in weights],
        out_specs=[blocked(a) for a in outs[:5]] + [whole(outs[5])] + [blocked(a) for a in outs[6:]],
        compiler_params=params(20),
        cost_estimate=cost(5.0),
        name="mlp",
    )(middle, nodes, cot, *flat, *weights)
    return result[:6], result[6:]


def weight_kernel(factor, pieces, mine, nodes, msg, act, gpre, gproj, cot, w_in, vec, out, direct, grads):
    width = nodes.shape[1]

    @pl.when(pl.program_id(0) == 0)
    def _():
        grads[...] = jnp.zeros_like(grads)
        grads[3 * width : 3 * width + 8] = vec[...] * factor

    gpre_b = gpre[...]
    grads[:width] += mm(nodes[...], gpre_b, TN) * factor
    grads[width : 2 * width] += mm(msg[...], gpre_b, TN) * factor
    grads[2 * width : 3 * width] += mm(act[...], gproj[...], TN) * factor
    direct[...] = cot[...].astype(F32) + mm(gpre_b, w_in[:width], NT)

    @pl.when(pl.program_id(0) == pl.num_programs(0) - 1)
    def _():
        if pieces == 1:
            out[...] = grads[: out.shape[0]]
        else:
            rows = grads.shape[0] // pieces
            for place, member in enumerate(SWAP_ORDER):
                where = pl.ds(pl.multiple_of((mine[0] ^ member) * rows, 8), rows)
                out[place * rows : (place + 1) * rows] = grads[where]


def weight_call(factor, pieces, mine, nodes, msg, act, gpre, gproj, cot, w_in, vec):
    rows, width = nodes.shape
    step = min(rows, 256)
    blocked = pl.BlockSpec((step, width), lambda i: (i, 0))

    def whole(shape):
        return pl.BlockSpec(shape, lambda i: (0, 0))

    padded = (3 * width + width // 2, width)
    if pieces == 1:
        out = jax.ShapeDtypeStruct((3 * width + 8, width), F32)
    else:
        out = jax.ShapeDtypeStruct(padded, F32)
    return pl.pallas_call(
        functools.partial(weight_kernel, factor, pieces),
        grid=(rows // step,),
        out_shape=[out, jax.ShapeDtypeStruct((rows, width), F32)],
        in_specs=[SMEM] + [blocked] * 6 + [whole(w_in.shape), whole(vec.shape)],
        out_specs=[whole(out.shape), blocked],
        scratch_shapes=[pltpu.VMEM(padded, F32)],
        compiler_params=params(16),
        cost_estimate=cost(3.0),
        name="weight_grads",
    )(mine, nodes, msg, act, gpre, gproj, cot, w_in, vec)


def unpack_kernel(mine, parts, w_in, w_out, vectors, grads):
    width = w_in.shape[1]
    rows = grads.shape[0] // len(SWAP_ORDER)
    for place, member in enumerate(SWAP_ORDER):
        where = pl.ds(pl.multiple_of((mine[0] ^ member) * rows, 8), rows)
        grads[where] = parts[place * rows : (place + 1) * rows].astype(F32)
    w_in[...] = grads[: 2 * width]
    w_out[...] = grads[2 * width : 3 * width]
    vectors[...] = grads[3 * width : 3 * width + 3]


def unpack_call(mine, parts, width):
    shapes = ((2 * width, width), (width, width), (3, width))
    return pl.pallas_call(
        unpack_kernel,
        out_shape=[jax.ShapeDtypeStruct(shape, F32) for shape in shapes],
        in_specs=[SMEM, VMEM],
        out_specs=[VMEM] * 3,
        scratch_shapes=[pltpu.VMEM((3 * width + width // 2, width), F32)],
        compiler_params=params(16),
        cost_estimate=cost(2.0),
        name="weight_unpack",
    )(mine, parts)


def grad_jobs(rows, refs, dst, sem, order, middle, groups=None):
    if len(refs) == 1:
        return [(None, pltpu.make_async_copy(refs[0], dst, sem.at[0]))]
    conditions = {None: None, "inner": middle[0] > 0, "outer": middle[0] == 0}
    jobs = []
    for group, index, kind in GRAD_PLAN:
        if groups is None:
            where = block_at(order[group], rows)
        elif group in groups:
            where = pl.ds(groups.index(group) * rows, rows)
        else:
            continue
        copy = pltpu.make_async_copy(refs[index], dst.at[where], sem.at[index])
        jobs.append((conditions[kind], copy))
    return jobs


def run_jobs(jobs, verb):
    for condition, copy in jobs:
        if condition is None:
            getattr(copy, verb)()
        else:
            pl.when(condition)(getattr(copy, verb))


def for_live(found, entry):
    def several(i, carry):
        for index in range(LIVE_STEP):
            entry(i * LIVE_STEP + index)
        return carry

    def one(i, carry):
        entry(i)
        return carry

    full = found // LIVE_STEP
    lax.fori_loop(0, full, several, 0)
    lax.fori_loop(full * LIVE_STEP, found, one, 0)


def back_kernel(rows, slots, n_grads, n_after, out_pieces, cols, counts, order, middle, *refs):
    grads, tiles = refs[:n_grads], refs[n_grads]
    refs = refs[n_grads + 1 + n_after :]
    outs = refs[: len(out_pieces)]
    grad_v, tiles_v, acc, live, sem, tile_sem = refs[len(out_pieces) :]
    n_tiles, block = tiles.shape[:2]
    jobs = grad_jobs(rows, grads, grad_v, sem, order, middle)
    run_jobs(jobs, "start")
    tile_copy = pltpu.make_async_copy(tiles, tiles_v, tile_sem.at[0])
    tile_copy.start()
    acc[...] = jnp.zeros_like(acc)

    def collect(row, found):
        count = counts[row]
        for slot in range(slots):
            live[found] = row * slots + slot
            found = found + (slot < count).astype(jnp.int32)
        return found

    found = lax.fori_loop(0, n_tiles // slots, collect, jnp.int32(0))
    run_jobs(jobs, "wait")
    tile_copy.wait()

    def entry(place):
        tile_index = live[place]
        part = mm(tiles_v[tile_index], grad_v[block_at(tile_index // slots, block)], TN)
        acc[block_at(cols[tile_index], block)] += part

    for_live(found, entry)
    piece = acc.shape[0] // sum(len(members) for members in out_pieces)
    for out, members in zip(outs, out_pieces):
        for index, member in enumerate(members):
            out[pl.ds(index * piece, piece)] = acc[pl.ds(member * piece, piece)].astype(BF16)


def back_call(cols, counts, order, middle, grads, tiles, total, gathered, out_pieces, after=()):
    rows, width = grads[0].shape
    rows = total if len(grads) == 1 else rows
    row_blocks, slots, block = tiles.shape[:3]
    piece = gathered // sum(len(members) for members in out_pieces)
    return pl.pallas_call(
        functools.partial(back_kernel, rows, slots, len(grads), len(after), out_pieces),
        out_shape=[jax.ShapeDtypeStruct((len(m) * piece, width), BF16) for m in out_pieces],
        in_specs=[SMEM] * 4 + [ANY] * (len(grads) + 1 + len(after)),
        out_specs=[VMEM] * len(out_pieces),
        scratch_shapes=[
            pltpu.VMEM((total, width), BF16),
            pltpu.VMEM((row_blocks * slots, block, block), BF16),
            pltpu.VMEM((gathered, width), F32),
            pltpu.SMEM((row_blocks * slots + 8,), jnp.int32),
            pltpu.SemaphoreType.DMA((len(grads),)),
            pltpu.SemaphoreType.DMA((1,)),
        ],
        compiler_params=params(24 if gathered <= 8192 else 56),
        cost_estimate=cost(5.0),
        name="back_terms",
    )(cols, counts, order, middle, *grads, tiles.reshape(row_blocks * slots, block, block), *after)


def tile_grad_kernel(
    rows, slots, n_grads, n_pieces, n_chunks, n_after, groups, cols, counts, order, middle, *refs
):
    grads = refs[: n_grads * n_chunks]
    refs = refs[n_grads * n_chunks :]
    pieces = refs[: n_pieces * n_chunks]
    out, grad_v, nodes_v, tiles_v, live, source, sem, piece_sem, out_sem = refs[n_pieces * n_chunks + n_after :]
    block = out.shape[1]
    width = nodes_v.shape[1]
    part = width // n_chunks
    scale = float(width) ** -0.5
    blocks = grad_v.shape[0] // (block * len(groups))
    jobs, copies = [], []
    for chunk in range(n_chunks):
        columns = pl.ds(chunk * part, part)
        jobs += grad_jobs(
            rows,
            grads[chunk * n_grads : (chunk + 1) * n_grads],
            grad_v.at[:, columns],
            sem.at[chunk],
            order,
            middle,
            groups,
        )
        copies += load_pieces(
            pieces[chunk * n_pieces : (chunk + 1) * n_pieces],
            nodes_v.at[:, columns],
            piece_sem.at[chunk],
            0,
        )
    run_jobs(jobs, "start")
    tiles_v[...] = jnp.zeros_like(tiles_v)
    found = jnp.int32(0)
    for index, group in enumerate(groups):
        first = order[group] * blocks

        def collect(i, found, first=first, index=index):
            row = first + i
            count = counts[row]
            for slot in range(slots):
                live[found] = (index * blocks + i) * slots + slot
                source[found] = cols[row * slots + slot]
                found = found + (slot < count).astype(jnp.int32)
            return found

        found = lax.fori_loop(0, blocks, collect, found)
    run_jobs(jobs, "wait")
    for copy in copies:
        copy.wait()

    def entry(place):
        tile_index = live[place]
        grad = grad_v[block_at(tile_index // slots, block)]
        node = nodes_v[block_at(source[place], block)]
        tiles_v[tile_index] = (mm(grad, node, NT) * scale).astype(BF16)

    for_live(found, entry)
    size = blocks * slots
    copies = []
    for index, group in enumerate(groups):
        copy = pltpu.make_async_copy(
            tiles_v.at[pl.ds(index * size, size)],
            out.at[pl.ds(order[group] * size, size)],
            out_sem.at[index],
        )
        copy.start()
        copies.append(copy)
    for copy in copies:
        copy.wait()


def tile_grad_call(cols, counts, order, middle, grads, pieces, shape, rows, groups, base=None, after=()):
    row_blocks, slots, block = shape[:3]
    chunks = len(grads)
    width = grads[0][0].shape[1] * chunks
    gathered = sum(piece.shape[0] for piece in pieces[0])
    flat = [a for chunk in grads for a in chunk] + [a for chunk in pieces for a in chunk]
    after = after if base is None else (base,) + tuple(after)
    entries = len(groups) * rows // block * slots
    return pl.pallas_call(
        functools.partial(
            tile_grad_kernel, rows, slots, len(grads[0]), len(pieces[0]), chunks, len(after), groups
        ),
        out_shape=jax.ShapeDtypeStruct((row_blocks * slots, block, block), BF16),
        in_specs=[SMEM] * 4 + [ANY] * (len(flat) + len(after)),
        out_specs=ANY,
        input_output_aliases={} if base is None else {4 + len(flat): 0},
        scratch_shapes=[
            pltpu.VMEM((len(groups) * rows, width), BF16),
            pltpu.VMEM((gathered, width), BF16),
            pltpu.VMEM((entries, block, block), BF16),
            pltpu.SMEM((entries + 8,), jnp.int32),
            pltpu.SMEM((entries + 8,), jnp.int32),
            pltpu.SemaphoreType.DMA((chunks, len(grads[0]))),
            pltpu.SemaphoreType.DMA((chunks, len(pieces[0]))),
            pltpu.SemaphoreType.DMA((len(groups),)),
        ],
        compiler_params=params(16 if gathered <= 8192 else 40),
        cost_estimate=cost(4.0),
        name="tile_grads",
    )(cols, counts, order, middle, *flat, *after)


def add(*terms):
    value = terms[0].astype(F32)
    for term in terms[1:]:
        value = value + term.astype(F32)
    return value.astype(BF16)


def swap(value, bit):
    return lax.ppermute(value, "row", [(i, i ^ bit) for i in range(8)])


def outer_swap(value):
    return lax.ppermute(value, "col", [(0, 1), (1, 0), (2, 3), (3, 2)])


def mirror_swap(value):
    return lax.ppermute(value, "col", [(0, 3), (3, 0), (1, 2), (2, 1)])


def inner_swap(value):
    return lax.ppermute(value, "col", [(0, 0), (1, 2), (2, 1), (3, 3)])


def held(value, *others):
    return lax.optimization_barrier((value, *others))[0]


def gather_square(nodes):
    pieces = []
    for piece in (nodes, swap(nodes, 2), swap(nodes, 4), swap(nodes, 6)):
        pieces += [piece, swap(piece, 1)]
    return pieces


def pair_sums(even, odd, rows):
    other = swap(odd, 1)
    places = [slice(place * rows, (place + 1) * rows) for place in range(4)]
    return (even[places[0]], other[places[0]]), [add(even[p], other[p]) for p in places[1:]]


def reduce_square(sums):
    return [swap(value, bit) for value, bit in zip(sums, (2, 4, 6))]


def scatter_weights(terms):
    for bit in (1, 2, 4):
        half = terms.shape[0] // 2
        terms = terms[:half] + swap(terms[half:], bit)
    return terms


def level_weights(value):
    value = value + outer_swap(value)
    return value + mirror_swap(value)


def gather_weights(value, width, mine):
    value = value.astype(BF16)
    for bit in (4, 2, 1):
        value = jnp.concatenate([value, swap(value, bit)], axis=0)
    return unpack_call(mine, value, width)


def reduce_line(far, near, pair, own, inner):
    far_in = outer_swap(far)
    near_in = outer_swap(held(near, far_in))
    far_sum = inner_swap(add(far, far_in))
    near_sum = inner_swap(add(near, near_in))
    pair_in = outer_swap(add(pair, jnp.where(inner, far_sum, jnp.zeros_like(far_sum))))
    return own, pair_in, near_sum


def reduce_line_joint(both, pair, own, inner):
    rows = own.shape[0]
    both_in = outer_swap(both)
    both_sum = inner_swap(add(both, both_in))
    far_sum = both_sum[:rows]
    pair_in = outer_swap(add(pair, jnp.where(inner, far_sum, jnp.zeros_like(far_sum))))
    return (own, pair_in, both_sum[rows:]), both_in


def gather_line(own):
    pair = outer_swap(own)
    near_inner = inner_swap(own)
    far_inner = inner_swap(pair)
    near_outer = outer_swap(near_inner)
    far_outer = outer_swap(far_inner)
    return [own, pair, near_inner, near_outer, far_inner, far_outer]


def body(n_row, n_col, nodes, tiles, tile_col, tile_count, w_in, bias_in, w_out, ln_gain, ln_shift, cotangent):
    rows, width = nodes.shape
    row_blocks, _, slots, block = tiles.shape[:4]
    tile_local = tiles.reshape(row_blocks, slots, block, block)
    cols = tile_col.reshape(row_blocks * slots)
    counts = tile_count.reshape(row_blocks)
    blocks = rows // block
    gathered, total = n_row * rows, n_col * rows
    square_line = n_row == 8 and n_col == 4
    live = lax.broadcasted_iota(jnp.int32, (row_blocks, slots), 1) < counts[:, None]
    tile_live = jnp.where(live[:, :, None, None], tile_local, jnp.zeros_like(tile_local))
    if square_line:
        mine = lax.axis_index("row").astype(jnp.int32)
        cols = ((cols // blocks) ^ mine) * blocks + cols % blocks
        level = lax.axis_index("col").astype(jnp.int32)
        low = level < 2
        order = jnp.stack([jnp.where(low, 3, 0), jnp.where(low, 2, 1), level ^ 1, level]).astype(jnp.int32)
        inner = (level == 1) | (level == 2)
        middle = inner.astype(jnp.int32).reshape(1)
        part = width // 2
        left = gather_square(nodes[:, :part])
        right = gather_square(held(nodes[:, part:], left[2], left[4], left[6]))
        pieces = [left, right]
        (both,) = forward_call(cols, order, left, tile_live, ((0, 1),), rows)
        pair, own = forward_call(cols, order, left, tile_live, ((2,), (3,)), rows)
        left_parts, both_in = reduce_line_joint(both, pair, own, inner)
        far, near = forward_call(cols, order, right, tile_live, ((0,), (1,)), rows)
        pair, own = forward_call(cols, order, right, tile_live, ((2,), (3,)), rows)
        parts = [left_parts, reduce_line(held(far, both_in), near, pair, own, inner)]
        kinds = [("all", "all", "inner")] * 2
    else:
        order = jnp.arange(n_col, dtype=jnp.int32)
        middle = jnp.zeros((1,), jnp.int32)
        pieces = [[lax.all_gather(nodes, "row", axis=0, tiled=True)]]
        (partial,) = forward_call(cols, order, pieces[0], tile_live, (tuple(range(n_col)),), rows)
        parts = [[lax.psum_scatter(partial, "col", scatter_dimension=0, tiled=True)]]
        kinds = [("all",)]
    vectors = [v.reshape(1, width) for v in (bias_in, ln_gain, ln_shift)]
    (updated, gpre_b, act, gproj, message, vec), gmsgs = mlp_call(
        middle, nodes, cotangent, parts, kinds, w_in, vectors[0], w_out, vectors[1], vectors[2]
    )
    factor = float(rows * n_row * n_col) ** -0.5
    mine = lax.axis_index("row").astype(jnp.int32).reshape(1)
    weight_terms, direct = weight_call(
        factor, n_row if square_line else 1, mine, nodes, message, act, gpre_b, gproj, cotangent, w_in, vec
    )
    if square_line:
        halves = ((1, 3, 5, 7), (0, 2, 4, 6))
        first = gather_line(gmsgs[0])
        second = gather_line(held(gmsgs[1], first[4]))
        grads = [first, second]
        row_weights = scatter_weights(weight_terms)
        odd, even = back_call(
            cols, counts, order, middle, first, tile_live, total, gathered, halves,
            (second[1], second[2], row_weights),
        )
        own_terms, sums = pair_sums(even, odd, rows)
        near_grads = tile_grad_call(
            cols, counts, order, middle, [chunk[:2] for chunk in grads], pieces, tile_local.shape, rows, (3, 2),
            after=(odd,),
        )
        all_weights = level_weights(row_weights)
        odd, even = back_call(
            cols, counts, order, middle, second, tile_live, total, gathered, halves,
            (*sums, all_weights, near_grads),
        )
        left_terms = (*own_terms, *reduce_square(sums))
        own_terms, sums = pair_sums(even, odd, rows)
        right_terms = (*own_terms, *reduce_square(sums))
        weights = gather_weights(all_weights, width, mine)
        back = jnp.concatenate(
            [sum(term.astype(F32) for term in terms) for terms in (left_terms, right_terms)], axis=1
        )
        grad_tiles = tile_grad_call(
            cols, counts, order, middle, grads, pieces, tile_local.shape, rows, (1, 0), near_grads, sums
        )
    else:
        grads = [[lax.all_gather(gmsgs[0], "col", axis=0, tiled=True)]]
        weight_sums = lax.psum(weight_terms, ("row", "col"))
        weights = (
            weight_sums[: 2 * width],
            weight_sums[2 * width : 3 * width],
            weight_sums[3 * width : 3 * width + 3],
        )
        (terms,) = back_call(
            cols, counts, order, middle, grads[0], tile_live, total, gathered, (tuple(range(n_row)),)
        )
        back = lax.psum_scatter(terms, "row", scatter_dimension=0, tiled=True).astype(F32)
        grad_tiles = tile_grad_call(
            cols, counts, order, middle, grads, pieces, tile_local.shape, rows, tuple(range(n_col))
        )
    grad_nodes = (direct + back).astype(BF16)
    grad_tiles = grad_tiles.reshape(tiles.shape)
    return (updated, grad_nodes, grad_tiles, *weights)


def solution(mesh):
    placed = (
        P(("row", "col"), None),
        P("row", "col", None, None, None),
        P("row", "col", None),
        P("row", "col"),
        P(),
        P(),
        P(),
        P(),
        P(),
        P(("row", "col"), None),
    )
    return jax.shard_map(
        functools.partial(body, mesh.shape["row"], mesh.shape["col"]),
        mesh=mesh,
        in_specs=placed,
        out_specs=(
            P(("row", "col"), None),
            P(("row", "col"), None),
            P("row", "col", None, None, None),
            P(),
            P(),
            P(),
        ),
        check_vma=False,
    )
```

```python
import functools

import jax
import jax.numpy as jnp
from jax import lax
from jax.experimental import pallas as pl
from jax.experimental.pallas import tpu as pltpu
from jax.sharding import PartitionSpec as P

F32 = jnp.float32
BF16 = jnp.bfloat16
ANY = pl.BlockSpec(memory_space=pl.ANY)
HBM = pl.BlockSpec(memory_space=pltpu.HBM)
SMEM = pl.BlockSpec(memory_space=pltpu.SMEM)
VMEM = pl.BlockSpec(memory_space=pltpu.VMEM)
MIB = 1 << 20
TN = (((0,), (0,)), ((), ()))
NT = (((1,), (1,)), ((), ()))
PEAK_FLOPS_PER_US = 1153.5e6


LIVE_STEP = 4
GRAD_PLAN = ((3, 0, None), (2, 1, None), (1, 2, "inner"), (1, 3, "outer"), (0, 4, "inner"), (0, 5, "outer"))
SWAP_ORDER = (0, 4, 2, 6, 1, 5, 3, 7)


def params(mib):
    return pltpu.CompilerParams(vmem_limit_bytes=mib * MIB)


def cost(microseconds):
    return pl.CostEstimate(flops=int(microseconds * PEAK_FLOPS_PER_US), bytes_accessed=MIB, transcendentals=0)


def mm(a, b, dims=(((1,), (0,)), ((), ()))):
    return lax.dot_general(a, b, dims, preferred_element_type=F32)


def block_at(index, block):
    return pl.ds(pl.multiple_of(index * block, block), block)


def load_pieces(pieces, dst, sem, first):
    copies = []
    offset = 0
    for index, piece in enumerate(pieces):
        copy = pltpu.make_async_copy(
            piece, dst.at[pl.ds(offset, piece.shape[0])], sem.at[first + index]
        )
        copy.start()
        copies.append(copy)
        offset += piece.shape[0]
    return copies


def masked_tile(tile, live):
    return jnp.where(live, tile, jnp.zeros_like(tile))


def forward_kernel(outputs, n_pieces, cols, counts, order, *refs):
    pieces, tiles = refs[:n_pieces], refs[n_pieces]
    outs = refs[n_pieces + 1 : n_pieces + 1 + len(outputs)]
    nodes_v, tiles_v, sem, tile_sem = refs[n_pieces + 1 + len(outputs) :]
    rows = outs[0].shape[0] // len(outputs[0])
    slots, block = tiles.shape[1], tiles.shape[2]
    blocks = rows // block
    copies = load_pieces(pieces, nodes_v, sem, 0)
    places = [(pick, out, index) for out, picks in zip(outs, outputs) for index, pick in enumerate(picks)]
    tile_copies = []
    for place, (pick, _, _) in enumerate(places):
        copy = pltpu.make_async_copy(
            tiles.at[pl.ds(order[pick] * blocks, blocks)],
            tiles_v.at[pl.ds(place * blocks, blocks)],
            tile_sem.at[place],
        )
        copy.start()
        tile_copies.append(copy)
    for copy in copies:
        copy.wait()
    for place, (pick, out, index) in enumerate(places):
        tile_copies[place].wait()
        first = order[pick] * blocks

        def step(i, carry, first=first, out=out, index=index, place=place):
            row = first + i
            count = counts[row]
            parts = []
            for pair in range(slots // 2):
                both = (2 * pair, 2 * pair + 1)
                tile = jnp.concatenate(
                    [masked_tile(tiles_v[place * blocks + i, slot], slot < count) for slot in both], axis=1
                )
                node = jnp.concatenate(
                    [nodes_v[block_at(cols[row * slots + slot], block)] for slot in both], axis=0
                )
                parts.append(mm(tile, node))
            value = parts[0]
            for part in parts[1:]:
                value = value + part
            out[block_at(index * blocks + i, block)] = value.astype(BF16)
            return carry

        lax.fori_loop(0, blocks, step, 0, unroll=4)


def forward_call(cols, counts, order, pieces, tiles, outputs, rows):
    width = pieces[0].shape[1]
    gathered = sum(piece.shape[0] for piece in pieces)
    slots, block = tiles.shape[1], tiles.shape[2]
    n_picks = sum(len(picks) for picks in outputs)
    return pl.pallas_call(
        functools.partial(forward_kernel, outputs, len(pieces)),
        out_shape=[jax.ShapeDtypeStruct((len(picks) * rows, width), BF16) for picks in outputs],
        in_specs=[SMEM] * 3 + [ANY] * len(pieces) + [HBM],
        out_specs=[VMEM] * len(outputs),
        scratch_shapes=[
            pltpu.VMEM((gathered, width), BF16),
            pltpu.VMEM((n_picks * (rows // block),) + tiles.shape[1:], BF16),
            pltpu.SemaphoreType.DMA((len(pieces),)),
            pltpu.SemaphoreType.DMA((n_picks,)),
        ],
        compiler_params=params(16 if gathered <= 8192 else 40),
        cost_estimate=cost(2.0),
        name="partial_messages",
    )(cols, counts, order, *pieces, tiles)


def mlp_kernel(kinds, middle, nodes_ref, cot_ref, *refs):
    nodes_v, cot_v, sem = refs[-3:]
    refs = refs[:-3]
    step = pl.program_id(0)
    rows = nodes_v.shape[1]

    def loads(index):
        where = block_at(index, rows)
        return (
            pltpu.make_async_copy(nodes_ref.at[where], nodes_v.at[index], sem.at[0, index]),
            pltpu.make_async_copy(cot_ref.at[where], cot_v.at[index], sem.at[1, index]),
        )

    @pl.when(step == 0)
    def _():
        for index in range(nodes_v.shape[0]):
            for copy in loads(index):
                copy.start()

    for copy in loads(step):
        copy.wait()
    nodes, cot = nodes_v.at[step], cot_v.at[step]
    n_parts = sum(len(chunk) for chunk in kinds)
    parts = refs[:n_parts]
    w_in, bias, w_out, gain, shift, updated, gpre_o, act_o, gproj_o, msg_o, vec = refs[
        n_parts : n_parts + 11
    ]
    gmsgs = refs[n_parts + 11 :]
    width = nodes.shape[1]
    inner = middle[0] > 0
    messages = []
    place = 0
    for chunk in kinds:
        total = None
        for kind in chunk:
            term = parts[place][...].astype(F32)
            place += 1
            if kind == "inner":
                term = jnp.where(inner, term, 0.0)
            total = term if total is None else total + term
        messages.append(total.astype(BF16))
    message = jnp.concatenate(messages, axis=1) if len(messages) > 1 else messages[0]
    node = nodes[...]
    pre = mm(node, w_in[:width]) + mm(message, w_in[width:]) + bias[...]
    sig = jax.nn.sigmoid(pre)
    act = (pre * sig).astype(BF16)
    proj = mm(act, w_out[...])
    mean = jnp.mean(proj, axis=-1, keepdims=True)
    var = jnp.mean((proj - mean) ** 2, axis=-1, keepdims=True)
    rstd = 1.0 / jnp.sqrt(var + 1e-05)
    normed = (proj - mean) * rstd
    updated[...] = (node.astype(F32) + normed * gain[...] + shift[...]).astype(BF16)
    grad_out = cot[...].astype(F32)
    gscaled = grad_out * gain[...]
    gproj = (
        (
            gscaled
            - jnp.mean(gscaled, axis=-1, keepdims=True)
            - normed * jnp.mean(gscaled * normed, axis=-1, keepdims=True)
        )
        * rstd
    ).astype(BF16)
    gact = mm(gproj, w_out[...], NT)
    gpre = gact * sig * (1.0 + pre * (1.0 - sig))
    gpre_b = gpre.astype(BF16)
    gmsg = mm(gpre_b, w_in[width:], NT).astype(BF16)
    part = width // len(gmsgs)
    for index, out in enumerate(gmsgs):
        out[...] = gmsg[:, index * part : (index + 1) * part]
    gpre_o[...] = gpre_b
    act_o[...] = act
    gproj_o[...] = gproj
    msg_o[...] = message

    @pl.when(pl.program_id(0) == 0)
    def _():
        vec[...] = jnp.zeros_like(vec)

    vec[0:1] += jnp.sum(gpre, axis=0, keepdims=True)
    vec[1:2] += jnp.sum(grad_out * normed, axis=0, keepdims=True)
    vec[2:3] += jnp.sum(grad_out, axis=0, keepdims=True)


def mlp_call(middle, nodes, cot, parts, kinds, w_in, bias, w_out, gain, shift):
    rows, width = nodes.shape
    step = min(rows, 256)

    def blocked(array):
        return pl.BlockSpec((step, array.shape[1]), lambda i: (i, 0))

    def whole(array):
        return pl.BlockSpec(array.shape, lambda i: (0, 0))

    flat = [term for chunk in parts for term in chunk]
    row_like = jax.ShapeDtypeStruct((rows, width), BF16)
    chunk_like = jax.ShapeDtypeStruct((rows, width // len(parts)), BF16)
    outs = [row_like] * 5 + [jax.ShapeDtypeStruct((8, width), F32)] + [chunk_like] * len(parts)
    weights = (w_in, bias, w_out, gain, shift)
    result = pl.pallas_call(
        functools.partial(mlp_kernel, kinds),
        grid=(rows // step,),
        out_shape=outs,
        in_specs=[SMEM, HBM, HBM] + [blocked(a) for a in flat] + [whole(a) for a in weights],
        out_specs=[blocked(a) for a in outs[:5]] + [whole(outs[5])] + [blocked(a) for a in outs[6:]],
        scratch_shapes=[
            pltpu.VMEM((rows // step, step, width), BF16),
            pltpu.VMEM((rows // step, step, width), BF16),
            pltpu.SemaphoreType.DMA((2, rows // step)),
        ],
        compiler_params=params(24),
        cost_estimate=cost(5.0),
        name="mlp",
    )(middle, nodes, cot, *flat, *weights)
    return result[:6], result[6:]


def weight_kernel(factor, pieces, mine, nodes, msg, act, gpre, gproj, cot, w_in, vec, out, direct, grads):
    width = nodes.shape[1]

    @pl.when(pl.program_id(0) == 0)
    def _():
        grads[...] = jnp.zeros_like(grads)
        grads[3 * width : 3 * width + 8] = vec[...] * factor

    gpre_b = gpre[...]
    grads[:width] += mm(nodes[...], gpre_b, TN) * factor
    grads[width : 2 * width] += mm(msg[...], gpre_b, TN) * factor
    grads[2 * width : 3 * width] += mm(act[...], gproj[...], TN) * factor
    direct[...] = cot[...].astype(F32) + mm(gpre_b, w_in[:width], NT)

    @pl.when(pl.program_id(0) == pl.num_programs(0) - 1)
    def _():
        if pieces == 1:
            out[...] = grads[: out.shape[0]]
        else:
            rows = grads.shape[0] // pieces
            for place, member in enumerate(SWAP_ORDER):
                where = pl.ds(pl.multiple_of((mine[0] ^ member) * rows, 8), rows)
                out[place * rows : (place + 1) * rows] = grads[where]


def weight_call(factor, pieces, mine, nodes, msg, act, gpre, gproj, cot, w_in, vec):
    rows, width = nodes.shape
    step = min(rows, 256)
    blocked = pl.BlockSpec((step, width), lambda i: (i, 0))

    def whole(shape):
        return pl.BlockSpec(shape, lambda i: (0, 0))

    padded = (3 * width + width // 2, width)
    if pieces == 1:
        out = jax.ShapeDtypeStruct((3 * width + 8, width), F32)
    else:
        out = jax.ShapeDtypeStruct(padded, F32)
    return pl.pallas_call(
        functools.partial(weight_kernel, factor, pieces),
        grid=(rows // step,),
        out_shape=[out, jax.ShapeDtypeStruct((rows, width), F32)],
        in_specs=[SMEM] + [blocked] * 6 + [whole(w_in.shape), whole(vec.shape)],
        out_specs=[whole(out.shape), blocked],
        scratch_shapes=[pltpu.VMEM(padded, F32)],
        compiler_params=params(16),
        cost_estimate=cost(3.0),
        name="weight_grads",
    )(mine, nodes, msg, act, gpre, gproj, cot, w_in, vec)


def unpack_kernel(mine, parts, w_in, w_out, vectors, grads):
    width = w_in.shape[1]
    rows = grads.shape[0] // len(SWAP_ORDER)
    for place, member in enumerate(SWAP_ORDER):
        where = pl.ds(pl.multiple_of((mine[0] ^ member) * rows, 8), rows)
        grads[where] = parts[place * rows : (place + 1) * rows].astype(F32)
    w_in[...] = grads[: 2 * width]
    w_out[...] = grads[2 * width : 3 * width]
    vectors[...] = grads[3 * width : 3 * width + 3]


def unpack_call(mine, parts, width):
    shapes = ((2 * width, width), (width, width), (3, width))
    return pl.pallas_call(
        unpack_kernel,
        out_shape=[jax.ShapeDtypeStruct(shape, F32) for shape in shapes],
        in_specs=[SMEM, VMEM],
        out_specs=[VMEM] * 3,
        scratch_shapes=[pltpu.VMEM((3 * width + width // 2, width), F32)],
        compiler_params=params(16),
        cost_estimate=cost(2.0),
        name="weight_unpack",
    )(mine, parts)


def grad_jobs(rows, refs, dst, sem, order, middle, groups=None):
    if len(refs) == 1:
        return [(None, pltpu.make_async_copy(refs[0], dst, sem.at[0]))]
    conditions = {None: None, "inner": middle[0] > 0, "outer": middle[0] == 0}
    jobs = []
    for group, index, kind in GRAD_PLAN:
        if groups is None:
            where = block_at(order[group], rows)
        elif group in groups:
            where = pl.ds(groups.index(group) * rows, rows)
        else:
            continue
        copy = pltpu.make_async_copy(refs[index], dst.at[where], sem.at[index])
        jobs.append((conditions[kind], copy))
    return jobs


def run_jobs(jobs, verb):
    for condition, copy in jobs:
        if condition is None:
            getattr(copy, verb)()
        else:
            pl.when(condition)(getattr(copy, verb))


def for_live(found, entry):
    def several(i, carry):
        for index in range(LIVE_STEP):
            entry(i * LIVE_STEP + index)
        return carry

    def one(i, carry):
        entry(i)
        return carry

    full = found // LIVE_STEP
    lax.fori_loop(0, full, several, 0)
    lax.fori_loop(full * LIVE_STEP, found, one, 0)


def back_kernel(rows, slots, n_grads, n_after, out_pieces, cols, counts, order, middle, *refs):
    grads, tiles = refs[:n_grads], refs[n_grads]
    refs = refs[n_grads + 1 + n_after :]
    outs = refs[: len(out_pieces)]
    grad_v, tiles_v, acc, live, sem, tile_sem = refs[len(out_pieces) :]
    n_tiles, block = tiles.shape[:2]
    jobs = grad_jobs(rows, grads, grad_v, sem, order, middle)
    run_jobs(jobs, "start")
    tile_copy = pltpu.make_async_copy(tiles, tiles_v, tile_sem.at[0])
    tile_copy.start()
    acc[...] = jnp.zeros_like(acc)

    def collect(row, found):
        count = counts[row]
        for slot in range(slots):
            live[found] = row * slots + slot
            found = found + (slot < count).astype(jnp.int32)
        return found

    found = lax.fori_loop(0, n_tiles // slots, collect, jnp.int32(0))
    run_jobs(jobs, "wait")
    tile_copy.wait()

    def entry(place):
        tile_index = live[place]
        part = mm(tiles_v[tile_index], grad_v[block_at(tile_index // slots, block)], TN)
        acc[block_at(cols[tile_index], block)] += part

    for_live(found, entry)
    piece = acc.shape[0] // sum(len(members) for members in out_pieces)
    for out, members in zip(outs, out_pieces):
        for index, member in enumerate(members):
            out[pl.ds(index * piece, piece)] = acc[pl.ds(member * piece, piece)].astype(BF16)


def back_call(cols, counts, order, middle, grads, tiles, total, gathered, out_pieces, after=()):
    rows, width = grads[0].shape
    rows = total if len(grads) == 1 else rows
    row_blocks, slots, block = tiles.shape[:3]
    piece = gathered // sum(len(members) for members in out_pieces)
    return pl.pallas_call(
        functools.partial(back_kernel, rows, slots, len(grads), len(after), out_pieces),
        out_shape=[jax.ShapeDtypeStruct((len(m) * piece, width), BF16) for m in out_pieces],
        in_specs=[SMEM] * 4 + [ANY] * len(grads) + [HBM] + [ANY] * len(after),
        out_specs=[VMEM] * len(out_pieces),
        scratch_shapes=[
            pltpu.VMEM((total, width), BF16),
            pltpu.VMEM((row_blocks * slots, block, block), BF16),
            pltpu.VMEM((gathered, width), F32),
            pltpu.SMEM((row_blocks * slots + 8,), jnp.int32),
            pltpu.SemaphoreType.DMA((len(grads),)),
            pltpu.SemaphoreType.DMA((1,)),
        ],
        compiler_params=params(28 if gathered <= 8192 else 56),
        cost_estimate=cost(5.0),
        name="back_terms",
    )(cols, counts, order, middle, *grads, tiles.reshape(row_blocks * slots, block, block), *after)


def tile_grad_kernel(
    rows, slots, n_grads, n_pieces, n_chunks, n_after, groups, cols, counts, order, middle, *refs
):
    grads = refs[: n_grads * n_chunks]
    refs = refs[n_grads * n_chunks :]
    pieces = refs[: n_pieces * n_chunks]
    out, grad_v, nodes_v, tiles_v, live, source, sem, piece_sem, out_sem = refs[n_pieces * n_chunks + n_after :]
    block = out.shape[1]
    width = nodes_v.shape[1]
    part = width // n_chunks
    scale = float(width) ** -0.5
    blocks = grad_v.shape[0] // (block * len(groups))
    jobs, copies = [], []
    for chunk in range(n_chunks):
        columns = pl.ds(chunk * part, part)
        jobs += grad_jobs(
            rows,
            grads[chunk * n_grads : (chunk + 1) * n_grads],
            grad_v.at[:, columns],
            sem.at[chunk],
            order,
            middle,
            groups,
        )
        copies += load_pieces(
            pieces[chunk * n_pieces : (chunk + 1) * n_pieces],
            nodes_v.at[:, columns],
            piece_sem.at[chunk],
            0,
        )
    run_jobs(jobs, "start")
    tiles_v[...] = jnp.zeros_like(tiles_v)
    found = jnp.int32(0)
    for index, group in enumerate(groups):
        first = order[group] * blocks

        def collect(i, found, first=first, index=index):
            row = first + i
            count = counts[row]
            for slot in range(slots):
                live[found] = (index * blocks + i) * slots + slot
                source[found] = cols[row * slots + slot]
                found = found + (slot < count).astype(jnp.int32)
            return found

        found = lax.fori_loop(0, blocks, collect, found)
    run_jobs(jobs, "wait")
    for copy in copies:
        copy.wait()

    def entry(place):
        tile_index = live[place]
        grad = grad_v[block_at(tile_index // slots, block)]
        node = nodes_v[block_at(source[place], block)]
        tiles_v[tile_index] = (mm(grad, node, NT) * scale).astype(BF16)

    for_live(found, entry)
    size = blocks * slots
    copies = []
    for index, group in enumerate(groups):
        copy = pltpu.make_async_copy(
            tiles_v.at[pl.ds(index * size, size)],
            out.at[pl.ds(order[group] * size, size)],
            out_sem.at[index],
        )
        copy.start()
        copies.append(copy)
    for copy in copies:
        copy.wait()


def tile_grad_call(cols, counts, order, middle, grads, pieces, shape, rows, groups, base=None, after=()):
    row_blocks, slots, block = shape[:3]
    chunks = len(grads)
    width = grads[0][0].shape[1] * chunks
    gathered = sum(piece.shape[0] for piece in pieces[0])
    flat = [a for chunk in grads for a in chunk] + [a for chunk in pieces for a in chunk]
    after = after if base is None else (base,) + tuple(after)
    entries = len(groups) * rows // block * slots
    return pl.pallas_call(
        functools.partial(
            tile_grad_kernel, rows, slots, len(grads[0]), len(pieces[0]), chunks, len(after), groups
        ),
        out_shape=jax.ShapeDtypeStruct((row_blocks * slots, block, block), BF16),
        in_specs=[SMEM] * 4 + [ANY] * (len(flat) + len(after)),
        out_specs=ANY,
        input_output_aliases={} if base is None else {4 + len(flat): 0},
        scratch_shapes=[
            pltpu.VMEM((len(groups) * rows, width), BF16),
            pltpu.VMEM((gathered, width), BF16),
            pltpu.VMEM((entries, block, block), BF16),
            pltpu.SMEM((entries + 8,), jnp.int32),
            pltpu.SMEM((entries + 8,), jnp.int32),
            pltpu.SemaphoreType.DMA((chunks, len(grads[0]))),
            pltpu.SemaphoreType.DMA((chunks, len(pieces[0]))),
            pltpu.SemaphoreType.DMA((len(groups),)),
        ],
        compiler_params=params(16 if gathered <= 8192 else 40),
        cost_estimate=cost(4.0),
        name="tile_grads",
    )(cols, counts, order, middle, *flat, *after)


def add(*terms):
    value = terms[0].astype(F32)
    for term in terms[1:]:
        value = value + term.astype(F32)
    return value.astype(BF16)


def swap(value, bit):
    return lax.ppermute(value, "row", [(i, i ^ bit) for i in range(8)])


def outer_swap(value):
    return lax.ppermute(value, "col", [(0, 1), (1, 0), (2, 3), (3, 2)])


def mirror_swap(value):
    return lax.ppermute(value, "col", [(0, 3), (3, 0), (1, 2), (2, 1)])


def inner_swap(value):
    return lax.ppermute(value, "col", [(0, 0), (1, 2), (2, 1), (3, 3)])


def held(value, *others):
    return lax.optimization_barrier((value, *others))[0]


def gather_square(nodes):
    pieces = []
    for piece in (nodes, swap(nodes, 2), swap(nodes, 4), swap(nodes, 6)):
        pieces += [piece, swap(piece, 1)]
    return pieces


def pair_sums(even, odd, rows):
    other = swap(odd, 1)
    places = [slice(place * rows, (place + 1) * rows) for place in range(4)]
    return (even[places[0]], other[places[0]]), [add(even[p], other[p]) for p in places[1:]]


def reduce_square(sums):
    return [swap(value, bit) for value, bit in zip(sums, (2, 4, 6))]


def scatter_weights(terms):
    for bit in (1, 2, 4):
        half = terms.shape[0] // 2
        terms = terms[:half] + swap(terms[half:], bit)
    return terms


def level_weights(value):
    value = value + outer_swap(value)
    return value + mirror_swap(value)


def gather_weights(value, width, mine):
    value = value.astype(BF16)
    for bit in (4, 2, 1):
        value = jnp.concatenate([value, swap(value, bit)], axis=0)
    return unpack_call(mine, value, width)


def reduce_line(far, near, pair, own, inner):
    far_in = outer_swap(far)
    near_in = outer_swap(held(near, far_in))
    far_sum = inner_swap(add(far, far_in))
    near_sum = inner_swap(add(near, near_in))
    pair_in = outer_swap(add(pair, jnp.where(inner, far_sum, jnp.zeros_like(far_sum))))
    return own, pair_in, near_sum


def gather_line(own):
    pair = outer_swap(own)
    near_inner = inner_swap(own)
    far_inner = inner_swap(pair)
    near_outer = outer_swap(near_inner)
    far_outer = outer_swap(far_inner)
    return [own, pair, near_inner, near_outer, far_inner, far_outer]


def body(n_row, n_col, nodes, tiles, tile_col, tile_count, w_in, bias_in, w_out, ln_gain, ln_shift, cotangent):
    rows, width = nodes.shape
    row_blocks, _, slots, block = tiles.shape[:4]
    tile_local = tiles.reshape(row_blocks, slots, block, block)
    cols = tile_col.reshape(row_blocks * slots)
    counts = tile_count.reshape(row_blocks)
    blocks = rows // block
    gathered, total = n_row * rows, n_col * rows
    square_line = n_row == 8 and n_col == 4
    if square_line:
        mine = lax.axis_index("row").astype(jnp.int32)
        cols = ((cols // blocks) ^ mine) * blocks + cols % blocks
        level = lax.axis_index("col").astype(jnp.int32)
        low = level < 2
        order = jnp.stack([jnp.where(low, 3, 0), jnp.where(low, 2, 1), level ^ 1, level]).astype(jnp.int32)
        inner = (level == 1) | (level == 2)
        middle = inner.astype(jnp.int32).reshape(1)
        pieces = [gather_square(nodes)]
        far, near = forward_call(cols, counts, order, pieces[0], tile_local, ((0,), (1,)), rows)
        pair, own = forward_call(cols, counts, order, pieces[0], tile_local, ((2,), (3,)), rows)
        parts = [reduce_line(far, near, pair, own, inner)]
        kinds = [("all", "all", "inner")]
    else:
        order = jnp.arange(n_col, dtype=jnp.int32)
        middle = jnp.zeros((1,), jnp.int32)
        pieces = [[lax.all_gather(nodes, "row", axis=0, tiled=True)]]
        (partial,) = forward_call(cols, counts, order, pieces[0], tile_local, (tuple(range(n_col)),), rows)
        parts = [[lax.psum_scatter(partial, "col", scatter_dimension=0, tiled=True)]]
        kinds = [("all",)]
    vectors = [v.reshape(1, width) for v in (bias_in, ln_gain, ln_shift)]
    (updated, gpre_b, act, gproj, message, vec), gmsgs = mlp_call(
        middle, nodes, cotangent, parts, kinds, w_in, vectors[0], w_out, vectors[1], vectors[2]
    )
    factor = float(rows * n_row * n_col) ** -0.5
    mine = lax.axis_index("row").astype(jnp.int32).reshape(1)
    weight_terms, direct = weight_call(
        factor, n_row if square_line else 1, mine, nodes, message, act, gpre_b, gproj, cotangent, w_in, vec
    )
    if square_line:
        halves = ((1, 3, 5, 7), (0, 2, 4, 6))
        grads = [gather_line(gmsgs[0])]
        near_grads = tile_grad_call(
            cols, counts, order, middle, [grads[0][:2]], pieces, tile_local.shape, rows, (3, 2)
        )
        all_weights = level_weights(scatter_weights(weight_terms))
        odd, even = back_call(
            cols, counts, order, middle, grads[0], tile_local, total, gathered, halves, (all_weights, near_grads)
        )
        own_terms, sums = pair_sums(even, odd, rows)
        terms = (*own_terms, *reduce_square(sums))
        weights = gather_weights(all_weights, width, mine)
        back = sum(term.astype(F32) for term in terms)
        grad_tiles = tile_grad_call(
            cols, counts, order, middle, grads, pieces, tile_local.shape, rows, (1, 0), near_grads, sums
        )
    else:
        grads = [[lax.all_gather(gmsgs[0], "col", axis=0, tiled=True)]]
        weight_sums = lax.psum(weight_terms, ("row", "col"))
        weights = (
            weight_sums[: 2 * width],
            weight_sums[2 * width : 3 * width],
            weight_sums[3 * width : 3 * width + 3],
        )
        (terms,) = back_call(
            cols, counts, order, middle, grads[0], tile_local, total, gathered, (tuple(range(n_row)),)
        )
        back = lax.psum_scatter(terms, "row", scatter_dimension=0, tiled=True).astype(F32)
        grad_tiles = tile_grad_call(
            cols, counts, order, middle, grads, pieces, tile_local.shape, rows, tuple(range(n_col))
        )
    grad_nodes = (direct + back).astype(BF16)
    grad_tiles = grad_tiles.reshape(tiles.shape)
    return (updated, grad_nodes, grad_tiles, *weights)


def solution(mesh):
    placed = (
        P(("row", "col"), None),
        P("row", "col", None, None, None),
        P("row", "col", None),
        P("row", "col"),
        P(),
        P(),
        P(),
        P(),
        P(),
        P(("row", "col"), None),
    )
    return jax.shard_map(
        functools.partial(body, mesh.shape["row"], mesh.shape["col"]),
        mesh=mesh,
        in_specs=placed,
        out_specs=(
            P(("row", "col"), None),
            P(("row", "col"), None),
            P("row", "col", None, None, None),
            P(),
            P(),
            P(),
        ),
        check_vma=False,
    )
```

```python
import functools

import jax
import jax.numpy as jnp
from jax import lax
from jax.experimental import pallas as pl
from jax.experimental.pallas import tpu as pltpu
from jax.sharding import PartitionSpec as P

F32 = jnp.float32
BF16 = jnp.bfloat16
ANY = pl.BlockSpec(memory_space=pl.ANY)
HBM = pl.BlockSpec(memory_space=pltpu.HBM)
SMEM = pl.BlockSpec(memory_space=pltpu.SMEM)
VMEM = pl.BlockSpec(memory_space=pltpu.VMEM)
MIB = 1 << 20
TN = (((0,), (0,)), ((), ()))
NT = (((1,), (1,)), ((), ()))
PEAK_FLOPS_PER_US = 1153.5e6


LIVE_STEP = 4
GRAD_PLAN = ((3, 0, None), (2, 1, None), (1, 2, "inner"), (1, 3, "outer"), (0, 4, "inner"), (0, 5, "outer"))
SWAP_ORDER = (0, 4, 2, 6, 1, 5, 3, 7)


def params(mib):
    return pltpu.CompilerParams(vmem_limit_bytes=mib * MIB)


def cost(microseconds):
    return pl.CostEstimate(flops=int(microseconds * PEAK_FLOPS_PER_US), bytes_accessed=MIB, transcendentals=0)


def mm(a, b, dims=(((1,), (0,)), ((), ()))):
    return lax.dot_general(a, b, dims, preferred_element_type=F32)


def block_at(index, block):
    return pl.ds(pl.multiple_of(index * block, block), block)


def load_pieces(pieces, dst, sem, first):
    copies = []
    offset = 0
    for index, piece in enumerate(pieces):
        copy = pltpu.make_async_copy(
            piece, dst.at[pl.ds(offset, piece.shape[0])], sem.at[first + index]
        )
        copy.start()
        copies.append(copy)
        offset += piece.shape[0]
    return copies


def masked_tile(tile, live):
    return jnp.where(live, tile, jnp.zeros_like(tile))


def forward_kernel(outputs, n_pieces, cols, counts, order, *refs):
    pieces, tiles = refs[:n_pieces], refs[n_pieces]
    outs = refs[n_pieces + 1 : n_pieces + 1 + len(outputs)]
    nodes_v, tiles_v, sem, tile_sem = refs[n_pieces + 1 + len(outputs) :]
    rows = outs[0].shape[0] // len(outputs[0])
    slots, block = tiles.shape[1], tiles.shape[2]
    blocks = rows // block
    copies = load_pieces(pieces, nodes_v, sem, 0)
    places = [(pick, out, index) for out, picks in zip(outs, outputs) for index, pick in enumerate(picks)]
    tile_copies = []
    for place, (pick, _, _) in enumerate(places):
        copy = pltpu.make_async_copy(
            tiles.at[pl.ds(order[pick] * blocks, blocks)],
            tiles_v.at[pl.ds(place * blocks, blocks)],
            tile_sem.at[place],
        )
        copy.start()
        tile_copies.append(copy)
    for copy in copies:
        copy.wait()
    for place, (pick, out, index) in enumerate(places):
        tile_copies[place].wait()
        first = order[pick] * blocks

        def step(i, carry, first=first, out=out, index=index, place=place):
            row = first + i
            count = counts[row]
            parts = []
            for pair in range(slots // 2):
                both = (2 * pair, 2 * pair + 1)
                tile = jnp.concatenate(
                    [masked_tile(tiles_v[place * blocks + i, slot], slot < count) for slot in both], axis=1
                )
                node = jnp.concatenate(
                    [nodes_v[block_at(cols[row * slots + slot], block)] for slot in both], axis=0
                )
                parts.append(mm(tile, node))
            value = parts[0]
            for part in parts[1:]:
                value = value + part
            out[block_at(index * blocks + i, block)] = value.astype(BF16)
            return carry

        lax.fori_loop(0, blocks, step, 0, unroll=4)


def forward_call(cols, counts, order, pieces, tiles, outputs, rows):
    width = pieces[0].shape[1]
    gathered = sum(piece.shape[0] for piece in pieces)
    slots, block = tiles.shape[1], tiles.shape[2]
    n_picks = sum(len(picks) for picks in outputs)
    return pl.pallas_call(
        functools.partial(forward_kernel, outputs, len(pieces)),
        out_shape=[jax.ShapeDtypeStruct((len(picks) * rows, width), BF16) for picks in outputs],
        in_specs=[SMEM] * 3 + [ANY] * len(pieces) + [HBM],
        out_specs=[VMEM] * len(outputs),
        scratch_shapes=[
            pltpu.VMEM((gathered, width), BF16),
            pltpu.VMEM((n_picks * (rows // block),) + tiles.shape[1:], BF16),
            pltpu.SemaphoreType.DMA((len(pieces),)),
            pltpu.SemaphoreType.DMA((n_picks,)),
        ],
        compiler_params=params(60),
        cost_estimate=cost(2.0),
        name="partial_messages",
    )(cols, counts, order, *pieces, tiles)


def mlp_kernel(kinds, middle, nodes, cot, *refs):
    n_parts = sum(len(chunk) for chunk in kinds)
    parts = refs[:n_parts]
    w_in, bias, w_out, gain, shift, updated, gpre_o, act_o, gproj_o, msg_o, vec = refs[
        n_parts : n_parts + 11
    ]
    gmsgs = refs[n_parts + 11 :]
    width = nodes.shape[1]
    inner = middle[0] > 0
    messages = []
    place = 0
    for chunk in kinds:
        total = None
        for kind in chunk:
            term = parts[place][...].astype(F32)
            place += 1
            if kind == "inner":
                term = jnp.where(inner, term, 0.0)
            total = term if total is None else total + term
        messages.append(total.astype(BF16))
    message = jnp.concatenate(messages, axis=1) if len(messages) > 1 else messages[0]
    node = nodes[...]
    pre = mm(node, w_in[:width]) + mm(message, w_in[width:]) + bias[...]
    sig = jax.nn.sigmoid(pre)
    act = (pre * sig).astype(BF16)
    proj = mm(act, w_out[...])
    mean = jnp.mean(proj, axis=-1, keepdims=True)
    var = jnp.mean((proj - mean) ** 2, axis=-1, keepdims=True)
    rstd = 1.0 / jnp.sqrt(var + 1e-05)
    normed = (proj - mean) * rstd
    updated[...] = (node.astype(F32) + normed * gain[...] + shift[...]).astype(BF16)
    grad_out = cot[...].astype(F32)
    gscaled = grad_out * gain[...]
    gproj = (
        (
            gscaled
            - jnp.mean(gscaled, axis=-1, keepdims=True)
            - normed * jnp.mean(gscaled * normed, axis=-1, keepdims=True)
        )
        * rstd
    ).astype(BF16)
    gact = mm(gproj, w_out[...], NT)
    gpre = gact * sig * (1.0 + pre * (1.0 - sig))
    gpre_b = gpre.astype(BF16)
    gmsg = mm(gpre_b, w_in[width:], NT).astype(BF16)
    part = width // len(gmsgs)
    for index, out in enumerate(gmsgs):
        out[...] = gmsg[:, index * part : (index + 1) * part]
    gpre_o[...] = gpre_b
    act_o[...] = act
    gproj_o[...] = gproj
    msg_o[...] = message

    @pl.when(pl.program_id(0) == 0)
    def _():
        vec[...] = jnp.zeros_like(vec)

    vec[0:1] += jnp.sum(gpre, axis=0, keepdims=True)
    vec[1:2] += jnp.sum(grad_out * normed, axis=0, keepdims=True)
    vec[2:3] += jnp.sum(grad_out, axis=0, keepdims=True)


def mlp_call(middle, nodes, cot, parts, kinds, w_in, bias, w_out, gain, shift):
    rows, width = nodes.shape
    step = min(rows, 256)

    def blocked(array):
        return pl.BlockSpec((step, array.shape[1]), lambda i: (i, 0))

    def whole(array):
        return pl.BlockSpec(array.shape, lambda i: (0, 0))

    flat = [term for chunk in parts for term in chunk]
    row_like = jax.ShapeDtypeStruct((rows, width), BF16)
    chunk_like = jax.ShapeDtypeStruct((rows, width // len(parts)), BF16)
    outs = [row_like] * 5 + [jax.ShapeDtypeStruct((8, width), F32)] + [chunk_like] * len(parts)
    weights = (w_in, bias, w_out, gain, shift)
    result = pl.pallas_call(
        functools.partial(mlp_kernel, kinds),
        grid=(rows // step,),
        out_shape=outs,
        in_specs=[SMEM] + [blocked(a) for a in (nodes, cot, *flat)] + [whole(a) for a in weights],
        out_specs=[blocked(a) for a in outs[:5]] + [whole(outs[5])] + [blocked(a) for a in outs[6:]],
        compiler_params=params(40),
        cost_estimate=cost(5.0),
        name="mlp",
    )(middle, nodes, cot, *flat, *weights)
    return result[:6], result[6:]


def weight_kernel(factor, pieces, mine, nodes, msg, act, gpre, gproj, cot, w_in, vec, out, direct, grads):
    width = nodes.shape[1]

    @pl.when(pl.program_id(0) == 0)
    def _():
        grads[...] = jnp.zeros_like(grads)
        grads[3 * width : 3 * width + 8] = vec[...] * factor

    gpre_b = gpre[...]
    grads[:width] += mm(nodes[...], gpre_b, TN) * factor
    grads[width : 2 * width] += mm(msg[...], gpre_b, TN) * factor
    grads[2 * width : 3 * width] += mm(act[...], gproj[...], TN) * factor
    direct[...] = cot[...].astype(F32) + mm(gpre_b, w_in[:width], NT)

    @pl.when(pl.program_id(0) == pl.num_programs(0) - 1)
    def _():
        if pieces == 1:
            out[...] = grads[: out.shape[0]]
        else:
            rows = grads.shape[0] // pieces
            for place, member in enumerate(SWAP_ORDER):
                where = pl.ds(pl.multiple_of((mine[0] ^ member) * rows, 8), rows)
                out[place * rows : (place + 1) * rows] = grads[where]


def weight_call(factor, pieces, mine, nodes, msg, act, gpre, gproj, cot, w_in, vec):
    rows, width = nodes.shape
    step = min(rows, 256)
    blocked = pl.BlockSpec((step, width), lambda i: (i, 0))

    def whole(shape):
        return pl.BlockSpec(shape, lambda i: (0, 0))

    padded = (3 * width + width // 2, width)
    if pieces == 1:
        out = jax.ShapeDtypeStruct((3 * width + 8, width), F32)
    else:
        out = jax.ShapeDtypeStruct(padded, F32)
    return pl.pallas_call(
        functools.partial(weight_kernel, factor, pieces),
        grid=(rows // step,),
        out_shape=[out, jax.ShapeDtypeStruct((rows, width), F32)],
        in_specs=[SMEM] + [blocked] * 6 + [whole(w_in.shape), whole(vec.shape)],
        out_specs=[whole(out.shape), blocked],
        scratch_shapes=[pltpu.VMEM(padded, F32)],
        compiler_params=params(40),
        cost_estimate=cost(3.0),
        name="weight_grads",
    )(mine, nodes, msg, act, gpre, gproj, cot, w_in, vec)


def unpack_kernel(mine, parts, w_in, w_out, vectors, grads):
    width = w_in.shape[1]
    rows = grads.shape[0] // len(SWAP_ORDER)
    for place, member in enumerate(SWAP_ORDER):
        where = pl.ds(pl.multiple_of((mine[0] ^ member) * rows, 8), rows)
        grads[where] = parts[place * rows : (place + 1) * rows].astype(F32)
    w_in[...] = grads[: 2 * width]
    w_out[...] = grads[2 * width : 3 * width]
    vectors[...] = grads[3 * width : 3 * width + 3]


def unpack_call(mine, parts, width):
    shapes = ((2 * width, width), (width, width), (3, width))
    return pl.pallas_call(
        unpack_kernel,
        out_shape=[jax.ShapeDtypeStruct(shape, F32) for shape in shapes],
        in_specs=[SMEM, VMEM],
        out_specs=[VMEM] * 3,
        scratch_shapes=[pltpu.VMEM((3 * width + width // 2, width), F32)],
        compiler_params=params(16),
        cost_estimate=cost(2.0),
        name="weight_unpack",
    )(mine, parts)


def grad_jobs(rows, refs, dst, sem, order, middle, groups=None):
    if len(refs) == 1:
        return [(None, pltpu.make_async_copy(refs[0], dst, sem.at[0]))]
    conditions = {None: None, "inner": middle[0] > 0, "outer": middle[0] == 0}
    jobs = []
    for group, index, kind in GRAD_PLAN:
        if groups is None:
            where = block_at(order[group], rows)
        elif group in groups:
            where = pl.ds(groups.index(group) * rows, rows)
        else:
            continue
        copy = pltpu.make_async_copy(refs[index], dst.at[where], sem.at[index])
        jobs.append((conditions[kind], copy))
    return jobs


def run_jobs(jobs, verb):
    for condition, copy in jobs:
        if condition is None:
            getattr(copy, verb)()
        else:
            pl.when(condition)(getattr(copy, verb))


def for_live(found, entry):
    def several(i, carry):
        for index in range(LIVE_STEP):
            entry(i * LIVE_STEP + index)
        return carry

    def one(i, carry):
        entry(i)
        return carry

    full = found // LIVE_STEP
    lax.fori_loop(0, full, several, 0)
    lax.fori_loop(full * LIVE_STEP, found, one, 0)


def back_kernel(rows, slots, n_grads, n_after, out_pieces, cols, counts, order, middle, *refs):
    grads, tiles = refs[:n_grads], refs[n_grads]
    refs = refs[n_grads + 1 + n_after :]
    outs = refs[: len(out_pieces)]
    grad_v, tiles_v, acc, live, sem, tile_sem = refs[len(out_pieces) :]
    n_tiles, block = tiles.shape[:2]
    jobs = grad_jobs(rows, grads, grad_v, sem, order, middle)
    run_jobs(jobs, "start")
    tile_copy = pltpu.make_async_copy(tiles, tiles_v, tile_sem.at[0])
    tile_copy.start()
    acc[...] = jnp.zeros_like(acc)

    def collect(row, found):
        count = counts[row]
        for slot in range(slots):
            live[found] = row * slots + slot
            found = found + (slot < count).astype(jnp.int32)
        return found

    found = lax.fori_loop(0, n_tiles // slots, collect, jnp.int32(0))
    run_jobs(jobs, "wait")
    tile_copy.wait()

    def entry(place):
        tile_index = live[place]
        part = mm(tiles_v[tile_index], grad_v[block_at(tile_index // slots, block)], TN)
        acc[block_at(cols[tile_index], block)] += part

    for_live(found, entry)
    piece = acc.shape[0] // sum(len(members) for members in out_pieces)
    for out, members in zip(outs, out_pieces):
        for index, member in enumerate(members):
            out[pl.ds(index * piece, piece)] = acc[pl.ds(member * piece, piece)].astype(BF16)


def back_call(cols, counts, order, middle, grads, tiles, total, gathered, out_pieces, after=()):
    rows, width = grads[0].shape
    rows = total if len(grads) == 1 else rows
    row_blocks, slots, block = tiles.shape[:3]
    piece = gathered // sum(len(members) for members in out_pieces)
    return pl.pallas_call(
        functools.partial(back_kernel, rows, slots, len(grads), len(after), out_pieces),
        out_shape=[jax.ShapeDtypeStruct((len(m) * piece, width), BF16) for m in out_pieces],
        in_specs=[SMEM] * 4 + [ANY] * len(grads) + [HBM] + [ANY] * len(after),
        out_specs=[VMEM] * len(out_pieces),
        scratch_shapes=[
            pltpu.VMEM((total, width), BF16),
            pltpu.VMEM((row_blocks * slots, block, block), BF16),
            pltpu.VMEM((gathered, width), F32),
            pltpu.SMEM((row_blocks * slots + 8,), jnp.int32),
            pltpu.SemaphoreType.DMA((len(grads),)),
            pltpu.SemaphoreType.DMA((1,)),
        ],
        compiler_params=params(60),
        cost_estimate=cost(5.0),
        name="back_terms",
    )(cols, counts, order, middle, *grads, tiles.reshape(row_blocks * slots, block, block), *after)


def tile_grad_kernel(
    rows, slots, n_grads, n_pieces, n_chunks, n_after, groups, cols, counts, order, middle, *refs
):
    grads = refs[: n_grads * n_chunks]
    refs = refs[n_grads * n_chunks :]
    pieces = refs[: n_pieces * n_chunks]
    out, token, grad_v, nodes_v, tiles_v, live, source, sem, piece_sem, out_sem = refs[n_pieces * n_chunks + n_after :]
    token[...] = jnp.zeros_like(token)
    block = out.shape[1]
    width = nodes_v.shape[1]
    part = width // n_chunks
    scale = float(width) ** -0.5
    blocks = grad_v.shape[0] // (block * len(groups))
    jobs, copies = [], []
    for chunk in range(n_chunks):
        columns = pl.ds(chunk * part, part)
        jobs += grad_jobs(
            rows,
            grads[chunk * n_grads : (chunk + 1) * n_grads],
            grad_v.at[:, columns],
            sem.at[chunk],
            order,
            middle,
            groups,
        )
        copies += load_pieces(
            pieces[chunk * n_pieces : (chunk + 1) * n_pieces],
            nodes_v.at[:, columns],
            piece_sem.at[chunk],
            0,
        )
    run_jobs(jobs, "start")
    tiles_v[...] = jnp.zeros_like(tiles_v)
    found = jnp.int32(0)
    for index, group in enumerate(groups):
        first = order[group] * blocks

        def collect(i, found, first=first, index=index):
            row = first + i
            count = counts[row]
            for slot in range(slots):
                live[found] = (index * blocks + i) * slots + slot
                source[found] = cols[row * slots + slot]
                found = found + (slot < count).astype(jnp.int32)
            return found

        found = lax.fori_loop(0, blocks, collect, found)
    run_jobs(jobs, "wait")
    for copy in copies:
        copy.wait()

    def entry(place):
        tile_index = live[place]
        grad = grad_v[block_at(tile_index // slots, block)]
        node = nodes_v[block_at(source[place], block)]
        tiles_v[tile_index] = (mm(grad, node, NT) * scale).astype(BF16)

    for_live(found, entry)
    size = blocks * slots
    copies = []
    for index, group in enumerate(groups):
        copy = pltpu.make_async_copy(
            tiles_v.at[pl.ds(index * size, size)],
            out.at[pl.ds(order[group] * size, size)],
            out_sem.at[index],
        )
        copy.start()
        copies.append(copy)
    for copy in copies:
        copy.wait()


def tile_grad_call(cols, counts, order, middle, grads, pieces, shape, rows, groups, base=None, after=()):
    row_blocks, slots, block = shape[:3]
    chunks = len(grads)
    width = grads[0][0].shape[1] * chunks
    gathered = sum(piece.shape[0] for piece in pieces[0])
    flat = [a for chunk in grads for a in chunk] + [a for chunk in pieces for a in chunk]
    after = after if base is None else (base,) + tuple(after)
    entries = len(groups) * rows // block * slots
    return pl.pallas_call(
        functools.partial(
            tile_grad_kernel, rows, slots, len(grads[0]), len(pieces[0]), chunks, len(after), groups
        ),
        out_shape=[
            jax.ShapeDtypeStruct((row_blocks * slots, block, block), BF16),
            jax.ShapeDtypeStruct((8, 128), F32),
        ],
        in_specs=[SMEM] * 4 + [ANY] * (len(flat) + len(after)),
        out_specs=[ANY, VMEM],
        input_output_aliases={} if base is None else {4 + len(flat): 0},
        scratch_shapes=[
            pltpu.VMEM((len(groups) * rows, width), BF16),
            pltpu.VMEM((gathered, width), BF16),
            pltpu.VMEM((entries, block, block), BF16),
            pltpu.SMEM((entries + 8,), jnp.int32),
            pltpu.SMEM((entries + 8,), jnp.int32),
            pltpu.SemaphoreType.DMA((chunks, len(grads[0]))),
            pltpu.SemaphoreType.DMA((chunks, len(pieces[0]))),
            pltpu.SemaphoreType.DMA((len(groups),)),
        ],
        compiler_params=params(60),
        cost_estimate=cost(4.0),
        name="tile_grads",
    )(cols, counts, order, middle, *flat, *after)


def add(*terms):
    value = terms[0].astype(F32)
    for term in terms[1:]:
        value = value + term.astype(F32)
    return value.astype(BF16)


def swap(value, bit):
    return lax.ppermute(value, "row", [(i, i ^ bit) for i in range(8)])


def outer_swap(value):
    return lax.ppermute(value, "col", [(0, 1), (1, 0), (2, 3), (3, 2)])


def mirror_swap(value):
    return lax.ppermute(value, "col", [(0, 3), (3, 0), (1, 2), (2, 1)])


def inner_swap(value):
    pairs = []
    for row in range(8):
        for col in range(4):
            partner = (row, 3 - col) if col in (1, 2) else (row ^ 1, col)
            pairs.append((row * 4 + col, partner[0] * 4 + partner[1]))
    return lax.ppermute(value, ("row", "col"), pairs)


def held(value, *others):
    return lax.optimization_barrier((value, *others))[0]


def gather_square(nodes):
    pieces = []
    for piece in (nodes, swap(nodes, 2), swap(nodes, 4), swap(nodes, 6)):
        pieces += [piece, swap(piece, 1)]
    return pieces


def pair_sums(even, odd, rows):
    other = swap(odd, 1)
    places = [slice(place * rows, (place + 1) * rows) for place in range(4)]
    return (even[places[0]], other[places[0]]), [add(even[p], other[p]) for p in places[1:]]


def reduce_square(sums):
    return [swap(value, bit) for value, bit in zip(sums, (2, 4, 6))]


def scatter_weights(terms):
    for bit in (1, 2, 4):
        half = terms.shape[0] // 2
        terms = terms[:half] + swap(terms[half:], bit)
    return terms


def level_weights(value):
    value = value + outer_swap(value)
    return value + mirror_swap(value)


def gather_weights(value, width, mine):
    value = value.astype(BF16)
    for bit in (4, 2, 1):
        value = jnp.concatenate([value, swap(value, bit)], axis=0)
    return unpack_call(mine, value, width)


def reduce_line(far, near, pair, own, inner):
    far_in = outer_swap(far)
    near_in = outer_swap(held(near, far_in))
    far_sum = inner_swap(add(far, far_in))
    near_sum = inner_swap(add(near, near_in))
    pair_in = outer_swap(add(pair, jnp.where(inner, far_sum, jnp.zeros_like(far_sum))))
    return own, pair_in, near_sum


def gather_line(own):
    pair = outer_swap(own)
    near_inner = inner_swap(own)
    far_inner = inner_swap(pair)
    near_outer = outer_swap(near_inner)
    far_outer = outer_swap(far_inner)
    return [own, pair, near_inner, near_outer, far_inner, far_outer]


def body(n_row, n_col, nodes, tiles, tile_col, tile_count, w_in, bias_in, w_out, ln_gain, ln_shift, cotangent):
    rows, width = nodes.shape
    row_blocks, _, slots, block = tiles.shape[:4]
    tile_local = tiles.reshape(row_blocks, slots, block, block)
    cols = tile_col.reshape(row_blocks * slots)
    counts = tile_count.reshape(row_blocks)
    blocks = rows // block
    gathered, total = n_row * rows, n_col * rows
    square_line = n_row == 8 and n_col == 4
    if square_line:
        mine = lax.axis_index("row").astype(jnp.int32)
        cols = ((cols // blocks) ^ mine) * blocks + cols % blocks
        level = lax.axis_index("col").astype(jnp.int32)
        low = level < 2
        order = jnp.stack([jnp.where(low, 3, 0), jnp.where(low, 2, 1), level ^ 1, level]).astype(jnp.int32)
        inner = (level == 1) | (level == 2)
        middle = inner.astype(jnp.int32).reshape(1)
        pieces = [gather_square(nodes)]
        far, near = forward_call(cols, counts, order, pieces[0], tile_local, ((0,), (1,)), rows)
        pair, own = forward_call(cols, counts, order, pieces[0], tile_local, ((2,), (3,)), rows)
        parts = [reduce_line(far, near, pair, own, inner)]
        kinds = [("all", "all", "inner")]
    else:
        order = jnp.arange(n_col, dtype=jnp.int32)
        middle = jnp.zeros((1,), jnp.int32)
        pieces = [[lax.all_gather(nodes, "row", axis=0, tiled=True)]]
        (partial,) = forward_call(cols, counts, order, pieces[0], tile_local, (tuple(range(n_col)),), rows)
        parts = [[lax.psum_scatter(partial, "col", scatter_dimension=0, tiled=True)]]
        kinds = [("all",)]
    vectors = [v.reshape(1, width) for v in (bias_in, ln_gain, ln_shift)]
    (updated, gpre_b, act, gproj, message, vec), gmsgs = mlp_call(
        middle, nodes, cotangent, parts, kinds, w_in, vectors[0], w_out, vectors[1], vectors[2]
    )
    factor = float(rows * n_row * n_col) ** -0.5
    mine = lax.axis_index("row").astype(jnp.int32).reshape(1)
    weight_terms, direct = weight_call(
        factor, n_row if square_line else 1, mine, nodes, message, act, gpre_b, gproj, cotangent, w_in, vec
    )
    if square_line:
        halves = ((1, 3, 5, 7), (0, 2, 4, 6))
        grads = [gather_line(gmsgs[0])]
        near_grads, token = tile_grad_call(
            cols, counts, order, middle, [grads[0][:2]], pieces, tile_local.shape, rows, (3, 2),
            after=(grads[0][3], grads[0][4]),
        )
        row_weights = scatter_weights(held(weight_terms, token))
        odd, even = back_call(
            cols, counts, order, middle, grads[0], tile_local, total, gathered, halves, (row_weights,)
        )
        all_weights = level_weights(row_weights)
        own_terms, sums = pair_sums(even, odd, rows)
        terms = (*own_terms, *reduce_square(sums))
        weights = gather_weights(held(all_weights, *sums), width, mine)
        terms = held(terms, *weights)
        back = sum(term.astype(F32) for term in terms)
        grad_tiles, _ = tile_grad_call(
            cols, counts, order, middle, grads, pieces, tile_local.shape, rows, (1, 0), near_grads, sums
        )
    else:
        grads = [[lax.all_gather(gmsgs[0], "col", axis=0, tiled=True)]]
        weight_sums = lax.psum(weight_terms, ("row", "col"))
        weights = (
            weight_sums[: 2 * width],
            weight_sums[2 * width : 3 * width],
            weight_sums[3 * width : 3 * width + 3],
        )
        (terms,) = back_call(
            cols, counts, order, middle, grads[0], tile_local, total, gathered, (tuple(range(n_row)),)
        )
        back = lax.psum_scatter(terms, "row", scatter_dimension=0, tiled=True).astype(F32)
        grad_tiles, _ = tile_grad_call(
            cols, counts, order, middle, grads, pieces, tile_local.shape, rows, tuple(range(n_col))
        )
    grad_nodes = (direct + back).astype(BF16)
    grad_tiles = grad_tiles.reshape(tiles.shape)
    return (updated, grad_nodes, grad_tiles, *weights)


def solution(mesh):
    placed = (
        P(("row", "col"), None),
        P("row", "col", None, None, None),
        P("row", "col", None),
        P("row", "col"),
        P(),
        P(),
        P(),
        P(),
        P(),
        P(("row", "col"), None),
    )
    return jax.shard_map(
        functools.partial(body, mesh.shape["row"], mesh.shape["col"]),
        mesh=mesh,
        in_specs=placed,
        out_specs=(
            P(("row", "col"), None),
            P(("row", "col"), None),
            P("row", "col", None, None, None),
            P(),
            P(),
            P(),
        ),
        check_vma=False,
    )
```

```python
import functools

import jax
import jax.numpy as jnp
from jax import lax
from jax.experimental import pallas as pl
from jax.experimental.pallas import tpu as pltpu
from jax.sharding import PartitionSpec as P

F32 = jnp.float32
BF16 = jnp.bfloat16
ANY = pl.BlockSpec(memory_space=pl.ANY)
HBM = pl.BlockSpec(memory_space=pltpu.HBM)
SMEM = pl.BlockSpec(memory_space=pltpu.SMEM)
VMEM = pl.BlockSpec(memory_space=pltpu.VMEM)
MIB = 1 << 20
TN = (((0,), (0,)), ((), ()))
NT = (((1,), (1,)), ((), ()))
SMALL = pl.CostEstimate(flops=1 << 20, bytes_accessed=1 << 16, transcendentals=0)


LIVE_STEP = 4
GRAD_PLAN = ((3, 0, None), (2, 1, None), (1, 2, "inner"), (1, 3, "outer"), (0, 4, "inner"), (0, 5, "outer"))
SWAP_ORDER = (0, 4, 2, 6, 1, 5, 3, 7)


def params(mib):
    return pltpu.CompilerParams(vmem_limit_bytes=mib * MIB)


def mm(a, b, dims=(((1,), (0,)), ((), ()))):
    return lax.dot_general(a, b, dims, preferred_element_type=F32)


def block_at(index, block):
    return pl.ds(pl.multiple_of(index * block, block), block)


def load_pieces(pieces, dst, sem, first):
    copies = []
    offset = 0
    for index, piece in enumerate(pieces):
        copy = pltpu.make_async_copy(
            piece, dst.at[pl.ds(offset, piece.shape[0])], sem.at[first + index]
        )
        copy.start()
        copies.append(copy)
        offset += piece.shape[0]
    return copies


def masked_tile(tile, live):
    return jnp.where(live, tile, jnp.zeros_like(tile))


def forward_kernel(outputs, n_pieces, cols, counts, order, *refs):
    pieces, tiles = refs[:n_pieces], refs[n_pieces]
    outs = refs[n_pieces + 1 : n_pieces + 1 + len(outputs)]
    nodes_v, tiles_v, sem, tile_sem = refs[n_pieces + 1 + len(outputs) :]
    rows = outs[0].shape[0] // len(outputs[0])
    slots, block = tiles.shape[1], tiles.shape[2]
    blocks = rows // block
    copies = load_pieces(pieces, nodes_v, sem, 0)
    places = [(pick, out, index) for out, picks in zip(outs, outputs) for index, pick in enumerate(picks)]
    tile_copies = []
    for place, (pick, _, _) in enumerate(places):
        copy = pltpu.make_async_copy(
            tiles.at[pl.ds(order[pick] * blocks, blocks)],
            tiles_v.at[pl.ds(place * blocks, blocks)],
            tile_sem.at[place],
        )
        copy.start()
        tile_copies.append(copy)
    for copy in copies:
        copy.wait()
    for place, (pick, out, index) in enumerate(places):
        tile_copies[place].wait()
        first = order[pick] * blocks

        def step(i, carry, first=first, out=out, index=index, place=place):
            row = first + i
            count = counts[row]
            parts = []
            for pair in range(slots // 2):
                both = (2 * pair, 2 * pair + 1)
                tile = jnp.concatenate(
                    [masked_tile(tiles_v[place * blocks + i, slot], slot < count) for slot in both], axis=1
                )
                node = jnp.concatenate(
                    [nodes_v[block_at(cols[row * slots + slot], block)] for slot in both], axis=0
                )
                parts.append(mm(tile, node))
            value = parts[0]
            for part in parts[1:]:
                value = value + part
            out[block_at(index * blocks + i, block)] = value.astype(BF16)
            return carry

        lax.fori_loop(0, blocks, step, 0, unroll=4)


def forward_call(cols, counts, order, pieces, tiles, outputs, rows):
    width = pieces[0].shape[1]
    gathered = sum(piece.shape[0] for piece in pieces)
    slots, block = tiles.shape[1], tiles.shape[2]
    n_picks = sum(len(picks) for picks in outputs)
    return pl.pallas_call(
        functools.partial(forward_kernel, outputs, len(pieces)),
        out_shape=[jax.ShapeDtypeStruct((len(picks) * rows, width), BF16) for picks in outputs],
        in_specs=[SMEM] * 3 + [ANY] * len(pieces) + [HBM],
        out_specs=[VMEM] * len(outputs),
        scratch_shapes=[
            pltpu.VMEM((gathered, width), BF16),
            pltpu.VMEM((n_picks * (rows // block),) + tiles.shape[1:], BF16),
            pltpu.SemaphoreType.DMA((len(pieces),)),
            pltpu.SemaphoreType.DMA((n_picks,)),
        ],
        compiler_params=params(60),
        cost_estimate=SMALL,
        name="partial_messages",
    )(cols, counts, order, *pieces, tiles)


def mlp_kernel(kinds, middle, nodes, cot, *refs):
    n_parts = sum(len(chunk) for chunk in kinds)
    parts = refs[:n_parts]
    w_in, bias, w_out, gain, shift, updated, gpre_o, act_o, gproj_o, msg_o, vec = refs[
        n_parts : n_parts + 11
    ]
    gmsgs = refs[n_parts + 11 :]
    width = nodes.shape[1]
    inner = middle[0] > 0
    messages = []
    place = 0
    for chunk in kinds:
        total = None
        for kind in chunk:
            term = parts[place][...].astype(F32)
            place += 1
            if kind == "inner":
                term = jnp.where(inner, term, 0.0)
            total = term if total is None else total + term
        messages.append(total.astype(BF16))
    message = jnp.concatenate(messages, axis=1) if len(messages) > 1 else messages[0]
    node = nodes[...]
    pre = mm(node, w_in[:width]) + mm(message, w_in[width:]) + bias[...]
    sig = jax.nn.sigmoid(pre)
    act = (pre * sig).astype(BF16)
    proj = mm(act, w_out[...])
    mean = jnp.mean(proj, axis=-1, keepdims=True)
    var = jnp.mean((proj - mean) ** 2, axis=-1, keepdims=True)
    rstd = 1.0 / jnp.sqrt(var + 1e-05)
    normed = (proj - mean) * rstd
    updated[...] = (node.astype(F32) + normed * gain[...] + shift[...]).astype(BF16)
    grad_out = cot[...].astype(F32)
    gscaled = grad_out * gain[...]
    gproj = (
        (
            gscaled
            - jnp.mean(gscaled, axis=-1, keepdims=True)
            - normed * jnp.mean(gscaled * normed, axis=-1, keepdims=True)
        )
        * rstd
    ).astype(BF16)
    gact = mm(gproj, w_out[...], NT)
    gpre = gact * sig * (1.0 + pre * (1.0 - sig))
    gpre_b = gpre.astype(BF16)
    gmsg = mm(gpre_b, w_in[width:], NT).astype(BF16)
    part = width // len(gmsgs)
    for index, out in enumerate(gmsgs):
        out[...] = gmsg[:, index * part : (index + 1) * part]
    gpre_o[...] = gpre_b
    act_o[...] = act
    gproj_o[...] = gproj
    msg_o[...] = message

    @pl.when(pl.program_id(0) == 0)
    def _():
        vec[...] = jnp.zeros_like(vec)

    vec[0:1] += jnp.sum(gpre, axis=0, keepdims=True)
    vec[1:2] += jnp.sum(grad_out * normed, axis=0, keepdims=True)
    vec[2:3] += jnp.sum(grad_out, axis=0, keepdims=True)


def mlp_call(middle, nodes, cot, parts, kinds, w_in, bias, w_out, gain, shift):
    rows, width = nodes.shape
    step = min(rows, 256)

    def blocked(array):
        return pl.BlockSpec((step, array.shape[1]), lambda i: (i, 0))

    def whole(array):
        return pl.BlockSpec(array.shape, lambda i: (0, 0))

    flat = [term for chunk in parts for term in chunk]
    row_like = jax.ShapeDtypeStruct((rows, width), BF16)
    chunk_like = jax.ShapeDtypeStruct((rows, width // len(parts)), BF16)
    outs = [row_like] * 5 + [jax.ShapeDtypeStruct((8, width), F32)] + [chunk_like] * len(parts)
    weights = (w_in, bias, w_out, gain, shift)
    result = pl.pallas_call(
        functools.partial(mlp_kernel, kinds),
        grid=(rows // step,),
        out_shape=outs,
        in_specs=[SMEM] + [blocked(a) for a in (nodes, cot, *flat)] + [whole(a) for a in weights],
        out_specs=[blocked(a) for a in outs[:5]] + [whole(outs[5])] + [blocked(a) for a in outs[6:]],
        compiler_params=params(40),
        cost_estimate=SMALL,
        name="mlp",
    )(middle, nodes, cot, *flat, *weights)
    return result[:6], result[6:]


def weight_kernel(factor, pieces, n_after, mine, nodes, msg, act, gpre, gproj, cot, w_in, vec, *refs):
    *outs, direct, grads = refs[n_after:]
    width = nodes.shape[1]

    @pl.when(pl.program_id(0) == 0)
    def _():
        grads[...] = jnp.zeros_like(grads)
        grads[3 * width : 3 * width + 8] = vec[...] * factor

    gpre_b = gpre[...]
    grads[:width] += mm(nodes[...], gpre_b, TN) * factor
    grads[width : 2 * width] += mm(msg[...], gpre_b, TN) * factor
    grads[2 * width : 3 * width] += mm(act[...], gproj[...], TN) * factor
    direct[...] = cot[...].astype(F32) + mm(gpre_b, w_in[:width], NT)

    @pl.when(pl.program_id(0) == pl.num_programs(0) - 1)
    def _():
        if pieces == 1:
            outs[0][...] = grads[: outs[0].shape[0]]
        else:
            rows = grads.shape[0] // pieces
            for place, member in enumerate(SWAP_ORDER):
                where = pl.ds(pl.multiple_of((mine[0] ^ member) * rows, 8), rows)
                out, index = outs[2 * place // pieces], place % (pieces // 2)
                out[index * rows : (index + 1) * rows] = grads[where]


def weight_call(factor, pieces, mine, nodes, msg, act, gpre, gproj, cot, w_in, vec, after=()):
    rows, width = nodes.shape
    step = min(rows, 256)
    blocked = pl.BlockSpec((step, width), lambda i: (i, 0))

    def whole(shape):
        return pl.BlockSpec(shape, lambda i: (0, 0))

    padded = (3 * width + width // 2, width)
    if pieces == 1:
        outs = [jax.ShapeDtypeStruct((3 * width + 8, width), F32)]
    else:
        outs = [jax.ShapeDtypeStruct((padded[0] // 2, width), F32)] * 2
    return pl.pallas_call(
        functools.partial(weight_kernel, factor, pieces, len(after)),
        grid=(rows // step,),
        out_shape=[*outs, jax.ShapeDtypeStruct((rows, width), F32)],
        in_specs=[SMEM] + [blocked] * 6 + [whole(w_in.shape), whole(vec.shape)] + [ANY] * len(after),
        out_specs=[whole(out.shape) for out in outs] + [blocked],
        scratch_shapes=[pltpu.VMEM(padded, F32)],
        compiler_params=params(40),
        cost_estimate=SMALL,
        name="weight_grads",
    )(mine, nodes, msg, act, gpre, gproj, cot, w_in, vec, *after)


def unpack_kernel(mine, parts, w_in, w_out, vectors, grads):
    width = w_in.shape[1]
    rows = grads.shape[0] // len(SWAP_ORDER)
    for place, member in enumerate(SWAP_ORDER):
        where = pl.ds(pl.multiple_of((mine[0] ^ member) * rows, 8), rows)
        grads[where] = parts[place * rows : (place + 1) * rows].astype(F32)
    w_in[...] = grads[: 2 * width]
    w_out[...] = grads[2 * width : 3 * width]
    vectors[...] = grads[3 * width : 3 * width + 3]


def unpack_call(mine, parts, width):
    shapes = ((2 * width, width), (width, width), (3, width))
    return pl.pallas_call(
        unpack_kernel,
        out_shape=[jax.ShapeDtypeStruct(shape, F32) for shape in shapes],
        in_specs=[SMEM, VMEM],
        out_specs=[VMEM] * 3,
        scratch_shapes=[pltpu.VMEM((3 * width + width // 2, width), F32)],
        compiler_params=params(16),
        cost_estimate=SMALL,
        name="weight_unpack",
    )(mine, parts)


def grad_jobs(rows, refs, dst, sem, order, middle, groups=None):
    if len(refs) == 1:
        return [(None, pltpu.make_async_copy(refs[0], dst, sem.at[0]))]
    conditions = {None: None, "inner": middle[0] > 0, "outer": middle[0] == 0}
    jobs = []
    for group, index, kind in GRAD_PLAN:
        if groups is None:
            where = block_at(order[group], rows)
        elif group in groups:
            where = pl.ds(groups.index(group) * rows, rows)
        else:
            continue
        copy = pltpu.make_async_copy(refs[index], dst.at[where], sem.at[index])
        jobs.append((conditions[kind], copy))
    return jobs


def run_jobs(jobs, verb):
    for condition, copy in jobs:
        if condition is None:
            getattr(copy, verb)()
        else:
            pl.when(condition)(getattr(copy, verb))


def for_live(found, entry):
    def several(i, carry):
        for index in range(LIVE_STEP):
            entry(i * LIVE_STEP + index)
        return carry

    def one(i, carry):
        entry(i)
        return carry

    full = found // LIVE_STEP
    lax.fori_loop(0, full, several, 0)
    lax.fori_loop(full * LIVE_STEP, found, one, 0)


def back_kernel(rows, slots, n_grads, n_after, out_pieces, cols, counts, order, middle, *refs):
    grads, tiles = refs[:n_grads], refs[n_grads]
    refs = refs[n_grads + 1 + n_after :]
    outs = refs[: len(out_pieces)]
    grad_v, tiles_v, acc, live, sem, tile_sem = refs[len(out_pieces) :]
    n_tiles, block = tiles.shape[:2]
    jobs = grad_jobs(rows, grads, grad_v, sem, order, middle)
    run_jobs(jobs, "start")
    tile_copy = pltpu.make_async_copy(tiles, tiles_v, tile_sem.at[0])
    tile_copy.start()
    acc[...] = jnp.zeros_like(acc)

    def collect(row, found):
        count = counts[row]
        for slot in range(slots):
            live[found] = row * slots + slot
            found = found + (slot < count).astype(jnp.int32)
        return found

    found = lax.fori_loop(0, n_tiles // slots, collect, jnp.int32(0))
    run_jobs(jobs, "wait")
    tile_copy.wait()

    def entry(place):
        tile_index = live[place]
        part = mm(tiles_v[tile_index], grad_v[block_at(tile_index // slots, block)], TN)
        acc[block_at(cols[tile_index], block)] += part

    for_live(found, entry)
    piece = acc.shape[0] // sum(len(members) for members in out_pieces)
    for out, members in zip(outs, out_pieces):
        for index, member in enumerate(members):
            out[pl.ds(index * piece, piece)] = acc[pl.ds(member * piece, piece)].astype(BF16)


def back_call(cols, counts, order, middle, grads, tiles, total, gathered, out_pieces, after=()):
    rows, width = grads[0].shape
    rows = total if len(grads) == 1 else rows
    row_blocks, slots, block = tiles.shape[:3]
    piece = gathered // sum(len(members) for members in out_pieces)
    return pl.pallas_call(
        functools.partial(back_kernel, rows, slots, len(grads), len(after), out_pieces),
        out_shape=[jax.ShapeDtypeStruct((len(m) * piece, width), BF16) for m in out_pieces],
        in_specs=[SMEM] * 4 + [ANY] * len(grads) + [HBM] + [ANY] * len(after),
        out_specs=[VMEM] * len(out_pieces),
        scratch_shapes=[
            pltpu.VMEM((total, width), BF16),
            pltpu.VMEM((row_blocks * slots, block, block), BF16),
            pltpu.VMEM((gathered, width), F32),
            pltpu.SMEM((row_blocks * slots + 8,), jnp.int32),
            pltpu.SemaphoreType.DMA((len(grads),)),
            pltpu.SemaphoreType.DMA((1,)),
        ],
        compiler_params=params(28 if gathered <= 8192 else 56),
        cost_estimate=SMALL,
        name="back_terms",
    )(cols, counts, order, middle, *grads, tiles.reshape(row_blocks * slots, block, block), *after)


def tile_grad_kernel(
    rows, slots, n_grads, n_pieces, n_chunks, n_after, groups, cols, counts, order, middle, *refs
):
    grads = refs[: n_grads * n_chunks]
    refs = refs[n_grads * n_chunks :]
    pieces = refs[: n_pieces * n_chunks]
    out, token, grad_v, nodes_v, tiles_v, live, source, sem, piece_sem, out_sem = refs[n_pieces * n_chunks + n_after :]
    token[...] = jnp.zeros_like(token)
    block = out.shape[1]
    width = nodes_v.shape[1]
    part = width // n_chunks
    scale = float(width) ** -0.5
    blocks = grad_v.shape[0] // (block * len(groups))
    jobs, copies = [], []
    for chunk in range(n_chunks):
        columns = pl.ds(chunk * part, part)
        jobs += grad_jobs(
            rows,
            grads[chunk * n_grads : (chunk + 1) * n_grads],
            grad_v.at[:, columns],
            sem.at[chunk],
            order,
            middle,
            groups,
        )
        copies += load_pieces(
            pieces[chunk * n_pieces : (chunk + 1) * n_pieces],
            nodes_v.at[:, columns],
            piece_sem.at[chunk],
            0,
        )
    run_jobs(jobs, "start")
    tiles_v[...] = jnp.zeros_like(tiles_v)
    found = jnp.int32(0)
    for index, group in enumerate(groups):
        first = order[group] * blocks

        def collect(i, found, first=first, index=index):
            row = first + i
            count = counts[row]
            for slot in range(slots):
                live[found] = (index * blocks + i) * slots + slot
                source[found] = cols[row * slots + slot]
                found = found + (slot < count).astype(jnp.int32)
            return found

        found = lax.fori_loop(0, blocks, collect, found)
    run_jobs(jobs, "wait")
    for copy in copies:
        copy.wait()

    def entry(place):
        tile_index = live[place]
        grad = grad_v[block_at(tile_index // slots, block)]
        node = nodes_v[block_at(source[place], block)]
        tiles_v[tile_index] = (mm(grad, node, NT) * scale).astype(BF16)

    for_live(found, entry)
    size = blocks * slots
    copies = []
    for index, group in enumerate(groups):
        copy = pltpu.make_async_copy(
            tiles_v.at[pl.ds(index * size, size)],
            out.at[pl.ds(order[group] * size, size)],
            out_sem.at[index],
        )
        copy.start()
        copies.append(copy)
    for copy in copies:
        copy.wait()


def tile_grad_call(cols, counts, order, middle, grads, pieces, shape, rows, groups, base=None, after=()):
    row_blocks, slots, block = shape[:3]
    chunks = len(grads)
    width = grads[0][0].shape[1] * chunks
    gathered = sum(piece.shape[0] for piece in pieces[0])
    flat = [a for chunk in grads for a in chunk] + [a for chunk in pieces for a in chunk]
    after = after if base is None else (base,) + tuple(after)
    entries = len(groups) * rows // block * slots
    return pl.pallas_call(
        functools.partial(
            tile_grad_kernel, rows, slots, len(grads[0]), len(pieces[0]), chunks, len(after), groups
        ),
        out_shape=[
            jax.ShapeDtypeStruct((row_blocks * slots, block, block), BF16),
            jax.ShapeDtypeStruct((8, 128), F32),
        ],
        in_specs=[SMEM] * 4 + [ANY] * (len(flat) + len(after)),
        out_specs=[ANY, VMEM],
        input_output_aliases={} if base is None else {4 + len(flat): 0},
        scratch_shapes=[
            pltpu.VMEM((len(groups) * rows, width), BF16),
            pltpu.VMEM((gathered, width), BF16),
            pltpu.VMEM((entries, block, block), BF16),
            pltpu.SMEM((entries + 8,), jnp.int32),
            pltpu.SMEM((entries + 8,), jnp.int32),
            pltpu.SemaphoreType.DMA((chunks, len(grads[0]))),
            pltpu.SemaphoreType.DMA((chunks, len(pieces[0]))),
            pltpu.SemaphoreType.DMA((len(groups),)),
        ],
        compiler_params=params(16 if gathered <= 8192 else 40),
        cost_estimate=SMALL,
        name="tile_grads",
    )(cols, counts, order, middle, *flat, *after)


def swap(value, bit):
    return lax.ppermute(value, "row", [(i, i ^ bit) for i in range(8)])


def outer_swap(value):
    return lax.ppermute(value, "col", [(0, 1), (1, 0), (2, 3), (3, 2)])


def mirror_swap(value):
    return lax.ppermute(value, "col", [(0, 3), (3, 0), (1, 2), (2, 1)])


def inner_swap(value):
    pairs = []
    for row in range(8):
        for col in range(4):
            partner = (row, 3 - col) if col in (1, 2) else (row ^ 1, col)
            pairs.append((row * 4 + col, partner[0] * 4 + partner[1]))
    return lax.ppermute(value, ("row", "col"), pairs)


def gather_square(nodes):
    pieces = []
    for piece in (nodes, swap(nodes, 2), swap(nodes, 4), swap(nodes, 6)):
        pieces += [piece, swap(piece, 1)]
    return pieces


def sum_kernel(n_terms, n_gated, *refs):
    flag, refs = refs[0], refs[1:]
    total = None
    for index, ref in enumerate(refs[: n_terms + n_gated]):
        term = ref[...].astype(F32)
        if index >= n_terms:
            term = jnp.where(flag[0] > 0, term, 0.0)
        total = term if total is None else total + term
    refs[-1][...] = total.astype(refs[-1].dtype)


def sum_call(flag, rows, terms, gated=(), dtype=BF16, after=()):
    both = [*terms, *gated]
    width = both[0][0].shape[1]
    step = min(rows, 256)
    steps = rows // step
    return pl.pallas_call(
        functools.partial(sum_kernel, len(terms), len(gated)),
        grid=(steps,),
        out_shape=jax.ShapeDtypeStruct((rows, width), dtype),
        in_specs=[SMEM]
        + [pl.BlockSpec((step, width), lambda i, piece=piece: (piece * steps + i, 0)) for _, piece in both]
        + [ANY] * len(after),
        out_specs=pl.BlockSpec((step, width), lambda i: (i, 0)),
        compiler_params=params(8),
        cost_estimate=SMALL,
        name="sum_terms",
    )(flag, *(array for array, _ in both), *after)


def scatter_weights(kept, sent):
    for bit in (1, 2):
        terms = kept + swap(sent, bit)
        half = terms.shape[0] // 2
        kept, sent = terms[:half], terms[half:]
    return kept, swap(sent, 4)


def level_weights(flag, kept, received):
    rows = kept.shape[0]
    value = sum_call(flag, rows, [(kept, 0), (received, 0)], dtype=BF16)
    value = sum_call(flag, rows, [(value, 0), (outer_swap(value), 0)])
    return sum_call(flag, rows, [(value, 0), (mirror_swap(value), 0)])


def gather_weights(value, width, mine):
    for bit in (4, 2, 1):
        value = jnp.concatenate([value, swap(value, bit)], axis=0)
    return unpack_call(mine, value, width)


def reduce_line(far, near, pair, own, flag):
    rows = own.shape[0]
    far_sum = inner_swap(sum_call(flag, rows, [(far, 0), (outer_swap(far), 0)]))
    near_sum = inner_swap(sum_call(flag, rows, [(near, 0), (outer_swap(near), 0)]))
    pair_in = outer_swap(sum_call(flag, rows, [(pair, 0)], [(far_sum, 0)]))
    return own, pair_in, near_sum


def gather_line(own):
    pair = outer_swap(own)
    near_inner = inner_swap(own)
    far_inner = inner_swap(pair)
    near_outer = outer_swap(near_inner)
    far_outer = outer_swap(far_inner)
    return [own, pair, near_inner, near_outer, far_inner, far_outer]


def body(n_row, n_col, nodes, tiles, tile_col, tile_count, w_in, bias_in, w_out, ln_gain, ln_shift, cotangent):
    rows, width = nodes.shape
    row_blocks, _, slots, block = tiles.shape[:4]
    tile_local = tiles.reshape(row_blocks, slots, block, block)
    cols = tile_col.reshape(row_blocks * slots)
    counts = tile_count.reshape(row_blocks)
    blocks = rows // block
    gathered, total = n_row * rows, n_col * rows
    square_line = n_row == 8 and n_col == 4
    if square_line:
        mine = lax.axis_index("row").astype(jnp.int32)
        cols = ((cols // blocks) ^ mine) * blocks + cols % blocks
        level = lax.axis_index("col").astype(jnp.int32)
        low = level < 2
        order = jnp.stack([jnp.where(low, 3, 0), jnp.where(low, 2, 1), level ^ 1, level]).astype(jnp.int32)
        inner = (level == 1) | (level == 2)
        middle = inner.astype(jnp.int32).reshape(1)
        pieces = [gather_square(nodes)]
        far, near = forward_call(cols, counts, order, pieces[0], tile_local, ((0,), (1,)), rows)
        pair, own = forward_call(cols, counts, order, pieces[0], tile_local, ((2,), (3,)), rows)
        parts = [reduce_line(far, near, pair, own, middle)]
        kinds = [("all", "all", "inner")]
    else:
        order = jnp.arange(n_col, dtype=jnp.int32)
        middle = jnp.zeros((1,), jnp.int32)
        pieces = [[lax.all_gather(nodes, "row", axis=0, tiled=True)]]
        (partial,) = forward_call(cols, counts, order, pieces[0], tile_local, (tuple(range(n_col)),), rows)
        parts = [[lax.psum_scatter(partial, "col", scatter_dimension=0, tiled=True)]]
        kinds = [("all",)]
    vectors = [v.reshape(1, width) for v in (bias_in, ln_gain, ln_shift)]
    (updated, gpre_b, act, gproj, message, vec), gmsgs = mlp_call(
        middle, nodes, cotangent, parts, kinds, w_in, vectors[0], w_out, vectors[1], vectors[2]
    )
    factor = float(rows * n_row * n_col) ** -0.5
    mine = lax.axis_index("row").astype(jnp.int32).reshape(1)
    weight_args = (mine, nodes, message, act, gpre_b, gproj, cotangent, w_in, vec)
    if square_line:
        halves = ((1, 3, 5, 7), (0, 2, 4, 6))
        grads = [gather_line(gmsgs[0])]
        kept, sent, direct = weight_call(factor, n_row, *weight_args, (grads[0][1], grads[0][2]))
        all_weights = level_weights(middle, *scatter_weights(kept, sent))
        weights = gather_weights(all_weights, width, mine)
        near_grads, token = tile_grad_call(
            cols, counts, order, middle, [grads[0][:2]], pieces, tile_local.shape, rows, (3, 2),
            after=(grads[0][3], grads[0][4]),
        )
        odd, even = back_call(
            cols, counts, order, middle, grads[0], tile_local, total, gathered, halves, (token, weights[2])
        )
        other = swap(odd, 1)
        sums = [sum_call(middle, rows, [(even, piece), (other, piece)]) for piece in (1, 2, 3)]
        x_side, y_side, diagonal = [swap(value, bit) for value, bit in zip(sums, (2, 4, 6))]
        grad_tiles, _ = tile_grad_call(
            cols, counts, order, middle, grads, pieces, tile_local.shape, rows, (1, 0), near_grads, sums
        )
        grad_nodes = sum_call(
            middle, rows, [(term, 0) for term in (direct, even, other, x_side, y_side, diagonal)]
        )
    else:
        grads = [[lax.all_gather(gmsgs[0], "col", axis=0, tiled=True)]]
        weight_terms, direct = weight_call(factor, 1, *weight_args)
        weight_sums = lax.psum(weight_terms, ("row", "col"))
        weights = (
            weight_sums[: 2 * width],
            weight_sums[2 * width : 3 * width],
            weight_sums[3 * width : 3 * width + 3],
        )
        (terms,) = back_call(
            cols, counts, order, middle, grads[0], tile_local, total, gathered, (tuple(range(n_row)),)
        )
        back = lax.psum_scatter(terms, "row", scatter_dimension=0, tiled=True)
        grad_nodes = sum_call(middle, rows, [(direct, 0), (back, 0)])
        grad_tiles, _ = tile_grad_call(
            cols, counts, order, middle, grads, pieces, tile_local.shape, rows, tuple(range(n_col))
        )
    grad_tiles = grad_tiles.reshape(tiles.shape)
    return (updated, grad_nodes, grad_tiles, *weights)


def solution(mesh):
    placed = (
        P(("row", "col"), None),
        P("row", "col", None, None, None),
        P("row", "col", None),
        P("row", "col"),
        P(),
        P(),
        P(),
        P(),
        P(),
        P(("row", "col"), None),
    )
    return jax.shard_map(
        functools.partial(body, mesh.shape["row"], mesh.shape["col"]),
        mesh=mesh,
        in_specs=placed,
        out_specs=(
            P(("row", "col"), None),
            P(("row", "col"), None),
            P("row", "col", None, None, None),
            P(),
            P(),
            P(),
        ),
        check_vma=False,
    )
```

```python
import functools

import jax
import jax.numpy as jnp
from jax import lax
from jax.experimental import pallas as pl
from jax.experimental.pallas import tpu as pltpu
from jax.sharding import PartitionSpec as P

F32 = jnp.float32
BF16 = jnp.bfloat16
ANY = pl.BlockSpec(memory_space=pl.ANY)
HBM = pl.BlockSpec(memory_space=pltpu.HBM)
SMEM = pl.BlockSpec(memory_space=pltpu.SMEM)
VMEM = pl.BlockSpec(memory_space=pltpu.VMEM)
MIB = 1 << 20
TN = (((0,), (0,)), ((), ()))
NT = (((1,), (1,)), ((), ()))
SMALL = pl.CostEstimate(flops=1 << 20, bytes_accessed=1 << 16, transcendentals=0)


LIVE_STEP = 4
SWAP_ORDER = (0, 4, 2, 6, 1, 5, 3, 7)


def params(mib):
    return pltpu.CompilerParams(vmem_limit_bytes=mib * MIB)


def mm(a, b, dims=(((1,), (0,)), ((), ()))):
    return lax.dot_general(a, b, dims, preferred_element_type=F32)


def block_at(index, block):
    return pl.ds(pl.multiple_of(index * block, block), block)


class Place:
    def __init__(self, ref, paired=True, blocks=1):
        self.mine, self.level = lax.shift_right_logical(ref[0], 2), ref[0] & 3
        self.paired, self.blocks = paired, blocks

    def source(self, col):
        if not self.paired:
            return col
        shift = self.blocks.bit_length() - 1
        if 1 << shift == self.blocks:
            return col ^ lax.shift_left(self.mine, jnp.int32(shift))
        return (lax.div(col, self.blocks) ^ self.mine) * self.blocks + lax.rem(col, self.blocks)


def load_pieces(pieces, dst, sem, first):
    copies = []
    offset = 0
    for index, piece in enumerate(pieces):
        copy = pltpu.make_async_copy(
            piece, dst.at[pl.ds(offset, piece.shape[0])], sem.at[first + index]
        )
        copy.start()
        copies.append(copy)
        offset += piece.shape[0]
    return copies


def masked_tile(tile, live):
    return jnp.where(live, tile, jnp.zeros_like(tile))


def forward_kernel(outputs, n_pieces, paired, here, cols, counts, *refs):
    pieces, tiles = refs[:n_pieces], refs[n_pieces]
    outs = refs[n_pieces + 1 : n_pieces + 1 + len(outputs)]
    nodes_v, tiles_v, sem, tile_sem = refs[n_pieces + 1 + len(outputs) :]
    rows = outs[0].shape[0] // len(outputs[0])
    slots, block = tiles.shape[1], tiles.shape[2]
    blocks = rows // block
    here = Place(here, paired, blocks)
    copies = load_pieces(pieces, nodes_v, sem, 0)
    places = [(pick, out, index) for out, picks in zip(outs, outputs) for index, pick in enumerate(picks)]
    tile_copies = []
    for place, (pick, _, _) in enumerate(places):
        copy = pltpu.make_async_copy(
            tiles.at[pl.ds(pick * blocks, blocks)],
            tiles_v.at[pl.ds(place * blocks, blocks)],
            tile_sem.at[place],
        )
        copy.start()
        tile_copies.append(copy)
    for copy in copies:
        copy.wait()
    for place, (pick, out, index) in enumerate(places):
        tile_copies[place].wait()
        first = pick * blocks

        def step(i, carry, first=first, out=out, index=index, place=place):
            row = first + i
            count = counts[row]
            parts = []
            for pair in range(slots // 2):
                both = (2 * pair, 2 * pair + 1)
                tile = jnp.concatenate(
                    [masked_tile(tiles_v[place * blocks + i, slot], slot < count) for slot in both], axis=1
                )
                node = jnp.concatenate(
                    [nodes_v[block_at(here.source(cols[slot, row]), block)] for slot in both], axis=0
                )
                parts.append(mm(tile, node))
            value = parts[0]
            for part in parts[1:]:
                value = value + part
            out[block_at(index * blocks + i, block)] = value.astype(BF16)
            return carry

        lax.fori_loop(0, blocks, step, 0, unroll=4)


def forward_call(paired, here, cols, counts, pieces, tiles, outputs, rows):
    width = pieces[0].shape[1]
    gathered = sum(piece.shape[0] for piece in pieces)
    slots, block = tiles.shape[1], tiles.shape[2]
    n_picks = sum(len(picks) for picks in outputs)
    return pl.pallas_call(
        functools.partial(forward_kernel, outputs, len(pieces), paired),
        out_shape=[jax.ShapeDtypeStruct((len(picks) * rows, width), BF16) for picks in outputs],
        in_specs=[SMEM] * 3 + [ANY] * len(pieces) + [HBM],
        out_specs=[VMEM] * len(outputs),
        scratch_shapes=[
            pltpu.VMEM((gathered, width), BF16),
            pltpu.VMEM((n_picks * (rows // block),) + tiles.shape[1:], BF16),
            pltpu.SemaphoreType.DMA((len(pieces),)),
            pltpu.SemaphoreType.DMA((n_picks,)),
        ],
        compiler_params=params(60),
        cost_estimate=SMALL,
        name="partial_messages",
    )(here, cols, counts, *pieces, tiles)


def mlp_kernel(kinds, nodes, cot, *refs):
    n_parts = sum(kinds)
    parts = refs[:n_parts]
    w_in, bias, w_out, gain, shift, updated, gpre_o, act_o, gproj_o, msg_o, vec = refs[
        n_parts : n_parts + 11
    ]
    gmsgs = refs[n_parts + 11 :]
    width = nodes.shape[1]
    messages = []
    place = 0
    for chunk in kinds:
        total = None
        for _ in range(chunk):
            term = parts[place][...].astype(F32)
            place += 1
            total = term if total is None else total + term
        messages.append(total.astype(BF16))
    message = jnp.concatenate(messages, axis=1) if len(messages) > 1 else messages[0]
    node = nodes[...]
    pre = mm(node, w_in[:width]) + mm(message, w_in[width:]) + bias[...]
    sig = jax.nn.sigmoid(pre)
    act = (pre * sig).astype(BF16)
    proj = mm(act, w_out[...])
    mean = jnp.mean(proj, axis=-1, keepdims=True)
    var = jnp.mean((proj - mean) ** 2, axis=-1, keepdims=True)
    rstd = 1.0 / jnp.sqrt(var + 1e-05)
    normed = (proj - mean) * rstd
    updated[...] = (node.astype(F32) + normed * gain[...] + shift[...]).astype(BF16)
    grad_out = cot[...].astype(F32)
    gscaled = grad_out * gain[...]
    gproj = (
        (
            gscaled
            - jnp.mean(gscaled, axis=-1, keepdims=True)
            - normed * jnp.mean(gscaled * normed, axis=-1, keepdims=True)
        )
        * rstd
    ).astype(BF16)
    gact = mm(gproj, w_out[...], NT)
    gpre = gact * sig * (1.0 + pre * (1.0 - sig))
    gpre_b = gpre.astype(BF16)
    gmsg = mm(gpre_b, w_in[width:], NT).astype(BF16)
    part = width // len(gmsgs)
    for index, out in enumerate(gmsgs):
        out[...] = gmsg[:, index * part : (index + 1) * part]
    gpre_o[...] = gpre_b
    act_o[...] = act
    gproj_o[...] = gproj
    msg_o[...] = message

    @pl.when(pl.program_id(0) == 0)
    def _():
        vec[...] = jnp.zeros_like(vec)

    vec[0:1] += jnp.sum(gpre, axis=0, keepdims=True)
    vec[1:2] += jnp.sum(grad_out * normed, axis=0, keepdims=True)
    vec[2:3] += jnp.sum(grad_out, axis=0, keepdims=True)


def mlp_call(nodes, cot, parts, w_in, bias, w_out, gain, shift):
    rows, width = nodes.shape
    step = min(rows, 256)

    def blocked(array):
        return pl.BlockSpec((step, array.shape[1]), lambda i: (i, 0))

    def whole(array):
        return pl.BlockSpec(array.shape, lambda i: (0, 0))

    flat = [term for chunk in parts for term in chunk]
    row_like = jax.ShapeDtypeStruct((rows, width), BF16)
    chunk_like = jax.ShapeDtypeStruct((rows, width // len(parts)), BF16)
    outs = [row_like] * 5 + [jax.ShapeDtypeStruct((8, width), F32)] + [chunk_like] * len(parts)
    weights = (w_in, bias, w_out, gain, shift)
    result = pl.pallas_call(
        functools.partial(mlp_kernel, [len(chunk) for chunk in parts]),
        grid=(rows // step,),
        out_shape=outs,
        in_specs=[blocked(a) for a in (nodes, cot, *flat)] + [whole(a) for a in weights],
        out_specs=[blocked(a) for a in outs[:5]] + [whole(outs[5])] + [blocked(a) for a in outs[6:]],
        compiler_params=params(40),
        cost_estimate=SMALL,
        name="mlp",
    )(nodes, cot, *flat, *weights)
    return result[:6], result[6:]


def weight_kernel(factor, pieces, n_after, here, nodes, msg, act, gpre, gproj, cot, w_in, vec, *refs):
    *outs, direct, grads = refs[n_after:]
    width = nodes.shape[1]

    @pl.when(pl.program_id(0) == 0)
    def _():
        grads[...] = jnp.zeros_like(grads)
        grads[3 * width : 3 * width + 8] = vec[...] * factor

    gpre_b = gpre[...]
    grads[:width] += mm(nodes[...], gpre_b, TN) * factor
    grads[width : 2 * width] += mm(msg[...], gpre_b, TN) * factor
    grads[2 * width : 3 * width] += mm(act[...], gproj[...], TN) * factor
    direct[...] = cot[...].astype(F32) + mm(gpre_b, w_in[:width], NT)

    @pl.when(pl.program_id(0) == pl.num_programs(0) - 1)
    def _():
        if pieces == 1:
            outs[0][...] = grads[: outs[0].shape[0]]
        else:
            rows = grads.shape[0] // pieces
            for place, member in enumerate(SWAP_ORDER):
                where = pl.ds(pl.multiple_of((Place(here).mine ^ member) * rows, 8), rows)
                out, index = outs[2 * place // pieces], place % (pieces // 2)
                out[index * rows : (index + 1) * rows] = grads[where]


def weight_call(factor, pieces, here, nodes, msg, act, gpre, gproj, cot, w_in, vec, after=()):
    rows, width = nodes.shape
    step = min(rows, 256)
    blocked = pl.BlockSpec((step, width), lambda i: (i, 0))

    def whole(shape):
        return pl.BlockSpec(shape, lambda i: (0, 0))

    padded = (3 * width + width // 2, width)
    if pieces == 1:
        outs = [jax.ShapeDtypeStruct((3 * width + 8, width), F32)]
    else:
        outs = [jax.ShapeDtypeStruct((padded[0] // 2, width), F32)] * 2
    return pl.pallas_call(
        functools.partial(weight_kernel, factor, pieces, len(after)),
        grid=(rows // step,),
        out_shape=[*outs, jax.ShapeDtypeStruct((rows, width), F32)],
        in_specs=[SMEM] + [blocked] * 6 + [whole(w_in.shape), whole(vec.shape)] + [ANY] * len(after),
        out_specs=[whole(out.shape) for out in outs] + [blocked],
        scratch_shapes=[pltpu.VMEM(padded, F32)],
        compiler_params=params(40),
        cost_estimate=SMALL,
        name="weight_grads",
    )(here, nodes, msg, act, gpre, gproj, cot, w_in, vec, *after)


def unpack_kernel(here, even, odd, w_in, w_out, vectors, grads):
    width = w_in.shape[1]
    rows = grads.shape[0] // 8
    for member in range(8):
        part = (even, odd)[member % 2]
        first = member // 2 * rows
        where = pl.ds(pl.multiple_of((Place(here).mine ^ member) * rows, 8), rows)
        grads[where] = part[first : first + rows].astype(F32)
    w_in[...] = grads[: 2 * width]
    w_out[...] = grads[2 * width : 3 * width]
    vectors[...] = grads[3 * width : 3 * width + 3]


def unpack_call(here, even, odd, width):
    shapes = ((2 * width, width), (width, width), (3, width))
    return pl.pallas_call(
        unpack_kernel,
        out_shape=[jax.ShapeDtypeStruct(shape, F32) for shape in shapes],
        in_specs=[SMEM, VMEM, VMEM],
        out_specs=[VMEM] * 3,
        scratch_shapes=[pltpu.VMEM((3 * width + width // 2, width), F32)],
        compiler_params=params(16),
        cost_estimate=SMALL,
        name="weight_unpack",
    )(here, even, odd)


def for_live(found, entry):
    def several(i, carry):
        for index in range(LIVE_STEP):
            entry(i * LIVE_STEP + index)
        return carry

    def one(i, carry):
        entry(i)
        return carry

    full = found // LIVE_STEP
    lax.fori_loop(0, full, several, 0)
    lax.fori_loop(full * LIVE_STEP, found, one, 0)


def back_kernel(blocks, slots, n_after, out_pieces, paired, here, cols, counts, grad, tiles, *refs):
    refs = refs[n_after:]
    outs = refs[: len(out_pieces)]
    grad_v, tiles_v, acc, live, source, sem = refs[len(out_pieces) :]
    n_tiles, block = tiles.shape[:2]
    here = Place(here, paired, blocks)
    copies = [
        pltpu.make_async_copy(grad, grad_v, sem.at[0]),
        pltpu.make_async_copy(tiles, tiles_v, sem.at[1]),
    ]
    for copy in copies:
        copy.start()
    acc[...] = jnp.zeros_like(acc)

    def collect(row, found):
        count = counts[row]
        for slot in range(slots):
            live[found] = row * slots + slot
            source[found] = here.source(cols[slot, row])
            found = found + (slot < count).astype(jnp.int32)
        return found

    found = lax.fori_loop(0, n_tiles // slots, collect, jnp.int32(0))
    for copy in copies:
        copy.wait()

    def entry(place):
        tile_index = live[place]
        part = mm(tiles_v[tile_index], grad_v[block_at(tile_index // slots, block)], TN)
        acc[block_at(source[place], block)] += part

    for_live(found, entry)
    piece = acc.shape[0] // sum(len(members) for members in out_pieces)
    for out, members in zip(outs, out_pieces):
        for index, member in enumerate(members):
            out[pl.ds(index * piece, piece)] = acc[pl.ds(member * piece, piece)].astype(BF16)


def back_call(paired, here, cols, counts, grad, tiles, rows, gathered, out_pieces, after=()):
    width = grad.shape[1]
    row_blocks, slots, block = tiles.shape[:3]
    piece = gathered // sum(len(members) for members in out_pieces)
    return pl.pallas_call(
        functools.partial(back_kernel, rows // block, slots, len(after), out_pieces, paired),
        out_shape=[jax.ShapeDtypeStruct((len(m) * piece, width), BF16) for m in out_pieces],
        in_specs=[SMEM] * 3 + [ANY, HBM] + [ANY] * len(after),
        out_specs=[VMEM] * len(out_pieces),
        scratch_shapes=[
            pltpu.VMEM(grad.shape, BF16),
            pltpu.VMEM((row_blocks * slots, block, block), BF16),
            pltpu.VMEM((gathered, width), F32),
            pltpu.SMEM((row_blocks * slots + 8,), jnp.int32),
            pltpu.SMEM((row_blocks * slots + 8,), jnp.int32),
            pltpu.SemaphoreType.DMA((2,)),
        ],
        compiler_params=params(28 if gathered <= 8192 else 56),
        cost_estimate=SMALL,
        name="back_terms",
    )(here, cols, counts, grad, tiles.reshape(row_blocks * slots, block, block), *after)


def tile_grad_kernel(blocks, n_pieces, n_chunks, n_after, paired, here, cols, counts, *refs):
    grads, refs = refs[:n_chunks], refs[n_chunks:]
    pieces = refs[: n_pieces * n_chunks]
    out, grad_v, nodes_v, tiles_v, live, source, sem, piece_sem, out_sem = refs[n_pieces * n_chunks + n_after :]
    block = out.shape[1]
    slots = out.shape[0] // counts.shape[0]
    width = nodes_v.shape[1]
    part = width // n_chunks
    scale = float(width) ** -0.5
    here = Place(here, paired, blocks)
    copies = []
    for chunk in range(n_chunks):
        columns = pl.ds(chunk * part, part)
        copy = pltpu.make_async_copy(grads[chunk], grad_v.at[:, columns], sem.at[chunk])
        copy.start()
        copies.append(copy)
        copies += load_pieces(
            pieces[chunk * n_pieces : (chunk + 1) * n_pieces],
            nodes_v.at[:, columns],
            piece_sem.at[chunk],
            0,
        )
    tiles_v[...] = jnp.zeros_like(tiles_v)

    def collect(row, found):
        count = counts[row]
        for slot in range(slots):
            live[found] = row * slots + slot
            source[found] = here.source(cols[slot, row])
            found = found + (slot < count).astype(jnp.int32)
        return found

    found = lax.fori_loop(0, counts.shape[0], collect, jnp.int32(0))
    for copy in copies:
        copy.wait()

    def entry(place):
        tile_index = live[place]
        grad = grad_v[block_at(tile_index // slots, block)]
        node = nodes_v[block_at(source[place], block)]
        tiles_v[tile_index] = (mm(grad, node, NT) * scale).astype(BF16)

    for_live(found, entry)
    copy = pltpu.make_async_copy(tiles_v, out, out_sem.at[0])
    copy.start()
    copy.wait()


def tile_grad_call(paired, here, cols, counts, grads, pieces, tiles, rows, after=()):
    row_blocks, slots, block = tiles.shape[:3]
    chunks = len(grads)
    width = grads[0].shape[1] * chunks
    gathered = sum(piece.shape[0] for piece in pieces[0])
    flat = [*grads, *(a for chunk in pieces for a in chunk)]
    entries = row_blocks * slots
    return pl.pallas_call(
        functools.partial(tile_grad_kernel, rows // block, len(pieces[0]), chunks, len(after), paired),
        out_shape=jax.ShapeDtypeStruct((entries, block, block), BF16),
        in_specs=[SMEM] * 3 + [ANY] * (len(flat) + len(after)),
        out_specs=ANY,
        scratch_shapes=[
            pltpu.VMEM((grads[0].shape[0], width), BF16),
            pltpu.VMEM((gathered, width), BF16),
            pltpu.VMEM((entries, block, block), BF16),
            pltpu.SMEM((entries + 8,), jnp.int32),
            pltpu.SMEM((entries + 8,), jnp.int32),
            pltpu.SemaphoreType.DMA((chunks,)),
            pltpu.SemaphoreType.DMA((chunks, len(pieces[0]))),
            pltpu.SemaphoreType.DMA((1,)),
        ],
        compiler_params=params(24 if gathered <= 8192 else 48),
        cost_estimate=SMALL,
        name="tile_grads",
    )(here, cols, counts, *flat, *after)


def swap(value, bit):
    return lax.ppermute(value, "row", [(i, i ^ bit) for i in range(8)])


def turn(value, by):
    return lax.ppermute(value, "col", [(i, (i + by) % 4) for i in range(4)])


def gather_square(nodes):
    pieces = []
    for piece in (nodes, swap(nodes, 2), swap(nodes, 4), swap(nodes, 6)):
        pieces += [piece, swap(piece, 1)]
    return pieces


def reduce_square(even, odd, rows):
    other = swap(odd, 1)
    sums = [sum_call(rows, [(even, piece), (other, piece)]) for piece in (1, 2, 3)]
    arrived = [swap(value, bits) for value, bits in zip(sums, (2, 4, 6))]
    return [even, other, *arrived]


def sum_kernel(n_terms, *refs):
    total = refs[0][...].astype(F32)
    for ref in refs[1:n_terms]:
        total = total + ref[...].astype(F32)
    refs[-1][...] = total.astype(refs[-1].dtype)


def sum_call(rows, terms, dtype=BF16, after=()):
    width = terms[0][0].shape[1]
    step = min(rows, 512)
    steps = rows // step
    return pl.pallas_call(
        functools.partial(sum_kernel, len(terms)),
        grid=(steps,),
        out_shape=jax.ShapeDtypeStruct((rows, width), dtype),
        in_specs=[
            pl.BlockSpec((step, width), lambda i, piece=piece: (piece * steps + i, 0)) for _, piece in terms
        ]
        + [ANY] * len(after),
        out_specs=pl.BlockSpec((step, width), lambda i: (i, 0)),
        compiler_params=params(8),
        cost_estimate=SMALL,
        name="sum_terms",
    )(*(array for array, _ in terms), *after)


def join_kernel(n_chunks, direct, *refs):
    *terms, out = refs
    part = out.shape[1] // n_chunks
    each = len(terms) // n_chunks
    for chunk in range(n_chunks):
        columns = slice(chunk * part, (chunk + 1) * part)
        total = direct[:, columns]
        for term in terms[chunk * each : (chunk + 1) * each]:
            total = total + term[...].astype(F32)
        out[:, columns] = total.astype(out.dtype)


def join_call(direct, chunks):
    rows, width = direct.shape
    step = min(rows, 512)
    terms = [term for chunk in chunks for term in chunk]

    def blocked(columns):
        return pl.BlockSpec((step, columns), lambda i: (i, 0))

    return pl.pallas_call(
        functools.partial(join_kernel, len(chunks)),
        grid=(rows // step,),
        out_shape=jax.ShapeDtypeStruct((rows, width), BF16),
        in_specs=[blocked(width)] + [blocked(term.shape[1]) for term in terms],
        out_specs=blocked(width),
        compiler_params=params(16),
        cost_estimate=SMALL,
        name="node_grads",
    )(direct, *terms)


def scatter_weights(kept, received):
    for bit in (2, 4):
        terms = kept + received
        half = terms.shape[0] // 2
        kept, received = terms[:half], swap(terms[half:], bit)
    return kept, received


def level_weights(kept, received):
    rows = kept.shape[0]
    value = sum_call(rows, [(kept, 0), (received, 0)], dtype=BF16)
    return sum_call(rows, [(term, 0) for term in (value, *(turn(value, by) for by in (1, 2, 3)))])


def gather_weights(here, value, width):
    near = [value, swap(value, 2), swap(value, 4), swap(value, 6)]
    joint = jnp.concatenate(near, axis=0)
    other = swap(joint, 1)
    return unpack_call(here, joint, other, width)


def body(n_row, n_col, nodes, tiles, tile_col, tile_count, w_in, bias_in, w_out, ln_gain, ln_shift, cotangent):
    rows, width = nodes.shape
    row_blocks, _, slots, block = tiles.shape[:4]
    tile_local = tiles.reshape(row_blocks, slots, block, block)
    cols = tile_col.reshape(row_blocks, slots).T
    counts = tile_count.reshape(row_blocks)
    gathered, total = n_row * rows, n_col * rows
    paired = n_row == 8 and n_col == 4
    here = lax.axis_index(("row", "col")).astype(jnp.int32).reshape(1)
    known = (paired, here, cols, counts)
    groups = (tuple(range(n_col)),)
    members = ((1, 3, 5, 7), (0, 2, 4, 6)) if paired else (tuple(range(n_row)),)
    chunks = 2 if paired else 1
    part = width // chunks
    pieces, parts = [], []
    for chunk in range(chunks):
        columns = nodes[:, chunk * part : (chunk + 1) * part]
        if paired:
            pieces.append(gather_square(columns))
        else:
            pieces.append([lax.all_gather(columns, "row", axis=0, tiled=True)])
        (partial,) = forward_call(*known, pieces[-1], tile_local, groups, rows)
        parts.append([lax.psum_scatter(partial, "col", scatter_dimension=0, tiled=True)])
    vectors = [v.reshape(1, width) for v in (bias_in, ln_gain, ln_shift)]
    (updated, gpre_b, act, gproj, message, vec), gmsgs = mlp_call(
        nodes, cotangent, parts, w_in, vectors[0], w_out, vectors[1], vectors[2]
    )
    factor = float(rows * n_row * n_col) ** -0.5
    weight_args = (here, nodes, message, act, gpre_b, gproj, cotangent, w_in, vec)
    if paired:
        first = lax.all_gather(gmsgs[0], "col", axis=0, tiled=True)
        second = lax.all_gather(gmsgs[1], "col", axis=0, tiled=True)
        grads = [first, second]
        kept, sent, direct = weight_call(factor, n_row, *weight_args)
        received = swap(sent, 1)
        row_weights = scatter_weights(kept, received)
        weights = gather_weights(here, level_weights(*row_weights), width)
        odd, even = back_call(*known, first, tile_local, rows, gathered, members, (received,))
        left = reduce_square(even, odd, rows)
        odd, even = back_call(*known, second, tile_local, rows, gathered, members, (*left[2:], weights[2]))
        right = reduce_square(even, odd, rows)
        grad_tiles = tile_grad_call(*known, grads, pieces, tile_local, rows, (right[1],))
        grad_nodes = join_call(direct, [left, right])
    else:
        grads = [lax.all_gather(gmsgs[0], "col", axis=0, tiled=True)]
        weight_terms, direct = weight_call(factor, 1, *weight_args)
        weight_sums = lax.psum(weight_terms, ("row", "col"))
        weights = (
            weight_sums[: 2 * width],
            weight_sums[2 * width : 3 * width],
            weight_sums[3 * width : 3 * width + 3],
        )
        (terms,) = back_call(*known, grads[0], tile_local, rows, gathered, members)
        back = lax.psum_scatter(terms, "row", scatter_dimension=0, tiled=True)
        grad_nodes = join_call(direct, [[back]])
        grad_tiles = tile_grad_call(*known, grads, pieces, tile_local, rows)
    grad_tiles = grad_tiles.reshape(tiles.shape)
    return (updated, grad_nodes, grad_tiles, *weights)


def solution(mesh):
    placed = (
        P(("row", "col"), None),
        P("row", "col", None, None, None),
        P("row", "col", None),
        P("row", "col"),
        P(),
        P(),
        P(),
        P(),
        P(),
        P(("row", "col"), None),
    )
    return jax.shard_map(
        functools.partial(body, mesh.shape["row"], mesh.shape["col"]),
        mesh=mesh,
        in_specs=placed,
        out_specs=(
            P(("row", "col"), None),
            P(("row", "col"), None),
            P("row", "col", None, None, None),
            P(),
            P(),
            P(),
        ),
        check_vma=False,
    )
```

```python
import functools

import jax
import jax.numpy as jnp
from jax import lax
from jax.experimental import pallas as pl
from jax.experimental.pallas import tpu as pltpu
from jax.sharding import PartitionSpec as P

F32 = jnp.float32
BF16 = jnp.bfloat16
ANY = pl.BlockSpec(memory_space=pl.ANY)
HBM = pl.BlockSpec(memory_space=pltpu.HBM)
SMEM = pl.BlockSpec(memory_space=pltpu.SMEM)
VMEM = pl.BlockSpec(memory_space=pltpu.VMEM)
MIB = 1 << 20
TN = (((0,), (0,)), ((), ()))
NT = (((1,), (1,)), ((), ()))
SMALL = pl.CostEstimate(flops=1 << 20, bytes_accessed=1 << 16, transcendentals=0)


LIVE_STEP = 4
GRAD_PLAN = ((3, 0, None), (2, 1, None), (1, 2, "inner"), (1, 3, "outer"), (0, 4, "inner"), (0, 5, "outer"))
SWAP_ORDER = (0, 4, 2, 6, 1, 5, 3, 7)


def params(mib):
    return pltpu.CompilerParams(vmem_limit_bytes=mib * MIB)


def mm(a, b, dims=(((1,), (0,)), ((), ()))):
    return lax.dot_general(a, b, dims, preferred_element_type=F32)


def block_at(index, block):
    return pl.ds(pl.multiple_of(index * block, block), block)


class Place:
    def __init__(self, ref, paired=True, blocks=1):
        self.mine, self.level = lax.shift_right_logical(ref[0], 2), ref[0] & 3
        self.paired, self.blocks = paired, blocks

    def inner(self):
        return (self.level == 1) | (self.level == 2)

    def group(self, pick):
        if not self.paired:
            return pick
        low = self.level < 2
        choices = (jnp.where(low, 3, 0), jnp.where(low, 2, 1), self.level ^ 1, self.level)
        return choices[pick]

    def source(self, col):
        if not self.paired:
            return col
        shift = self.blocks.bit_length() - 1
        if 1 << shift == self.blocks:
            return col ^ lax.shift_left(self.mine, jnp.int32(shift))
        return (lax.div(col, self.blocks) ^ self.mine) * self.blocks + lax.rem(col, self.blocks)


def load_pieces(pieces, dst, sem, first):
    copies = []
    offset = 0
    for index, piece in enumerate(pieces):
        copy = pltpu.make_async_copy(
            piece, dst.at[pl.ds(offset, piece.shape[0])], sem.at[first + index]
        )
        copy.start()
        copies.append(copy)
        offset += piece.shape[0]
    return copies


def masked_tile(tile, live):
    return jnp.where(live, tile, jnp.zeros_like(tile))


def forward_kernel(outputs, n_pieces, paired, here, cols, counts, *refs):
    pieces, tiles = refs[:n_pieces], refs[n_pieces]
    outs = refs[n_pieces + 1 : n_pieces + 1 + len(outputs)]
    nodes_v, tiles_v, sem, tile_sem = refs[n_pieces + 1 + len(outputs) :]
    rows = outs[0].shape[0] // len(outputs[0])
    slots, block = tiles.shape[1], tiles.shape[2]
    blocks = rows // block
    here = Place(here, paired, blocks)
    copies = load_pieces(pieces, nodes_v, sem, 0)
    places = [(pick, out, index) for out, picks in zip(outs, outputs) for index, pick in enumerate(picks)]
    tile_copies = []
    for place, (pick, _, _) in enumerate(places):
        copy = pltpu.make_async_copy(
            tiles.at[pl.ds(here.group(pick) * blocks, blocks)],
            tiles_v.at[pl.ds(place * blocks, blocks)],
            tile_sem.at[place],
        )
        copy.start()
        tile_copies.append(copy)
    for copy in copies:
        copy.wait()
    for place, (pick, out, index) in enumerate(places):
        tile_copies[place].wait()
        first = here.group(pick) * blocks

        def step(i, carry, first=first, out=out, index=index, place=place):
            row = first + i
            count = counts[row]
            parts = []
            for pair in range(slots // 2):
                both = (2 * pair, 2 * pair + 1)
                tile = jnp.concatenate(
                    [masked_tile(tiles_v[place * blocks + i, slot], slot < count) for slot in both], axis=1
                )
                node = jnp.concatenate(
                    [nodes_v[block_at(here.source(cols[slot, row]), block)] for slot in both], axis=0
                )
                parts.append(mm(tile, node))
            value = parts[0]
            for part in parts[1:]:
                value = value + part
            out[block_at(index * blocks + i, block)] = value.astype(BF16)
            return carry

        lax.fori_loop(0, blocks, step, 0, unroll=4)


def forward_call(paired, here, cols, counts, pieces, tiles, outputs, rows):
    width = pieces[0].shape[1]
    gathered = sum(piece.shape[0] for piece in pieces)
    slots, block = tiles.shape[1], tiles.shape[2]
    n_picks = sum(len(picks) for picks in outputs)
    return pl.pallas_call(
        functools.partial(forward_kernel, outputs, len(pieces), paired),
        out_shape=[jax.ShapeDtypeStruct((len(picks) * rows, width), BF16) for picks in outputs],
        in_specs=[SMEM] * 3 + [ANY] * len(pieces) + [HBM],
        out_specs=[VMEM] * len(outputs),
        scratch_shapes=[
            pltpu.VMEM((gathered, width), BF16),
            pltpu.VMEM((n_picks * (rows // block),) + tiles.shape[1:], BF16),
            pltpu.SemaphoreType.DMA((len(pieces),)),
            pltpu.SemaphoreType.DMA((n_picks,)),
        ],
        compiler_params=params(60),
        cost_estimate=SMALL,
        name="partial_messages",
    )(here, cols, counts, *pieces, tiles)


def mlp_kernel(kinds, here, nodes, cot, *refs):
    n_parts = sum(len(chunk) for chunk in kinds)
    parts = refs[:n_parts]
    w_in, bias, w_out, gain, shift, updated, gpre_o, act_o, gproj_o, msg_o, vec = refs[
        n_parts : n_parts + 11
    ]
    gmsgs = refs[n_parts + 11 :]
    width = nodes.shape[1]
    inner = Place(here).inner()
    messages = []
    place = 0
    for chunk in kinds:
        total = None
        for kind in chunk:
            term = parts[place][...].astype(F32)
            place += 1
            if kind == "inner":
                term = jnp.where(inner, term, 0.0)
            total = term if total is None else total + term
        messages.append(total.astype(BF16))
    message = jnp.concatenate(messages, axis=1) if len(messages) > 1 else messages[0]
    node = nodes[...]
    pre = mm(node, w_in[:width]) + mm(message, w_in[width:]) + bias[...]
    sig = jax.nn.sigmoid(pre)
    act = (pre * sig).astype(BF16)
    proj = mm(act, w_out[...])
    mean = jnp.mean(proj, axis=-1, keepdims=True)
    var = jnp.mean((proj - mean) ** 2, axis=-1, keepdims=True)
    rstd = 1.0 / jnp.sqrt(var + 1e-05)
    normed = (proj - mean) * rstd
    updated[...] = (node.astype(F32) + normed * gain[...] + shift[...]).astype(BF16)
    grad_out = cot[...].astype(F32)
    gscaled = grad_out * gain[...]
    gproj = (
        (
            gscaled
            - jnp.mean(gscaled, axis=-1, keepdims=True)
            - normed * jnp.mean(gscaled * normed, axis=-1, keepdims=True)
        )
        * rstd
    ).astype(BF16)
    gact = mm(gproj, w_out[...], NT)
    gpre = gact * sig * (1.0 + pre * (1.0 - sig))
    gpre_b = gpre.astype(BF16)
    gmsg = mm(gpre_b, w_in[width:], NT).astype(BF16)
    part = width // len(gmsgs)
    for index, out in enumerate(gmsgs):
        out[...] = gmsg[:, index * part : (index + 1) * part]
    gpre_o[...] = gpre_b
    act_o[...] = act
    gproj_o[...] = gproj
    msg_o[...] = message

    @pl.when(pl.program_id(0) == 0)
    def _():
        vec[...] = jnp.zeros_like(vec)

    vec[0:1] += jnp.sum(gpre, axis=0, keepdims=True)
    vec[1:2] += jnp.sum(grad_out * normed, axis=0, keepdims=True)
    vec[2:3] += jnp.sum(grad_out, axis=0, keepdims=True)


def mlp_call(here, nodes, cot, parts, kinds, w_in, bias, w_out, gain, shift):
    rows, width = nodes.shape
    step = min(rows, 256)

    def blocked(array):
        return pl.BlockSpec((step, array.shape[1]), lambda i: (i, 0))

    def whole(array):
        return pl.BlockSpec(array.shape, lambda i: (0, 0))

    flat = [term for chunk in parts for term in chunk]
    row_like = jax.ShapeDtypeStruct((rows, width), BF16)
    chunk_like = jax.ShapeDtypeStruct((rows, width // len(parts)), BF16)
    outs = [row_like] * 5 + [jax.ShapeDtypeStruct((8, width), F32)] + [chunk_like] * len(parts)
    weights = (w_in, bias, w_out, gain, shift)
    result = pl.pallas_call(
        functools.partial(mlp_kernel, kinds),
        grid=(rows // step,),
        out_shape=outs,
        in_specs=[SMEM] + [blocked(a) for a in (nodes, cot, *flat)] + [whole(a) for a in weights],
        out_specs=[blocked(a) for a in outs[:5]] + [whole(outs[5])] + [blocked(a) for a in outs[6:]],
        compiler_params=params(40),
        cost_estimate=SMALL,
        name="mlp",
    )(here, nodes, cot, *flat, *weights)
    return result[:6], result[6:]


def weight_kernel(factor, pieces, n_after, here, nodes, msg, act, gpre, gproj, cot, w_in, vec, *refs):
    *outs, direct, grads = refs[n_after:]
    width = nodes.shape[1]

    @pl.when(pl.program_id(0) == 0)
    def _():
        grads[...] = jnp.zeros_like(grads)
        grads[3 * width : 3 * width + 8] = vec[...] * factor

    gpre_b = gpre[...]
    grads[:width] += mm(nodes[...], gpre_b, TN) * factor
    grads[width : 2 * width] += mm(msg[...], gpre_b, TN) * factor
    grads[2 * width : 3 * width] += mm(act[...], gproj[...], TN) * factor
    direct[...] = cot[...].astype(F32) + mm(gpre_b, w_in[:width], NT)

    @pl.when(pl.program_id(0) == pl.num_programs(0) - 1)
    def _():
        if pieces == 1:
            outs[0][...] = grads[: outs[0].shape[0]]
        else:
            rows = grads.shape[0] // pieces
            for place, member in enumerate(SWAP_ORDER):
                where = pl.ds(pl.multiple_of((Place(here).mine ^ member) * rows, 8), rows)
                out, index = outs[2 * place // pieces], place % (pieces // 2)
                out[index * rows : (index + 1) * rows] = grads[where]


def weight_call(factor, pieces, here, nodes, msg, act, gpre, gproj, cot, w_in, vec, after=()):
    rows, width = nodes.shape
    step = min(rows, 256)
    blocked = pl.BlockSpec((step, width), lambda i: (i, 0))

    def whole(shape):
        return pl.BlockSpec(shape, lambda i: (0, 0))

    padded = (3 * width + width // 2, width)
    if pieces == 1:
        outs = [jax.ShapeDtypeStruct((3 * width + 8, width), F32)]
    else:
        outs = [jax.ShapeDtypeStruct((padded[0] // 2, width), F32)] * 2
    return pl.pallas_call(
        functools.partial(weight_kernel, factor, pieces, len(after)),
        grid=(rows // step,),
        out_shape=[*outs, jax.ShapeDtypeStruct((rows, width), F32)],
        in_specs=[SMEM] + [blocked] * 6 + [whole(w_in.shape), whole(vec.shape)] + [ANY] * len(after),
        out_specs=[whole(out.shape) for out in outs] + [blocked],
        scratch_shapes=[pltpu.VMEM(padded, F32)],
        compiler_params=params(40),
        cost_estimate=SMALL,
        name="weight_grads",
    )(here, nodes, msg, act, gpre, gproj, cot, w_in, vec, *after)


def unpack_kernel(here, even, odd, w_in, w_out, vectors, grads):
    width = w_in.shape[1]
    rows = grads.shape[0] // 8
    for member in range(8):
        part = (even, odd)[member % 2]
        first = member // 2 * rows
        where = pl.ds(pl.multiple_of((Place(here).mine ^ member) * rows, 8), rows)
        grads[where] = part[first : first + rows].astype(F32)
    w_in[...] = grads[: 2 * width]
    w_out[...] = grads[2 * width : 3 * width]
    vectors[...] = grads[3 * width : 3 * width + 3]


def unpack_call(here, even, odd, width):
    shapes = ((2 * width, width), (width, width), (3, width))
    return pl.pallas_call(
        unpack_kernel,
        out_shape=[jax.ShapeDtypeStruct(shape, F32) for shape in shapes],
        in_specs=[SMEM, VMEM, VMEM],
        out_specs=[VMEM] * 3,
        scratch_shapes=[pltpu.VMEM((3 * width + width // 2, width), F32)],
        compiler_params=params(16),
        cost_estimate=SMALL,
        name="weight_unpack",
    )(here, even, odd)


def grad_jobs(rows, refs, dst, sem, here, groups=None):
    if len(refs) == 1:
        return [(None, pltpu.make_async_copy(refs[0], dst, sem.at[0]))]
    inner = here.inner()
    conditions = {None: None, "inner": inner, "outer": jnp.logical_not(inner)}
    jobs = []
    for group, index, kind in GRAD_PLAN:
        if groups is None:
            where = block_at(here.group(group), rows)
        elif group in groups:
            where = pl.ds(groups.index(group) * rows, rows)
        else:
            continue
        copy = pltpu.make_async_copy(refs[index], dst.at[where], sem.at[index])
        jobs.append((conditions[kind], copy))
    return jobs


def run_jobs(jobs, verb):
    for condition, copy in jobs:
        if condition is None:
            getattr(copy, verb)()
        else:
            pl.when(condition)(getattr(copy, verb))


def for_live(found, entry):
    def several(i, carry):
        for index in range(LIVE_STEP):
            entry(i * LIVE_STEP + index)
        return carry

    def one(i, carry):
        entry(i)
        return carry

    full = found // LIVE_STEP
    lax.fori_loop(0, full, several, 0)
    lax.fori_loop(full * LIVE_STEP, found, one, 0)


def back_kernel(rows, slots, n_grads, n_after, out_pieces, paired, here, cols, counts, *refs):
    grads, tiles = refs[:n_grads], refs[n_grads]
    refs = refs[n_grads + 1 + n_after :]
    outs = refs[: len(out_pieces)]
    grad_v, tiles_v, acc, live, source, sem, tile_sem = refs[len(out_pieces) :]
    n_tiles, block = tiles.shape[:2]
    here = Place(here, paired, rows // block)
    jobs = grad_jobs(rows, grads, grad_v, sem, here)
    run_jobs(jobs, "start")
    tile_copy = pltpu.make_async_copy(tiles, tiles_v, tile_sem.at[0])
    tile_copy.start()
    acc[...] = jnp.zeros_like(acc)

    def collect(row, found):
        count = counts[row]
        for slot in range(slots):
            live[found] = row * slots + slot
            source[found] = here.source(cols[slot, row])
            found = found + (slot < count).astype(jnp.int32)
        return found

    found = lax.fori_loop(0, n_tiles // slots, collect, jnp.int32(0))
    run_jobs(jobs, "wait")
    tile_copy.wait()

    def entry(place):
        tile_index = live[place]
        part = mm(tiles_v[tile_index], grad_v[block_at(tile_index // slots, block)], TN)
        acc[block_at(source[place], block)] += part

    for_live(found, entry)
    piece = acc.shape[0] // sum(len(members) for members in out_pieces)
    for out, members in zip(outs, out_pieces):
        for index, member in enumerate(members):
            out[pl.ds(index * piece, piece)] = acc[pl.ds(member * piece, piece)].astype(BF16)


def back_call(paired, here, cols, counts, grads, tiles, total, gathered, out_pieces, after=()):
    rows, width = grads[0].shape
    rows = total if len(grads) == 1 else rows
    row_blocks, slots, block = tiles.shape[:3]
    piece = gathered // sum(len(members) for members in out_pieces)
    return pl.pallas_call(
        functools.partial(back_kernel, rows, slots, len(grads), len(after), out_pieces, paired),
        out_shape=[jax.ShapeDtypeStruct((len(m) * piece, width), BF16) for m in out_pieces],
        in_specs=[SMEM] * 3 + [ANY] * len(grads) + [HBM] + [ANY] * len(after),
        out_specs=[VMEM] * len(out_pieces),
        scratch_shapes=[
            pltpu.VMEM((total, width), BF16),
            pltpu.VMEM((row_blocks * slots, block, block), BF16),
            pltpu.VMEM((gathered, width), F32),
            pltpu.SMEM((row_blocks * slots + 8,), jnp.int32),
            pltpu.SMEM((row_blocks * slots + 8,), jnp.int32),
            pltpu.SemaphoreType.DMA((len(grads),)),
            pltpu.SemaphoreType.DMA((1,)),
        ],
        compiler_params=params(28 if gathered <= 8192 else 56),
        cost_estimate=SMALL,
        name="back_terms",
    )(here, cols, counts, *grads, tiles.reshape(row_blocks * slots, block, block), *after)


def tile_grad_kernel(
    rows, slots, n_grads, n_pieces, n_chunks, n_after, groups, paired, here, cols, counts, *refs
):
    grads = refs[: n_grads * n_chunks]
    refs = refs[n_grads * n_chunks :]
    pieces = refs[: n_pieces * n_chunks]
    out, token, grad_v, nodes_v, tiles_v, live, source, sem, piece_sem, out_sem = refs[n_pieces * n_chunks + n_after :]
    token[...] = jnp.zeros_like(token)
    block = out.shape[1]
    width = nodes_v.shape[1]
    part = width // n_chunks
    scale = float(width) ** -0.5
    blocks = grad_v.shape[0] // (block * len(groups))
    here = Place(here, paired, blocks)
    jobs, copies = [], []
    for chunk in range(n_chunks):
        columns = pl.ds(chunk * part, part)
        jobs += grad_jobs(
            rows,
            grads[chunk * n_grads : (chunk + 1) * n_grads],
            grad_v.at[:, columns],
            sem.at[chunk],
            here,
            groups,
        )
        copies += load_pieces(
            pieces[chunk * n_pieces : (chunk + 1) * n_pieces],
            nodes_v.at[:, columns],
            piece_sem.at[chunk],
            0,
        )
    run_jobs(jobs, "start")
    tiles_v[...] = jnp.zeros_like(tiles_v)
    found = jnp.int32(0)
    for index, group in enumerate(groups):
        first = here.group(group) * blocks

        def collect(i, found, first=first, index=index):
            row = first + i
            count = counts[row]
            for slot in range(slots):
                live[found] = (index * blocks + i) * slots + slot
                source[found] = here.source(cols[slot, row])
                found = found + (slot < count).astype(jnp.int32)
            return found

        found = lax.fori_loop(0, blocks, collect, found)
    run_jobs(jobs, "wait")
    for copy in copies:
        copy.wait()

    def entry(place):
        tile_index = live[place]
        grad = grad_v[block_at(tile_index // slots, block)]
        node = nodes_v[block_at(source[place], block)]
        tiles_v[tile_index] = (mm(grad, node, NT) * scale).astype(BF16)

    for_live(found, entry)
    size = blocks * slots
    copies = []
    for index, group in enumerate(groups):
        copy = pltpu.make_async_copy(
            tiles_v.at[pl.ds(index * size, size)],
            out.at[pl.ds(here.group(group) * size, size)],
            out_sem.at[index],
        )
        copy.start()
        copies.append(copy)
    for copy in copies:
        copy.wait()


def tile_grad_call(paired, here, cols, counts, grads, pieces, shape, rows, groups, base=None, after=()):
    row_blocks, slots, block = shape[:3]
    chunks = len(grads)
    width = grads[0][0].shape[1] * chunks
    gathered = sum(piece.shape[0] for piece in pieces[0])
    flat = [a for chunk in grads for a in chunk] + [a for chunk in pieces for a in chunk]
    after = after if base is None else (base,) + tuple(after)
    entries = len(groups) * rows // block * slots
    return pl.pallas_call(
        functools.partial(
            tile_grad_kernel, rows, slots, len(grads[0]), len(pieces[0]), chunks, len(after), groups, paired
        ),
        out_shape=[
            jax.ShapeDtypeStruct((row_blocks * slots, block, block), BF16),
            jax.ShapeDtypeStruct((8, 128), F32),
        ],
        in_specs=[SMEM] * 3 + [ANY] * (len(flat) + len(after)),
        out_specs=[ANY, VMEM],
        input_output_aliases={} if base is None else {3 + len(flat): 0},
        scratch_shapes=[
            pltpu.VMEM((len(groups) * rows, width), BF16),
            pltpu.VMEM((gathered, width), BF16),
            pltpu.VMEM((entries, block, block), BF16),
            pltpu.SMEM((entries + 8,), jnp.int32),
            pltpu.SMEM((entries + 8,), jnp.int32),
            pltpu.SemaphoreType.DMA((chunks, len(grads[0]))),
            pltpu.SemaphoreType.DMA((chunks, len(pieces[0]))),
            pltpu.SemaphoreType.DMA((len(groups),)),
        ],
        compiler_params=params(16 if gathered <= 8192 else 40),
        cost_estimate=SMALL,
        name="tile_grads",
    )(here, cols, counts, *flat, *after)


def swap(value, bit):
    return lax.ppermute(value, "row", [(i, i ^ bit) for i in range(8)])


def outer_swap(value):
    return lax.ppermute(value, "col", [(0, 1), (1, 0), (2, 3), (3, 2)])


def turn(value, by):
    return lax.ppermute(value, "col", [(i, (i + by) % 4) for i in range(4)])


def inner_swap(value):
    pairs = []
    for row in range(8):
        for col in range(4):
            partner = (row, 3 - col) if col in (1, 2) else (row ^ 1, col)
            pairs.append((row * 4 + col, partner[0] * 4 + partner[1]))
    return lax.ppermute(value, ("row", "col"), pairs)


def gather_square(nodes):
    half = nodes.shape[0] // 2
    lower, upper = nodes[:half], nodes[half:]
    y_lower, x_upper = swap(lower, 4), swap(upper, 2)
    x_lower, y_upper = swap(lower, 2), swap(upper, 4)
    d_lower, d_upper = swap(y_lower, 2), swap(x_upper, 4)
    pieces = [nodes, swap(nodes, 1)]
    for pair in ((x_lower, x_upper), (y_lower, y_upper), (d_lower, d_upper)):
        pieces += [*pair, *(swap(piece, 1) for piece in pair)]
    return pieces


def reduce_square(here, even, other, rows, after):
    sums = [sum_call(here, rows, [(even, piece), (other, piece)], after=after) for piece in (1, 2, 3)]
    return [swap(value, bits) for value, bits in zip(sums, (2, 4, 6))], sums


def sum_kernel(n_terms, n_gated, n_split, *refs):
    inner, refs = Place(refs[0]).inner(), refs[1:]
    total = None
    for index, ref in enumerate(refs[: n_terms + n_gated]):
        term = ref[...].astype(F32)
        if index >= n_terms:
            term = jnp.where(inner, term, 0.0)
        total = term if total is None else total + term
    for index in range(n_split):
        first, second = refs[n_terms + n_gated + 2 * index :][:2]
        early = pl.program_id(0) < pl.num_programs(0) // 2
        total = total + jnp.where(early, first[...], second[...]).astype(F32)
    refs[-1][...] = total.astype(refs[-1].dtype)


def sum_call(here, rows, terms, gated=(), split=(), dtype=BF16, after=()):
    both = [*terms, *gated]
    width = both[0][0].shape[1]
    step = min(rows, 256)
    steps = rows // step
    return pl.pallas_call(
        functools.partial(sum_kernel, len(terms), len(gated), len(split)),
        grid=(steps,),
        out_shape=jax.ShapeDtypeStruct((rows, width), dtype),
        in_specs=[SMEM]
        + [pl.BlockSpec((step, width), lambda i, piece=piece: (piece * steps + i, 0)) for _, piece in both]
        + [
            pl.BlockSpec((step, width), lambda i: (jnp.minimum(i, steps // 2 - 1), 0)),
            pl.BlockSpec((step, width), lambda i: (jnp.maximum(i - steps // 2, 0), 0)),
        ]
        * len(split)
        + [ANY] * len(after),
        out_specs=pl.BlockSpec((step, width), lambda i: (i, 0)),
        compiler_params=params(8),
        cost_estimate=SMALL,
        name="sum_terms",
    )(here, *(array for array, _ in both), *(half for pair in split for half in pair), *after)


def scatter_weights(kept, sent):
    for bit in (1, 2):
        terms = kept + swap(sent, bit)
        half = terms.shape[0] // 2
        kept, sent = terms[:half], terms[half:]
    return kept, swap(sent, 4)


def level_weights(here, kept, received, after):
    rows = kept.shape[0]
    value = sum_call(here, rows, [(kept, 0), (received, 0)], dtype=BF16, after=after)
    return sum_call(here, rows, [(term, 0) for term in (value, *(turn(value, by) for by in (1, 2, 3)))])


def reduce_line(here, far, near, pair, own):
    rows = own.shape[0]
    far_sum = inner_swap(sum_call(here, rows, [(far, 0), (outer_swap(far), 0)]))
    near_sum = inner_swap(sum_call(here, rows, [(near, 0), (outer_swap(near), 0)]))
    pair_in = outer_swap(sum_call(here, rows, [(pair, 0)], [(far_sum, 0)]))
    return own, pair_in, near_sum


def gather_line(own):
    pair = outer_swap(own)
    near_inner = inner_swap(own)
    far_inner = inner_swap(pair)
    near_outer = outer_swap(near_inner)
    far_outer = outer_swap(far_inner)
    return [own, pair, near_inner, near_outer, far_inner, far_outer]


def body(n_row, n_col, nodes, tiles, tile_col, tile_count, w_in, bias_in, w_out, ln_gain, ln_shift, cotangent):
    rows, width = nodes.shape
    row_blocks, _, slots, block = tiles.shape[:4]
    tile_local = tiles.reshape(row_blocks, slots, block, block)
    cols = tile_col.reshape(row_blocks, slots).T
    counts = tile_count.reshape(row_blocks)
    gathered, total = n_row * rows, n_col * rows
    paired = n_row == 8 and n_col == 4
    here = lax.axis_index(("row", "col")).astype(jnp.int32).reshape(1)
    known = (paired, here, cols, counts)
    if paired:
        pieces = [gather_square(nodes)]
        far, near = forward_call(*known, pieces[0], tile_local, ((0,), (1,)), rows)
        pair, own = forward_call(*known, pieces[0], tile_local, ((2,), (3,)), rows)
        parts = [reduce_line(here, far, near, pair, own)]
        kinds = [("all", "all", "inner")]
    else:
        pieces = [[lax.all_gather(nodes, "row", axis=0, tiled=True)]]
        (partial,) = forward_call(*known, pieces[0], tile_local, (tuple(range(n_col)),), rows)
        parts = [[lax.psum_scatter(partial, "col", scatter_dimension=0, tiled=True)]]
        kinds = [("all",)]
    vectors = [v.reshape(1, width) for v in (bias_in, ln_gain, ln_shift)]
    (updated, gpre_b, act, gproj, message, vec), gmsgs = mlp_call(
        here, nodes, cotangent, parts, kinds, w_in, vectors[0], w_out, vectors[1], vectors[2]
    )
    factor = float(rows * n_row * n_col) ** -0.5
    weight_args = (here, nodes, message, act, gpre_b, gproj, cotangent, w_in, vec)
    if paired:
        halves = ((1, 3, 5, 7), (0, 2, 4, 6))
        grads = [gather_line(gmsgs[0])]
        kept, sent, direct = weight_call(factor, n_row, *weight_args, ())
        row_weights = scatter_weights(kept, sent)
        near_grads, token = tile_grad_call(
            *known, [grads[0][:2]], pieces, tile_local.shape, rows, (3, 2), after=(grads[0][3], grads[0][4])
        )
        all_weights = level_weights(here, *row_weights, (token,))
        odd, even = back_call(*known, grads[0], tile_local, total, gathered, halves, (token, all_weights))
        other = swap(odd, 1)
        joint = jnp.concatenate([all_weights] + [swap(all_weights, bits) for bits in (2, 4, 6)], axis=0)
        arrived, sums = reduce_square(here, even, other, rows, (joint,))
        weights = unpack_call(here, joint, swap(joint, 1), width)
        grad_tiles, _ = tile_grad_call(
            *known, grads, pieces, tile_local.shape, rows, (1, 0), near_grads, sums
        )
        grad_nodes = sum_call(
            here, rows, [(direct, 0), (even, 0), (other, 0)] + [(term, 0) for term in arrived]
        )
    else:
        grads = [[lax.all_gather(gmsgs[0], "col", axis=0, tiled=True)]]
        weight_terms, direct = weight_call(factor, 1, *weight_args)
        weight_sums = lax.psum(weight_terms, ("row", "col"))
        weights = (
            weight_sums[: 2 * width],
            weight_sums[2 * width : 3 * width],
            weight_sums[3 * width : 3 * width + 3],
        )
        (terms,) = back_call(*known, grads[0], tile_local, total, gathered, (tuple(range(n_row)),))
        back = lax.psum_scatter(terms, "row", scatter_dimension=0, tiled=True)
        grad_nodes = sum_call(here, rows, [(direct, 0), (back, 0)])
        grad_tiles, _ = tile_grad_call(
            *known, grads, pieces, tile_local.shape, rows, tuple(range(n_col))
        )
    grad_tiles = grad_tiles.reshape(tiles.shape)
    return (updated, grad_nodes, grad_tiles, *weights)


def solution(mesh):
    placed = (
        P(("row", "col"), None),
        P("row", "col", None, None, None),
        P("row", "col", None),
        P("row", "col"),
        P(),
        P(),
        P(),
        P(),
        P(),
        P(("row", "col"), None),
    )
    return jax.shard_map(
        functools.partial(body, mesh.shape["row"], mesh.shape["col"]),
        mesh=mesh,
        in_specs=placed,
        out_specs=(
            P(("row", "col"), None),
            P(("row", "col"), None),
            P("row", "col", None, None, None),
            P(),
            P(),
            P(),
        ),
        check_vma=False,
    )
```

```python
import functools

import jax
import jax.numpy as jnp
from jax import lax
from jax.experimental import pallas as pl
from jax.experimental.pallas import tpu as pltpu
from jax.sharding import PartitionSpec as P

F32 = jnp.float32
BF16 = jnp.bfloat16
ANY = pl.BlockSpec(memory_space=pl.ANY)
HBM = pl.BlockSpec(memory_space=pltpu.HBM)
SMEM = pl.BlockSpec(memory_space=pltpu.SMEM)
VMEM = pl.BlockSpec(memory_space=pltpu.VMEM)
MIB = 1 << 20
TN = (((0,), (0,)), ((), ()))
NT = (((1,), (1,)), ((), ()))
SMALL = pl.CostEstimate(flops=1 << 20, bytes_accessed=1 << 16, transcendentals=0)


LIVE_STEP = 4
GRAD_PLAN = ((3, 0, None), (2, 1, None), (1, 2, "inner"), (1, 3, "outer"), (0, 4, "inner"), (0, 5, "outer"))
SWAP_ORDER = (0, 4, 2, 6, 1, 5, 3, 7)


def params(mib):
    return pltpu.CompilerParams(vmem_limit_bytes=mib * MIB)


def mm(a, b, dims=(((1,), (0,)), ((), ()))):
    return lax.dot_general(a, b, dims, preferred_element_type=F32)


def block_at(index, block):
    return pl.ds(pl.multiple_of(index * block, block), block)


class Place:
    def __init__(self, ref, paired=True, blocks=1):
        self.mine, self.level = lax.shift_right_logical(ref[0], 2), ref[0] & 3
        self.paired, self.blocks = paired, blocks

    def inner(self):
        return (self.level == 1) | (self.level == 2)

    def group(self, pick):
        if not self.paired:
            return pick
        low = self.level < 2
        choices = (jnp.where(low, 3, 0), jnp.where(low, 2, 1), self.level ^ 1, self.level)
        return choices[pick]

    def source(self, col):
        if not self.paired:
            return col
        shift = self.blocks.bit_length() - 1
        if 1 << shift == self.blocks:
            return col ^ lax.shift_left(self.mine, jnp.int32(shift))
        return (lax.div(col, self.blocks) ^ self.mine) * self.blocks + lax.rem(col, self.blocks)


def load_pieces(pieces, dst, sem, first):
    copies = []
    offset = 0
    for index, piece in enumerate(pieces):
        copy = pltpu.make_async_copy(
            piece, dst.at[pl.ds(offset, piece.shape[0])], sem.at[first + index]
        )
        copy.start()
        copies.append(copy)
        offset += piece.shape[0]
    return copies


def masked_tile(tile, live):
    return jnp.where(live, tile, jnp.zeros_like(tile))


def forward_kernel(outputs, n_pieces, paired, here, cols, counts, *refs):
    pieces, tiles = refs[:n_pieces], refs[n_pieces]
    outs = refs[n_pieces + 1 : n_pieces + 1 + len(outputs)]
    nodes_v, tiles_v, sem, tile_sem = refs[n_pieces + 1 + len(outputs) :]
    rows = outs[0].shape[0] // len(outputs[0])
    slots, block = tiles.shape[1], tiles.shape[2]
    blocks = rows // block
    here = Place(here, paired, blocks)
    copies = load_pieces(pieces, nodes_v, sem, 0)
    places = [(pick, out, index) for out, picks in zip(outs, outputs) for index, pick in enumerate(picks)]
    tile_copies = []
    for place, (pick, _, _) in enumerate(places):
        copy = pltpu.make_async_copy(
            tiles.at[pl.ds(here.group(pick) * blocks, blocks)],
            tiles_v.at[pl.ds(place * blocks, blocks)],
            tile_sem.at[place],
        )
        copy.start()
        tile_copies.append(copy)
    for copy in copies:
        copy.wait()
    for place, (pick, out, index) in enumerate(places):
        tile_copies[place].wait()
        first = here.group(pick) * blocks

        def step(i, carry, first=first, out=out, index=index, place=place):
            row = first + i
            count = counts[row]
            parts = []
            for pair in range(slots // 2):
                both = (2 * pair, 2 * pair + 1)
                tile = jnp.concatenate(
                    [masked_tile(tiles_v[place * blocks + i, slot], slot < count) for slot in both], axis=1
                )
                node = jnp.concatenate(
                    [nodes_v[block_at(here.source(cols[slot, row]), block)] for slot in both], axis=0
                )
                parts.append(mm(tile, node))
            value = parts[0]
            for part in parts[1:]:
                value = value + part
            out[block_at(index * blocks + i, block)] = value.astype(BF16)
            return carry

        lax.fori_loop(0, blocks, step, 0, unroll=4)


def forward_call(paired, here, cols, counts, pieces, tiles, outputs, rows):
    width = pieces[0].shape[1]
    gathered = sum(piece.shape[0] for piece in pieces)
    slots, block = tiles.shape[1], tiles.shape[2]
    n_picks = sum(len(picks) for picks in outputs)
    return pl.pallas_call(
        functools.partial(forward_kernel, outputs, len(pieces), paired),
        out_shape=[jax.ShapeDtypeStruct((len(picks) * rows, width), BF16) for picks in outputs],
        in_specs=[SMEM] * 3 + [ANY] * len(pieces) + [HBM],
        out_specs=[VMEM] * len(outputs),
        scratch_shapes=[
            pltpu.VMEM((gathered, width), BF16),
            pltpu.VMEM((n_picks * (rows // block),) + tiles.shape[1:], BF16),
            pltpu.SemaphoreType.DMA((len(pieces),)),
            pltpu.SemaphoreType.DMA((n_picks,)),
        ],
        compiler_params=params(60),
        cost_estimate=SMALL,
        name="partial_messages",
    )(here, cols, counts, *pieces, tiles)


def mlp_kernel(kinds, here, nodes, cot, *refs):
    n_parts = sum(len(chunk) for chunk in kinds)
    parts = refs[:n_parts]
    w_in, bias, w_out, gain, shift, updated, gpre_o, act_o, gproj_o, msg_o, vec = refs[
        n_parts : n_parts + 11
    ]
    gmsgs = refs[n_parts + 11 :]
    width = nodes.shape[1]
    inner = Place(here).inner()
    messages = []
    place = 0
    for chunk in kinds:
        total = None
        for kind in chunk:
            term = parts[place][...].astype(F32)
            place += 1
            if kind == "inner":
                term = jnp.where(inner, term, 0.0)
            total = term if total is None else total + term
        messages.append(total.astype(BF16))
    message = jnp.concatenate(messages, axis=1) if len(messages) > 1 else messages[0]
    node = nodes[...]
    pre = mm(node, w_in[:width]) + mm(message, w_in[width:]) + bias[...]
    sig = jax.nn.sigmoid(pre)
    act = (pre * sig).astype(BF16)
    proj = mm(act, w_out[...])
    mean = jnp.mean(proj, axis=-1, keepdims=True)
    var = jnp.mean((proj - mean) ** 2, axis=-1, keepdims=True)
    rstd = 1.0 / jnp.sqrt(var + 1e-05)
    normed = (proj - mean) * rstd
    updated[...] = (node.astype(F32) + normed * gain[...] + shift[...]).astype(BF16)
    grad_out = cot[...].astype(F32)
    gscaled = grad_out * gain[...]
    gproj = (
        (
            gscaled
            - jnp.mean(gscaled, axis=-1, keepdims=True)
            - normed * jnp.mean(gscaled * normed, axis=-1, keepdims=True)
        )
        * rstd
    ).astype(BF16)
    gact = mm(gproj, w_out[...], NT)
    gpre = gact * sig * (1.0 + pre * (1.0 - sig))
    gpre_b = gpre.astype(BF16)
    gmsg = mm(gpre_b, w_in[width:], NT).astype(BF16)
    part = width // len(gmsgs)
    for index, out in enumerate(gmsgs):
        out[...] = gmsg[:, index * part : (index + 1) * part]
    gpre_o[...] = gpre_b
    act_o[...] = act
    gproj_o[...] = gproj
    msg_o[...] = message

    @pl.when(pl.program_id(0) == 0)
    def _():
        vec[...] = jnp.zeros_like(vec)

    vec[0:1] += jnp.sum(gpre, axis=0, keepdims=True)
    vec[1:2] += jnp.sum(grad_out * normed, axis=0, keepdims=True)
    vec[2:3] += jnp.sum(grad_out, axis=0, keepdims=True)


def mlp_call(here, nodes, cot, parts, kinds, w_in, bias, w_out, gain, shift):
    rows, width = nodes.shape
    step = min(rows, 256)

    def blocked(array):
        return pl.BlockSpec((step, array.shape[1]), lambda i: (i, 0))

    def whole(array):
        return pl.BlockSpec(array.shape, lambda i: (0, 0))

    flat = [term for chunk in parts for term in chunk]
    row_like = jax.ShapeDtypeStruct((rows, width), BF16)
    chunk_like = jax.ShapeDtypeStruct((rows, width // len(parts)), BF16)
    outs = [row_like] * 5 + [jax.ShapeDtypeStruct((8, width), F32)] + [chunk_like] * len(parts)
    weights = (w_in, bias, w_out, gain, shift)
    result = pl.pallas_call(
        functools.partial(mlp_kernel, kinds),
        grid=(rows // step,),
        out_shape=outs,
        in_specs=[SMEM] + [blocked(a) for a in (nodes, cot, *flat)] + [whole(a) for a in weights],
        out_specs=[blocked(a) for a in outs[:5]] + [whole(outs[5])] + [blocked(a) for a in outs[6:]],
        compiler_params=params(40),
        cost_estimate=SMALL,
        name="mlp",
    )(here, nodes, cot, *flat, *weights)
    return result[:6], result[6:]


def weight_kernel(factor, pieces, n_after, here, nodes, msg, act, gpre, gproj, cot, w_in, vec, *refs):
    *outs, direct, grads = refs[n_after:]
    width = nodes.shape[1]

    @pl.when(pl.program_id(0) == 0)
    def _():
        grads[...] = jnp.zeros_like(grads)
        grads[3 * width : 3 * width + 8] = vec[...] * factor

    gpre_b = gpre[...]
    grads[:width] += mm(nodes[...], gpre_b, TN) * factor
    grads[width : 2 * width] += mm(msg[...], gpre_b, TN) * factor
    grads[2 * width : 3 * width] += mm(act[...], gproj[...], TN) * factor
    direct[...] = cot[...].astype(F32) + mm(gpre_b, w_in[:width], NT)

    @pl.when(pl.program_id(0) == pl.num_programs(0) - 1)
    def _():
        if pieces == 1:
            outs[0][...] = grads[: outs[0].shape[0]]
        else:
            rows = grads.shape[0] // pieces
            for place, member in enumerate(SWAP_ORDER):
                where = pl.ds(pl.multiple_of((Place(here).mine ^ member) * rows, 8), rows)
                out, index = outs[2 * place // pieces], place % (pieces // 2)
                out[index * rows : (index + 1) * rows] = grads[where]


def weight_call(factor, pieces, here, nodes, msg, act, gpre, gproj, cot, w_in, vec, after=()):
    rows, width = nodes.shape
    step = min(rows, 256)
    blocked = pl.BlockSpec((step, width), lambda i: (i, 0))

    def whole(shape):
        return pl.BlockSpec(shape, lambda i: (0, 0))

    padded = (3 * width + width // 2, width)
    if pieces == 1:
        outs = [jax.ShapeDtypeStruct((3 * width + 8, width), F32)]
    else:
        outs = [jax.ShapeDtypeStruct((padded[0] // 2, width), F32)] * 2
    return pl.pallas_call(
        functools.partial(weight_kernel, factor, pieces, len(after)),
        grid=(rows // step,),
        out_shape=[*outs, jax.ShapeDtypeStruct((rows, width), F32)],
        in_specs=[SMEM] + [blocked] * 6 + [whole(w_in.shape), whole(vec.shape)] + [ANY] * len(after),
        out_specs=[whole(out.shape) for out in outs] + [blocked],
        scratch_shapes=[pltpu.VMEM(padded, F32)],
        compiler_params=params(40),
        cost_estimate=SMALL,
        name="weight_grads",
    )(here, nodes, msg, act, gpre, gproj, cot, w_in, vec, *after)


def unpack_kernel(here, even, odd, w_in, w_out, vectors, grads):
    width = w_in.shape[1]
    rows = grads.shape[0] // 8
    for member in range(8):
        part = (even, odd)[member % 2]
        first = member // 2 * rows
        where = pl.ds(pl.multiple_of((Place(here).mine ^ member) * rows, 8), rows)
        grads[where] = part[first : first + rows].astype(F32)
    w_in[...] = grads[: 2 * width]
    w_out[...] = grads[2 * width : 3 * width]
    vectors[...] = grads[3 * width : 3 * width + 3]


def unpack_call(here, even, odd, width):
    shapes = ((2 * width, width), (width, width), (3, width))
    return pl.pallas_call(
        unpack_kernel,
        out_shape=[jax.ShapeDtypeStruct(shape, F32) for shape in shapes],
        in_specs=[SMEM, VMEM, VMEM],
        out_specs=[VMEM] * 3,
        scratch_shapes=[pltpu.VMEM((3 * width + width // 2, width), F32)],
        compiler_params=params(16),
        cost_estimate=SMALL,
        name="weight_unpack",
    )(here, even, odd)


def grad_jobs(rows, refs, dst, sem, here, groups=None):
    if len(refs) == 1:
        return [(None, pltpu.make_async_copy(refs[0], dst, sem.at[0]))]
    inner = here.inner()
    conditions = {None: None, "inner": inner, "outer": jnp.logical_not(inner)}
    jobs = []
    for group, index, kind in GRAD_PLAN:
        if groups is None:
            where = block_at(here.group(group), rows)
        elif group in groups:
            where = pl.ds(groups.index(group) * rows, rows)
        else:
            continue
        copy = pltpu.make_async_copy(refs[index], dst.at[where], sem.at[index])
        jobs.append((conditions[kind], copy))
    return jobs


def run_jobs(jobs, verb):
    for condition, copy in jobs:
        if condition is None:
            getattr(copy, verb)()
        else:
            pl.when(condition)(getattr(copy, verb))


def for_live(found, entry):
    def several(i, carry):
        for index in range(LIVE_STEP):
            entry(i * LIVE_STEP + index)
        return carry

    def one(i, carry):
        entry(i)
        return carry

    full = found // LIVE_STEP
    lax.fori_loop(0, full, several, 0)
    lax.fori_loop(full * LIVE_STEP, found, one, 0)


def back_kernel(rows, slots, n_grads, n_after, out_pieces, paired, here, cols, counts, *refs):
    grads, tiles = refs[:n_grads], refs[n_grads]
    refs = refs[n_grads + 1 + n_after :]
    outs = refs[: len(out_pieces)]
    grad_v, tiles_v, acc, live, source, sem, tile_sem = refs[len(out_pieces) :]
    n_tiles, block = tiles.shape[:2]
    here = Place(here, paired, rows // block)
    jobs = grad_jobs(rows, grads, grad_v, sem, here)
    run_jobs(jobs, "start")
    tile_copy = pltpu.make_async_copy(tiles, tiles_v, tile_sem.at[0])
    tile_copy.start()
    acc[...] = jnp.zeros_like(acc)

    def collect(row, found):
        count = counts[row]
        for slot in range(slots):
            live[found] = row * slots + slot
            source[found] = here.source(cols[slot, row])
            found = found + (slot < count).astype(jnp.int32)
        return found

    found = lax.fori_loop(0, n_tiles // slots, collect, jnp.int32(0))
    run_jobs(jobs, "wait")
    tile_copy.wait()

    def entry(place):
        tile_index = live[place]
        part = mm(tiles_v[tile_index], grad_v[block_at(tile_index // slots, block)], TN)
        acc[block_at(source[place], block)] += part

    for_live(found, entry)
    piece = acc.shape[0] // sum(len(members) for members in out_pieces)
    for out, members in zip(outs, out_pieces):
        for index, member in enumerate(members):
            out[pl.ds(index * piece, piece)] = acc[pl.ds(member * piece, piece)].astype(BF16)


def back_call(paired, here, cols, counts, grads, tiles, total, gathered, out_pieces, after=()):
    rows, width = grads[0].shape
    rows = total if len(grads) == 1 else rows
    row_blocks, slots, block = tiles.shape[:3]
    piece = gathered // sum(len(members) for members in out_pieces)
    return pl.pallas_call(
        functools.partial(back_kernel, rows, slots, len(grads), len(after), out_pieces, paired),
        out_shape=[jax.ShapeDtypeStruct((len(m) * piece, width), BF16) for m in out_pieces],
        in_specs=[SMEM] * 3 + [ANY] * len(grads) + [HBM] + [ANY] * len(after),
        out_specs=[VMEM] * len(out_pieces),
        scratch_shapes=[
            pltpu.VMEM((total, width), BF16),
            pltpu.VMEM((row_blocks * slots, block, block), BF16),
            pltpu.VMEM((gathered, width), F32),
            pltpu.SMEM((row_blocks * slots + 8,), jnp.int32),
            pltpu.SMEM((row_blocks * slots + 8,), jnp.int32),
            pltpu.SemaphoreType.DMA((len(grads),)),
            pltpu.SemaphoreType.DMA((1,)),
        ],
        compiler_params=params(28 if gathered <= 8192 else 56),
        cost_estimate=SMALL,
        name="back_terms",
    )(here, cols, counts, *grads, tiles.reshape(row_blocks * slots, block, block), *after)


def tile_grad_kernel(
    rows, slots, n_grads, n_pieces, n_chunks, n_after, groups, paired, here, cols, counts, *refs
):
    grads = refs[: n_grads * n_chunks]
    refs = refs[n_grads * n_chunks :]
    pieces = refs[: n_pieces * n_chunks]
    out, token, grad_v, nodes_v, tiles_v, live, source, sem, piece_sem, out_sem = refs[n_pieces * n_chunks + n_after :]
    token[...] = jnp.zeros_like(token)
    block = out.shape[1]
    width = nodes_v.shape[1]
    part = width // n_chunks
    scale = float(width) ** -0.5
    blocks = grad_v.shape[0] // (block * len(groups))
    here = Place(here, paired, blocks)
    jobs, copies = [], []
    for chunk in range(n_chunks):
        columns = pl.ds(chunk * part, part)
        jobs += grad_jobs(
            rows,
            grads[chunk * n_grads : (chunk + 1) * n_grads],
            grad_v.at[:, columns],
            sem.at[chunk],
            here,
            groups,
        )
        copies += load_pieces(
            pieces[chunk * n_pieces : (chunk + 1) * n_pieces],
            nodes_v.at[:, columns],
            piece_sem.at[chunk],
            0,
        )
    run_jobs(jobs, "start")
    tiles_v[...] = jnp.zeros_like(tiles_v)
    found = jnp.int32(0)
    for index, group in enumerate(groups):
        first = here.group(group) * blocks

        def collect(i, found, first=first, index=index):
            row = first + i
            count = counts[row]
            for slot in range(slots):
                live[found] = (index * blocks + i) * slots + slot
                source[found] = here.source(cols[slot, row])
                found = found + (slot < count).astype(jnp.int32)
            return found

        found = lax.fori_loop(0, blocks, collect, found)
    run_jobs(jobs, "wait")
    for copy in copies:
        copy.wait()

    def entry(place):
        tile_index = live[place]
        grad = grad_v[block_at(tile_index // slots, block)]
        node = nodes_v[block_at(source[place], block)]
        tiles_v[tile_index] = (mm(grad, node, NT) * scale).astype(BF16)

    for_live(found, entry)
    size = blocks * slots
    copies = []
    for index, group in enumerate(groups):
        copy = pltpu.make_async_copy(
            tiles_v.at[pl.ds(index * size, size)],
            out.at[pl.ds(here.group(group) * size, size)],
            out_sem.at[index],
        )
        copy.start()
        copies.append(copy)
    for copy in copies:
        copy.wait()


def tile_grad_call(paired, here, cols, counts, grads, pieces, shape, rows, groups, base=None, after=()):
    row_blocks, slots, block = shape[:3]
    chunks = len(grads)
    width = grads[0][0].shape[1] * chunks
    gathered = sum(piece.shape[0] for piece in pieces[0])
    flat = [a for chunk in grads for a in chunk] + [a for chunk in pieces for a in chunk]
    after = after if base is None else (base,) + tuple(after)
    entries = len(groups) * rows // block * slots
    return pl.pallas_call(
        functools.partial(
            tile_grad_kernel, rows, slots, len(grads[0]), len(pieces[0]), chunks, len(after), groups, paired
        ),
        out_shape=[
            jax.ShapeDtypeStruct((row_blocks * slots, block, block), BF16),
            jax.ShapeDtypeStruct((8, 128), F32),
        ],
        in_specs=[SMEM] * 3 + [ANY] * (len(flat) + len(after)),
        out_specs=[ANY, VMEM],
        input_output_aliases={} if base is None else {3 + len(flat): 0},
        scratch_shapes=[
            pltpu.VMEM((len(groups) * rows, width), BF16),
            pltpu.VMEM((gathered, width), BF16),
            pltpu.VMEM((entries, block, block), BF16),
            pltpu.SMEM((entries + 8,), jnp.int32),
            pltpu.SMEM((entries + 8,), jnp.int32),
            pltpu.SemaphoreType.DMA((chunks, len(grads[0]))),
            pltpu.SemaphoreType.DMA((chunks, len(pieces[0]))),
            pltpu.SemaphoreType.DMA((len(groups),)),
        ],
        compiler_params=params(16 if gathered <= 8192 else 40),
        cost_estimate=SMALL,
        name="tile_grads",
    )(here, cols, counts, *flat, *after)


def swap(value, bit):
    return lax.ppermute(value, "row", [(i, i ^ bit) for i in range(8)])


def outer_swap(value):
    return lax.ppermute(value, "col", [(0, 1), (1, 0), (2, 3), (3, 2)])


def turn(value, by):
    return lax.ppermute(value, "col", [(i, (i + by) % 4) for i in range(4)])


def inner_swap(value):
    pairs = []
    for row in range(8):
        for col in range(4):
            partner = (row, 3 - col) if col in (1, 2) else (row ^ 1, col)
            pairs.append((row * 4 + col, partner[0] * 4 + partner[1]))
    return lax.ppermute(value, ("row", "col"), pairs)


def gather_square(nodes):
    half = nodes.shape[0] // 2
    lower, upper = nodes[:half], nodes[half:]
    y_lower, x_upper = swap(lower, 4), swap(upper, 2)
    x_lower, y_upper = swap(lower, 2), swap(upper, 4)
    d_lower, d_upper = swap(y_lower, 2), swap(x_upper, 4)
    pieces = [nodes, swap(nodes, 1)]
    for pair in ((x_lower, x_upper), (y_lower, y_upper), (d_lower, d_upper)):
        pieces += [*pair, *(swap(piece, 1) for piece in pair)]
    return pieces


def reduce_square(here, even, other, rows):
    half = rows // 2
    first = [
        sum_call(here, rows, [(even, places), (other, places)]) for places in ((6, 2), (7, 5))
    ]
    x_first, y_first = swap(first[0], 2), swap(first[1], 4)
    y_lower = swap(sum_call(here, half, [(even, 4), (other, 4), (x_first, 0)]), 4)
    x_upper = swap(sum_call(here, half, [(even, 3), (other, 3), (y_first, 0)]), 2)
    return [((x_first, 1), (x_upper, 0)), ((y_lower, 0), (y_first, 1))], first


def sum_kernel(n_terms, n_gated, n_split, *refs):
    inner, refs = Place(refs[0]).inner(), refs[1:]
    total = None
    for index, ref in enumerate(refs[: n_terms + n_gated]):
        term = ref[...].astype(F32)
        if index >= n_terms:
            term = jnp.where(inner, term, 0.0)
        total = term if total is None else total + term
    for index in range(n_split):
        first, second = refs[n_terms + n_gated + 2 * index :][:2]
        early = pl.program_id(0) < pl.num_programs(0) // 2
        total = total + jnp.where(early, first[...], second[...]).astype(F32)
    refs[-1][...] = total.astype(refs[-1].dtype)


def sum_call(here, rows, terms, gated=(), split=(), dtype=BF16, after=()):
    both = [*terms, *gated]
    width = both[0][0].shape[1]
    step = min(rows, 256)
    steps = rows // step
    half = steps // 2

    def spec(piece):
        if isinstance(piece, int):
            return pl.BlockSpec((step, width), lambda i: (piece * steps + i, 0))
        lower, upper = piece
        return pl.BlockSpec(
            (step, width), lambda i: (jnp.where(i < half, lower * half + i, (upper - 1) * half + i), 0)
        )

    def early(piece):
        return pl.BlockSpec((step, width), lambda i: (piece * half + jnp.minimum(i, half - 1), 0))

    def late(piece):
        return pl.BlockSpec((step, width), lambda i: (piece * half + jnp.maximum(i - half, 0), 0))

    return pl.pallas_call(
        functools.partial(sum_kernel, len(terms), len(gated), len(split)),
        grid=(steps,),
        out_shape=jax.ShapeDtypeStruct((rows, width), dtype),
        in_specs=[SMEM]
        + [spec(piece) for _, piece in both]
        + [spec_of(piece) for pair in split for spec_of, (_, piece) in zip((early, late), pair)]
        + [ANY] * len(after),
        out_specs=pl.BlockSpec((step, width), lambda i: (i, 0)),
        compiler_params=params(8),
        cost_estimate=SMALL,
        name="sum_terms",
    )(here, *(array for array, _ in both), *(array for pair in split for array, _ in pair), *after)


def scatter_weights(kept, sent):
    for bit in (1, 2):
        terms = kept + swap(sent, bit)
        half = terms.shape[0] // 2
        kept, sent = terms[:half], terms[half:]
    return kept, swap(sent, 4)


def level_weights(here, value, after):
    terms = [value] + [turn(value, by) for by in (1, 2, 3)]
    return sum_call(here, value.shape[0], [(term, 0) for term in terms], after=after)


def reduce_line(here, far, near, pair, own):
    rows = own.shape[0]
    far_sum = inner_swap(sum_call(here, rows, [(far, 0), (outer_swap(far), 0)]))
    near_sum = inner_swap(sum_call(here, rows, [(near, 0), (outer_swap(near), 0)]))
    pair_in = outer_swap(sum_call(here, rows, [(pair, 0)], [(far_sum, 0)]))
    return own, pair_in, near_sum


def gather_line(own):
    pair = outer_swap(own)
    near_inner = inner_swap(own)
    far_inner = inner_swap(pair)
    near_outer = outer_swap(near_inner)
    far_outer = outer_swap(far_inner)
    return [own, pair, near_inner, near_outer, far_inner, far_outer]


def body(n_row, n_col, nodes, tiles, tile_col, tile_count, w_in, bias_in, w_out, ln_gain, ln_shift, cotangent):
    rows, width = nodes.shape
    row_blocks, _, slots, block = tiles.shape[:4]
    tile_local = tiles.reshape(row_blocks, slots, block, block)
    cols = tile_col.reshape(row_blocks, slots).T
    counts = tile_count.reshape(row_blocks)
    gathered, total = n_row * rows, n_col * rows
    paired = n_row == 8 and n_col == 4
    here = lax.axis_index(("row", "col")).astype(jnp.int32).reshape(1)
    known = (paired, here, cols, counts)
    if paired:
        pieces = [gather_square(nodes)]
        (far,) = forward_call(*known, pieces[0], tile_local, ((0,),), rows)
        (near,) = forward_call(*known, pieces[0], tile_local, ((1,),), rows)
        pair, own = forward_call(*known, pieces[0], tile_local, ((2,), (3,)), rows)
        parts = [reduce_line(here, far, near, pair, own)]
        kinds = [("all", "all", "inner")]
    else:
        pieces = [[lax.all_gather(nodes, "row", axis=0, tiled=True)]]
        (partial,) = forward_call(*known, pieces[0], tile_local, (tuple(range(n_col)),), rows)
        parts = [[lax.psum_scatter(partial, "col", scatter_dimension=0, tiled=True)]]
        kinds = [("all",)]
    vectors = [v.reshape(1, width) for v in (bias_in, ln_gain, ln_shift)]
    (updated, gpre_b, act, gproj, message, vec), gmsgs = mlp_call(
        here, nodes, cotangent, parts, kinds, w_in, vectors[0], w_out, vectors[1], vectors[2]
    )
    factor = float(rows * n_row * n_col) ** -0.5
    weight_args = (here, nodes, message, act, gpre_b, gproj, cotangent, w_in, vec)
    if paired:
        halves = ((1, 3, 5, 7), (0, 2, 4, 6))
        grads = [gather_line(gmsgs[0])]
        kept, sent, direct = weight_call(factor, n_row, *weight_args, ())
        row_weights = scatter_weights(kept, sent)
        near_grads, token = tile_grad_call(
            *known, [grads[0][:2]], pieces, tile_local.shape, rows, (3, 2), after=(grads[0][3], grads[0][4])
        )
        row_weights = sum_call(here, kept.shape[0] // 4, [(term, 0) for term in row_weights], after=(token,))
        odd, even = back_call(*known, grads[0], tile_local, total, gathered, halves, (row_weights,))
        other = swap(odd, 1)
        arrived, first = reduce_square(here, even, other, rows)
        all_weights = level_weights(here, row_weights, first)
        joint = jnp.concatenate([all_weights] + [swap(all_weights, bits) for bits in (2, 4, 6)], axis=0)
        weights = unpack_call(here, joint, swap(joint, 1), width)
        grad_tiles, _ = tile_grad_call(
            *known, grads, pieces, tile_local.shape, rows, (1, 0), near_grads, first
        )
        grad_nodes = sum_call(here, rows, [(direct, 0), (even, 0), (other, 0)], split=arrived)
    else:
        grads = [[lax.all_gather(gmsgs[0], "col", axis=0, tiled=True)]]
        weight_terms, direct = weight_call(factor, 1, *weight_args)
        weight_sums = lax.psum(weight_terms, ("row", "col"))
        weights = (
            weight_sums[: 2 * width],
            weight_sums[2 * width : 3 * width],
            weight_sums[3 * width : 3 * width + 3],
        )
        (terms,) = back_call(*known, grads[0], tile_local, total, gathered, (tuple(range(n_row)),))
        back = lax.psum_scatter(terms, "row", scatter_dimension=0, tiled=True)
        grad_nodes = sum_call(here, rows, [(direct, 0), (back, 0)])
        grad_tiles, _ = tile_grad_call(
            *known, grads, pieces, tile_local.shape, rows, tuple(range(n_col))
        )
    grad_tiles = grad_tiles.reshape(tiles.shape)
    return (updated, grad_nodes, grad_tiles, *weights)


def solution(mesh):
    placed = (
        P(("row", "col"), None),
        P("row", "col", None, None, None),
        P("row", "col", None),
        P("row", "col"),
        P(),
        P(),
        P(),
        P(),
        P(),
        P(("row", "col"), None),
    )
    return jax.shard_map(
        functools.partial(body, mesh.shape["row"], mesh.shape["col"]),
        mesh=mesh,
        in_specs=placed,
        out_specs=(
            P(("row", "col"), None),
            P(("row", "col"), None),
            P("row", "col", None, None, None),
            P(),
            P(),
            P(),
        ),
        check_vma=False,
    )
```

```python
import functools

import jax
import jax.numpy as jnp
from jax import lax
from jax.experimental import pallas as pl
from jax.experimental.pallas import tpu as pltpu
from jax.sharding import PartitionSpec as P

F32 = jnp.float32
BF16 = jnp.bfloat16
ANY = pl.BlockSpec(memory_space=pl.ANY)
HBM = pl.BlockSpec(memory_space=pltpu.HBM)
SMEM = pl.BlockSpec(memory_space=pltpu.SMEM)
VMEM = pl.BlockSpec(memory_space=pltpu.VMEM)
MIB = 1 << 20
TN = (((0,), (0,)), ((), ()))
NT = (((1,), (1,)), ((), ()))
SMALL = pl.CostEstimate(flops=1 << 20, bytes_accessed=1 << 16, transcendentals=0)


LIVE_STEP = 4
GRAD_PLAN = ((3, 0, None), (2, 1, None), (1, 2, "inner"), (1, 3, "outer"), (0, 4, "inner"), (0, 5, "outer"))
SWAP_ORDER = (0, 4, 2, 6, 1, 5, 3, 7)


def params(mib):
    return pltpu.CompilerParams(vmem_limit_bytes=mib * MIB)


def mm(a, b, dims=(((1,), (0,)), ((), ()))):
    return lax.dot_general(a, b, dims, preferred_element_type=F32)


def block_at(index, block):
    return pl.ds(pl.multiple_of(index * block, block), block)


class Place:
    def __init__(self, ref, paired=True, blocks=1):
        self.mine, self.level = lax.shift_right_logical(ref[0], 2), ref[0] & 3
        self.paired, self.blocks = paired, blocks

    def inner(self):
        return (self.level == 1) | (self.level == 2)

    def group(self, pick):
        if not self.paired:
            return pick
        low = self.level < 2
        choices = (jnp.where(low, 3, 0), jnp.where(low, 2, 1), self.level ^ 1, self.level)
        return choices[pick]

    def source(self, col):
        if not self.paired:
            return col
        shift = self.blocks.bit_length() - 1
        if 1 << shift == self.blocks:
            return col ^ lax.shift_left(self.mine, jnp.int32(shift))
        return (lax.div(col, self.blocks) ^ self.mine) * self.blocks + lax.rem(col, self.blocks)


def load_pieces(pieces, dst, sem, first):
    copies = []
    offset = 0
    for index, piece in enumerate(pieces):
        copy = pltpu.make_async_copy(
            piece, dst.at[pl.ds(offset, piece.shape[0])], sem.at[first + index]
        )
        copy.start()
        copies.append(copy)
        offset += piece.shape[0]
    return copies


def masked_tile(tile, live):
    return jnp.where(live, tile, jnp.zeros_like(tile))


def forward_kernel(outputs, n_pieces, paired, here, cols, counts, *refs):
    pieces, tiles = refs[:n_pieces], refs[n_pieces]
    outs = refs[n_pieces + 1 : n_pieces + 1 + len(outputs)]
    nodes_v, tiles_v, sem, tile_sem = refs[n_pieces + 1 + len(outputs) :]
    rows = outs[0].shape[0] // len(outputs[0])
    slots, block = tiles.shape[1], tiles.shape[2]
    blocks = rows // block
    here = Place(here, paired, blocks)
    copies = load_pieces(pieces, nodes_v, sem, 0)
    places = [(pick, out, index) for out, picks in zip(outs, outputs) for index, pick in enumerate(picks)]
    tile_copies = []
    for place, (pick, _, _) in enumerate(places):
        copy = pltpu.make_async_copy(
            tiles.at[pl.ds(here.group(pick) * blocks, blocks)],
            tiles_v.at[pl.ds(place * blocks, blocks)],
            tile_sem.at[place],
        )
        copy.start()
        tile_copies.append(copy)
    for copy in copies:
        copy.wait()
    for place, (pick, out, index) in enumerate(places):
        tile_copies[place].wait()
        first = here.group(pick) * blocks

        def step(i, carry, first=first, out=out, index=index, place=place):
            row = first + i
            count = counts[row]
            parts = []
            for pair in range(slots // 2):
                both = (2 * pair, 2 * pair + 1)
                tile = jnp.concatenate(
                    [masked_tile(tiles_v[place * blocks + i, slot], slot < count) for slot in both], axis=1
                )
                node = jnp.concatenate(
                    [nodes_v[block_at(here.source(cols[slot, row]), block)] for slot in both], axis=0
                )
                parts.append(mm(tile, node))
            value = parts[0]
            for part in parts[1:]:
                value = value + part
            out[block_at(index * blocks + i, block)] = value.astype(BF16)
            return carry

        lax.fori_loop(0, blocks, step, 0, unroll=4)


def forward_call(paired, here, cols, counts, pieces, tiles, outputs, rows):
    width = pieces[0].shape[1]
    gathered = sum(piece.shape[0] for piece in pieces)
    slots, block = tiles.shape[1], tiles.shape[2]
    n_picks = sum(len(picks) for picks in outputs)
    return pl.pallas_call(
        functools.partial(forward_kernel, outputs, len(pieces), paired),
        out_shape=[jax.ShapeDtypeStruct((len(picks) * rows, width), BF16) for picks in outputs],
        in_specs=[SMEM] * 3 + [ANY] * len(pieces) + [HBM],
        out_specs=[VMEM] * len(outputs),
        scratch_shapes=[
            pltpu.VMEM((gathered, width), BF16),
            pltpu.VMEM((n_picks * (rows // block),) + tiles.shape[1:], BF16),
            pltpu.SemaphoreType.DMA((len(pieces),)),
            pltpu.SemaphoreType.DMA((n_picks,)),
        ],
        compiler_params=params(60),
        cost_estimate=SMALL,
        name="partial_messages",
    )(here, cols, counts, *pieces, tiles)


def mlp_kernel(kinds, here, nodes, cot, *refs):
    n_parts = sum(len(chunk) for chunk in kinds)
    parts = refs[:n_parts]
    w_in, bias, w_out, gain, shift, updated, gpre_o, act_o, gproj_o, msg_o, vec = refs[
        n_parts : n_parts + 11
    ]
    gmsgs = refs[n_parts + 11 :]
    width = nodes.shape[1]
    inner = Place(here).inner()
    messages = []
    place = 0
    for chunk in kinds:
        total = None
        for kind in chunk:
            term = parts[place][...].astype(F32)
            place += 1
            if kind == "inner":
                term = jnp.where(inner, term, 0.0)
            total = term if total is None else total + term
        messages.append(total.astype(BF16))
    message = jnp.concatenate(messages, axis=1) if len(messages) > 1 else messages[0]
    node = nodes[...]
    pre = mm(node, w_in[:width]) + mm(message, w_in[width:]) + bias[...]
    sig = 0.5 + 0.5 * jnp.tanh(0.5 * pre)
    act = (pre * sig).astype(BF16)
    proj = mm(act, w_out[...])
    mean = jnp.mean(proj, axis=-1, keepdims=True)
    var = jnp.mean((proj - mean) ** 2, axis=-1, keepdims=True)
    rstd = 1.0 / jnp.sqrt(var + 1e-05)
    normed = (proj - mean) * rstd
    updated[...] = (node.astype(F32) + normed * gain[...] + shift[...]).astype(BF16)
    grad_out = cot[...].astype(F32)
    gscaled = grad_out * gain[...]
    gproj = (
        (
            gscaled
            - jnp.mean(gscaled, axis=-1, keepdims=True)
            - normed * jnp.mean(gscaled * normed, axis=-1, keepdims=True)
        )
        * rstd
    ).astype(BF16)
    gact = mm(gproj, w_out[...], NT)
    gpre = gact * sig * (1.0 + pre * (1.0 - sig))
    gpre_b = gpre.astype(BF16)
    gmsg = mm(gpre_b, w_in[width:], NT).astype(BF16)
    part = width // len(gmsgs)
    for index, out in enumerate(gmsgs):
        out[...] = gmsg[:, index * part : (index + 1) * part]
    gpre_o[...] = gpre_b
    act_o[...] = act
    gproj_o[...] = gproj
    msg_o[...] = message

    @pl.when(pl.program_id(0) == 0)
    def _():
        vec[...] = jnp.zeros_like(vec)

    vec[0:1] += jnp.sum(gpre, axis=0, keepdims=True)
    vec[1:2] += jnp.sum(grad_out * normed, axis=0, keepdims=True)
    vec[2:3] += jnp.sum(grad_out, axis=0, keepdims=True)


def mlp_call(here, nodes, cot, parts, kinds, w_in, bias, w_out, gain, shift):
    rows, width = nodes.shape
    step = min(rows, 512)

    def blocked(array):
        return pl.BlockSpec((step, array.shape[1]), lambda i: (i, 0))

    def whole(array):
        return pl.BlockSpec(array.shape, lambda i: (0, 0))

    flat = [term for chunk in parts for term in chunk]
    row_like = jax.ShapeDtypeStruct((rows, width), BF16)
    chunk_like = jax.ShapeDtypeStruct((rows, width // len(parts)), BF16)
    outs = [row_like] * 5 + [jax.ShapeDtypeStruct((8, width), F32)] + [chunk_like] * len(parts)
    weights = (w_in, bias, w_out, gain, shift)
    result = pl.pallas_call(
        functools.partial(mlp_kernel, kinds),
        grid=(rows // step,),
        out_shape=outs,
        in_specs=[SMEM] + [blocked(a) for a in (nodes, cot, *flat)] + [whole(a) for a in weights],
        out_specs=[blocked(a) for a in outs[:5]] + [whole(outs[5])] + [blocked(a) for a in outs[6:]],
        compiler_params=params(40),
        cost_estimate=SMALL,
        name="mlp",
    )(here, nodes, cot, *flat, *weights)
    return result[:6], result[6:]


def weight_kernel(factor, pieces, n_after, here, nodes, msg, act, gpre, gproj, cot, w_in, vec, *refs):
    *outs, direct, grads = refs[n_after:]
    width = nodes.shape[1]

    @pl.when(pl.program_id(0) == 0)
    def _():
        grads[...] = jnp.zeros_like(grads)
        grads[3 * width : 3 * width + 8] = vec[...] * factor

    gpre_b = gpre[...]
    grads[:width] += mm(nodes[...], gpre_b, TN) * factor
    grads[width : 2 * width] += mm(msg[...], gpre_b, TN) * factor
    grads[2 * width : 3 * width] += mm(act[...], gproj[...], TN) * factor
    direct[...] = cot[...].astype(F32) + mm(gpre_b, w_in[:width], NT)

    @pl.when(pl.program_id(0) == pl.num_programs(0) - 1)
    def _():
        if pieces == 1:
            outs[0][...] = grads[: outs[0].shape[0]]
        else:
            rows = grads.shape[0] // pieces
            for place, member in enumerate(SWAP_ORDER):
                where = pl.ds(pl.multiple_of((Place(here).mine ^ member) * rows, 8), rows)
                out, index = outs[2 * place // pieces], place % (pieces // 2)
                out[index * rows : (index + 1) * rows] = grads[where]


def weight_call(factor, pieces, here, nodes, msg, act, gpre, gproj, cot, w_in, vec, after=()):
    rows, width = nodes.shape
    step = min(rows, 256)
    blocked = pl.BlockSpec((step, width), lambda i: (i, 0))

    def whole(shape):
        return pl.BlockSpec(shape, lambda i: (0, 0))

    padded = (3 * width + width // 2, width)
    if pieces == 1:
        outs = [jax.ShapeDtypeStruct((3 * width + 8, width), F32)]
    else:
        outs = [jax.ShapeDtypeStruct((padded[0] // 2, width), F32)] * 2
    return pl.pallas_call(
        functools.partial(weight_kernel, factor, pieces, len(after)),
        grid=(rows // step,),
        out_shape=[*outs, jax.ShapeDtypeStruct((rows, width), F32)],
        in_specs=[SMEM] + [blocked] * 6 + [whole(w_in.shape), whole(vec.shape)] + [ANY] * len(after),
        out_specs=[whole(out.shape) for out in outs] + [blocked],
        scratch_shapes=[pltpu.VMEM(padded, F32)],
        compiler_params=params(40),
        cost_estimate=SMALL,
        name="weight_grads",
    )(here, nodes, msg, act, gpre, gproj, cot, w_in, vec, *after)


def unpack_kernel(here, even, odd, w_in, w_out, vectors, grads):
    width = w_in.shape[1]
    rows = grads.shape[0] // 8
    for member in range(8):
        part = (even, odd)[member % 2]
        first = member // 2 * rows
        where = pl.ds(pl.multiple_of((Place(here).mine ^ member) * rows, 8), rows)
        grads[where] = part[first : first + rows].astype(F32)
    w_in[...] = grads[: 2 * width]
    w_out[...] = grads[2 * width : 3 * width]
    vectors[...] = grads[3 * width : 3 * width + 3]


def unpack_call(here, even, odd, width):
    shapes = ((2 * width, width), (width, width), (3, width))
    return pl.pallas_call(
        unpack_kernel,
        out_shape=[jax.ShapeDtypeStruct(shape, F32) for shape in shapes],
        in_specs=[SMEM, VMEM, VMEM],
        out_specs=[VMEM] * 3,
        scratch_shapes=[pltpu.VMEM((3 * width + width // 2, width), F32)],
        compiler_params=params(16),
        cost_estimate=SMALL,
        name="weight_unpack",
    )(here, even, odd)


def grad_jobs(rows, refs, dst, sem, here, groups=None):
    if len(refs) == 1:
        return [(None, pltpu.make_async_copy(refs[0], dst, sem.at[0]))]
    inner = here.inner()
    conditions = {None: None, "inner": inner, "outer": jnp.logical_not(inner)}
    jobs = []
    for group, index, kind in GRAD_PLAN:
        if groups is None:
            where = block_at(here.group(group), rows)
        elif group in groups:
            where = pl.ds(groups.index(group) * rows, rows)
        else:
            continue
        copy = pltpu.make_async_copy(refs[index], dst.at[where], sem.at[index])
        jobs.append((conditions[kind], copy))
    return jobs


def run_jobs(jobs, verb):
    for condition, copy in jobs:
        if condition is None:
            getattr(copy, verb)()
        else:
            pl.when(condition)(getattr(copy, verb))


def for_live(found, entry):
    def several(i, carry):
        for index in range(LIVE_STEP):
            entry(i * LIVE_STEP + index)
        return carry

    def one(i, carry):
        entry(i)
        return carry

    full = found // LIVE_STEP
    lax.fori_loop(0, full, several, 0)
    lax.fori_loop(full * LIVE_STEP, found, one, 0)


def back_kernel(rows, slots, n_grads, n_after, out_pieces, paired, here, cols, counts, *refs):
    grads, tiles = refs[:n_grads], refs[n_grads]
    refs = refs[n_grads + 1 + n_after :]
    outs = refs[: len(out_pieces)]
    grad_v, tiles_v, acc, live, source, sem, tile_sem = refs[len(out_pieces) :]
    n_tiles, block = tiles.shape[:2]
    here = Place(here, paired, rows // block)
    jobs = grad_jobs(rows, grads, grad_v, sem, here)
    run_jobs(jobs, "start")
    tile_copy = pltpu.make_async_copy(tiles, tiles_v, tile_sem.at[0])
    tile_copy.start()
    acc[...] = jnp.zeros_like(acc)

    def collect(row, found):
        count = counts[row]
        for slot in range(slots):
            live[found] = row * slots + slot
            source[found] = here.source(cols[slot, row])
            found = found + (slot < count).astype(jnp.int32)
        return found

    found = lax.fori_loop(0, n_tiles // slots, collect, jnp.int32(0))
    run_jobs(jobs, "wait")
    tile_copy.wait()

    def entry(place):
        tile_index = live[place]
        part = mm(tiles_v[tile_index], grad_v[block_at(tile_index // slots, block)], TN)
        acc[block_at(source[place], block)] += part

    for_live(found, entry)
    piece = acc.shape[0] // sum(len(members) for members in out_pieces)
    for out, members in zip(outs, out_pieces):
        for index, member in enumerate(members):
            out[pl.ds(index * piece, piece)] = acc[pl.ds(member * piece, piece)].astype(BF16)


def back_call(paired, here, cols, counts, grads, tiles, total, gathered, out_pieces, after=()):
    rows, width = grads[0].shape
    rows = total if len(grads) == 1 else rows
    row_blocks, slots, block = tiles.shape[:3]
    piece = gathered // sum(len(members) for members in out_pieces)
    return pl.pallas_call(
        functools.partial(back_kernel, rows, slots, len(grads), len(after), out_pieces, paired),
        out_shape=[jax.ShapeDtypeStruct((len(m) * piece, width), BF16) for m in out_pieces],
        in_specs=[SMEM] * 3 + [ANY] * len(grads) + [HBM] + [ANY] * len(after),
        out_specs=[VMEM] * len(out_pieces),
        scratch_shapes=[
            pltpu.VMEM((total, width), BF16),
            pltpu.VMEM((row_blocks * slots, block, block), BF16),
            pltpu.VMEM((gathered, width), F32),
            pltpu.SMEM((row_blocks * slots + 8,), jnp.int32),
            pltpu.SMEM((row_blocks * slots + 8,), jnp.int32),
            pltpu.SemaphoreType.DMA((len(grads),)),
            pltpu.SemaphoreType.DMA((1,)),
        ],
        compiler_params=params(28 if gathered <= 8192 else 56),
        cost_estimate=SMALL,
        name="back_terms",
    )(here, cols, counts, *grads, tiles.reshape(row_blocks * slots, block, block), *after)


def tile_grad_kernel(
    rows, slots, n_grads, n_pieces, n_chunks, n_after, groups, paired, here, cols, counts, *refs
):
    grads = refs[: n_grads * n_chunks]
    refs = refs[n_grads * n_chunks :]
    pieces = refs[: n_pieces * n_chunks]
    out, token, grad_v, nodes_v, tiles_v, live, source, sem, piece_sem, out_sem = refs[n_pieces * n_chunks + n_after :]
    token[...] = jnp.zeros_like(token)
    block = out.shape[1]
    width = nodes_v.shape[1]
    part = width // n_chunks
    scale = float(width) ** -0.5
    blocks = grad_v.shape[0] // (block * len(groups))
    here = Place(here, paired, blocks)
    jobs, copies = [], []
    for chunk in range(n_chunks):
        columns = pl.ds(chunk * part, part)
        jobs += grad_jobs(
            rows,
            grads[chunk * n_grads : (chunk + 1) * n_grads],
            grad_v.at[:, columns],
            sem.at[chunk],
            here,
            groups,
        )
        copies += load_pieces(
            pieces[chunk * n_pieces : (chunk + 1) * n_pieces],
            nodes_v.at[:, columns],
            piece_sem.at[chunk],
            0,
        )
    run_jobs(jobs, "start")
    tiles_v[...] = jnp.zeros_like(tiles_v)
    found = jnp.int32(0)
    for index, group in enumerate(groups):
        first = here.group(group) * blocks

        def collect(i, found, first=first, index=index):
            row = first + i
            count = counts[row]
            for slot in range(slots):
                live[found] = (index * blocks + i) * slots + slot
                source[found] = here.source(cols[slot, row])
                found = found + (slot < count).astype(jnp.int32)
            return found

        found = lax.fori_loop(0, blocks, collect, found)
    run_jobs(jobs, "wait")
    for copy in copies:
        copy.wait()

    def entry(place):
        tile_index = live[place]
        grad = grad_v[block_at(tile_index // slots, block)]
        node = nodes_v[block_at(source[place], block)]
        tiles_v[tile_index] = (mm(grad, node, NT) * scale).astype(BF16)

    for_live(found, entry)
    size = blocks * slots
    copies = []
    for index, group in enumerate(groups):
        copy = pltpu.make_async_copy(
            tiles_v.at[pl.ds(index * size, size)],
            out.at[pl.ds(here.group(group) * size, size)],
            out_sem.at[index],
        )
        copy.start()
        copies.append(copy)
    for copy in copies:
        copy.wait()


def tile_grad_call(paired, here, cols, counts, grads, pieces, shape, rows, groups, base=None, after=()):
    row_blocks, slots, block = shape[:3]
    chunks = len(grads)
    width = grads[0][0].shape[1] * chunks
    gathered = sum(piece.shape[0] for piece in pieces[0])
    flat = [a for chunk in grads for a in chunk] + [a for chunk in pieces for a in chunk]
    after = after if base is None else (base,) + tuple(after)
    entries = len(groups) * rows // block * slots
    return pl.pallas_call(
        functools.partial(
            tile_grad_kernel, rows, slots, len(grads[0]), len(pieces[0]), chunks, len(after), groups, paired
        ),
        out_shape=[
            jax.ShapeDtypeStruct((row_blocks * slots, block, block), BF16),
            jax.ShapeDtypeStruct((8, 128), F32),
        ],
        in_specs=[SMEM] * 3 + [ANY] * (len(flat) + len(after)),
        out_specs=[ANY, VMEM],
        input_output_aliases={} if base is None else {3 + len(flat): 0},
        scratch_shapes=[
            pltpu.VMEM((len(groups) * rows, width), BF16),
            pltpu.VMEM((gathered, width), BF16),
            pltpu.VMEM((entries, block, block), BF16),
            pltpu.SMEM((entries + 8,), jnp.int32),
            pltpu.SMEM((entries + 8,), jnp.int32),
            pltpu.SemaphoreType.DMA((chunks, len(grads[0]))),
            pltpu.SemaphoreType.DMA((chunks, len(pieces[0]))),
            pltpu.SemaphoreType.DMA((len(groups),)),
        ],
        compiler_params=params(16 if gathered <= 8192 else 40),
        cost_estimate=SMALL,
        name="tile_grads",
    )(here, cols, counts, *flat, *after)


def swap(value, bit):
    return lax.ppermute(value, "row", [(i, i ^ bit) for i in range(8)])


def outer_swap(value):
    return lax.ppermute(value, "col", [(0, 1), (1, 0), (2, 3), (3, 2)])


def turn(value, by):
    return lax.ppermute(value, "col", [(i, (i + by) % 4) for i in range(4)])


def inner_swap(value):
    pairs = []
    for row in range(8):
        for col in range(4):
            partner = (row, 3 - col) if col in (1, 2) else (row ^ 1, col)
            pairs.append((row * 4 + col, partner[0] * 4 + partner[1]))
    return lax.ppermute(value, ("row", "col"), pairs)


def gather_square(nodes):
    half = nodes.shape[0] // 2
    lower, upper = nodes[:half], nodes[half:]
    y_lower, x_upper = swap(lower, 4), swap(upper, 2)
    x_lower, y_upper = swap(lower, 2), swap(upper, 4)
    d_lower, d_upper = swap(y_lower, 2), swap(x_upper, 4)
    pieces = [nodes, swap(nodes, 1)]
    for pair in ((x_lower, x_upper), (y_lower, y_upper), (d_lower, d_upper)):
        pieces += [*pair, *(swap(piece, 1) for piece in pair)]
    return pieces


def reduce_square(here, even, urgent, rest, rows):
    half = rows // 2
    first = [
        sum_call(here, rows, [(even, (6, 2)), (urgent, (0, 2))]),
        sum_call(here, rows, [(even, (7, 5)), (urgent, (1, 3))]),
    ]
    x_first, y_first = swap(first[0], 2), swap(first[1], 4)
    y_lower = swap(sum_call(here, half, [(even, 4), (rest, 3), (x_first, 0)]), 4)
    x_upper = swap(sum_call(here, half, [(even, 3), (rest, 2), (y_first, 0)]), 2)
    return [((x_first, 1), (x_upper, 0)), ((y_lower, 0), (y_first, 1))], first


def sum_kernel(n_terms, n_gated, n_split, *refs):
    inner, refs = Place(refs[0]).inner(), refs[1:]
    total = None
    for index, ref in enumerate(refs[: n_terms + n_gated]):
        term = ref[...].astype(F32)
        if index >= n_terms:
            term = jnp.where(inner, term, 0.0)
        total = term if total is None else total + term
    for index in range(n_split):
        first, second = refs[n_terms + n_gated + 2 * index :][:2]
        early = pl.program_id(0) < pl.num_programs(0) // 2
        total = total + jnp.where(early, first[...], second[...]).astype(F32)
    refs[-1][...] = total.astype(refs[-1].dtype)


def sum_call(here, rows, terms, gated=(), split=(), dtype=BF16, after=()):
    both = [*terms, *gated]
    width = both[0][0].shape[1]
    step = min(rows, 256)
    steps = rows // step
    half = steps // 2

    def spec(piece):
        if isinstance(piece, int):
            return pl.BlockSpec((step, width), lambda i: (piece * steps + i, 0))
        lower, upper = piece
        return pl.BlockSpec(
            (step, width), lambda i: (jnp.where(i < half, lower * half + i, (upper - 1) * half + i), 0)
        )

    def early(piece):
        return pl.BlockSpec((step, width), lambda i: (piece * half + jnp.minimum(i, half - 1), 0))

    def late(piece):
        return pl.BlockSpec((step, width), lambda i: (piece * half + jnp.maximum(i - half, 0), 0))

    return pl.pallas_call(
        functools.partial(sum_kernel, len(terms), len(gated), len(split)),
        grid=(steps,),
        out_shape=jax.ShapeDtypeStruct((rows, width), dtype),
        in_specs=[SMEM]
        + [spec(piece) for _, piece in both]
        + [spec_of(piece) for pair in split for spec_of, (_, piece) in zip((early, late), pair)]
        + [ANY] * len(after),
        out_specs=pl.BlockSpec((step, width), lambda i: (i, 0)),
        compiler_params=params(8),
        cost_estimate=SMALL,
        name="sum_terms",
    )(here, *(array for array, _ in both), *(array for pair in split for array, _ in pair), *after)


def scatter_weights(here, kept, sent, after):
    rows = kept.shape[0] // 4
    received = swap(sent, 1)
    pieces = [
        sum_call(here, rows, [(kept, place), (received, place)], dtype=F32) for place in range(4)
    ]
    terms = [pieces[0]] + [swap(piece, bits) for piece, bits in zip(pieces[1:], SWAP_ORDER[1:4])]
    return sum_call(here, rows, [(term, 0) for term in terms], after=after)


def level_weights(here, value, after):
    terms = [value] + [turn(value, by) for by in (1, 2, 3)]
    return sum_call(here, value.shape[0], [(term, 0) for term in terms], after=after)


def reduce_line(here, far, near, pair, own):
    rows = own.shape[0]
    far_sum = inner_swap(sum_call(here, rows, [(far, 0), (outer_swap(far), 0)]))
    near_sum = inner_swap(sum_call(here, rows, [(near, 0), (outer_swap(near), 0)]))
    pair_in = outer_swap(sum_call(here, rows, [(pair, 0)], [(far_sum, 0)]))
    return own, pair_in, near_sum


def gather_line(own):
    pair = outer_swap(own)
    near_inner = inner_swap(own)
    far_inner = inner_swap(pair)
    near_outer = outer_swap(near_inner)
    far_outer = outer_swap(far_inner)
    return [own, pair, near_inner, near_outer, far_inner, far_outer]


def body(n_row, n_col, nodes, tiles, tile_col, tile_count, w_in, bias_in, w_out, ln_gain, ln_shift, cotangent):
    rows, width = nodes.shape
    row_blocks, _, slots, block = tiles.shape[:4]
    tile_local = tiles.reshape(row_blocks, slots, block, block)
    cols = tile_col.reshape(row_blocks, slots).T
    counts = tile_count.reshape(row_blocks)
    gathered, total = n_row * rows, n_col * rows
    paired = n_row == 8 and n_col == 4
    here = lax.axis_index(("row", "col")).astype(jnp.int32).reshape(1)
    known = (paired, here, cols, counts)
    if paired:
        pieces = [gather_square(nodes)]
        (far,) = forward_call(*known, pieces[0], tile_local, ((0,),), rows)
        (near,) = forward_call(*known, pieces[0], tile_local, ((1,),), rows)
        pair, own = forward_call(*known, pieces[0], tile_local, ((2,), (3,)), rows)
        parts = [reduce_line(here, far, near, pair, own)]
        kinds = [("all", "all", "inner")]
    else:
        pieces = [[lax.all_gather(nodes, "row", axis=0, tiled=True)]]
        (partial,) = forward_call(*known, pieces[0], tile_local, (tuple(range(n_col)),), rows)
        parts = [[lax.psum_scatter(partial, "col", scatter_dimension=0, tiled=True)]]
        kinds = [("all",)]
    vectors = [v.reshape(1, width) for v in (bias_in, ln_gain, ln_shift)]
    (updated, gpre_b, act, gproj, message, vec), gmsgs = mlp_call(
        here, nodes, cotangent, parts, kinds, w_in, vectors[0], w_out, vectors[1], vectors[2]
    )
    factor = float(rows * n_row * n_col) ** -0.5
    weight_args = (here, nodes, message, act, gpre_b, gproj, cotangent, w_in, vec)
    if paired:
        halves = ((14, 15, 6, 11), (2, 3, 7, 10), (0, 1, 4, 5, 8, 9, 12, 13))
        grads = [gather_line(gmsgs[0])]
        kept, sent, direct = weight_call(factor, n_row, *weight_args, (grads[0][1], grads[0][2]))
        near_grads, token = tile_grad_call(
            *known, [grads[0][:2]], pieces, tile_local.shape, rows, (3, 2), after=(grads[0][3], grads[0][4])
        )
        row_weights = scatter_weights(here, kept, sent, (token,))
        urgent, rest, even = back_call(
            *known, grads[0], tile_local, total, gathered, halves, (row_weights,)
        )
        urgent, rest = swap(urgent, 1), swap(rest, 1)
        arrived, first = reduce_square(here, even, urgent, rest, rows)
        grad_tiles, token = tile_grad_call(
            *known, grads, pieces, tile_local.shape, rows, (1, 0), near_grads, first
        )
        all_weights = level_weights(here, row_weights, (token,))
        joint = jnp.concatenate([all_weights] + [swap(all_weights, bits) for bits in (2, 4, 6)], axis=0)
        weights = unpack_call(here, joint, swap(joint, 1), width)
        grad_nodes = sum_call(here, rows, [(direct, 0), (even, 0), (rest, 0)], split=arrived)
    else:
        grads = [[lax.all_gather(gmsgs[0], "col", axis=0, tiled=True)]]
        weight_terms, direct = weight_call(factor, 1, *weight_args)
        weight_sums = lax.psum(weight_terms, ("row", "col"))
        weights = (
            weight_sums[: 2 * width],
            weight_sums[2 * width : 3 * width],
            weight_sums[3 * width : 3 * width + 3],
        )
        (terms,) = back_call(*known, grads[0], tile_local, total, gathered, (tuple(range(n_row)),))
        back = lax.psum_scatter(terms, "row", scatter_dimension=0, tiled=True)
        grad_nodes = sum_call(here, rows, [(direct, 0), (back, 0)])
        grad_tiles, _ = tile_grad_call(
            *known, grads, pieces, tile_local.shape, rows, tuple(range(n_col))
        )
    grad_tiles = grad_tiles.reshape(tiles.shape)
    return (updated, grad_nodes, grad_tiles, *weights)


def solution(mesh):
    placed = (
        P(("row", "col"), None),
        P("row", "col", None, None, None),
        P("row", "col", None),
        P("row", "col"),
        P(),
        P(),
        P(),
        P(),
        P(),
        P(("row", "col"), None),
    )
    return jax.shard_map(
        functools.partial(body, mesh.shape["row"], mesh.shape["col"]),
        mesh=mesh,
        in_specs=placed,
        out_specs=(
            P(("row", "col"), None),
            P(("row", "col"), None),
            P("row", "col", None, None, None),
            P(),
            P(),
            P(),
        ),
        check_vma=False,
    )
```

```python
import functools

import jax
import jax.numpy as jnp
from jax import lax
from jax.experimental import pallas as pl
from jax.experimental.pallas import tpu as pltpu
from jax.sharding import PartitionSpec as P

F32 = jnp.float32
BF16 = jnp.bfloat16
ANY = pl.BlockSpec(memory_space=pl.ANY)
HBM = pl.BlockSpec(memory_space=pltpu.HBM)
SMEM = pl.BlockSpec(memory_space=pltpu.SMEM)
VMEM = pl.BlockSpec(memory_space=pltpu.VMEM)
MIB = 1 << 20
TN = (((0,), (0,)), ((), ()))
NT = (((1,), (1,)), ((), ()))
SMALL = pl.CostEstimate(flops=1 << 20, bytes_accessed=1 << 16, transcendentals=0)


LIVE_STEP = 4
GRAD_PLAN = ((3, 0, None), (2, 1, None), (1, 2, "inner"), (1, 3, "outer"), (0, 4, "inner"), (0, 5, "outer"))
SWAP_ORDER = (0, 4, 2, 6, 1, 5, 3, 7)


def params(mib):
    return pltpu.CompilerParams(vmem_limit_bytes=mib * MIB)


def mm(a, b, dims=(((1,), (0,)), ((), ()))):
    return lax.dot_general(a, b, dims, preferred_element_type=F32)


def block_at(index, block):
    return pl.ds(pl.multiple_of(index * block, block), block)


class Place:
    def __init__(self, ref, paired=True, blocks=1):
        self.mine, self.level = lax.shift_right_logical(ref[0], 2), ref[0] & 3
        self.paired, self.blocks = paired, blocks

    def inner(self):
        return (self.level == 1) | (self.level == 2)

    def group(self, pick):
        if not self.paired:
            return pick
        low = self.level < 2
        choices = (jnp.where(low, 3, 0), jnp.where(low, 2, 1), self.level ^ 1, self.level)
        return choices[pick]

    def source(self, col):
        if not self.paired:
            return col
        shift = self.blocks.bit_length() - 1
        if 1 << shift == self.blocks:
            return col ^ lax.shift_left(self.mine, jnp.int32(shift))
        return (lax.div(col, self.blocks) ^ self.mine) * self.blocks + lax.rem(col, self.blocks)


def load_pieces(pieces, dst, sem, first):
    copies = []
    offset = 0
    for index, piece in enumerate(pieces):
        copy = pltpu.make_async_copy(
            piece, dst.at[pl.ds(offset, piece.shape[0])], sem.at[first + index]
        )
        copy.start()
        copies.append(copy)
        offset += piece.shape[0]
    return copies


def masked_tile(tile, live):
    return jnp.where(live, tile, jnp.zeros_like(tile))


def forward_kernel(outputs, n_pieces, paired, here, cols, counts, *refs):
    pieces, tiles = refs[:n_pieces], refs[n_pieces]
    outs = refs[n_pieces + 1 : n_pieces + 1 + len(outputs)]
    nodes_v, tiles_v, sem, tile_sem = refs[n_pieces + 1 + len(outputs) :]
    rows = outs[0].shape[0] // len(outputs[0])
    slots, block = tiles.shape[1], tiles.shape[2]
    blocks = rows // block
    here = Place(here, paired, blocks)
    copies = load_pieces(pieces, nodes_v, sem, 0)
    places = [(pick, out, index) for out, picks in zip(outs, outputs) for index, pick in enumerate(picks)]
    tile_copies = []
    for place, (pick, _, _) in enumerate(places):
        copy = pltpu.make_async_copy(
            tiles.at[pl.ds(here.group(pick) * blocks, blocks)],
            tiles_v.at[pl.ds(place * blocks, blocks)],
            tile_sem.at[place],
        )
        copy.start()
        tile_copies.append(copy)
    for copy in copies:
        copy.wait()
    for place, (pick, out, index) in enumerate(places):
        tile_copies[place].wait()
        first = here.group(pick) * blocks

        def step(i, carry, first=first, out=out, index=index, place=place):
            row = first + i
            count = counts[row]
            parts = []
            for pair in range(slots // 2):
                both = (2 * pair, 2 * pair + 1)
                tile = jnp.concatenate(
                    [masked_tile(tiles_v[place * blocks + i, slot], slot < count) for slot in both], axis=1
                )
                node = jnp.concatenate(
                    [nodes_v[block_at(here.source(cols[slot, row]), block)] for slot in both], axis=0
                )
                parts.append(mm(tile, node))
            value = parts[0]
            for part in parts[1:]:
                value = value + part
            out[block_at(index * blocks + i, block)] = value.astype(BF16)
            return carry

        lax.fori_loop(0, blocks, step, 0, unroll=4)


def forward_call(paired, here, cols, counts, pieces, tiles, outputs, rows):
    width = pieces[0].shape[1]
    gathered = sum(piece.shape[0] for piece in pieces)
    slots, block = tiles.shape[1], tiles.shape[2]
    n_picks = sum(len(picks) for picks in outputs)
    return pl.pallas_call(
        functools.partial(forward_kernel, outputs, len(pieces), paired),
        out_shape=[jax.ShapeDtypeStruct((len(picks) * rows, width), BF16) for picks in outputs],
        in_specs=[SMEM] * 3 + [ANY] * len(pieces) + [HBM],
        out_specs=[VMEM] * len(outputs),
        scratch_shapes=[
            pltpu.VMEM((gathered, width), BF16),
            pltpu.VMEM((n_picks * (rows // block),) + tiles.shape[1:], BF16),
            pltpu.SemaphoreType.DMA((len(pieces),)),
            pltpu.SemaphoreType.DMA((n_picks,)),
        ],
        compiler_params=params(48),
        cost_estimate=SMALL,
        name="partial_messages",
    )(here, cols, counts, *pieces, tiles)


def mlp_kernel(kinds, here, nodes, cot, *refs):
    n_parts = sum(len(chunk) for chunk in kinds)
    parts = refs[:n_parts]
    w_in, bias, w_out, gain, shift, updated, gpre_o, act_o, gproj_o, msg_o, vec = refs[
        n_parts : n_parts + 11
    ]
    gmsgs = refs[n_parts + 11 :]
    width = nodes.shape[1]
    inner = Place(here).inner()
    messages = []
    place = 0
    for chunk in kinds:
        total = None
        for kind in chunk:
            term = parts[place][...].astype(F32)
            place += 1
            if kind == "inner":
                term = jnp.where(inner, term, 0.0)
            total = term if total is None else total + term
        messages.append(total.astype(BF16))
    message = jnp.concatenate(messages, axis=1) if len(messages) > 1 else messages[0]
    node = nodes[...]
    pre = mm(node, w_in[:width]) + mm(message, w_in[width:]) + bias[...]
    sig = 0.5 + 0.5 * jnp.tanh(0.5 * pre)
    act = (pre * sig).astype(BF16)
    proj = mm(act, w_out[...])
    mean = jnp.mean(proj, axis=-1, keepdims=True)
    var = jnp.mean((proj - mean) ** 2, axis=-1, keepdims=True)
    rstd = 1.0 / jnp.sqrt(var + 1e-05)
    normed = (proj - mean) * rstd
    updated[...] = (node.astype(F32) + normed * gain[...] + shift[...]).astype(BF16)
    grad_out = cot[...].astype(F32)
    gscaled = grad_out * gain[...]
    gproj = (
        (
            gscaled
            - jnp.mean(gscaled, axis=-1, keepdims=True)
            - normed * jnp.mean(gscaled * normed, axis=-1, keepdims=True)
        )
        * rstd
    ).astype(BF16)
    gact = mm(gproj, w_out[...], NT)
    gpre = gact * sig * (1.0 + pre * (1.0 - sig))
    gpre_b = gpre.astype(BF16)
    gmsg = mm(gpre_b, w_in[width:], NT).astype(BF16)
    part = width // len(gmsgs)
    for index, out in enumerate(gmsgs):
        out[...] = gmsg[:, index * part : (index + 1) * part]
    gpre_o[...] = gpre_b
    act_o[...] = act
    gproj_o[...] = gproj
    msg_o[...] = message

    @pl.when(pl.program_id(0) == 0)
    def _():
        vec[...] = jnp.zeros_like(vec)

    vec[0:1] += jnp.sum(gpre, axis=0, keepdims=True)
    vec[1:2] += jnp.sum(grad_out * normed, axis=0, keepdims=True)
    vec[2:3] += jnp.sum(grad_out, axis=0, keepdims=True)


def mlp_call(here, nodes, cot, parts, kinds, w_in, bias, w_out, gain, shift):
    rows, width = nodes.shape
    step = min(rows, 512)

    def blocked(array):
        return pl.BlockSpec((step, array.shape[1]), lambda i: (i, 0))

    def whole(array):
        return pl.BlockSpec(array.shape, lambda i: (0, 0))

    flat = [term for chunk in parts for term in chunk]
    row_like = jax.ShapeDtypeStruct((rows, width), BF16)
    chunk_like = jax.ShapeDtypeStruct((rows, width // len(parts)), BF16)
    outs = [row_like] * 5 + [jax.ShapeDtypeStruct((8, width), F32)] + [chunk_like] * len(parts)
    weights = (w_in, bias, w_out, gain, shift)
    result = pl.pallas_call(
        functools.partial(mlp_kernel, kinds),
        grid=(rows // step,),
        out_shape=outs,
        in_specs=[SMEM] + [blocked(a) for a in (nodes, cot, *flat)] + [whole(a) for a in weights],
        out_specs=[blocked(a) for a in outs[:5]] + [whole(outs[5])] + [blocked(a) for a in outs[6:]],
        compiler_params=params(40),
        cost_estimate=SMALL,
        name="mlp",
    )(here, nodes, cot, *flat, *weights)
    return result[:6], result[6:]


def weight_kernel(factor, pieces, n_after, here, nodes, msg, act, gpre, gproj, cot, w_in, vec, *refs):
    *outs, direct, grads = refs[n_after:]
    width = nodes.shape[1]

    @pl.when(pl.program_id(0) == 0)
    def _():
        grads[...] = jnp.zeros_like(grads)
        grads[3 * width : 3 * width + 8] = vec[...] * factor

    gpre_b = gpre[...]
    grads[:width] += mm(nodes[...], gpre_b, TN) * factor
    grads[width : 2 * width] += mm(msg[...], gpre_b, TN) * factor
    grads[2 * width : 3 * width] += mm(act[...], gproj[...], TN) * factor
    direct[...] = cot[...].astype(F32) + mm(gpre_b, w_in[:width], NT)

    @pl.when(pl.program_id(0) == pl.num_programs(0) - 1)
    def _():
        if pieces == 1:
            outs[0][...] = grads[: outs[0].shape[0]]
        else:
            rows = grads.shape[0] // pieces
            for place, member in enumerate(SWAP_ORDER):
                where = pl.ds(pl.multiple_of((Place(here).mine ^ member) * rows, 8), rows)
                out, index = outs[2 * place // pieces], place % (pieces // 2)
                out[index * rows : (index + 1) * rows] = grads[where]


def weight_call(factor, pieces, here, nodes, msg, act, gpre, gproj, cot, w_in, vec, after=()):
    rows, width = nodes.shape
    step = min(rows, 256)
    blocked = pl.BlockSpec((step, width), lambda i: (i, 0))

    def whole(shape):
        return pl.BlockSpec(shape, lambda i: (0, 0))

    padded = (3 * width + width // 2, width)
    if pieces == 1:
        outs = [jax.ShapeDtypeStruct((3 * width + 8, width), F32)]
    else:
        outs = [jax.ShapeDtypeStruct((padded[0] // 2, width), F32)] * 2
    return pl.pallas_call(
        functools.partial(weight_kernel, factor, pieces, len(after)),
        grid=(rows // step,),
        out_shape=[*outs, jax.ShapeDtypeStruct((rows, width), F32)],
        in_specs=[SMEM] + [blocked] * 6 + [whole(w_in.shape), whole(vec.shape)] + [ANY] * len(after),
        out_specs=[whole(out.shape) for out in outs] + [blocked],
        scratch_shapes=[pltpu.VMEM(padded, F32)],
        compiler_params=params(40),
        cost_estimate=SMALL,
        name="weight_grads",
    )(here, nodes, msg, act, gpre, gproj, cot, w_in, vec, *after)


def unpack_kernel(here, even, odd, w_in, w_out, vectors, grads):
    width = w_in.shape[1]
    rows = grads.shape[0] // 8
    for member in range(8):
        part = (even, odd)[member % 2]
        first = member // 2 * rows
        where = pl.ds(pl.multiple_of((Place(here).mine ^ member) * rows, 8), rows)
        grads[where] = part[first : first + rows].astype(F32)
    w_in[...] = grads[: 2 * width]
    w_out[...] = grads[2 * width : 3 * width]
    vectors[...] = grads[3 * width : 3 * width + 3]


def unpack_call(here, even, odd, width):
    shapes = ((2 * width, width), (width, width), (3, width))
    return pl.pallas_call(
        unpack_kernel,
        out_shape=[jax.ShapeDtypeStruct(shape, F32) for shape in shapes],
        in_specs=[SMEM, VMEM, VMEM],
        out_specs=[VMEM] * 3,
        scratch_shapes=[pltpu.VMEM((3 * width + width // 2, width), F32)],
        compiler_params=params(16),
        cost_estimate=SMALL,
        name="weight_unpack",
    )(here, even, odd)


def grad_jobs(rows, refs, dst, sem, here, groups=None):
    if len(refs) == 1:
        return [(None, pltpu.make_async_copy(refs[0], dst, sem.at[0]))]
    inner = here.inner()
    conditions = {None: None, "inner": inner, "outer": jnp.logical_not(inner)}
    jobs = []
    for group, index, kind in GRAD_PLAN:
        if groups is None:
            where = block_at(here.group(group), rows)
        elif group in groups:
            where = pl.ds(groups.index(group) * rows, rows)
        else:
            continue
        copy = pltpu.make_async_copy(refs[index], dst.at[where], sem.at[index])
        jobs.append((conditions[kind], copy))
    return jobs


def run_jobs(jobs, verb):
    for condition, copy in jobs:
        if condition is None:
            getattr(copy, verb)()
        else:
            pl.when(condition)(getattr(copy, verb))


def for_live(found, entry):
    def several(i, carry):
        for index in range(LIVE_STEP):
            entry(i * LIVE_STEP + index)
        return carry

    def one(i, carry):
        entry(i)
        return carry

    full = found // LIVE_STEP
    lax.fori_loop(0, full, several, 0)
    lax.fori_loop(full * LIVE_STEP, found, one, 0)


def back_kernel(rows, slots, n_grads, n_after, out_pieces, paired, here, cols, counts, *refs):
    grads, tiles = refs[:n_grads], refs[n_grads]
    refs = refs[n_grads + 1 + n_after :]
    outs = refs[: len(out_pieces)]
    grad_v, tiles_v, acc, live, source, sem, tile_sem = refs[len(out_pieces) :]
    n_tiles, block = tiles.shape[:2]
    here = Place(here, paired, rows // block)
    jobs = grad_jobs(rows, grads, grad_v, sem, here)
    run_jobs(jobs, "start")
    tile_copy = pltpu.make_async_copy(tiles, tiles_v, tile_sem.at[0])
    tile_copy.start()
    acc[...] = jnp.zeros_like(acc)

    def collect(row, found):
        count = counts[row]
        for slot in range(slots):
            live[found] = row * slots + slot
            source[found] = here.source(cols[slot, row])
            found = found + (slot < count).astype(jnp.int32)
        return found

    found = lax.fori_loop(0, n_tiles // slots, collect, jnp.int32(0))
    run_jobs(jobs, "wait")
    tile_copy.wait()

    def entry(place):
        tile_index = live[place]
        part = mm(tiles_v[tile_index], grad_v[block_at(tile_index // slots, block)], TN)
        acc[block_at(source[place], block)] += part

    for_live(found, entry)
    piece = acc.shape[0] // sum(len(members) for members in out_pieces)
    for out, members in zip(outs, out_pieces):
        for index, member in enumerate(members):
            out[pl.ds(index * piece, piece)] = acc[pl.ds(member * piece, piece)].astype(BF16)


def back_call(paired, here, cols, counts, grads, tiles, total, gathered, out_pieces, after=()):
    rows, width = grads[0].shape
    rows = total if len(grads) == 1 else rows
    row_blocks, slots, block = tiles.shape[:3]
    piece = gathered // sum(len(members) for members in out_pieces)
    return pl.pallas_call(
        functools.partial(back_kernel, rows, slots, len(grads), len(after), out_pieces, paired),
        out_shape=[jax.ShapeDtypeStruct((len(m) * piece, width), BF16) for m in out_pieces],
        in_specs=[SMEM] * 3 + [ANY] * len(grads) + [HBM] + [ANY] * len(after),
        out_specs=[VMEM] * len(out_pieces),
        scratch_shapes=[
            pltpu.VMEM((total, width), BF16),
            pltpu.VMEM((row_blocks * slots, block, block), BF16),
            pltpu.VMEM((gathered, width), F32),
            pltpu.SMEM((row_blocks * slots + 8,), jnp.int32),
            pltpu.SMEM((row_blocks * slots + 8,), jnp.int32),
            pltpu.SemaphoreType.DMA((len(grads),)),
            pltpu.SemaphoreType.DMA((1,)),
        ],
        compiler_params=params(28 if gathered <= 8192 else 56),
        cost_estimate=SMALL,
        name="back_terms",
    )(here, cols, counts, *grads, tiles.reshape(row_blocks * slots, block, block), *after)


def tile_grad_kernel(
    rows, slots, n_grads, n_pieces, n_chunks, n_after, groups, paired, here, cols, counts, *refs
):
    grads = refs[: n_grads * n_chunks]
    refs = refs[n_grads * n_chunks :]
    pieces = refs[: n_pieces * n_chunks]
    out, token, grad_v, nodes_v, tiles_v, live, source, sem, piece_sem, out_sem = refs[n_pieces * n_chunks + n_after :]
    token[...] = jnp.zeros_like(token)
    block = out.shape[1]
    width = nodes_v.shape[1]
    part = width // n_chunks
    scale = float(width) ** -0.5
    blocks = grad_v.shape[0] // (block * len(groups))
    here = Place(here, paired, blocks)
    jobs, copies = [], []
    for chunk in range(n_chunks):
        columns = pl.ds(chunk * part, part)
        jobs += grad_jobs(
            rows,
            grads[chunk * n_grads : (chunk + 1) * n_grads],
            grad_v.at[:, columns],
            sem.at[chunk],
            here,
            groups,
        )
        copies += load_pieces(
            pieces[chunk * n_pieces : (chunk + 1) * n_pieces],
            nodes_v.at[:, columns],
            piece_sem.at[chunk],
            0,
        )
    run_jobs(jobs, "start")
    tiles_v[...] = jnp.zeros_like(tiles_v)
    found = jnp.int32(0)
    for index, group in enumerate(groups):
        first = here.group(group) * blocks

        def collect(i, found, first=first, index=index):
            row = first + i
            count = counts[row]
            for slot in range(slots):
                live[found] = (index * blocks + i) * slots + slot
                source[found] = here.source(cols[slot, row])
                found = found + (slot < count).astype(jnp.int32)
            return found

        found = lax.fori_loop(0, blocks, collect, found)
    run_jobs(jobs, "wait")
    for copy in copies:
        copy.wait()

    def entry(place):
        tile_index = live[place]
        grad = grad_v[block_at(tile_index // slots, block)]
        node = nodes_v[block_at(source[place], block)]
        tiles_v[tile_index] = (mm(grad, node, NT) * scale).astype(BF16)

    for_live(found, entry)
    size = blocks * slots
    copies = []
    for index, group in enumerate(groups):
        copy = pltpu.make_async_copy(
            tiles_v.at[pl.ds(index * size, size)],
            out.at[pl.ds(here.group(group) * size, size)],
            out_sem.at[index],
        )
        copy.start()
        copies.append(copy)
    for copy in copies:
        copy.wait()


def tile_grad_call(paired, here, cols, counts, grads, pieces, shape, rows, groups, base=None, after=()):
    row_blocks, slots, block = shape[:3]
    chunks = len(grads)
    width = grads[0][0].shape[1] * chunks
    gathered = sum(piece.shape[0] for piece in pieces[0])
    flat = [a for chunk in grads for a in chunk] + [a for chunk in pieces for a in chunk]
    after = after if base is None else (base,) + tuple(after)
    entries = len(groups) * rows // block * slots
    return pl.pallas_call(
        functools.partial(
            tile_grad_kernel, rows, slots, len(grads[0]), len(pieces[0]), chunks, len(after), groups, paired
        ),
        out_shape=[
            jax.ShapeDtypeStruct((row_blocks * slots, block, block), BF16),
            jax.ShapeDtypeStruct((8, 128), F32),
        ],
        in_specs=[SMEM] * 3 + [ANY] * (len(flat) + len(after)),
        out_specs=[ANY, VMEM],
        input_output_aliases={} if base is None else {3 + len(flat): 0},
        scratch_shapes=[
            pltpu.VMEM((len(groups) * rows, width), BF16),
            pltpu.VMEM((gathered, width), BF16),
            pltpu.VMEM((entries, block, block), BF16),
            pltpu.SMEM((entries + 8,), jnp.int32),
            pltpu.SMEM((entries + 8,), jnp.int32),
            pltpu.SemaphoreType.DMA((chunks, len(grads[0]))),
            pltpu.SemaphoreType.DMA((chunks, len(pieces[0]))),
            pltpu.SemaphoreType.DMA((len(groups),)),
        ],
        compiler_params=params(16 if gathered <= 8192 else 40),
        cost_estimate=SMALL,
        name="tile_grads",
    )(here, cols, counts, *flat, *after)


def swap(value, bit):
    return lax.ppermute(value, "row", [(i, i ^ bit) for i in range(8)])


def outer_swap(value):
    return lax.ppermute(value, "col", [(0, 1), (1, 0), (2, 3), (3, 2)])


def turn(value, by):
    return lax.ppermute(value, "col", [(i, (i + by) % 4) for i in range(4)])


def inner_swap(value):
    pairs = []
    for row in range(8):
        for col in range(4):
            partner = (row, 3 - col) if col in (1, 2) else (row ^ 1, col)
            pairs.append((row * 4 + col, partner[0] * 4 + partner[1]))
    return lax.ppermute(value, ("row", "col"), pairs)


def gather_square(nodes):
    half = nodes.shape[0] // 2
    lower, upper = nodes[:half], nodes[half:]
    y_lower, x_upper = swap(lower, 4), swap(upper, 2)
    x_lower, y_upper = swap(lower, 2), swap(upper, 4)
    d_lower, d_upper = swap(y_lower, 2), swap(x_upper, 4)
    pieces = [nodes, swap(nodes, 1)]
    for pair in ((x_lower, x_upper), (y_lower, y_upper), (d_lower, d_upper)):
        pieces += [*pair, *(swap(piece, 1) for piece in pair)]
    return pieces


def reduce_square(here, even, urgent, rest, rows):
    half = rows // 2
    first = [
        sum_call(here, rows, [(even, (6, 2)), (urgent, (0, 2))]),
        sum_call(here, rows, [(even, (7, 5)), (urgent, (1, 3))]),
    ]
    x_first, y_first = swap(first[0], 2), swap(first[1], 4)
    y_lower = swap(sum_call(here, half, [(even, 4), (rest, 3), (x_first, 0)]), 4)
    x_upper = swap(sum_call(here, half, [(even, 3), (rest, 2), (y_first, 0)]), 2)
    return [((x_first, 1), (x_upper, 0)), ((y_lower, 0), (y_first, 1))], first


def sum_kernel(n_terms, n_gated, n_split, *refs):
    inner, refs = Place(refs[0]).inner(), refs[1:]
    total = None
    for index, ref in enumerate(refs[: n_terms + n_gated]):
        term = ref[...].astype(F32)
        if index >= n_terms:
            term = jnp.where(inner, term, 0.0)
        total = term if total is None else total + term
    for index in range(n_split):
        first, second = refs[n_terms + n_gated + 2 * index :][:2]
        early = pl.program_id(0) < pl.num_programs(0) // 2
        total = total + jnp.where(early, first[...], second[...]).astype(F32)
    refs[-1][...] = total.astype(refs[-1].dtype)


def sum_call(here, rows, terms, gated=(), split=(), dtype=BF16, after=()):
    both = [*terms, *gated]
    width = both[0][0].shape[1]
    step = min(rows, 256)
    steps = rows // step
    half = steps // 2

    def spec(piece):
        if isinstance(piece, int):
            return pl.BlockSpec((step, width), lambda i: (piece * steps + i, 0))
        lower, upper = piece
        return pl.BlockSpec(
            (step, width), lambda i: (jnp.where(i < half, lower * half + i, (upper - 1) * half + i), 0)
        )

    def early(piece):
        return pl.BlockSpec((step, width), lambda i: (piece * half + jnp.minimum(i, half - 1), 0))

    def late(piece):
        return pl.BlockSpec((step, width), lambda i: (piece * half + jnp.maximum(i - half, 0), 0))

    return pl.pallas_call(
        functools.partial(sum_kernel, len(terms), len(gated), len(split)),
        grid=(steps,),
        out_shape=jax.ShapeDtypeStruct((rows, width), dtype),
        in_specs=[SMEM]
        + [spec(piece) for _, piece in both]
        + [spec_of(piece) for pair in split for spec_of, (_, piece) in zip((early, late), pair)]
        + [ANY] * len(after),
        out_specs=pl.BlockSpec((step, width), lambda i: (i, 0)),
        compiler_params=params(8),
        cost_estimate=SMALL,
        name="sum_terms",
    )(here, *(array for array, _ in both), *(array for pair in split for array, _ in pair), *after)


def scatter_weights(here, kept, sent, after):
    rows = kept.shape[0] // 4
    received = swap(sent, 1)
    pieces = [
        sum_call(here, rows, [(kept, place), (received, place)], dtype=F32) for place in range(4)
    ]
    terms = [pieces[0]] + [swap(piece, bits) for piece, bits in zip(pieces[1:], SWAP_ORDER[1:4])]
    return sum_call(here, rows, [(term, 0) for term in terms], after=after)


def level_weights(here, value, after):
    terms = [value] + [turn(value, by) for by in (1, 2, 3)]
    return sum_call(here, value.shape[0], [(term, 0) for term in terms], after=after)


def reduce_line(here, far, near, pair, own):
    rows = own.shape[0]
    far_sum = inner_swap(sum_call(here, rows, [(far, 0), (outer_swap(far), 0)]))
    near_sum = inner_swap(sum_call(here, rows, [(near, 0), (outer_swap(near), 0)]))
    pair_in = outer_swap(sum_call(here, rows, [(pair, 0)], [(far_sum, 0)]))
    return own, pair_in, near_sum


def gather_line(own):
    pair = outer_swap(own)
    near_inner = inner_swap(own)
    far_inner = inner_swap(pair)
    near_outer = outer_swap(near_inner)
    far_outer = outer_swap(far_inner)
    return [own, pair, near_inner, near_outer, far_inner, far_outer]


def body(n_row, n_col, nodes, tiles, tile_col, tile_count, w_in, bias_in, w_out, ln_gain, ln_shift, cotangent):
    rows, width = nodes.shape
    row_blocks, _, slots, block = tiles.shape[:4]
    tile_local = tiles.reshape(row_blocks, slots, block, block)
    cols = tile_col.reshape(row_blocks, slots).T
    counts = tile_count.reshape(row_blocks)
    gathered, total = n_row * rows, n_col * rows
    paired = n_row == 8 and n_col == 4
    here = lax.axis_index(("row", "col")).astype(jnp.int32).reshape(1)
    known = (paired, here, cols, counts)
    if paired:
        pieces = [gather_square(nodes)]
        (far,) = forward_call(*known, pieces[0], tile_local, ((0,),), rows)
        (near,) = forward_call(*known, pieces[0], tile_local, ((1,),), rows)
        pair, own = forward_call(*known, pieces[0], tile_local, ((2,), (3,)), rows)
        parts = [reduce_line(here, far, near, pair, own)]
        kinds = [("all", "all", "inner")]
    else:
        pieces = [[lax.all_gather(nodes, "row", axis=0, tiled=True)]]
        (partial,) = forward_call(*known, pieces[0], tile_local, (tuple(range(n_col)),), rows)
        parts = [[lax.psum_scatter(partial, "col", scatter_dimension=0, tiled=True)]]
        kinds = [("all",)]
    vectors = [v.reshape(1, width) for v in (bias_in, ln_gain, ln_shift)]
    (updated, gpre_b, act, gproj, message, vec), gmsgs = mlp_call(
        here, nodes, cotangent, parts, kinds, w_in, vectors[0], w_out, vectors[1], vectors[2]
    )
    factor = float(rows * n_row * n_col) ** -0.5
    weight_args = (here, nodes, message, act, gpre_b, gproj, cotangent, w_in, vec)
    if paired:
        halves = ((14, 15, 6, 11), (2, 3, 7, 10), (0, 1, 4, 5, 8, 9, 12, 13))
        grads = [gather_line(gmsgs[0])]
        kept, sent, direct = weight_call(factor, n_row, *weight_args, (grads[0][1], grads[0][2]))
        near_grads, token = tile_grad_call(
            *known, [grads[0][:2]], pieces, tile_local.shape, rows, (3, 2), after=(grads[0][3], grads[0][4])
        )
        row_weights = scatter_weights(here, kept, sent, (token,))
        urgent, rest, even = back_call(
            *known, grads[0], tile_local, total, gathered, halves, (row_weights,)
        )
        urgent, rest = swap(urgent, 1), swap(rest, 1)
        arrived, first = reduce_square(here, even, urgent, rest, rows)
        grad_tiles, token = tile_grad_call(
            *known, grads, pieces, tile_local.shape, rows, (1, 0), near_grads, first
        )
        row_weights = sum_call(here, row_weights.shape[0], [(row_weights, 0)], after=(rest, *first))
        all_weights = level_weights(here, row_weights, (token,))
        joint = jnp.concatenate([all_weights] + [swap(all_weights, bits) for bits in (2, 4, 6)], axis=0)
        weights = unpack_call(here, joint, swap(joint, 1), width)
        grad_nodes = sum_call(here, rows, [(direct, 0), (even, 0), (rest, 0)], split=arrived)
    else:
        grads = [[lax.all_gather(gmsgs[0], "col", axis=0, tiled=True)]]
        weight_terms, direct = weight_call(factor, 1, *weight_args)
        weight_sums = lax.psum(weight_terms, ("row", "col"))
        weights = (
            weight_sums[: 2 * width],
            weight_sums[2 * width : 3 * width],
            weight_sums[3 * width : 3 * width + 3],
        )
        (terms,) = back_call(*known, grads[0], tile_local, total, gathered, (tuple(range(n_row)),))
        back = lax.psum_scatter(terms, "row", scatter_dimension=0, tiled=True)
        grad_nodes = sum_call(here, rows, [(direct, 0), (back, 0)])
        grad_tiles, _ = tile_grad_call(
            *known, grads, pieces, tile_local.shape, rows, tuple(range(n_col))
        )
    grad_tiles = grad_tiles.reshape(tiles.shape)
    return (updated, grad_nodes, grad_tiles, *weights)


def solution(mesh):
    placed = (
        P(("row", "col"), None),
        P("row", "col", None, None, None),
        P("row", "col", None),
        P("row", "col"),
        P(),
        P(),
        P(),
        P(),
        P(),
        P(("row", "col"), None),
    )
    return jax.shard_map(
        functools.partial(body, mesh.shape["row"], mesh.shape["col"]),
        mesh=mesh,
        in_specs=placed,
        out_specs=(
            P(("row", "col"), None),
            P(("row", "col"), None),
            P("row", "col", None, None, None),
            P(),
            P(),
            P(),
        ),
        check_vma=False,
    )
```

```python
import functools

import jax
import jax.numpy as jnp
from jax import lax
from jax.experimental import pallas as pl
from jax.experimental.pallas import tpu as pltpu
from jax.sharding import PartitionSpec as P

F32 = jnp.float32
BF16 = jnp.bfloat16
ANY = pl.BlockSpec(memory_space=pl.ANY)
HBM = pl.BlockSpec(memory_space=pltpu.HBM)
SMEM = pl.BlockSpec(memory_space=pltpu.SMEM)
VMEM = pl.BlockSpec(memory_space=pltpu.VMEM)
MIB = 1 << 20
TN = (((0,), (0,)), ((), ()))
NT = (((1,), (1,)), ((), ()))
SMALL = pl.CostEstimate(flops=1 << 20, bytes_accessed=1 << 16, transcendentals=0)


LIVE_STEP = 4
GRAD_PLAN = ((3, 0, None), (2, 1, None), (1, 2, "inner"), (1, 3, "outer"), (0, 4, "inner"), (0, 5, "outer"))
SWAP_ORDER = (0, 4, 2, 6, 1, 5, 3, 7)


def params(mib):
    return pltpu.CompilerParams(vmem_limit_bytes=mib * MIB)


def mm(a, b, dims=(((1,), (0,)), ((), ()))):
    return lax.dot_general(a, b, dims, preferred_element_type=F32)


def block_at(index, block):
    return pl.ds(pl.multiple_of(index * block, block), block)


class Place:
    def __init__(self, ref, paired=True, blocks=1):
        self.mine, self.level = lax.shift_right_logical(ref[0], 2), ref[0] & 3
        self.paired, self.blocks = paired, blocks

    def inner(self):
        return (self.level == 1) | (self.level == 2)

    def group(self, pick):
        if not self.paired:
            return pick
        low = self.level < 2
        choices = (jnp.where(low, 3, 0), jnp.where(low, 2, 1), self.level ^ 1, self.level)
        return choices[pick]

    def source(self, col):
        if not self.paired:
            return col
        shift = self.blocks.bit_length() - 1
        if 1 << shift == self.blocks:
            return col ^ lax.shift_left(self.mine, jnp.int32(shift))
        return (lax.div(col, self.blocks) ^ self.mine) * self.blocks + lax.rem(col, self.blocks)


def load_pieces(pieces, dst, sem, first):
    copies = []
    offset = 0
    for index, piece in enumerate(pieces):
        copy = pltpu.make_async_copy(
            piece, dst.at[pl.ds(offset, piece.shape[0])], sem.at[first + index]
        )
        copy.start()
        copies.append(copy)
        offset += piece.shape[0]
    return copies


def masked_tile(tile, live):
    return jnp.where(live, tile, jnp.zeros_like(tile))


def forward_kernel(outputs, n_pieces, paired, here, cols, *refs):
    pieces, tiles = refs[:n_pieces], refs[n_pieces]
    outs = refs[n_pieces + 1 : n_pieces + 1 + len(outputs)]
    nodes_v, tiles_v, sem, tile_sem = refs[n_pieces + 1 + len(outputs) :]
    rows = outs[0].shape[0] // len(outputs[0])
    slots, block = tiles.shape[1], tiles.shape[2]
    blocks = rows // block
    here = Place(here, paired, blocks)
    copies = load_pieces(pieces, nodes_v, sem, 0)
    places = [(pick, out, index) for out, picks in zip(outs, outputs) for index, pick in enumerate(picks)]
    tile_copies = []
    for place, (pick, _, _) in enumerate(places):
        copy = pltpu.make_async_copy(
            tiles.at[pl.ds(here.group(pick) * blocks, blocks)],
            tiles_v.at[pl.ds(place * blocks, blocks)],
            tile_sem.at[place],
        )
        copy.start()
        tile_copies.append(copy)
    for copy in copies:
        copy.wait()
    for place, (pick, out, index) in enumerate(places):
        tile_copies[place].wait()
        first = here.group(pick) * blocks

        def step(i, carry, first=first, out=out, index=index, place=place):
            row = first + i
            count = cols[slots, row]
            parts = []
            for pair in range(slots // 2):
                both = (2 * pair, 2 * pair + 1)
                tile = jnp.concatenate(
                    [masked_tile(tiles_v[place * blocks + i, slot], slot < count) for slot in both], axis=1
                )
                node = jnp.concatenate(
                    [nodes_v[block_at(here.source(cols[slot, row]), block)] for slot in both], axis=0
                )
                parts.append(mm(tile, node))
            value = parts[0]
            for part in parts[1:]:
                value = value + part
            out[block_at(index * blocks + i, block)] = value.astype(BF16)
            return carry

        lax.fori_loop(0, blocks, step, 0, unroll=4)


def forward_call(paired, here, cols, pieces, tiles, outputs, rows):
    width = pieces[0].shape[1]
    gathered = sum(piece.shape[0] for piece in pieces)
    slots, block = tiles.shape[1], tiles.shape[2]
    n_picks = sum(len(picks) for picks in outputs)
    return pl.pallas_call(
        functools.partial(forward_kernel, outputs, len(pieces), paired),
        out_shape=[jax.ShapeDtypeStruct((len(picks) * rows, width), BF16) for picks in outputs],
        in_specs=[SMEM] * 2 + [ANY] * len(pieces) + [HBM],
        out_specs=[VMEM] * len(outputs),
        scratch_shapes=[
            pltpu.VMEM((gathered, width), BF16),
            pltpu.VMEM((n_picks * (rows // block),) + tiles.shape[1:], BF16),
            pltpu.SemaphoreType.DMA((len(pieces),)),
            pltpu.SemaphoreType.DMA((n_picks,)),
        ],
        compiler_params=params(48),
        cost_estimate=SMALL,
        name="partial_messages",
    )(here, cols, *pieces, tiles)


def mlp_kernel(kinds, here, nodes, cot, *refs):
    n_parts = sum(len(chunk) for chunk in kinds)
    parts = refs[:n_parts]
    w_in, bias, w_out, gain, shift, updated, gpre_o, act_o, gproj_o, msg_o, vec = refs[
        n_parts : n_parts + 11
    ]
    gmsgs = refs[n_parts + 11 :]
    width = nodes.shape[1]
    inner = Place(here).inner()
    messages = []
    place = 0
    for chunk in kinds:
        total = None
        for kind in chunk:
            term = parts[place][...].astype(F32)
            place += 1
            if kind == "inner":
                term = jnp.where(inner, term, 0.0)
            total = term if total is None else total + term
        messages.append(total.astype(BF16))
    message = jnp.concatenate(messages, axis=1) if len(messages) > 1 else messages[0]
    node = nodes[...]
    pre = mm(node, w_in[:width]) + mm(message, w_in[width:]) + bias[...]
    sig = 0.5 + 0.5 * jnp.tanh(0.5 * pre)
    act = (pre * sig).astype(BF16)
    proj = mm(act, w_out[...])
    mean = jnp.mean(proj, axis=-1, keepdims=True)
    var = jnp.mean((proj - mean) ** 2, axis=-1, keepdims=True)
    rstd = 1.0 / jnp.sqrt(var + 1e-05)
    normed = (proj - mean) * rstd
    updated[...] = (node.astype(F32) + normed * gain[...] + shift[...]).astype(BF16)
    grad_out = cot[...].astype(F32)
    gscaled = grad_out * gain[...]
    gproj = (
        (
            gscaled
            - jnp.mean(gscaled, axis=-1, keepdims=True)
            - normed * jnp.mean(gscaled * normed, axis=-1, keepdims=True)
        )
        * rstd
    ).astype(BF16)
    gact = mm(gproj, w_out[...], NT)
    gpre = gact * sig * (1.0 + pre * (1.0 - sig))
    gpre_b = gpre.astype(BF16)
    gmsg = mm(gpre_b, w_in[width:], NT).astype(BF16)
    part = width // len(gmsgs)
    for index, out in enumerate(gmsgs):
        out[...] = gmsg[:, index * part : (index + 1) * part]
    gpre_o[...] = gpre_b
    act_o[...] = act
    gproj_o[...] = gproj
    msg_o[...] = message

    @pl.when(pl.program_id(0) == 0)
    def _():
        vec[...] = jnp.zeros_like(vec)

    vec[0:1] += jnp.sum(gpre, axis=0, keepdims=True)
    vec[1:2] += jnp.sum(grad_out * normed, axis=0, keepdims=True)
    vec[2:3] += jnp.sum(grad_out, axis=0, keepdims=True)


def mlp_call(here, nodes, cot, parts, kinds, w_in, bias, w_out, gain, shift):
    rows, width = nodes.shape
    step = min(rows, 512)

    def blocked(array):
        return pl.BlockSpec((step, array.shape[1]), lambda i: (i, 0))

    def whole(array):
        return pl.BlockSpec(array.shape, lambda i: (0, 0))

    flat = [term for chunk in parts for term in chunk]
    row_like = jax.ShapeDtypeStruct((rows, width), BF16)
    chunk_like = jax.ShapeDtypeStruct((rows, width // len(parts)), BF16)
    outs = [row_like] * 5 + [jax.ShapeDtypeStruct((8, width), F32)] + [chunk_like] * len(parts)
    weights = (w_in, bias, w_out, gain, shift)
    result = pl.pallas_call(
        functools.partial(mlp_kernel, kinds),
        grid=(rows // step,),
        out_shape=outs,
        in_specs=[SMEM] + [blocked(a) for a in (nodes, cot, *flat)] + [whole(a) for a in weights],
        out_specs=[blocked(a) for a in outs[:5]] + [whole(outs[5])] + [blocked(a) for a in outs[6:]],
        compiler_params=params(40),
        cost_estimate=SMALL,
        name="mlp",
    )(here, nodes, cot, *flat, *weights)
    return result[:6], result[6:]


def weight_kernel(factor, pieces, n_after, here, nodes, msg, act, gpre, gproj, cot, w_in, vec, *refs):
    *outs, direct, grads = refs[n_after:]
    width = nodes.shape[1]

    @pl.when(pl.program_id(0) == 0)
    def _():
        grads[...] = jnp.zeros_like(grads)
        grads[3 * width : 3 * width + 8] = vec[...] * factor

    gpre_b = gpre[...]
    grads[:width] += mm(nodes[...], gpre_b, TN) * factor
    grads[width : 2 * width] += mm(msg[...], gpre_b, TN) * factor
    grads[2 * width : 3 * width] += mm(act[...], gproj[...], TN) * factor
    direct[...] = cot[...].astype(F32) + mm(gpre_b, w_in[:width], NT)

    @pl.when(pl.program_id(0) == pl.num_programs(0) - 1)
    def _():
        if pieces == 1:
            outs[0][...] = grads[: outs[0].shape[0]]
        else:
            rows = grads.shape[0] // pieces
            for place, member in enumerate(SWAP_ORDER):
                where = pl.ds(pl.multiple_of((Place(here).mine ^ member) * rows, 8), rows)
                out, index = outs[2 * place // pieces], place % (pieces // 2)
                out[index * rows : (index + 1) * rows] = grads[where]


def weight_call(factor, pieces, here, nodes, msg, act, gpre, gproj, cot, w_in, vec, after=()):
    rows, width = nodes.shape
    step = min(rows, 256)
    blocked = pl.BlockSpec((step, width), lambda i: (i, 0))

    def whole(shape):
        return pl.BlockSpec(shape, lambda i: (0, 0))

    padded = (3 * width + width // 2, width)
    if pieces == 1:
        outs = [jax.ShapeDtypeStruct((3 * width + 8, width), F32)]
    else:
        outs = [jax.ShapeDtypeStruct((padded[0] // 2, width), F32)] * 2
    return pl.pallas_call(
        functools.partial(weight_kernel, factor, pieces, len(after)),
        grid=(rows // step,),
        out_shape=[*outs, jax.ShapeDtypeStruct((rows, width), F32)],
        in_specs=[SMEM] + [blocked] * 6 + [whole(w_in.shape), whole(vec.shape)] + [ANY] * len(after),
        out_specs=[whole(out.shape) for out in outs] + [blocked],
        scratch_shapes=[pltpu.VMEM(padded, F32)],
        compiler_params=params(40),
        cost_estimate=SMALL,
        name="weight_grads",
    )(here, nodes, msg, act, gpre, gproj, cot, w_in, vec, *after)


def unpack_kernel(here, even, odd, w_in, w_out, vectors, grads):
    width = w_in.shape[1]
    rows = grads.shape[0] // 8
    for member in range(8):
        part = (even, odd)[member % 2]
        first = member // 2 * rows
        where = pl.ds(pl.multiple_of((Place(here).mine ^ member) * rows, 8), rows)
        grads[where] = part[first : first + rows].astype(F32)
    w_in[...] = grads[: 2 * width]
    w_out[...] = grads[2 * width : 3 * width]
    vectors[...] = grads[3 * width : 3 * width + 3]


def unpack_call(here, even, odd, width):
    shapes = ((2 * width, width), (width, width), (3, width))
    return pl.pallas_call(
        unpack_kernel,
        out_shape=[jax.ShapeDtypeStruct(shape, F32) for shape in shapes],
        in_specs=[SMEM, VMEM, VMEM],
        out_specs=[VMEM] * 3,
        scratch_shapes=[pltpu.VMEM((3 * width + width // 2, width), F32)],
        compiler_params=params(16),
        cost_estimate=SMALL,
        name="weight_unpack",
    )(here, even, odd)


def grad_jobs(rows, refs, dst, sem, here, groups=None):
    if len(refs) == 1:
        return [(None, pltpu.make_async_copy(refs[0], dst, sem.at[0]))]
    inner = here.inner()
    conditions = {None: None, "inner": inner, "outer": jnp.logical_not(inner)}
    jobs = []
    for group, index, kind in GRAD_PLAN:
        if groups is None:
            where = block_at(here.group(group), rows)
        elif group in groups:
            where = pl.ds(groups.index(group) * rows, rows)
        else:
            continue
        copy = pltpu.make_async_copy(refs[index], dst.at[where], sem.at[index])
        jobs.append((conditions[kind], copy))
    return jobs


def run_jobs(jobs, verb):
    for condition, copy in jobs:
        if condition is None:
            getattr(copy, verb)()
        else:
            pl.when(condition)(getattr(copy, verb))


def for_live(found, entry):
    def several(i, carry):
        for index in range(LIVE_STEP):
            entry(i * LIVE_STEP + index)
        return carry

    def one(i, carry):
        entry(i)
        return carry

    full = found // LIVE_STEP
    lax.fori_loop(0, full, several, 0)
    lax.fori_loop(full * LIVE_STEP, found, one, 0)


def turn_kernel(slots, cols, tiles, out, tiles_v, live, sem):
    copy = pltpu.make_async_copy(tiles, tiles_v, sem.at[0])
    copy.start()

    def collect(row, found):
        count = cols[slots, row]
        for slot in range(slots):
            live[found] = row * slots + slot
            found = found + (slot < count).astype(jnp.int32)
        return found

    found = lax.fori_loop(0, tiles.shape[0] // slots, collect, jnp.int32(0))
    copy.wait()

    def entry(place):
        tile_index = live[place]
        out[tile_index] = tiles_v[tile_index].T

    for_live(found, entry)


def turn_call(cols, tiles):
    row_blocks, slots, block = tiles.shape[:3]
    shape = (row_blocks * slots, block, block)
    return pl.pallas_call(
        functools.partial(turn_kernel, slots),
        out_shape=jax.ShapeDtypeStruct(shape, BF16),
        in_specs=[SMEM, HBM],
        out_specs=VMEM,
        scratch_shapes=[
            pltpu.VMEM(shape, BF16),
            pltpu.SMEM((row_blocks * slots + 8,), jnp.int32),
            pltpu.SemaphoreType.DMA((1,)),
        ],
        compiler_params=params(16 if row_blocks <= 32 else 32),
        cost_estimate=SMALL,
        name="turned_tiles",
    )(cols, tiles.reshape(shape))


def back_kernel(rows, slots, n_grads, n_after, out_pieces, paired, here, cols, *refs):
    grads, tiles = refs[:n_grads], refs[n_grads]
    refs = refs[n_grads + 1 + n_after :]
    outs = refs[: len(out_pieces)]
    grad_v, tiles_v, acc, live, source, sem, tile_sem = refs[len(out_pieces) :]
    n_tiles, block = tiles.shape[:2]
    here = Place(here, paired, rows // block)
    jobs = grad_jobs(rows, grads, grad_v, sem, here)
    run_jobs(jobs, "start")
    tile_copy = pltpu.make_async_copy(tiles, tiles_v, tile_sem.at[0])
    tile_copy.start()
    acc[...] = jnp.zeros_like(acc)

    def collect(row, found):
        count = cols[slots, row]
        for slot in range(slots):
            live[found] = row * slots + slot
            source[found] = here.source(cols[slot, row])
            found = found + (slot < count).astype(jnp.int32)
        return found

    found = lax.fori_loop(0, n_tiles // slots, collect, jnp.int32(0))
    run_jobs(jobs, "wait")
    tile_copy.wait()

    def entry(place):
        tile_index = live[place]
        part = mm(tiles_v[tile_index], grad_v[block_at(tile_index // slots, block)])
        acc[block_at(source[place], block)] += part

    for_live(found, entry)
    piece = acc.shape[0] // sum(len(members) for members in out_pieces)
    for out, members in zip(outs, out_pieces):
        for index, member in enumerate(members):
            out[pl.ds(index * piece, piece)] = acc[pl.ds(member * piece, piece)].astype(BF16)


def back_call(paired, here, cols, grads, tiles, total, gathered, out_pieces, after=()):
    rows, width = grads[0].shape
    rows = total if len(grads) == 1 else rows
    n_tiles, block = tiles.shape[:2]
    slots = cols.shape[0] - 1
    piece = gathered // sum(len(members) for members in out_pieces)
    return pl.pallas_call(
        functools.partial(back_kernel, rows, slots, len(grads), len(after), out_pieces, paired),
        out_shape=[jax.ShapeDtypeStruct((len(m) * piece, width), BF16) for m in out_pieces],
        in_specs=[SMEM] * 2 + [ANY] * len(grads) + [HBM] + [ANY] * len(after),
        out_specs=[VMEM] * len(out_pieces),
        scratch_shapes=[
            pltpu.VMEM((total, width), BF16),
            pltpu.VMEM((n_tiles, block, block), BF16),
            pltpu.VMEM((gathered, width), F32),
            pltpu.SMEM((n_tiles + 8,), jnp.int32),
            pltpu.SMEM((n_tiles + 8,), jnp.int32),
            pltpu.SemaphoreType.DMA((len(grads),)),
            pltpu.SemaphoreType.DMA((1,)),
        ],
        compiler_params=params(28 if gathered <= 8192 else 56),
        cost_estimate=SMALL,
        name="back_terms",
    )(here, cols, *grads, tiles, *after)


def tile_grad_kernel(
    rows, slots, n_grads, n_pieces, n_chunks, n_after, groups, paired, here, cols, *refs
):
    grads = refs[: n_grads * n_chunks]
    refs = refs[n_grads * n_chunks :]
    pieces = refs[: n_pieces * n_chunks]
    out, token, grad_v, nodes_v, tiles_v, live, source, sem, piece_sem, out_sem = refs[n_pieces * n_chunks + n_after :]
    token[...] = jnp.zeros_like(token)
    block = out.shape[1]
    width = nodes_v.shape[1]
    part = width // n_chunks
    scale = float(width) ** -0.5
    blocks = grad_v.shape[0] // (block * len(groups))
    here = Place(here, paired, blocks)
    jobs, copies = [], []
    for chunk in range(n_chunks):
        columns = pl.ds(chunk * part, part)
        jobs += grad_jobs(
            rows,
            grads[chunk * n_grads : (chunk + 1) * n_grads],
            grad_v.at[:, columns],
            sem.at[chunk],
            here,
            groups,
        )
        copies += load_pieces(
            pieces[chunk * n_pieces : (chunk + 1) * n_pieces],
            nodes_v.at[:, columns],
            piece_sem.at[chunk],
            0,
        )
    run_jobs(jobs, "start")
    tiles_v[...] = jnp.zeros_like(tiles_v)
    found = jnp.int32(0)
    for index, group in enumerate(groups):
        first = here.group(group) * blocks

        def collect(i, found, first=first, index=index):
            row = first + i
            count = cols[slots, row]
            for slot in range(slots):
                live[found] = (index * blocks + i) * slots + slot
                source[found] = here.source(cols[slot, row])
                found = found + (slot < count).astype(jnp.int32)
            return found

        found = lax.fori_loop(0, blocks, collect, found)
    run_jobs(jobs, "wait")
    for copy in copies:
        copy.wait()

    def entry(place):
        tile_index = live[place]
        grad = grad_v[block_at(tile_index // slots, block)]
        node = nodes_v[block_at(source[place], block)]
        tiles_v[tile_index] = (mm(grad, node, NT) * scale).astype(BF16)

    for_live(found, entry)
    size = blocks * slots
    copies = []
    for index, group in enumerate(groups):
        copy = pltpu.make_async_copy(
            tiles_v.at[pl.ds(index * size, size)],
            out.at[pl.ds(here.group(group) * size, size)],
            out_sem.at[index],
        )
        copy.start()
        copies.append(copy)
    for copy in copies:
        copy.wait()


def tile_grad_call(paired, here, cols, grads, pieces, shape, rows, groups, base=None, after=()):
    row_blocks, slots, block = shape[:3]
    chunks = len(grads)
    width = grads[0][0].shape[1] * chunks
    gathered = sum(piece.shape[0] for piece in pieces[0])
    flat = [a for chunk in grads for a in chunk] + [a for chunk in pieces for a in chunk]
    after = after if base is None else (base,) + tuple(after)
    entries = len(groups) * rows // block * slots
    return pl.pallas_call(
        functools.partial(
            tile_grad_kernel, rows, slots, len(grads[0]), len(pieces[0]), chunks, len(after), groups, paired
        ),
        out_shape=[
            jax.ShapeDtypeStruct((row_blocks * slots, block, block), BF16),
            jax.ShapeDtypeStruct((8, 128), F32),
        ],
        in_specs=[SMEM] * 2 + [ANY] * (len(flat) + len(after)),
        out_specs=[ANY, VMEM],
        input_output_aliases={} if base is None else {2 + len(flat): 0},
        scratch_shapes=[
            pltpu.VMEM((len(groups) * rows, width), BF16),
            pltpu.VMEM((gathered, width), BF16),
            pltpu.VMEM((entries, block, block), BF16),
            pltpu.SMEM((entries + 8,), jnp.int32),
            pltpu.SMEM((entries + 8,), jnp.int32),
            pltpu.SemaphoreType.DMA((chunks, len(grads[0]))),
            pltpu.SemaphoreType.DMA((chunks, len(pieces[0]))),
            pltpu.SemaphoreType.DMA((len(groups),)),
        ],
        compiler_params=params(16 if gathered <= 8192 else 40),
        cost_estimate=SMALL,
        name="tile_grads",
    )(here, cols, *flat, *after)


def swap(value, bit):
    return lax.ppermute(value, "row", [(i, i ^ bit) for i in range(8)])


def outer_swap(value):
    return lax.ppermute(value, "col", [(0, 1), (1, 0), (2, 3), (3, 2)])


def turn(value, by):
    return lax.ppermute(value, "col", [(i, (i + by) % 4) for i in range(4)])


def inner_swap(value):
    pairs = []
    for row in range(8):
        for col in range(4):
            partner = (row, 3 - col) if col in (1, 2) else (row ^ 1, col)
            pairs.append((row * 4 + col, partner[0] * 4 + partner[1]))
    return lax.ppermute(value, ("row", "col"), pairs)


def gather_square(nodes):
    half = nodes.shape[0] // 2
    lower, upper = nodes[:half], nodes[half:]
    y_lower, x_upper = swap(lower, 4), swap(upper, 2)
    x_lower, y_upper = swap(lower, 2), swap(upper, 4)
    d_lower, d_upper = swap(y_lower, 2), swap(x_upper, 4)
    pieces = [lower, upper, swap(nodes, 1)]
    for pair in ((x_lower, x_upper), (y_lower, y_upper), (d_lower, d_upper)):
        pieces += [*pair, *(swap(piece, 1) for piece in pair)]
    return pieces


def reduce_square(here, even, urgent, rest, rows):
    half = rows // 2
    first = [
        sum_call(here, rows, [(even, (6, 2)), (urgent, (0, 2))]),
        sum_call(here, rows, [(even, (7, 5)), (urgent, (1, 3))]),
    ]
    x_first, y_first = swap(first[0], 2), swap(first[1], 4)
    y_lower = swap(sum_call(here, half, [(even, 4), (rest, 3), (x_first, 0)]), 4)
    x_upper = swap(sum_call(here, half, [(even, 3), (rest, 2), (y_first, 0)]), 2)
    return [((x_first, 1), (x_upper, 0)), ((y_lower, 0), (y_first, 1))], first


def sum_kernel(n_terms, n_gated, n_split, *refs):
    inner, refs = Place(refs[0]).inner(), refs[1:]
    total = None
    for index, ref in enumerate(refs[: n_terms + n_gated]):
        term = ref[...].astype(F32)
        if index >= n_terms:
            term = jnp.where(inner, term, 0.0)
        total = term if total is None else total + term
    for index in range(n_split):
        first, second = refs[n_terms + n_gated + 2 * index :][:2]
        early = pl.program_id(0) < pl.num_programs(0) // 2
        total = total + jnp.where(early, first[...], second[...]).astype(F32)
    refs[-1][...] = total.astype(refs[-1].dtype)


def sum_call(here, rows, terms, gated=(), split=(), dtype=BF16, after=()):
    both = [*terms, *gated]
    width = both[0][0].shape[1]
    step = min(rows, 256)
    steps = rows // step
    half = steps // 2

    def spec(piece):
        if isinstance(piece, int):
            return pl.BlockSpec((step, width), lambda i: (piece * steps + i, 0))
        lower, upper = piece
        return pl.BlockSpec(
            (step, width), lambda i: (jnp.where(i < half, lower * half + i, (upper - 1) * half + i), 0)
        )

    def early(piece):
        return pl.BlockSpec((step, width), lambda i: (piece * half + jnp.minimum(i, half - 1), 0))

    def late(piece):
        return pl.BlockSpec((step, width), lambda i: (piece * half + jnp.maximum(i - half, 0), 0))

    return pl.pallas_call(
        functools.partial(sum_kernel, len(terms), len(gated), len(split)),
        grid=(steps,),
        out_shape=jax.ShapeDtypeStruct((rows, width), dtype),
        in_specs=[SMEM]
        + [spec(piece) for _, piece in both]
        + [spec_of(piece) for pair in split for spec_of, (_, piece) in zip((early, late), pair)]
        + [ANY] * len(after),
        out_specs=pl.BlockSpec((step, width), lambda i: (i, 0)),
        compiler_params=params(8),
        cost_estimate=SMALL,
        name="sum_terms",
    )(here, *(array for array, _ in both), *(array for pair in split for array, _ in pair), *after)


def scatter_weights(here, kept, sent, after):
    rows = kept.shape[0] // 4
    received = swap(sent, 1)
    pieces = [
        sum_call(here, rows, [(kept, place), (received, place)], dtype=F32) for place in range(4)
    ]
    terms = [pieces[0]] + [swap(piece, bits) for piece, bits in zip(pieces[1:], SWAP_ORDER[1:4])]
    return sum_call(here, rows, [(term, 0) for term in terms], after=after)


def level_weights(here, value, after):
    terms = [value] + [turn(value, by) for by in (1, 2, 3)]
    return sum_call(here, value.shape[0], [(term, 0) for term in terms], after=after)


def reduce_line(here, far, near, pair, own, after):
    rows = own.shape[0]
    far_sum = inner_swap(sum_call(here, rows, [(far, 0), (outer_swap(far), 0)], after=after))
    near_sum = inner_swap(sum_call(here, rows, [(near, 0), (outer_swap(near), 0)]))
    pair_in = outer_swap(sum_call(here, rows, [(pair, 0)], [(far_sum, 0)]))
    return own, pair_in, near_sum


def gather_line(own):
    pair = outer_swap(own)
    near_inner = inner_swap(own)
    far_inner = inner_swap(pair)
    near_outer = outer_swap(near_inner)
    far_outer = outer_swap(far_inner)
    return [own, pair, near_inner, near_outer, far_inner, far_outer]


def body(n_row, n_col, nodes, tiles, tile_col, tile_count, w_in, bias_in, w_out, ln_gain, ln_shift, cotangent):
    rows, width = nodes.shape
    row_blocks, _, slots, block = tiles.shape[:4]
    tile_local = tiles.reshape(row_blocks, slots, block, block)
    table = jnp.concatenate([tile_col.reshape(row_blocks, slots).T, tile_count.reshape(1, row_blocks)], axis=0)
    gathered, total = n_row * rows, n_col * rows
    paired = n_row == 8 and n_col == 4
    here = lax.axis_index(("row", "col")).astype(jnp.int32).reshape(1)
    known = (paired, here, table)
    turned = turn_call(table, tile_local)
    if paired:
        pieces = [gather_square(nodes)]
        (far,) = forward_call(*known, pieces[0], tile_local, ((0,),), rows)
        (near,) = forward_call(*known, pieces[0], tile_local, ((1,),), rows)
        pair, own = forward_call(*known, pieces[0], tile_local, ((2,), (3,)), rows)
        parts = [reduce_line(here, far, near, pair, own, (turned,))]
        kinds = [("all", "all", "inner")]
    else:
        pieces = [[lax.all_gather(nodes, "row", axis=0, tiled=True)]]
        (partial,) = forward_call(*known, pieces[0], tile_local, (tuple(range(n_col)),), rows)
        parts = [[lax.psum_scatter(partial, "col", scatter_dimension=0, tiled=True)]]
        kinds = [("all",)]
    vectors = [v.reshape(1, width) for v in (bias_in, ln_gain, ln_shift)]
    (updated, gpre_b, act, gproj, message, vec), gmsgs = mlp_call(
        here, nodes, cotangent, parts, kinds, w_in, vectors[0], w_out, vectors[1], vectors[2]
    )
    factor = float(rows * n_row * n_col) ** -0.5
    weight_args = (here, nodes, message, act, gpre_b, gproj, cotangent, w_in, vec)
    if paired:
        halves = ((14, 15, 6, 11), (2, 3, 7, 10), (0, 1, 4, 5, 8, 9, 12, 13))
        grads = [gather_line(gmsgs[0])]
        kept, sent, direct = weight_call(factor, n_row, *weight_args, (grads[0][1], grads[0][2]))
        near_grads, token = tile_grad_call(
            *known, [grads[0][:2]], pieces, tile_local.shape, rows, (3, 2), after=(grads[0][3], grads[0][4])
        )
        row_weights = scatter_weights(here, kept, sent, (token,))
        urgent, rest, even = back_call(
            *known, grads[0], turned, total, gathered, halves, (row_weights,)
        )
        urgent, rest = swap(urgent, 1), swap(rest, 1)
        arrived, first = reduce_square(here, even, urgent, rest, rows)
        grad_tiles, token = tile_grad_call(
            *known, grads, pieces, tile_local.shape, rows, (1, 0), near_grads, first
        )
        row_weights = sum_call(here, row_weights.shape[0], [(row_weights, 0)], after=(rest, *first))
        all_weights = level_weights(here, row_weights, (token,))
        joint = jnp.concatenate([all_weights] + [swap(all_weights, bits) for bits in (2, 4, 6)], axis=0)
        weights = unpack_call(here, joint, swap(joint, 1), width)
        grad_nodes = sum_call(here, rows, [(direct, 0), (even, 0), (rest, 0)], split=arrived)
    else:
        grads = [[lax.all_gather(gmsgs[0], "col", axis=0, tiled=True)]]
        weight_terms, direct = weight_call(factor, 1, *weight_args)
        weight_sums = lax.psum(weight_terms, ("row", "col"))
        weights = (
            weight_sums[: 2 * width],
            weight_sums[2 * width : 3 * width],
            weight_sums[3 * width : 3 * width + 3],
        )
        (terms,) = back_call(*known, grads[0], turned, total, gathered, (tuple(range(n_row)),))
        back = lax.psum_scatter(terms, "row", scatter_dimension=0, tiled=True)
        grad_nodes = sum_call(here, rows, [(direct, 0), (back, 0)])
        grad_tiles, _ = tile_grad_call(
            *known, grads, pieces, tile_local.shape, rows, tuple(range(n_col))
        )
    grad_tiles = grad_tiles.reshape(tiles.shape)
    return (updated, grad_nodes, grad_tiles, *weights)


def solution(mesh):
    placed = (
        P(("row", "col"), None),
        P("row", "col", None, None, None),
        P("row", "col", None),
        P("row", "col"),
        P(),
        P(),
        P(),
        P(),
        P(),
        P(("row", "col"), None),
    )
    return jax.shard_map(
        functools.partial(body, mesh.shape["row"], mesh.shape["col"]),
        mesh=mesh,
        in_specs=placed,
        out_specs=(
            P(("row", "col"), None),
            P(("row", "col"), None),
            P("row", "col", None, None, None),
            P(),
            P(),
            P(),
        ),
        check_vma=False,
    )
```

```python
import functools

import jax
import jax.numpy as jnp
from jax import lax
from jax.experimental import pallas as pl
from jax.experimental.pallas import tpu as pltpu
from jax.sharding import PartitionSpec as P

F32 = jnp.float32
BF16 = jnp.bfloat16
ANY = pl.BlockSpec(memory_space=pl.ANY)
HBM = pl.BlockSpec(memory_space=pltpu.HBM)
SMEM = pl.BlockSpec(memory_space=pltpu.SMEM)
VMEM = pl.BlockSpec(memory_space=pltpu.VMEM)
MIB = 1 << 20
TN = (((0,), (0,)), ((), ()))
NT = (((1,), (1,)), ((), ()))
SMALL = pl.CostEstimate(flops=1 << 20, bytes_accessed=1 << 16, transcendentals=0)


LIVE_STEP = 4
TILE_PARTS = 4
GRAD_PLAN = ((3, 0, None), (2, 1, None), (1, 2, "inner"), (1, 3, "outer"), (0, 4, "inner"), (0, 5, "outer"))
SWAP_ORDER = (0, 4, 2, 6, 1, 5, 3, 7)


def params(mib):
    return pltpu.CompilerParams(vmem_limit_bytes=mib * MIB)


def mm(a, b, dims=(((1,), (0,)), ((), ()))):
    return lax.dot_general(a, b, dims, preferred_element_type=F32)


def block_at(index, block):
    return pl.ds(pl.multiple_of(index * block, block), block)


class Place:
    def __init__(self, ref, paired=True, blocks=1):
        self.mine, self.level = lax.shift_right_logical(ref[0], 2), ref[0] & 3
        self.paired, self.blocks = paired, blocks

    def inner(self):
        return (self.level == 1) | (self.level == 2)

    def group(self, pick):
        if not self.paired:
            return pick
        low = self.level < 2
        choices = (jnp.where(low, 3, 0), jnp.where(low, 2, 1), self.level ^ 1, self.level)
        return choices[pick]

    def source(self, col):
        if not self.paired:
            return col
        shift = self.blocks.bit_length() - 1
        if 1 << shift == self.blocks:
            return col ^ lax.shift_left(self.mine, jnp.int32(shift))
        return (lax.div(col, self.blocks) ^ self.mine) * self.blocks + lax.rem(col, self.blocks)


def load_pieces(pieces, dst, sem, first):
    copies = []
    offset = 0
    for index, piece in enumerate(pieces):
        copy = pltpu.make_async_copy(
            piece, dst.at[pl.ds(offset, piece.shape[0])], sem.at[first + index]
        )
        copy.start()
        copies.append(copy)
        offset += piece.shape[0]
    return copies


def masked_tile(tile, live):
    return jnp.where(live, tile, jnp.zeros_like(tile))


def forward_kernel(outputs, n_pieces, paired, here, cols, *refs):
    pieces, tiles = refs[:n_pieces], refs[n_pieces]
    outs = refs[n_pieces + 1 : n_pieces + 1 + len(outputs)]
    nodes_v, tiles_v, sem, tile_sem = refs[n_pieces + 1 + len(outputs) :]
    rows = outs[0].shape[0] // len(outputs[0])
    slots, block = tiles.shape[1], tiles.shape[2]
    blocks = rows // block
    here = Place(here, paired, blocks)
    copies = load_pieces(pieces, nodes_v, sem, 0)
    places = [(pick, out, index) for out, picks in zip(outs, outputs) for index, pick in enumerate(picks)]
    tile_copies = []
    for place, (pick, _, _) in enumerate(places):
        copy = pltpu.make_async_copy(
            tiles.at[pl.ds(here.group(pick) * blocks, blocks)],
            tiles_v.at[pl.ds(place * blocks, blocks)],
            tile_sem.at[place],
        )
        copy.start()
        tile_copies.append(copy)
    for copy in copies:
        copy.wait()
    for place, (pick, out, index) in enumerate(places):
        tile_copies[place].wait()
        first = here.group(pick) * blocks

        def step(i, carry, first=first, out=out, index=index, place=place):
            row = first + i
            count = cols[slots, row]
            parts = []
            for pair in range(slots // 2):
                both = (2 * pair, 2 * pair + 1)
                tile = jnp.concatenate(
                    [masked_tile(tiles_v[place * blocks + i, slot], slot < count) for slot in both], axis=1
                )
                node = jnp.concatenate(
                    [nodes_v[block_at(here.source(cols[slot, row]), block)] for slot in both], axis=0
                )
                parts.append(mm(tile, node))
            value = parts[0]
            for part in parts[1:]:
                value = value + part
            out[block_at(index * blocks + i, block)] = value.astype(BF16)
            return carry

        lax.fori_loop(0, blocks, step, 0, unroll=4)


def forward_call(paired, here, cols, pieces, tiles, outputs, rows):
    width = pieces[0].shape[1]
    gathered = sum(piece.shape[0] for piece in pieces)
    slots, block = tiles.shape[1], tiles.shape[2]
    n_picks = sum(len(picks) for picks in outputs)
    return pl.pallas_call(
        functools.partial(forward_kernel, outputs, len(pieces), paired),
        out_shape=[jax.ShapeDtypeStruct((len(picks) * rows, width), BF16) for picks in outputs],
        in_specs=[SMEM] * 2 + [ANY] * len(pieces) + [HBM],
        out_specs=[VMEM] * len(outputs),
        scratch_shapes=[
            pltpu.VMEM((gathered, width), BF16),
            pltpu.VMEM((n_picks * (rows // block),) + tiles.shape[1:], BF16),
            pltpu.SemaphoreType.DMA((len(pieces),)),
            pltpu.SemaphoreType.DMA((n_picks,)),
        ],
        compiler_params=params(48),
        cost_estimate=SMALL,
        name="partial_messages",
    )(here, cols, *pieces, tiles)


def mlp_kernel(kinds, here, nodes, cot, *refs):
    n_parts = sum(len(chunk) for chunk in kinds)
    parts = refs[:n_parts]
    w_in, bias, w_out, gain, shift, updated, gpre_o, act_o, gproj_o, msg_o, vec = refs[
        n_parts : n_parts + 11
    ]
    gmsgs = refs[n_parts + 11 :]
    width = nodes.shape[1]
    inner = Place(here).inner()
    messages = []
    place = 0
    for chunk in kinds:
        total = None
        for kind in chunk:
            term = parts[place][...].astype(F32)
            place += 1
            if kind == "inner":
                term = jnp.where(inner, term, 0.0)
            total = term if total is None else total + term
        messages.append(total.astype(BF16))
    message = jnp.concatenate(messages, axis=1) if len(messages) > 1 else messages[0]
    node = nodes[...]
    pre = mm(node, w_in[:width]) + mm(message, w_in[width:]) + bias[...]
    sig = 0.5 + 0.5 * jnp.tanh(0.5 * pre)
    act = (pre * sig).astype(BF16)
    proj = mm(act, w_out[...])
    mean = jnp.mean(proj, axis=-1, keepdims=True)
    var = jnp.mean((proj - mean) ** 2, axis=-1, keepdims=True)
    rstd = 1.0 / jnp.sqrt(var + 1e-05)
    normed = (proj - mean) * rstd
    updated[...] = (node.astype(F32) + normed * gain[...] + shift[...]).astype(BF16)
    grad_out = cot[...].astype(F32)
    gscaled = grad_out * gain[...]
    gproj = (
        (
            gscaled
            - jnp.mean(gscaled, axis=-1, keepdims=True)
            - normed * jnp.mean(gscaled * normed, axis=-1, keepdims=True)
        )
        * rstd
    ).astype(BF16)
    gact = mm(gproj, w_out[...], NT)
    gpre = gact * sig * (1.0 + pre * (1.0 - sig))
    gpre_b = gpre.astype(BF16)
    gmsg = mm(gpre_b, w_in[width:], NT).astype(BF16)
    part = width // len(gmsgs)
    for index, out in enumerate(gmsgs):
        out[...] = gmsg[:, index * part : (index + 1) * part]
    gpre_o[...] = gpre_b
    act_o[...] = act
    gproj_o[...] = gproj
    msg_o[...] = message

    @pl.when(pl.program_id(0) == 0)
    def _():
        vec[...] = jnp.zeros_like(vec)

    vec[0:1] += jnp.sum(gpre, axis=0, keepdims=True)
    vec[1:2] += jnp.sum(grad_out * normed, axis=0, keepdims=True)
    vec[2:3] += jnp.sum(grad_out, axis=0, keepdims=True)


def mlp_call(here, nodes, cot, parts, kinds, w_in, bias, w_out, gain, shift):
    rows, width = nodes.shape
    step = min(rows, 512)

    def blocked(array):
        return pl.BlockSpec((step, array.shape[1]), lambda i: (i, 0))

    def whole(array):
        return pl.BlockSpec(array.shape, lambda i: (0, 0))

    flat = [term for chunk in parts for term in chunk]
    row_like = jax.ShapeDtypeStruct((rows, width), BF16)
    chunk_like = jax.ShapeDtypeStruct((rows, width // len(parts)), BF16)
    outs = [row_like] * 5 + [jax.ShapeDtypeStruct((8, width), F32)] + [chunk_like] * len(parts)
    weights = (w_in, bias, w_out, gain, shift)
    result = pl.pallas_call(
        functools.partial(mlp_kernel, kinds),
        grid=(rows // step,),
        out_shape=outs,
        in_specs=[SMEM] + [blocked(a) for a in (nodes, cot, *flat)] + [whole(a) for a in weights],
        out_specs=[blocked(a) for a in outs[:5]] + [whole(outs[5])] + [blocked(a) for a in outs[6:]],
        compiler_params=params(40),
        cost_estimate=SMALL,
        name="mlp",
    )(here, nodes, cot, *flat, *weights)
    return result[:6], result[6:]


def weight_kernel(factor, pieces, n_after, here, nodes, msg, act, gpre, gproj, cot, w_in, vec, *refs):
    *outs, direct, grads = refs[n_after:]
    width = nodes.shape[1]

    @pl.when(pl.program_id(0) == 0)
    def _():
        grads[...] = jnp.zeros_like(grads)
        grads[3 * width : 3 * width + 8] = vec[...] * factor

    gpre_b = gpre[...]
    grads[:width] += mm(nodes[...], gpre_b, TN) * factor
    grads[width : 2 * width] += mm(msg[...], gpre_b, TN) * factor
    grads[2 * width : 3 * width] += mm(act[...], gproj[...], TN) * factor
    direct[...] = cot[...].astype(F32) + mm(gpre_b, w_in[:width], NT)

    @pl.when(pl.program_id(0) == pl.num_programs(0) - 1)
    def _():
        if pieces == 1:
            outs[0][...] = grads[: outs[0].shape[0]]
        else:
            rows = grads.shape[0] // pieces
            for place, member in enumerate(SWAP_ORDER):
                where = pl.ds(pl.multiple_of((Place(here).mine ^ member) * rows, 8), rows)
                out, index = outs[2 * place // pieces], place % (pieces // 2)
                out[index * rows : (index + 1) * rows] = grads[where]


def weight_call(factor, pieces, here, nodes, msg, act, gpre, gproj, cot, w_in, vec, after=()):
    rows, width = nodes.shape
    step = min(rows, 256)
    blocked = pl.BlockSpec((step, width), lambda i: (i, 0))

    def whole(shape):
        return pl.BlockSpec(shape, lambda i: (0, 0))

    padded = (3 * width + width // 2, width)
    if pieces == 1:
        outs = [jax.ShapeDtypeStruct((3 * width + 8, width), F32)]
    else:
        outs = [jax.ShapeDtypeStruct((padded[0] // 2, width), F32)] * 2
    return pl.pallas_call(
        functools.partial(weight_kernel, factor, pieces, len(after)),
        grid=(rows // step,),
        out_shape=[*outs, jax.ShapeDtypeStruct((rows, width), F32)],
        in_specs=[SMEM] + [blocked] * 6 + [whole(w_in.shape), whole(vec.shape)] + [ANY] * len(after),
        out_specs=[whole(out.shape) for out in outs] + [blocked],
        scratch_shapes=[pltpu.VMEM(padded, F32)],
        compiler_params=params(40),
        cost_estimate=SMALL,
        name="weight_grads",
    )(here, nodes, msg, act, gpre, gproj, cot, w_in, vec, *after)


def unpack_kernel(here, even, odd, w_in, w_out, vectors, grads):
    width = w_in.shape[1]
    rows = grads.shape[0] // 8
    for member in range(8):
        part = (even, odd)[member % 2]
        first = member // 2 * rows
        where = pl.ds(pl.multiple_of((Place(here).mine ^ member) * rows, 8), rows)
        grads[where] = part[first : first + rows].astype(F32)
    w_in[...] = grads[: 2 * width]
    w_out[...] = grads[2 * width : 3 * width]
    vectors[...] = grads[3 * width : 3 * width + 3]


def unpack_call(here, even, odd, width):
    shapes = ((2 * width, width), (width, width), (3, width))
    return pl.pallas_call(
        unpack_kernel,
        out_shape=[jax.ShapeDtypeStruct(shape, F32) for shape in shapes],
        in_specs=[SMEM, VMEM, VMEM],
        out_specs=[VMEM] * 3,
        scratch_shapes=[pltpu.VMEM((3 * width + width // 2, width), F32)],
        compiler_params=params(16),
        cost_estimate=SMALL,
        name="weight_unpack",
    )(here, even, odd)


def grad_jobs(rows, refs, dst, sem, here, groups=None):
    if len(refs) == 1:
        return [(None, pltpu.make_async_copy(refs[0], dst, sem.at[0]))]
    inner = here.inner()
    conditions = {None: None, "inner": inner, "outer": jnp.logical_not(inner)}
    jobs = []
    for group, index, kind in GRAD_PLAN:
        if groups is None:
            where = block_at(here.group(group), rows)
        elif group in groups:
            where = pl.ds(groups.index(group) * rows, rows)
        else:
            continue
        copy = pltpu.make_async_copy(refs[index], dst.at[where], sem.at[index])
        jobs.append((conditions[kind], copy))
    return jobs


def run_jobs(jobs, verb):
    for condition, copy in jobs:
        if condition is None:
            getattr(copy, verb)()
        else:
            pl.when(condition)(getattr(copy, verb))


def for_live(first, last, entry):
    def several(i, carry):
        for index in range(LIVE_STEP):
            entry(first + i * LIVE_STEP + index)
        return carry

    def one(i, carry):
        entry(i)
        return carry

    full = jnp.maximum(last - first, 0) // LIVE_STEP
    lax.fori_loop(0, full, several, 0)
    lax.fori_loop(first + full * LIVE_STEP, last, one, 0)


def turn_kernel(slots, cols, tiles, out, tiles_v, live, sem):
    copy = pltpu.make_async_copy(tiles, tiles_v, sem.at[0])
    copy.start()

    def collect(row, found):
        count = cols[slots, row]
        for slot in range(slots):
            live[found] = row * slots + slot
            found = found + (slot < count).astype(jnp.int32)
        return found

    found = lax.fori_loop(0, tiles.shape[0] // slots, collect, jnp.int32(0))
    copy.wait()

    def entry(place):
        out[place] = tiles_v[live[place]].T

    for_live(0, found, entry)


def turn_call(cols, tiles):
    row_blocks, slots, block = tiles.shape[:3]
    shape = (row_blocks * slots, block, block)
    return pl.pallas_call(
        functools.partial(turn_kernel, slots),
        out_shape=jax.ShapeDtypeStruct(shape, BF16),
        in_specs=[SMEM, HBM],
        out_specs=VMEM,
        scratch_shapes=[
            pltpu.VMEM(shape, BF16),
            pltpu.SMEM((row_blocks * slots + 8,), jnp.int32),
            pltpu.SemaphoreType.DMA((1,)),
        ],
        compiler_params=params(16 if row_blocks <= 32 else 32),
        cost_estimate=SMALL,
        name="turned_tiles",
    )(cols, tiles.reshape(shape))


def back_kernel(rows, slots, n_grads, n_after, out_pieces, paired, here, cols, *refs):
    grads, tiles = refs[:n_grads], refs[n_grads]
    refs = refs[n_grads + 1 + n_after :]
    outs = refs[: len(out_pieces)]
    grad_v, tiles_v, acc, stage, live, source, sem, tile_sem, out_sem = refs[len(out_pieces) :]
    n_tiles, block = tiles.shape[:2]
    here = Place(here, paired, rows // block)
    jobs = grad_jobs(rows, grads, grad_v, sem, here)
    run_jobs(jobs, "start")
    part = n_tiles // TILE_PARTS
    tile_copies = [
        pltpu.make_async_copy(
            tiles.at[pl.ds(index * part, part)], tiles_v.at[pl.ds(index * part, part)], tile_sem.at[index]
        )
        for index in range(TILE_PARTS)
    ]
    tile_copies[0].start()

    def collect(row, found):
        count = cols[slots, row]
        for slot in range(slots):
            live[found] = row
            source[found] = here.source(cols[slot, row])
            found = found + (slot < count).astype(jnp.int32)
        return found

    found = lax.fori_loop(0, n_tiles // slots, collect, jnp.int32(0))
    for index in range(1, TILE_PARTS):
        pl.when(index * part < found)(tile_copies[index].start)
    acc[...] = jnp.zeros_like(acc)
    run_jobs(jobs, "wait")

    def entry(place):
        term = mm(tiles_v[place], grad_v[block_at(live[place], block)])
        acc[block_at(source[place], block)] += term

    tile_copies[0].wait()
    for index in range(TILE_PARTS):
        if index:
            pl.when(index * part < found)(tile_copies[index].wait)
        for_live(index * part, jnp.minimum(found, (index + 1) * part), entry)
    piece = acc.shape[0] // sum(len(members) for members in out_pieces)
    copies = []
    for out, members in zip(outs, out_pieces):
        for index, member in enumerate(members):
            where = pl.ds(member * piece, piece)
            stage[where] = acc[where].astype(BF16)
            copy = pltpu.make_async_copy(
                stage.at[where], out.at[pl.ds(index * piece, piece)], out_sem.at[len(copies)]
            )
            copy.start()
            copies.append(copy)
    for copy in copies:
        copy.wait()


def back_call(paired, here, cols, grads, tiles, total, gathered, out_pieces, after=()):
    rows, width = grads[0].shape
    rows = total if len(grads) == 1 else rows
    n_tiles, block = tiles.shape[:2]
    slots = cols.shape[0] - 1
    piece = gathered // sum(len(members) for members in out_pieces)
    return pl.pallas_call(
        functools.partial(back_kernel, rows, slots, len(grads), len(after), out_pieces, paired),
        out_shape=[jax.ShapeDtypeStruct((len(m) * piece, width), BF16) for m in out_pieces],
        in_specs=[SMEM] * 2 + [ANY] * len(grads) + [HBM] + [ANY] * len(after),
        out_specs=[ANY] * len(out_pieces),
        scratch_shapes=[
            pltpu.VMEM((total, width), BF16),
            pltpu.VMEM((n_tiles, block, block), BF16),
            pltpu.VMEM((gathered, width), F32),
            pltpu.VMEM((gathered, width), BF16),
            pltpu.SMEM((n_tiles + 8,), jnp.int32),
            pltpu.SMEM((n_tiles + 8,), jnp.int32),
            pltpu.SemaphoreType.DMA((len(grads),)),
            pltpu.SemaphoreType.DMA((TILE_PARTS,)),
            pltpu.SemaphoreType.DMA((sum(len(members) for members in out_pieces),)),
        ],
        compiler_params=params(28 if gathered <= 8192 else 56),
        cost_estimate=SMALL,
        name="back_terms",
    )(here, cols, *grads, tiles, *after)


def tile_grad_kernel(
    rows, slots, n_grads, n_pieces, n_chunks, n_after, groups, paired, here, cols, *refs
):
    grads = refs[: n_grads * n_chunks]
    refs = refs[n_grads * n_chunks :]
    pieces = refs[: n_pieces * n_chunks]
    out, token, grad_v, nodes_v, tiles_v, live, source, sem, piece_sem, out_sem = refs[n_pieces * n_chunks + n_after :]
    token[...] = jnp.zeros_like(token)
    block = out.shape[1]
    width = nodes_v.shape[1]
    part = width // n_chunks
    scale = float(width) ** -0.5
    blocks = grad_v.shape[0] // (block * len(groups))
    here = Place(here, paired, blocks)
    jobs, copies = [], []
    for chunk in range(n_chunks):
        columns = pl.ds(chunk * part, part)
        jobs += grad_jobs(
            rows,
            grads[chunk * n_grads : (chunk + 1) * n_grads],
            grad_v.at[:, columns],
            sem.at[chunk],
            here,
            groups,
        )
        copies += load_pieces(
            pieces[chunk * n_pieces : (chunk + 1) * n_pieces],
            nodes_v.at[:, columns],
            piece_sem.at[chunk],
            0,
        )
    run_jobs(jobs, "start")
    tiles_v[...] = jnp.zeros_like(tiles_v)
    found = jnp.int32(0)
    for index, group in enumerate(groups):
        first = here.group(group) * blocks

        def collect(i, found, first=first, index=index):
            row = first + i
            count = cols[slots, row]
            for slot in range(slots):
                live[found] = (index * blocks + i) * slots + slot
                source[found] = here.source(cols[slot, row])
                found = found + (slot < count).astype(jnp.int32)
            return found

        found = lax.fori_loop(0, blocks, collect, found)
    run_jobs(jobs, "wait")
    for copy in copies:
        copy.wait()

    def entry(place):
        tile_index = live[place]
        grad = grad_v[block_at(tile_index // slots, block)]
        node = nodes_v[block_at(source[place], block)]
        tiles_v[tile_index] = (mm(grad, node, NT) * scale).astype(BF16)

    for_live(0, found, entry)
    size = blocks * slots
    copies = []
    for index, group in enumerate(groups):
        copy = pltpu.make_async_copy(
            tiles_v.at[pl.ds(index * size, size)],
            out.at[pl.ds(here.group(group) * size, size)],
            out_sem.at[index],
        )
        copy.start()
        copies.append(copy)
    for copy in copies:
        copy.wait()


def tile_grad_call(paired, here, cols, grads, pieces, shape, rows, groups, base=None, after=()):
    row_blocks, slots, block = shape[:3]
    chunks = len(grads)
    width = grads[0][0].shape[1] * chunks
    gathered = sum(piece.shape[0] for piece in pieces[0])
    flat = [a for chunk in grads for a in chunk] + [a for chunk in pieces for a in chunk]
    after = after if base is None else (base,) + tuple(after)
    entries = len(groups) * rows // block * slots
    return pl.pallas_call(
        functools.partial(
            tile_grad_kernel, rows, slots, len(grads[0]), len(pieces[0]), chunks, len(after), groups, paired
        ),
        out_shape=[
            jax.ShapeDtypeStruct((row_blocks * slots, block, block), BF16),
            jax.ShapeDtypeStruct((8, 128), F32),
        ],
        in_specs=[SMEM] * 2 + [ANY] * (len(flat) + len(after)),
        out_specs=[ANY, VMEM],
        input_output_aliases={} if base is None else {2 + len(flat): 0},
        scratch_shapes=[
            pltpu.VMEM((len(groups) * rows, width), BF16),
            pltpu.VMEM((gathered, width), BF16),
            pltpu.VMEM((entries, block, block), BF16),
            pltpu.SMEM((entries + 8,), jnp.int32),
            pltpu.SMEM((entries + 8,), jnp.int32),
            pltpu.SemaphoreType.DMA((chunks, len(grads[0]))),
            pltpu.SemaphoreType.DMA((chunks, len(pieces[0]))),
            pltpu.SemaphoreType.DMA((len(groups),)),
        ],
        compiler_params=params(16 if gathered <= 8192 else 40),
        cost_estimate=SMALL,
        name="tile_grads",
    )(here, cols, *flat, *after)


def swap(value, bit):
    return lax.ppermute(value, "row", [(i, i ^ bit) for i in range(8)])


def outer_swap(value):
    return lax.ppermute(value, "col", [(0, 1), (1, 0), (2, 3), (3, 2)])


def turn(value, by):
    return lax.ppermute(value, "col", [(i, (i + by) % 4) for i in range(4)])


def inner_swap(value):
    pairs = []
    for row in range(8):
        for col in range(4):
            partner = (row, 3 - col) if col in (1, 2) else (row ^ 1, col)
            pairs.append((row * 4 + col, partner[0] * 4 + partner[1]))
    return lax.ppermute(value, ("row", "col"), pairs)


def gather_square(nodes):
    half = nodes.shape[0] // 2
    lower, upper = nodes[:half], nodes[half:]
    y_lower, x_upper = swap(lower, 4), swap(upper, 2)
    x_lower, y_upper = swap(lower, 2), swap(upper, 4)
    d_lower, d_upper = swap(y_lower, 2), swap(x_upper, 4)
    pieces = [lower, upper, swap(nodes, 1)]
    for pair in ((x_lower, x_upper), (y_lower, y_upper), (d_lower, d_upper)):
        pieces += [*pair, *(swap(piece, 1) for piece in pair)]
    return pieces


def reduce_square(here, even, urgent, rest, rows):
    half = rows // 2
    first = [
        sum_call(here, rows, [(even, (6, 2)), (urgent, (0, 2))]),
        sum_call(here, rows, [(even, (7, 5)), (urgent, (1, 3))]),
    ]
    x_first, y_first = swap(first[0], 2), swap(first[1], 4)
    y_lower = swap(sum_call(here, half, [(even, 4), (rest, 3), (x_first, 0)]), 4)
    x_upper = swap(sum_call(here, half, [(even, 3), (rest, 2), (y_first, 0)]), 2)
    return [((x_first, 1), (x_upper, 0)), ((y_lower, 0), (y_first, 1))], first


def sum_kernel(n_terms, n_gated, n_split, *refs):
    inner, refs = Place(refs[0]).inner(), refs[1:]
    total = None
    for index, ref in enumerate(refs[: n_terms + n_gated]):
        term = ref[...].astype(F32)
        if index >= n_terms:
            term = jnp.where(inner, term, 0.0)
        total = term if total is None else total + term
    for index in range(n_split):
        first, second = refs[n_terms + n_gated + 2 * index :][:2]
        early = pl.program_id(0) < pl.num_programs(0) // 2
        total = total + jnp.where(early, first[...], second[...]).astype(F32)
    refs[-1][...] = total.astype(refs[-1].dtype)


def sum_call(here, rows, terms, gated=(), split=(), dtype=BF16, after=()):
    both = [*terms, *gated]
    width = both[0][0].shape[1]
    step = min(rows, 512)
    steps = rows // step
    half = steps // 2

    def spec(piece):
        if isinstance(piece, int):
            return pl.BlockSpec((step, width), lambda i: (piece * steps + i, 0))
        lower, upper = piece
        return pl.BlockSpec(
            (step, width), lambda i: (jnp.where(i < half, lower * half + i, (upper - 1) * half + i), 0)
        )

    def early(piece):
        return pl.BlockSpec((step, width), lambda i: (piece * half + jnp.minimum(i, half - 1), 0))

    def late(piece):
        return pl.BlockSpec((step, width), lambda i: (piece * half + jnp.maximum(i - half, 0), 0))

    return pl.pallas_call(
        functools.partial(sum_kernel, len(terms), len(gated), len(split)),
        grid=(steps,),
        out_shape=jax.ShapeDtypeStruct((rows, width), dtype),
        in_specs=[SMEM]
        + [spec(piece) for _, piece in both]
        + [spec_of(piece) for pair in split for spec_of, (_, piece) in zip((early, late), pair)]
        + [ANY] * len(after),
        out_specs=pl.BlockSpec((step, width), lambda i: (i, 0)),
        compiler_params=params(16),
        cost_estimate=SMALL,
        name="sum_terms",
    )(here, *(array for array, _ in both), *(array for pair in split for array, _ in pair), *after)


def scatter_weights(here, kept, sent, after):
    rows = kept.shape[0] // 4
    received = swap(sent, 1)
    pieces = [
        sum_call(here, rows, [(kept, place), (received, place)], dtype=F32) for place in range(4)
    ]
    terms = [pieces[0]] + [swap(piece, bits) for piece, bits in zip(pieces[1:], SWAP_ORDER[1:4])]
    return sum_call(here, rows, [(term, 0) for term in terms], after=after)


def level_weights(here, value, after):
    terms = [value] + [turn(value, by) for by in (1, 2, 3)]
    return sum_call(here, value.shape[0], [(term, 0) for term in terms], after=after)


def reduce_line(here, far, near, pair, own, after):
    rows = own.shape[0]
    far_sum = inner_swap(sum_call(here, rows, [(far, 0), (outer_swap(far), 0)], after=after))
    near_sum = inner_swap(sum_call(here, rows, [(near, 0), (outer_swap(near), 0)]))
    pair_in = outer_swap(sum_call(here, rows, [(pair, 0)], [(far_sum, 0)]))
    return own, pair_in, near_sum


def gather_line(own):
    pair = outer_swap(own)
    near_inner = inner_swap(own)
    far_inner = inner_swap(pair)
    near_outer = outer_swap(near_inner)
    far_outer = outer_swap(far_inner)
    return [own, pair, near_inner, near_outer, far_inner, far_outer]


def body(n_row, n_col, nodes, tiles, tile_col, tile_count, w_in, bias_in, w_out, ln_gain, ln_shift, cotangent):
    rows, width = nodes.shape
    row_blocks, _, slots, block = tiles.shape[:4]
    tile_local = tiles.reshape(row_blocks, slots, block, block)
    table = jnp.concatenate([tile_col.reshape(row_blocks, slots).T, tile_count.reshape(1, row_blocks)], axis=0)
    gathered, total = n_row * rows, n_col * rows
    paired = n_row == 8 and n_col == 4
    here = lax.axis_index(("row", "col")).astype(jnp.int32).reshape(1)
    known = (paired, here, table)
    turned = turn_call(table, tile_local)
    if paired:
        pieces = [gather_square(nodes)]
        (far,) = forward_call(*known, pieces[0], tile_local, ((0,),), rows)
        (near,) = forward_call(*known, pieces[0], tile_local, ((1,),), rows)
        pair, own = forward_call(*known, pieces[0], tile_local, ((2,), (3,)), rows)
        parts = [reduce_line(here, far, near, pair, own, (turned,))]
        kinds = [("all", "all", "inner")]
    else:
        pieces = [[lax.all_gather(nodes, "row", axis=0, tiled=True)]]
        (partial,) = forward_call(*known, pieces[0], tile_local, (tuple(range(n_col)),), rows)
        parts = [[lax.psum_scatter(partial, "col", scatter_dimension=0, tiled=True)]]
        kinds = [("all",)]
    vectors = [v.reshape(1, width) for v in (bias_in, ln_gain, ln_shift)]
    (updated, gpre_b, act, gproj, message, vec), gmsgs = mlp_call(
        here, nodes, cotangent, parts, kinds, w_in, vectors[0], w_out, vectors[1], vectors[2]
    )
    factor = float(rows * n_row * n_col) ** -0.5
    weight_args = (here, nodes, message, act, gpre_b, gproj, cotangent, w_in, vec)
    if paired:
        halves = ((14, 15, 6, 11), (2, 3, 7, 10), (0, 1, 4, 5, 8, 9, 12, 13))
        grads = [gather_line(gmsgs[0])]
        kept, sent, direct = weight_call(factor, n_row, *weight_args, (grads[0][1], grads[0][2]))
        near_grads, token = tile_grad_call(
            *known, [grads[0][:2]], pieces, tile_local.shape, rows, (3, 2), after=(grads[0][3], grads[0][4])
        )
        row_weights = scatter_weights(here, kept, sent, (token,))
        urgent, rest, even = back_call(
            *known, grads[0], turned, total, gathered, halves, (row_weights,)
        )
        urgent, rest = swap(urgent, 1), swap(rest, 1)
        arrived, first = reduce_square(here, even, urgent, rest, rows)
        grad_tiles, token = tile_grad_call(
            *known, grads, pieces, tile_local.shape, rows, (1, 0), near_grads, first
        )
        row_weights = sum_call(here, row_weights.shape[0], [(row_weights, 0)], after=(rest, *first))
        all_weights = level_weights(here, row_weights, (token,))
        joint = jnp.concatenate([all_weights] + [swap(all_weights, bits) for bits in (2, 4, 6)], axis=0)
        weights = unpack_call(here, joint, swap(joint, 1), width)
        grad_nodes = sum_call(here, rows, [(direct, 0), (even, 0), (rest, 0)], split=arrived)
    else:
        grads = [[lax.all_gather(gmsgs[0], "col", axis=0, tiled=True)]]
        weight_terms, direct = weight_call(factor, 1, *weight_args)
        weight_sums = lax.psum(weight_terms, ("row", "col"))
        weights = (
            weight_sums[: 2 * width],
            weight_sums[2 * width : 3 * width],
            weight_sums[3 * width : 3 * width + 3],
        )
        (terms,) = back_call(*known, grads[0], turned, total, gathered, (tuple(range(n_row)),))
        back = lax.psum_scatter(terms, "row", scatter_dimension=0, tiled=True)
        grad_nodes = sum_call(here, rows, [(direct, 0), (back, 0)])
        grad_tiles, _ = tile_grad_call(
            *known, grads, pieces, tile_local.shape, rows, tuple(range(n_col))
        )
    grad_tiles = grad_tiles.reshape(tiles.shape)
    return (updated, grad_nodes, grad_tiles, *weights)


def solution(mesh):
    placed = (
        P(("row", "col"), None),
        P("row", "col", None, None, None),
        P("row", "col", None),
        P("row", "col"),
        P(),
        P(),
        P(),
        P(),
        P(),
        P(("row", "col"), None),
    )
    return jax.shard_map(
        functools.partial(body, mesh.shape["row"], mesh.shape["col"]),
        mesh=mesh,
        in_specs=placed,
        out_specs=(
            P(("row", "col"), None),
            P(("row", "col"), None),
            P("row", "col", None, None, None),
            P(),
            P(),
            P(),
        ),
        check_vma=False,
    )
```

```python
import functools

import jax
import jax.numpy as jnp
from jax import lax
from jax.experimental import pallas as pl
from jax.experimental.pallas import tpu as pltpu
from jax.sharding import PartitionSpec as P

F32 = jnp.float32
BF16 = jnp.bfloat16
ANY = pl.BlockSpec(memory_space=pl.ANY)
HBM = pl.BlockSpec(memory_space=pltpu.HBM)
SMEM = pl.BlockSpec(memory_space=pltpu.SMEM)
VMEM = pl.BlockSpec(memory_space=pltpu.VMEM)
MIB = 1 << 20
TN = (((0,), (0,)), ((), ()))
NT = (((1,), (1,)), ((), ()))
SMALL = pl.CostEstimate(flops=1 << 20, bytes_accessed=1 << 16, transcendentals=0)


LIVE_STEP = 4
GRAD_PLAN = ((3, 0, None), (2, 1, None), (1, 2, "inner"), (1, 3, "outer"), (0, 4, "inner"), (0, 5, "outer"))
SWAP_ORDER = (0, 4, 2, 6, 1, 5, 3, 7)


def params(mib):
    return pltpu.CompilerParams(vmem_limit_bytes=mib * MIB)


def mm(a, b, dims=(((1,), (0,)), ((), ()))):
    return lax.dot_general(a, b, dims, preferred_element_type=F32)


def block_at(index, block):
    return pl.ds(pl.multiple_of(index * block, block), block)


class Place:
    def __init__(self, ref, paired=True, blocks=1):
        self.mine, self.level = lax.shift_right_logical(ref[0], 2), ref[0] & 3
        self.paired, self.blocks = paired, blocks

    def inner(self):
        return (self.level == 1) | (self.level == 2)

    def group(self, pick):
        if not self.paired:
            return pick
        low = self.level < 2
        choices = (jnp.where(low, 3, 0), jnp.where(low, 2, 1), self.level ^ 1, self.level)
        return choices[pick]

    def source(self, col):
        if not self.paired:
            return col
        shift = self.blocks.bit_length() - 1
        if 1 << shift == self.blocks:
            return col ^ lax.shift_left(self.mine, jnp.int32(shift))
        return (lax.div(col, self.blocks) ^ self.mine) * self.blocks + lax.rem(col, self.blocks)


def load_pieces(pieces, dst, sem, first):
    copies = []
    offset = 0
    for index, piece in enumerate(pieces):
        copy = pltpu.make_async_copy(
            piece, dst.at[pl.ds(offset, piece.shape[0])], sem.at[first + index]
        )
        copy.start()
        copies.append(copy)
        offset += piece.shape[0]
    return copies


def masked_tile(tile, live):
    return jnp.where(live, tile, jnp.zeros_like(tile))


def forward_kernel(outputs, n_pieces, paired, here, cols, *refs):
    pieces, tiles = refs[:n_pieces], refs[n_pieces]
    outs = refs[n_pieces + 1 : n_pieces + 1 + len(outputs)]
    nodes_v, tiles_v, sem, tile_sem = refs[n_pieces + 1 + len(outputs) :]
    rows = outs[0].shape[0] // len(outputs[0])
    slots, block = tiles.shape[1], tiles.shape[2]
    blocks = rows // block
    here = Place(here, paired, blocks)
    copies = load_pieces(pieces, nodes_v, sem, 0)
    places = [(pick, out, index) for out, picks in zip(outs, outputs) for index, pick in enumerate(picks)]
    tile_copies = []
    for place, (pick, _, _) in enumerate(places):
        copy = pltpu.make_async_copy(
            tiles.at[pl.ds(here.group(pick) * blocks, blocks)],
            tiles_v.at[pl.ds(place * blocks, blocks)],
            tile_sem.at[place],
        )
        copy.start()
        tile_copies.append(copy)
    for copy in copies:
        copy.wait()
    for place, (pick, out, index) in enumerate(places):
        tile_copies[place].wait()
        first = here.group(pick) * blocks

        def step(i, carry, first=first, out=out, index=index, place=place):
            row = first + i
            count = cols[slots, row]
            parts = []
            for pair in range(slots // 2):
                both = (2 * pair, 2 * pair + 1)
                tile = jnp.concatenate(
                    [masked_tile(tiles_v[place * blocks + i, slot], slot < count) for slot in both], axis=1
                )
                node = jnp.concatenate(
                    [nodes_v[block_at(here.source(cols[slot, row]), block)] for slot in both], axis=0
                )
                parts.append(mm(tile, node))
            value = parts[0]
            for part in parts[1:]:
                value = value + part
            out[block_at(index * blocks + i, block)] = value.astype(BF16)
            return carry

        lax.fori_loop(0, blocks, step, 0, unroll=4)


def forward_call(paired, here, cols, pieces, tiles, outputs, rows):
    width = pieces[0].shape[1]
    gathered = sum(piece.shape[0] for piece in pieces)
    slots, block = tiles.shape[1], tiles.shape[2]
    n_picks = sum(len(picks) for picks in outputs)
    return pl.pallas_call(
        functools.partial(forward_kernel, outputs, len(pieces), paired),
        out_shape=[jax.ShapeDtypeStruct((len(picks) * rows, width), BF16) for picks in outputs],
        in_specs=[SMEM] * 2 + [ANY] * len(pieces) + [HBM],
        out_specs=[VMEM] * len(outputs),
        scratch_shapes=[
            pltpu.VMEM((gathered, width), BF16),
            pltpu.VMEM((n_picks * (rows // block),) + tiles.shape[1:], BF16),
            pltpu.SemaphoreType.DMA((len(pieces),)),
            pltpu.SemaphoreType.DMA((n_picks,)),
        ],
        compiler_params=params(48),
        cost_estimate=SMALL,
        name="partial_messages",
    )(here, cols, *pieces, tiles)


def mlp_kernel(kinds, step, here, nodes, cot, *refs):
    n_parts = sum(len(chunk) for chunk in kinds)
    parts = refs[:n_parts]
    w_in, bias, w_out, gain, shift, updated, gpre_o, act_o, gproj_o, msg_o, vec = refs[
        n_parts : n_parts + 11
    ]
    gmsgs = refs[n_parts + 11 :]
    rows, width = nodes.shape
    inner = Place(here).inner()
    vec[...] = jnp.zeros_like(vec)
    for first in range(0, rows, step):
        where = slice(first, first + step)
        messages = []
        place = 0
        for chunk in kinds:
            total = None
            for kind in chunk:
                term = parts[place][where].astype(F32)
                place += 1
                if kind == "inner":
                    term = jnp.where(inner, term, 0.0)
                total = term if total is None else total + term
            messages.append(total.astype(BF16))
        message = jnp.concatenate(messages, axis=1) if len(messages) > 1 else messages[0]
        node = nodes[where]
        pre = mm(node, w_in[:width]) + mm(message, w_in[width:]) + bias[...]
        sig = 0.5 + 0.5 * jnp.tanh(0.5 * pre)
        act = (pre * sig).astype(BF16)
        proj = mm(act, w_out[...])
        mean = jnp.mean(proj, axis=-1, keepdims=True)
        var = jnp.mean((proj - mean) ** 2, axis=-1, keepdims=True)
        rstd = 1.0 / jnp.sqrt(var + 1e-05)
        normed = (proj - mean) * rstd
        updated[where] = (node.astype(F32) + normed * gain[...] + shift[...]).astype(BF16)
        grad_out = cot[where].astype(F32)
        gscaled = grad_out * gain[...]
        gproj = (
            (
                gscaled
                - jnp.mean(gscaled, axis=-1, keepdims=True)
                - normed * jnp.mean(gscaled * normed, axis=-1, keepdims=True)
            )
            * rstd
        ).astype(BF16)
        gact = mm(gproj, w_out[...], NT)
        gpre = gact * sig * (1.0 + pre * (1.0 - sig))
        gpre_b = gpre.astype(BF16)
        gmsg = mm(gpre_b, w_in[width:], NT).astype(BF16)
        part = width // len(gmsgs)
        for index, out in enumerate(gmsgs):
            out[where] = gmsg[:, index * part : (index + 1) * part]
        gpre_o[where] = gpre_b
        act_o[where] = act
        gproj_o[where] = gproj
        msg_o[where] = message
        vec[0:1] += jnp.sum(gpre, axis=0, keepdims=True)
        vec[1:2] += jnp.sum(grad_out * normed, axis=0, keepdims=True)
        vec[2:3] += jnp.sum(grad_out, axis=0, keepdims=True)


def mlp_call(here, nodes, cot, parts, kinds, w_in, bias, w_out, gain, shift):
    rows, width = nodes.shape
    step = min(rows, 512)

    flat = [term for chunk in parts for term in chunk]
    row_like = jax.ShapeDtypeStruct((rows, width), BF16)
    chunk_like = jax.ShapeDtypeStruct((rows, width // len(parts)), BF16)
    outs = [row_like] * 5 + [jax.ShapeDtypeStruct((8, width), F32)] + [chunk_like] * len(parts)
    weights = (w_in, bias, w_out, gain, shift)
    result = pl.pallas_call(
        functools.partial(mlp_kernel, kinds, step),
        out_shape=outs,
        in_specs=[SMEM] + [VMEM] * (2 + len(flat) + len(weights)),
        out_specs=[VMEM] * len(outs),
        compiler_params=params(40),
        cost_estimate=SMALL,
        name="mlp",
    )(here, nodes, cot, *flat, *weights)
    return result[:6], result[6:]


def weight_kernel(factor, pieces, step, n_after, here, nodes, msg, act, gpre, gproj, cot, w_in, vec, *refs):
    *outs, direct, grads = refs[n_after:]
    rows, width = nodes.shape
    for first in range(0, rows, step):
        where = slice(first, first + step)
        gpre_b = gpre[where]
        terms = (mm(nodes[where], gpre_b, TN), mm(msg[where], gpre_b, TN), mm(act[where], gproj[where], TN))
        for index, term in enumerate(terms):
            own = slice(index * width, (index + 1) * width)
            grads[own] = term if first == 0 else grads[own] + term
        direct[where] = cot[where].astype(F32) + mm(gpre_b, w_in[:width], NT)
    grads[3 * width : 3 * width + 8] = vec[...]
    grads[3 * width + 8 :] = jnp.zeros((grads.shape[0] - 3 * width - 8, width), F32)
    if pieces == 1:
        outs[0][...] = grads[: outs[0].shape[0]] * factor
    else:
        rows = grads.shape[0] // pieces
        for place, member in enumerate(SWAP_ORDER):
            where = pl.ds(pl.multiple_of((Place(here).mine ^ member) * rows, 8), rows)
            out, index = outs[2 * place // pieces], place % (pieces // 2)
            out[index * rows : (index + 1) * rows] = grads[where] * factor


def weight_call(factor, pieces, here, nodes, msg, act, gpre, gproj, cot, w_in, vec, after=()):
    rows, width = nodes.shape
    step = min(rows, 256)
    padded = (3 * width + width // 2, width)
    if pieces == 1:
        outs = [jax.ShapeDtypeStruct((3 * width + 8, width), F32)]
    else:
        outs = [jax.ShapeDtypeStruct((padded[0] // 2, width), F32)] * 2
    return pl.pallas_call(
        functools.partial(weight_kernel, factor, pieces, step, len(after)),
        out_shape=[*outs, jax.ShapeDtypeStruct((rows, width), F32)],
        in_specs=[SMEM] + [VMEM] * 8 + [ANY] * len(after),
        out_specs=[VMEM] * (len(outs) + 1),
        scratch_shapes=[pltpu.VMEM(padded, F32)],
        compiler_params=params(40),
        cost_estimate=SMALL,
        name="weight_grads",
    )(here, nodes, msg, act, gpre, gproj, cot, w_in, vec, *after)


def unpack_kernel(here, even, odd, w_in, w_out, vectors, grads):
    width = w_in.shape[1]
    rows = grads.shape[0] // 8
    for member in range(8):
        part = (even, odd)[member % 2]
        first = member // 2 * rows
        where = pl.ds(pl.multiple_of((Place(here).mine ^ member) * rows, 8), rows)
        grads[where] = part[first : first + rows].astype(F32)
    w_in[...] = grads[: 2 * width]
    w_out[...] = grads[2 * width : 3 * width]
    vectors[...] = grads[3 * width : 3 * width + 3]


def unpack_call(here, even, odd, width):
    shapes = ((2 * width, width), (width, width), (3, width))
    return pl.pallas_call(
        unpack_kernel,
        out_shape=[jax.ShapeDtypeStruct(shape, F32) for shape in shapes],
        in_specs=[SMEM, VMEM, VMEM],
        out_specs=[VMEM] * 3,
        scratch_shapes=[pltpu.VMEM((3 * width + width // 2, width), F32)],
        compiler_params=params(16),
        cost_estimate=SMALL,
        name="weight_unpack",
    )(here, even, odd)


def grad_jobs(rows, refs, dst, sem, here, groups=None):
    if len(refs) == 1:
        return [(None, pltpu.make_async_copy(refs[0], dst, sem.at[0]))]
    inner = here.inner()
    conditions = {None: None, "inner": inner, "outer": jnp.logical_not(inner)}
    jobs = []
    for group, index, kind in GRAD_PLAN:
        if groups is None:
            where = block_at(here.group(group), rows)
        elif group in groups:
            where = pl.ds(groups.index(group) * rows, rows)
        else:
            continue
        copy = pltpu.make_async_copy(refs[index], dst.at[where], sem.at[index])
        jobs.append((conditions[kind], copy))
    return jobs


def run_jobs(jobs, verb):
    for condition, copy in jobs:
        if condition is None:
            getattr(copy, verb)()
        else:
            pl.when(condition)(getattr(copy, verb))


def for_live(first, last, entry):
    def several(i, carry):
        for index in range(LIVE_STEP):
            entry(first + i * LIVE_STEP + index)
        return carry

    def one(i, carry):
        entry(i)
        return carry

    full = jnp.maximum(last - first, 0) // LIVE_STEP
    lax.fori_loop(0, full, several, 0)
    lax.fori_loop(first + full * LIVE_STEP, last, one, 0)


def turn_kernel(slots, cols, tiles, out, tiles_v, live, sem):
    copy = pltpu.make_async_copy(tiles, tiles_v, sem.at[0])
    copy.start()

    def collect(row, found):
        count = cols[slots, row]
        for slot in range(slots):
            live[found] = row * slots + slot
            found = found + (slot < count).astype(jnp.int32)
        return found

    found = lax.fori_loop(0, tiles.shape[0] // slots, collect, jnp.int32(0))
    copy.wait()

    def entry(place):
        out[place] = tiles_v[live[place]].T

    for_live(0, found, entry)


def turn_call(cols, tiles):
    row_blocks, slots, block = tiles.shape[:3]
    shape = (row_blocks * slots, block, block)
    return pl.pallas_call(
        functools.partial(turn_kernel, slots),
        out_shape=jax.ShapeDtypeStruct(shape, BF16),
        in_specs=[SMEM, HBM],
        out_specs=VMEM,
        scratch_shapes=[
            pltpu.VMEM(shape, BF16),
            pltpu.SMEM((row_blocks * slots + 8,), jnp.int32),
            pltpu.SemaphoreType.DMA((1,)),
        ],
        compiler_params=params(16 if row_blocks <= 32 else 32),
        cost_estimate=SMALL,
        name="turned_tiles",
    )(cols, tiles.reshape(shape))


def back_kernel(rows, slots, n_grads, n_after, out_pieces, paired, here, cols, *refs):
    grads, tiles = refs[:n_grads], refs[n_grads]
    refs = refs[n_grads + 1 + n_after :]
    outs = refs[: len(out_pieces)]
    grad_v, acc, live, source, sem = refs[len(out_pieces) :]
    n_tiles, block = tiles.shape[:2]
    here = Place(here, paired, rows // block)
    jobs = grad_jobs(rows, grads, grad_v, sem, here)
    run_jobs(jobs, "start")

    def collect(row, found):
        count = cols[slots, row]
        for slot in range(slots):
            live[found] = row
            source[found] = here.source(cols[slot, row])
            found = found + (slot < count).astype(jnp.int32)
        return found

    found = lax.fori_loop(0, n_tiles // slots, collect, jnp.int32(0))
    acc[...] = jnp.zeros_like(acc)
    run_jobs(jobs, "wait")

    def entry(place):
        term = mm(tiles[place], grad_v[block_at(live[place], block)])
        acc[block_at(source[place], block)] += term

    for_live(0, found, entry)
    piece = acc.shape[0] // sum(len(members) for members in out_pieces)
    for out, members in zip(outs, out_pieces):
        for index, member in enumerate(members):
            out[pl.ds(index * piece, piece)] = acc[pl.ds(member * piece, piece)].astype(BF16)


def back_call(paired, here, cols, grads, tiles, total, gathered, out_pieces, after=()):
    rows, width = grads[0].shape
    rows = total if len(grads) == 1 else rows
    n_tiles, block = tiles.shape[:2]
    slots = cols.shape[0] - 1
    piece = gathered // sum(len(members) for members in out_pieces)
    return pl.pallas_call(
        functools.partial(back_kernel, rows, slots, len(grads), len(after), out_pieces, paired),
        out_shape=[jax.ShapeDtypeStruct((len(m) * piece, width), BF16) for m in out_pieces],
        in_specs=[SMEM] * 2 + [ANY] * len(grads) + [VMEM] + [ANY] * len(after),
        out_specs=[VMEM] * len(out_pieces),
        scratch_shapes=[
            pltpu.VMEM((total, width), BF16),
            pltpu.VMEM((gathered, width), F32),
            pltpu.SMEM((n_tiles + 8,), jnp.int32),
            pltpu.SMEM((n_tiles + 8,), jnp.int32),
            pltpu.SemaphoreType.DMA((len(grads),)),
        ],
        compiler_params=params(28 if gathered <= 8192 else 56),
        cost_estimate=SMALL,
        name="back_terms",
    )(here, cols, *grads, tiles, *after)


def tile_grad_kernel(
    rows, slots, n_grads, n_pieces, n_chunks, n_after, groups, paired, here, cols, *refs
):
    grads = refs[: n_grads * n_chunks]
    refs = refs[n_grads * n_chunks :]
    pieces = refs[: n_pieces * n_chunks]
    out, token, grad_v, nodes_v, tiles_v, live, source, sem, piece_sem, out_sem = refs[n_pieces * n_chunks + n_after :]
    token[...] = jnp.zeros_like(token)
    block = out.shape[1]
    width = nodes_v.shape[1]
    part = width // n_chunks
    scale = float(width) ** -0.5
    blocks = grad_v.shape[0] // (block * len(groups))
    here = Place(here, paired, blocks)
    jobs, copies = [], []
    for chunk in range(n_chunks):
        columns = pl.ds(chunk * part, part)
        jobs += grad_jobs(
            rows,
            grads[chunk * n_grads : (chunk + 1) * n_grads],
            grad_v.at[:, columns],
            sem.at[chunk],
            here,
            groups,
        )
        copies += load_pieces(
            pieces[chunk * n_pieces : (chunk + 1) * n_pieces],
            nodes_v.at[:, columns],
            piece_sem.at[chunk],
            0,
        )
    run_jobs(jobs, "start")
    tiles_v[...] = jnp.zeros_like(tiles_v)
    found = jnp.int32(0)
    for index, group in enumerate(groups):
        first = here.group(group) * blocks

        def collect(i, found, first=first, index=index):
            row = first + i
            count = cols[slots, row]
            for slot in range(slots):
                live[found] = (index * blocks + i) * slots + slot
                source[found] = here.source(cols[slot, row])
                found = found + (slot < count).astype(jnp.int32)
            return found

        found = lax.fori_loop(0, blocks, collect, found)
    run_jobs(jobs, "wait")
    for copy in copies:
        copy.wait()

    def entry(place):
        tile_index = live[place]
        grad = grad_v[block_at(tile_index // slots, block)]
        node = nodes_v[block_at(source[place], block)]
        tiles_v[tile_index] = (mm(grad, node, NT) * scale).astype(BF16)

    for_live(0, found, entry)
    size = blocks * slots
    copies = []
    for index, group in enumerate(groups):
        copy = pltpu.make_async_copy(
            tiles_v.at[pl.ds(index * size, size)],
            out.at[pl.ds(here.group(group) * size, size)],
            out_sem.at[index],
        )
        copy.start()
        copies.append(copy)
    for copy in copies:
        copy.wait()


def tile_grad_call(paired, here, cols, grads, pieces, shape, rows, groups, base=None, after=()):
    row_blocks, slots, block = shape[:3]
    chunks = len(grads)
    width = grads[0][0].shape[1] * chunks
    gathered = sum(piece.shape[0] for piece in pieces[0])
    flat = [a for chunk in grads for a in chunk] + [a for chunk in pieces for a in chunk]
    after = after if base is None else (base,) + tuple(after)
    entries = len(groups) * rows // block * slots
    return pl.pallas_call(
        functools.partial(
            tile_grad_kernel, rows, slots, len(grads[0]), len(pieces[0]), chunks, len(after), groups, paired
        ),
        out_shape=[
            jax.ShapeDtypeStruct((row_blocks * slots, block, block), BF16),
            jax.ShapeDtypeStruct((8, 128), F32),
        ],
        in_specs=[SMEM] * 2 + [ANY] * (len(flat) + len(after)),
        out_specs=[ANY, VMEM],
        input_output_aliases={} if base is None else {2 + len(flat): 0},
        scratch_shapes=[
            pltpu.VMEM((len(groups) * rows, width), BF16),
            pltpu.VMEM((gathered, width), BF16),
            pltpu.VMEM((entries, block, block), BF16),
            pltpu.SMEM((entries + 8,), jnp.int32),
            pltpu.SMEM((entries + 8,), jnp.int32),
            pltpu.SemaphoreType.DMA((chunks, len(grads[0]))),
            pltpu.SemaphoreType.DMA((chunks, len(pieces[0]))),
            pltpu.SemaphoreType.DMA((len(groups),)),
        ],
        compiler_params=params(16 if gathered <= 8192 else 40),
        cost_estimate=SMALL,
        name="tile_grads",
    )(here, cols, *flat, *after)


def swap(value, bit):
    return lax.ppermute(value, "row", [(i, i ^ bit) for i in range(8)])


def outer_swap(value):
    return lax.ppermute(value, "col", [(0, 1), (1, 0), (2, 3), (3, 2)])


def turn(value, by):
    return lax.ppermute(value, "col", [(i, (i + by) % 4) for i in range(4)])


def inner_swap(value):
    pairs = []
    for row in range(8):
        for col in range(4):
            partner = (row, 3 - col) if col in (1, 2) else (row ^ 1, col)
            pairs.append((row * 4 + col, partner[0] * 4 + partner[1]))
    return lax.ppermute(value, ("row", "col"), pairs)


def gather_square(nodes):
    half = nodes.shape[0] // 2
    lower, upper = nodes[:half], nodes[half:]
    y_lower, x_upper = swap(lower, 4), swap(upper, 2)
    x_lower, y_upper = swap(lower, 2), swap(upper, 4)
    d_lower, d_upper = swap(y_lower, 2), swap(x_upper, 4)
    pieces = [lower, upper, swap(nodes, 1)]
    for pair in ((x_lower, x_upper), (y_lower, y_upper), (d_lower, d_upper)):
        pieces += [*pair, *(swap(piece, 1) for piece in pair)]
    return pieces


def reduce_square(here, even, urgent, rest, rows):
    half = rows // 2
    first = [
        sum_call(here, rows, [(even, (6, 2)), (urgent, (0, 2))]),
        sum_call(here, rows, [(even, (7, 5)), (urgent, (1, 3))]),
    ]
    x_first, y_first = swap(first[0], 2), swap(first[1], 4)
    y_lower = swap(sum_call(here, half, [(even, 4), (rest, 3), (x_first, 0)]), 4)
    x_upper = swap(sum_call(here, half, [(even, 3), (rest, 2), (y_first, 0)]), 2)
    return [((x_first, 1), (x_upper, 0)), ((y_lower, 0), (y_first, 1))], first


def sum_kernel(n_terms, n_gated, n_split, *refs):
    inner, refs = Place(refs[0]).inner(), refs[1:]
    total = None
    for index, ref in enumerate(refs[: n_terms + n_gated]):
        term = ref[...].astype(F32)
        if index >= n_terms:
            term = jnp.where(inner, term, 0.0)
        total = term if total is None else total + term
    for index in range(n_split):
        first, second = refs[n_terms + n_gated + 2 * index :][:2]
        early = pl.program_id(0) < pl.num_programs(0) // 2
        total = total + jnp.where(early, first[...], second[...]).astype(F32)
    refs[-1][...] = total.astype(refs[-1].dtype)


def sum_call(here, rows, terms, gated=(), split=(), dtype=BF16, after=()):
    both = [*terms, *gated]
    width = both[0][0].shape[1]
    step = min(rows, 512)
    steps = rows // step
    half = steps // 2

    def spec(piece):
        if isinstance(piece, int):
            return pl.BlockSpec((step, width), lambda i: (piece * steps + i, 0))
        lower, upper = piece
        return pl.BlockSpec(
            (step, width), lambda i: (jnp.where(i < half, lower * half + i, (upper - 1) * half + i), 0)
        )

    def early(piece):
        return pl.BlockSpec((step, width), lambda i: (piece * half + jnp.minimum(i, half - 1), 0))

    def late(piece):
        return pl.BlockSpec((step, width), lambda i: (piece * half + jnp.maximum(i - half, 0), 0))

    return pl.pallas_call(
        functools.partial(sum_kernel, len(terms), len(gated), len(split)),
        grid=(steps,),
        out_shape=jax.ShapeDtypeStruct((rows, width), dtype),
        in_specs=[SMEM]
        + [spec(piece) for _, piece in both]
        + [spec_of(piece) for pair in split for spec_of, (_, piece) in zip((early, late), pair)]
        + [ANY] * len(after),
        out_specs=pl.BlockSpec((step, width), lambda i: (i, 0)),
        compiler_params=params(16),
        cost_estimate=SMALL,
        name="sum_terms",
    )(here, *(array for array, _ in both), *(array for pair in split for array, _ in pair), *after)


def scatter_weights(here, kept, sent, after):
    rows = kept.shape[0] // 4
    received = swap(sent, 1)
    pieces = [
        sum_call(here, rows, [(kept, place), (received, place)], dtype=F32) for place in range(4)
    ]
    terms = [pieces[0]] + [swap(piece, bits) for piece, bits in zip(pieces[1:], SWAP_ORDER[1:4])]
    return sum_call(here, rows, [(term, 0) for term in terms], after=after)


def level_weights(here, value, after):
    terms = [value] + [turn(value, by) for by in (1, 2, 3)]
    return sum_call(here, value.shape[0], [(term, 0) for term in terms], after=after)


def reduce_line(here, far, near, pair, own, after):
    rows = own.shape[0]
    far_sum = inner_swap(sum_call(here, rows, [(far, 0), (outer_swap(far), 0)], after=after))
    near_sum = inner_swap(sum_call(here, rows, [(near, 0), (outer_swap(near), 0)]))
    pair_in = outer_swap(sum_call(here, rows, [(pair, 0)], [(far_sum, 0)]))
    return own, pair_in, near_sum


def gather_line(own):
    pair = outer_swap(own)
    near_inner = inner_swap(own)
    far_inner = inner_swap(pair)
    near_outer = outer_swap(near_inner)
    far_outer = outer_swap(far_inner)
    return [own, pair, near_inner, near_outer, far_inner, far_outer]


def body(n_row, n_col, nodes, tiles, tile_col, tile_count, w_in, bias_in, w_out, ln_gain, ln_shift, cotangent):
    rows, width = nodes.shape
    row_blocks, _, slots, block = tiles.shape[:4]
    tile_local = tiles.reshape(row_blocks, slots, block, block)
    table = jnp.concatenate([tile_col.reshape(row_blocks, slots).T, tile_count.reshape(1, row_blocks)], axis=0)
    gathered, total = n_row * rows, n_col * rows
    paired = n_row == 8 and n_col == 4
    here = lax.axis_index(("row", "col")).astype(jnp.int32).reshape(1)
    known = (paired, here, table)
    turned = turn_call(table, tile_local)
    if paired:
        pieces = [gather_square(nodes)]
        (far,) = forward_call(*known, pieces[0], tile_local, ((0,),), rows)
        (near,) = forward_call(*known, pieces[0], tile_local, ((1,),), rows)
        pair, own = forward_call(*known, pieces[0], tile_local, ((2,), (3,)), rows)
        parts = [reduce_line(here, far, near, pair, own, (turned,))]
        kinds = [("all", "all", "inner")]
    else:
        pieces = [[lax.all_gather(nodes, "row", axis=0, tiled=True)]]
        (partial,) = forward_call(*known, pieces[0], tile_local, (tuple(range(n_col)),), rows)
        parts = [[lax.psum_scatter(partial, "col", scatter_dimension=0, tiled=True)]]
        kinds = [("all",)]
    vectors = [v.reshape(1, width) for v in (bias_in, ln_gain, ln_shift)]
    (updated, gpre_b, act, gproj, message, vec), gmsgs = mlp_call(
        here, nodes, cotangent, parts, kinds, w_in, vectors[0], w_out, vectors[1], vectors[2]
    )
    factor = float(rows * n_row * n_col) ** -0.5
    weight_args = (here, nodes, message, act, gpre_b, gproj, cotangent, w_in, vec)
    if paired:
        halves = ((14, 15, 6, 11), (2, 3, 7, 10), (0, 1, 4, 5, 8, 9, 12, 13))
        grads = [gather_line(gmsgs[0])]
        kept, sent, direct = weight_call(factor, n_row, *weight_args, (grads[0][1], grads[0][2]))
        near_grads, token = tile_grad_call(
            *known, [grads[0][:2]], pieces, tile_local.shape, rows, (3, 2), after=(grads[0][3], grads[0][4])
        )
        row_weights = scatter_weights(here, kept, sent, (token,))
        urgent, rest, even = back_call(
            *known, grads[0], turned, total, gathered, halves, (row_weights,)
        )
        urgent, rest = swap(urgent, 1), swap(rest, 1)
        arrived, first = reduce_square(here, even, urgent, rest, rows)
        grad_tiles, token = tile_grad_call(
            *known, grads, pieces, tile_local.shape, rows, (1, 0), near_grads, first
        )
        row_weights = sum_call(here, row_weights.shape[0], [(row_weights, 0)], after=(rest, *first))
        all_weights = level_weights(here, row_weights, (token,))
        joint = jnp.concatenate([all_weights] + [swap(all_weights, bits) for bits in (2, 4, 6)], axis=0)
        weights = unpack_call(here, joint, swap(joint, 1), width)
        grad_nodes = sum_call(here, rows, [(direct, 0), (even, 0), (rest, 0)], split=arrived)
    else:
        grads = [[lax.all_gather(gmsgs[0], "col", axis=0, tiled=True)]]
        weight_terms, direct = weight_call(factor, 1, *weight_args)
        weight_sums = lax.psum(weight_terms, ("row", "col"))
        weights = (
            weight_sums[: 2 * width],
            weight_sums[2 * width : 3 * width],
            weight_sums[3 * width : 3 * width + 3],
        )
        (terms,) = back_call(*known, grads[0], turned, total, gathered, (tuple(range(n_row)),))
        back = lax.psum_scatter(terms, "row", scatter_dimension=0, tiled=True)
        grad_nodes = sum_call(here, rows, [(direct, 0), (back, 0)])
        grad_tiles, _ = tile_grad_call(
            *known, grads, pieces, tile_local.shape, rows, tuple(range(n_col))
        )
    grad_tiles = grad_tiles.reshape(tiles.shape)
    return (updated, grad_nodes, grad_tiles, *weights)


def solution(mesh):
    placed = (
        P(("row", "col"), None),
        P("row", "col", None, None, None),
        P("row", "col", None),
        P("row", "col"),
        P(),
        P(),
        P(),
        P(),
        P(),
        P(("row", "col"), None),
    )
    return jax.shard_map(
        functools.partial(body, mesh.shape["row"], mesh.shape["col"]),
        mesh=mesh,
        in_specs=placed,
        out_specs=(
            P(("row", "col"), None),
            P(("row", "col"), None),
            P("row", "col", None, None, None),
            P(),
            P(),
            P(),
        ),
        check_vma=False,
    )
```

```python
import functools

import jax
import jax.numpy as jnp
from jax import lax
from jax.experimental import pallas as pl
from jax.experimental.pallas import tpu as pltpu
from jax.sharding import PartitionSpec as P

F32 = jnp.float32
BF16 = jnp.bfloat16
ANY = pl.BlockSpec(memory_space=pl.ANY)
HBM = pl.BlockSpec(memory_space=pltpu.HBM)
SMEM = pl.BlockSpec(memory_space=pltpu.SMEM)
VMEM = pl.BlockSpec(memory_space=pltpu.VMEM)
MIB = 1 << 20
TN = (((0,), (0,)), ((), ()))
NT = (((1,), (1,)), ((), ()))
SMALL = pl.CostEstimate(flops=1 << 20, bytes_accessed=1 << 16, transcendentals=0)


LIVE_STEP = 4
GRAD_PLAN = ((3, 0, None), (2, 1, None), (1, 2, "inner"), (1, 3, "outer"), (0, 4, "inner"), (0, 5, "outer"))
SWAP_ORDER = (0, 4, 2, 6, 1, 5, 3, 7)


def params(mib):
    return pltpu.CompilerParams(vmem_limit_bytes=mib * MIB)


def mm(a, b, dims=(((1,), (0,)), ((), ()))):
    return lax.dot_general(a, b, dims, preferred_element_type=F32)


def block_at(index, block):
    return pl.ds(pl.multiple_of(index * block, block), block)


class Place:
    def __init__(self, ref, paired=True, blocks=1):
        self.mine, self.level = lax.shift_right_logical(ref[0], 2), ref[0] & 3
        self.paired, self.blocks = paired, blocks

    def inner(self):
        return (self.level == 1) | (self.level == 2)

    def group(self, pick):
        if not self.paired:
            return pick
        low = self.level < 2
        choices = (jnp.where(low, 3, 0), jnp.where(low, 2, 1), self.level ^ 1, self.level)
        return choices[pick]

    def source(self, col):
        if not self.paired:
            return col
        shift = self.blocks.bit_length() - 1
        if 1 << shift == self.blocks:
            return col ^ lax.shift_left(self.mine, jnp.int32(shift))
        return (lax.div(col, self.blocks) ^ self.mine) * self.blocks + lax.rem(col, self.blocks)


def load_pieces(pieces, dst, sem, first):
    copies = []
    offset = 0
    for index, piece in enumerate(pieces):
        copy = pltpu.make_async_copy(
            piece, dst.at[pl.ds(offset, piece.shape[0])], sem.at[first + index]
        )
        copy.start()
        copies.append(copy)
        offset += piece.shape[0]
    return copies


def masked_tile(tile, live):
    return jnp.where(live, tile, jnp.zeros_like(tile))


def forward_kernel(outputs, n_pieces, paired, here, cols, *refs):
    pieces, tiles = refs[:n_pieces], refs[n_pieces]
    outs = refs[n_pieces + 1 : n_pieces + 1 + len(outputs)]
    nodes_v, tiles_v, sem, tile_sem = refs[n_pieces + 1 + len(outputs) :]
    rows = outs[0].shape[0] // len(outputs[0])
    slots, block = tiles.shape[1], tiles.shape[2]
    blocks = rows // block
    here = Place(here, paired, blocks)
    copies = load_pieces(pieces, nodes_v, sem, 0)
    places = [(pick, out, index) for out, picks in zip(outs, outputs) for index, pick in enumerate(picks)]
    tile_copies = []
    for place, (pick, _, _) in enumerate(places):
        copy = pltpu.make_async_copy(
            tiles.at[pl.ds(here.group(pick) * blocks, blocks)],
            tiles_v.at[pl.ds(place * blocks, blocks)],
            tile_sem.at[place],
        )
        copy.start()
        tile_copies.append(copy)
    for copy in copies:
        copy.wait()
    for place, (pick, out, index) in enumerate(places):
        tile_copies[place].wait()
        first = here.group(pick) * blocks

        def step(i, carry, first=first, out=out, index=index, place=place):
            row = first + i
            count = cols[slots, row]
            parts = []
            for pair in range(slots // 2):
                both = (2 * pair, 2 * pair + 1)
                tile = jnp.concatenate(
                    [masked_tile(tiles_v[place * blocks + i, slot], slot < count) for slot in both], axis=1
                )
                node = jnp.concatenate(
                    [nodes_v[block_at(here.source(cols[slot, row]), block)] for slot in both], axis=0
                )
                parts.append(mm(tile, node))
            value = parts[0]
            for part in parts[1:]:
                value = value + part
            out[block_at(index * blocks + i, block)] = value.astype(BF16)
            return carry

        lax.fori_loop(0, blocks, step, 0, unroll=4)


def forward_call(paired, here, cols, pieces, tiles, outputs, rows):
    width = pieces[0].shape[1]
    gathered = sum(piece.shape[0] for piece in pieces)
    slots, block = tiles.shape[1], tiles.shape[2]
    n_picks = sum(len(picks) for picks in outputs)
    return pl.pallas_call(
        functools.partial(forward_kernel, outputs, len(pieces), paired),
        out_shape=[jax.ShapeDtypeStruct((len(picks) * rows, width), BF16) for picks in outputs],
        in_specs=[SMEM] * 2 + [ANY] * len(pieces) + [HBM],
        out_specs=[VMEM] * len(outputs),
        scratch_shapes=[
            pltpu.VMEM((gathered, width), BF16),
            pltpu.VMEM((n_picks * (rows // block),) + tiles.shape[1:], BF16),
            pltpu.SemaphoreType.DMA((len(pieces),)),
            pltpu.SemaphoreType.DMA((n_picks,)),
        ],
        compiler_params=params(48),
        cost_estimate=SMALL,
        name="partial_messages",
    )(here, cols, *pieces, tiles)


def mlp_kernel(kinds, step, here, nodes, cot, *refs):
    n_parts = sum(len(chunk) for chunk in kinds)
    parts = refs[:n_parts]
    w_in, bias, w_out, gain, shift, updated, gpre_o, act_o, gproj_o, msg_o, vec = refs[
        n_parts : n_parts + 11
    ]
    gmsgs = refs[n_parts + 11 :]
    rows, width = nodes.shape
    inner = Place(here).inner()
    vec[...] = jnp.zeros_like(vec)
    for first in range(0, rows, step):
        where = slice(first, first + step)
        messages = []
        place = 0
        for chunk in kinds:
            total = None
            for kind in chunk:
                term = parts[place][where].astype(F32)
                place += 1
                if kind == "inner":
                    term = jnp.where(inner, term, 0.0)
                total = term if total is None else total + term
            messages.append(total.astype(BF16))
        message = jnp.concatenate(messages, axis=1) if len(messages) > 1 else messages[0]
        node = nodes[where]
        pre = mm(node, w_in[:width]) + mm(message, w_in[width:]) + bias[...]
        sig = 0.5 + 0.5 * jnp.tanh(0.5 * pre)
        act = (pre * sig).astype(BF16)
        proj = mm(act, w_out[...])
        mean = jnp.mean(proj, axis=-1, keepdims=True)
        var = jnp.mean((proj - mean) ** 2, axis=-1, keepdims=True)
        rstd = 1.0 / jnp.sqrt(var + 1e-05)
        normed = (proj - mean) * rstd
        updated[where] = (node.astype(F32) + normed * gain[...] + shift[...]).astype(BF16)
        grad_out = cot[where].astype(F32)
        gscaled = grad_out * gain[...]
        gproj = (
            (
                gscaled
                - jnp.mean(gscaled, axis=-1, keepdims=True)
                - normed * jnp.mean(gscaled * normed, axis=-1, keepdims=True)
            )
            * rstd
        ).astype(BF16)
        gact = mm(gproj, w_out[...], NT)
        gpre = gact * sig * (1.0 + pre * (1.0 - sig))
        gpre_b = gpre.astype(BF16)
        gmsg = mm(gpre_b, w_in[width:], NT).astype(BF16)
        part = width // len(gmsgs)
        for index, out in enumerate(gmsgs):
            out[where] = gmsg[:, index * part : (index + 1) * part]
        gpre_o[where] = gpre_b
        act_o[where] = act
        gproj_o[where] = gproj
        msg_o[where] = message
        vec[0:1] += jnp.sum(gpre, axis=0, keepdims=True)
        vec[1:2] += jnp.sum(grad_out * normed, axis=0, keepdims=True)
        vec[2:3] += jnp.sum(grad_out, axis=0, keepdims=True)


def mlp_call(here, nodes, cot, parts, kinds, w_in, bias, w_out, gain, shift):
    rows, width = nodes.shape
    step = min(rows, 512)

    flat = [term for chunk in parts for term in chunk]
    row_like = jax.ShapeDtypeStruct((rows, width), BF16)
    chunk_like = jax.ShapeDtypeStruct((rows, width // len(parts)), BF16)
    outs = [row_like] * 5 + [jax.ShapeDtypeStruct((8, width), F32)] + [chunk_like] * len(parts)
    weights = (w_in, bias, w_out, gain, shift)
    result = pl.pallas_call(
        functools.partial(mlp_kernel, kinds, step),
        out_shape=outs,
        in_specs=[SMEM] + [VMEM] * (2 + len(flat) + len(weights)),
        out_specs=[VMEM] * len(outs),
        compiler_params=params(40),
        cost_estimate=SMALL,
        name="mlp",
    )(here, nodes, cot, *flat, *weights)
    return result[:6], result[6:]


def weight_kernel(factor, pieces, step, n_after, here, nodes, msg, act, gpre, gproj, cot, w_in, vec, *refs):
    *outs, direct, grads = refs[n_after:]
    rows, width = nodes.shape
    for first in range(0, rows, step):
        where = slice(first, first + step)
        gpre_b = gpre[where]
        terms = (mm(nodes[where], gpre_b, TN), mm(msg[where], gpre_b, TN), mm(act[where], gproj[where], TN))
        for index, term in enumerate(terms):
            own = slice(index * width, (index + 1) * width)
            grads[own] = term if first == 0 else grads[own] + term
        direct[where] = cot[where].astype(F32) + mm(gpre_b, w_in[:width], NT)
    grads[3 * width : 3 * width + 8] = vec[...]
    grads[3 * width + 8 :] = jnp.zeros((grads.shape[0] - 3 * width - 8, width), F32)
    if pieces == 1:
        outs[0][...] = grads[: outs[0].shape[0]] * factor
    else:
        rows = grads.shape[0] // pieces
        for place, member in enumerate(SWAP_ORDER):
            where = pl.ds(pl.multiple_of((Place(here).mine ^ member) * rows, 8), rows)
            out, index = outs[2 * place // pieces], place % (pieces // 2)
            out[index * rows : (index + 1) * rows] = grads[where] * factor


def weight_call(factor, pieces, here, nodes, msg, act, gpre, gproj, cot, w_in, vec, after=()):
    rows, width = nodes.shape
    step = min(rows, 256)
    padded = (3 * width + width // 2, width)
    if pieces == 1:
        outs = [jax.ShapeDtypeStruct((3 * width + 8, width), F32)]
    else:
        outs = [jax.ShapeDtypeStruct((padded[0] // 2, width), F32)] * 2
    return pl.pallas_call(
        functools.partial(weight_kernel, factor, pieces, step, len(after)),
        out_shape=[*outs, jax.ShapeDtypeStruct((rows, width), F32)],
        in_specs=[SMEM] + [VMEM] * 8 + [ANY] * len(after),
        out_specs=[VMEM] * (len(outs) + 1),
        scratch_shapes=[pltpu.VMEM(padded, F32)],
        compiler_params=params(40),
        cost_estimate=SMALL,
        name="weight_grads",
    )(here, nodes, msg, act, gpre, gproj, cot, w_in, vec, *after)


def unpack_kernel(here, even, odd, w_in, w_out, vectors, grads):
    width = w_in.shape[1]
    rows = grads.shape[0] // 8
    for member in range(8):
        part = (even, odd)[member % 2]
        first = member // 2 * rows
        where = pl.ds(pl.multiple_of((Place(here).mine ^ member) * rows, 8), rows)
        grads[where] = part[first : first + rows].astype(F32)
    w_in[...] = grads[: 2 * width]
    w_out[...] = grads[2 * width : 3 * width]
    vectors[...] = grads[3 * width : 3 * width + 3]


def unpack_call(here, even, odd, width):
    shapes = ((2 * width, width), (width, width), (3, width))
    return pl.pallas_call(
        unpack_kernel,
        out_shape=[jax.ShapeDtypeStruct(shape, F32) for shape in shapes],
        in_specs=[SMEM, VMEM, VMEM],
        out_specs=[VMEM] * 3,
        scratch_shapes=[pltpu.VMEM((3 * width + width // 2, width), F32)],
        compiler_params=params(16),
        cost_estimate=SMALL,
        name="weight_unpack",
    )(here, even, odd)


def grad_jobs(rows, refs, dst, sem, here, groups=None):
    if len(refs) == 1:
        return [(None, pltpu.make_async_copy(refs[0], dst, sem.at[0]))]
    inner = here.inner()
    conditions = {None: None, "inner": inner, "outer": jnp.logical_not(inner)}
    jobs = []
    for group, index, kind in GRAD_PLAN:
        if groups is None:
            where = block_at(here.group(group), rows)
        elif group in groups:
            where = pl.ds(groups.index(group) * rows, rows)
        else:
            continue
        copy = pltpu.make_async_copy(refs[index], dst.at[where], sem.at[index])
        jobs.append((conditions[kind], copy))
    return jobs


def run_jobs(jobs, verb):
    for condition, copy in jobs:
        if condition is None:
            getattr(copy, verb)()
        else:
            pl.when(condition)(getattr(copy, verb))


def for_live(first, last, entry):
    def several(i, carry):
        for index in range(LIVE_STEP):
            entry(first + i * LIVE_STEP + index)
        return carry

    def one(i, carry):
        entry(i)
        return carry

    full = jnp.maximum(last - first, 0) // LIVE_STEP
    lax.fori_loop(0, full, several, 0)
    lax.fori_loop(first + full * LIVE_STEP, last, one, 0)


def turn_kernel(slots, cols, tiles, out, tiles_v, live, sem):
    copy = pltpu.make_async_copy(tiles, tiles_v, sem.at[0])
    copy.start()

    def collect(row, found):
        count = cols[slots, row]
        for slot in range(slots):
            live[found] = row * slots + slot
            found = found + (slot < count).astype(jnp.int32)
        return found

    found = lax.fori_loop(0, tiles.shape[0] // slots, collect, jnp.int32(0))
    copy.wait()

    def entry(place):
        out[place] = tiles_v[live[place]].T

    for_live(0, found, entry)


def turn_call(cols, tiles):
    row_blocks, slots, block = tiles.shape[:3]
    shape = (row_blocks * slots, block, block)
    return pl.pallas_call(
        functools.partial(turn_kernel, slots),
        out_shape=jax.ShapeDtypeStruct(shape, BF16),
        in_specs=[SMEM, HBM],
        out_specs=VMEM,
        scratch_shapes=[
            pltpu.VMEM(shape, BF16),
            pltpu.SMEM((row_blocks * slots + 8,), jnp.int32),
            pltpu.SemaphoreType.DMA((1,)),
        ],
        compiler_params=params(16 if row_blocks <= 32 else 32),
        cost_estimate=SMALL,
        name="turned_tiles",
    )(cols, tiles.reshape(shape))


def back_kernel(rows, slots, n_grads, n_after, out_pieces, paired, here, cols, *refs):
    grads, tiles = refs[:n_grads], refs[n_grads]
    refs = refs[n_grads + 1 + n_after :]
    outs = refs[: len(out_pieces)]
    grad_v, acc, live, source, sem = refs[len(out_pieces) :]
    n_tiles, block = tiles.shape[:2]
    here = Place(here, paired, rows // block)
    jobs = grad_jobs(rows, grads, grad_v, sem, here)
    run_jobs(jobs, "start")

    def collect(row, found):
        count = cols[slots, row]
        for slot in range(slots):
            live[found] = row
            source[found] = here.source(cols[slot, row])
            found = found + (slot < count).astype(jnp.int32)
        return found

    found = lax.fori_loop(0, n_tiles // slots, collect, jnp.int32(0))
    acc[...] = jnp.zeros_like(acc)
    run_jobs(jobs, "wait")

    def entry(place):
        term = mm(tiles[place], grad_v[block_at(live[place], block)])
        acc[block_at(source[place], block)] += term

    for_live(0, found, entry)
    piece = acc.shape[0] // sum(len(members) for members in out_pieces)
    for out, members in zip(outs, out_pieces):
        for index, member in enumerate(members):
            out[pl.ds(index * piece, piece)] = acc[pl.ds(member * piece, piece)].astype(BF16)


def back_call(paired, here, cols, grads, tiles, total, gathered, out_pieces, after=()):
    rows, width = grads[0].shape
    rows = total if len(grads) == 1 else rows
    n_tiles, block = tiles.shape[:2]
    slots = cols.shape[0] - 1
    piece = gathered // sum(len(members) for members in out_pieces)
    return pl.pallas_call(
        functools.partial(back_kernel, rows, slots, len(grads), len(after), out_pieces, paired),
        out_shape=[jax.ShapeDtypeStruct((len(m) * piece, width), BF16) for m in out_pieces],
        in_specs=[SMEM] * 2 + [ANY] * len(grads) + [VMEM] + [ANY] * len(after),
        out_specs=[VMEM] * len(out_pieces),
        scratch_shapes=[
            pltpu.VMEM((total, width), BF16),
            pltpu.VMEM((gathered, width), F32),
            pltpu.SMEM((n_tiles + 8,), jnp.int32),
            pltpu.SMEM((n_tiles + 8,), jnp.int32),
            pltpu.SemaphoreType.DMA((len(grads),)),
        ],
        compiler_params=params(28 if gathered <= 8192 else 56),
        cost_estimate=SMALL,
        name="back_terms",
    )(here, cols, *grads, tiles, *after)


def tile_grad_kernel(
    rows, slots, n_grads, n_pieces, n_chunks, n_after, groups, paired, here, cols, *refs
):
    grads = refs[: n_grads * n_chunks]
    refs = refs[n_grads * n_chunks :]
    pieces = refs[: n_pieces * n_chunks]
    out, token, grad_v, nodes_v, tiles_v, live, source, sem, piece_sem, out_sem = refs[n_pieces * n_chunks + n_after :]
    token[...] = jnp.zeros_like(token)
    block = out.shape[1]
    width = nodes_v.shape[1]
    part = width // n_chunks
    scale = float(width) ** -0.5
    blocks = grad_v.shape[0] // (block * len(groups))
    here = Place(here, paired, blocks)
    jobs, copies = [], []
    for chunk in range(n_chunks):
        columns = pl.ds(chunk * part, part)
        jobs += grad_jobs(
            rows,
            grads[chunk * n_grads : (chunk + 1) * n_grads],
            grad_v.at[:, columns],
            sem.at[chunk],
            here,
            groups,
        )
        copies += load_pieces(
            pieces[chunk * n_pieces : (chunk + 1) * n_pieces],
            nodes_v.at[:, columns],
            piece_sem.at[chunk],
            0,
        )
    run_jobs(jobs, "start")
    tiles_v[...] = jnp.zeros_like(tiles_v)
    found = jnp.int32(0)
    for index, group in enumerate(groups):
        first = here.group(group) * blocks

        def collect(i, found, first=first, index=index):
            row = first + i
            count = cols[slots, row]
            for slot in range(slots):
                live[found] = (index * blocks + i) * slots + slot
                source[found] = here.source(cols[slot, row])
                found = found + (slot < count).astype(jnp.int32)
            return found

        found = lax.fori_loop(0, blocks, collect, found)
    run_jobs(jobs, "wait")
    for copy in copies:
        copy.wait()

    def entry(place):
        tile_index = live[place]
        grad = grad_v[block_at(tile_index // slots, block)]
        node = nodes_v[block_at(source[place], block)]
        tiles_v[tile_index] = (mm(grad, node, NT) * scale).astype(BF16)

    for_live(0, found, entry)
    size = blocks * slots
    copies = []
    for index, group in enumerate(groups):
        copy = pltpu.make_async_copy(
            tiles_v.at[pl.ds(index * size, size)],
            out.at[pl.ds(here.group(group) * size, size)],
            out_sem.at[index],
        )
        copy.start()
        copies.append(copy)
    for copy in copies:
        copy.wait()


def tile_grad_call(paired, here, cols, grads, pieces, shape, rows, groups, base=None, after=()):
    row_blocks, slots, block = shape[:3]
    chunks = len(grads)
    width = grads[0][0].shape[1] * chunks
    gathered = sum(piece.shape[0] for piece in pieces[0])
    flat = [a for chunk in grads for a in chunk] + [a for chunk in pieces for a in chunk]
    after = after if base is None else (base,) + tuple(after)
    entries = len(groups) * rows // block * slots
    return pl.pallas_call(
        functools.partial(
            tile_grad_kernel, rows, slots, len(grads[0]), len(pieces[0]), chunks, len(after), groups, paired
        ),
        out_shape=[
            jax.ShapeDtypeStruct((row_blocks * slots, block, block), BF16),
            jax.ShapeDtypeStruct((8, 128), F32),
        ],
        in_specs=[SMEM] * 2 + [ANY] * (len(flat) + len(after)),
        out_specs=[ANY, VMEM],
        input_output_aliases={} if base is None else {2 + len(flat): 0},
        scratch_shapes=[
            pltpu.VMEM((len(groups) * rows, width), BF16),
            pltpu.VMEM((gathered, width), BF16),
            pltpu.VMEM((entries, block, block), BF16),
            pltpu.SMEM((entries + 8,), jnp.int32),
            pltpu.SMEM((entries + 8,), jnp.int32),
            pltpu.SemaphoreType.DMA((chunks, len(grads[0]))),
            pltpu.SemaphoreType.DMA((chunks, len(pieces[0]))),
            pltpu.SemaphoreType.DMA((len(groups),)),
        ],
        compiler_params=params(16 if gathered <= 8192 else 40),
        cost_estimate=SMALL,
        name="tile_grads",
    )(here, cols, *flat, *after)


def swap(value, bit):
    return lax.ppermute(value, "row", [(i, i ^ bit) for i in range(8)])


def outer_swap(value):
    return lax.ppermute(value, "col", [(0, 1), (1, 0), (2, 3), (3, 2)])


def turn(value, by):
    return lax.ppermute(value, "col", [(i, (i + by) % 4) for i in range(4)])


def inner_swap(value):
    pairs = []
    for row in range(8):
        for col in range(4):
            partner = (row, 3 - col) if col in (1, 2) else (row ^ 1, col)
            pairs.append((row * 4 + col, partner[0] * 4 + partner[1]))
    return lax.ppermute(value, ("row", "col"), pairs)


def gather_square(nodes):
    half = nodes.shape[0] // 2
    lower, upper = nodes[:half], nodes[half:]
    y_lower, x_upper = swap(lower, 4), swap(upper, 2)
    x_lower, y_upper = swap(lower, 2), swap(upper, 4)
    d_lower, d_upper = swap(y_lower, 2), swap(x_upper, 4)
    pieces = [lower, upper, swap(nodes, 1)]
    for pair in ((x_lower, x_upper), (y_lower, y_upper), (d_lower, d_upper)):
        pieces += [*pair, *(swap(piece, 1) for piece in pair)]
    return pieces


def reduce_square(here, even, urgent, rest, rows):
    half = rows // 2
    first = [
        sum_call(here, rows, [(even, (6, 2)), (urgent, (0, 2))]),
        sum_call(here, rows, [(even, (7, 5)), (urgent, (1, 3))]),
    ]
    x_first, y_first = swap(first[0], 2), swap(first[1], 4)
    y_lower = swap(sum_call(here, half, [(even, 4), (rest, 3), (x_first, 0)]), 4)
    x_upper = swap(sum_call(here, half, [(even, 3), (rest, 2), (y_first, 0)]), 2)
    return [((x_first, 1), (x_upper, 0)), ((y_lower, 0), (y_first, 1))], first


def sum_kernel(n_terms, n_gated, n_split, *refs):
    inner, refs = Place(refs[0]).inner(), refs[1:]
    total = None
    for index, ref in enumerate(refs[: n_terms + n_gated]):
        term = ref[...].astype(F32)
        if index >= n_terms:
            term = jnp.where(inner, term, 0.0)
        total = term if total is None else total + term
    for index in range(n_split):
        first, second = refs[n_terms + n_gated + 2 * index :][:2]
        early = pl.program_id(0) < pl.num_programs(0) // 2
        total = total + jnp.where(early, first[...], second[...]).astype(F32)
    refs[-1][...] = total.astype(refs[-1].dtype)


def sum_call(here, rows, terms, gated=(), split=(), dtype=BF16, after=()):
    both = [*terms, *gated]
    width = both[0][0].shape[1]
    step = min(rows, 512)
    steps = rows // step
    half = steps // 2

    def spec(piece):
        if isinstance(piece, int):
            return pl.BlockSpec((step, width), lambda i: (piece * steps + i, 0))
        lower, upper = piece
        return pl.BlockSpec(
            (step, width), lambda i: (jnp.where(i < half, lower * half + i, (upper - 1) * half + i), 0)
        )

    def early(piece):
        return pl.BlockSpec((step, width), lambda i: (piece * half + jnp.minimum(i, half - 1), 0))

    def late(piece):
        return pl.BlockSpec((step, width), lambda i: (piece * half + jnp.maximum(i - half, 0), 0))

    return pl.pallas_call(
        functools.partial(sum_kernel, len(terms), len(gated), len(split)),
        grid=(steps,),
        out_shape=jax.ShapeDtypeStruct((rows, width), dtype),
        in_specs=[SMEM]
        + [spec(piece) for _, piece in both]
        + [spec_of(piece) for pair in split for spec_of, (_, piece) in zip((early, late), pair)]
        + [ANY] * len(after),
        out_specs=pl.BlockSpec((step, width), lambda i: (i, 0)),
        compiler_params=params(16),
        cost_estimate=SMALL,
        name="sum_terms",
    )(here, *(array for array, _ in both), *(array for pair in split for array, _ in pair), *after)


def scatter_weights(here, kept, sent, after):
    rows = kept.shape[0] // 4
    received = swap(sent, 1)
    pieces = [
        sum_call(here, rows, [(kept, place), (received, place)], dtype=F32) for place in range(4)
    ]
    terms = [pieces[0]] + [swap(piece, bits) for piece, bits in zip(pieces[1:], SWAP_ORDER[1:4])]
    return sum_call(here, rows, [(term, 0) for term in terms], after=after)


def level_weights(here, value, after):
    terms = [value] + [turn(value, by) for by in (1, 2, 3)]
    return sum_call(here, value.shape[0], [(term, 0) for term in terms], after=after)


def reduce_line(here, far, near, pair, own, after):
    rows = own.shape[0]
    far_sum = inner_swap(sum_call(here, rows, [(far, 0), (outer_swap(far), 0)], after=after))
    near_sum = inner_swap(sum_call(here, rows, [(near, 0), (outer_swap(near), 0)]))
    pair_in = outer_swap(sum_call(here, rows, [(pair, 0)], [(far_sum, 0)]))
    return own, pair_in, near_sum


def gather_line(own):
    pair = outer_swap(own)
    near_inner = inner_swap(own)
    far_inner = inner_swap(pair)
    near_outer = outer_swap(near_inner)
    far_outer = outer_swap(far_inner)
    return [own, pair, near_inner, near_outer, far_inner, far_outer]


def body(n_row, n_col, nodes, tiles, tile_col, tile_count, w_in, bias_in, w_out, ln_gain, ln_shift, cotangent):
    rows, width = nodes.shape
    row_blocks, _, slots, block = tiles.shape[:4]
    tile_local = tiles.reshape(row_blocks, slots, block, block)
    table = jnp.concatenate([tile_col.reshape(row_blocks, slots).T, tile_count.reshape(1, row_blocks)], axis=0)
    gathered, total = n_row * rows, n_col * rows
    paired = n_row == 8 and n_col == 4
    here = lax.axis_index(("row", "col")).astype(jnp.int32).reshape(1)
    known = (paired, here, table)
    turned = turn_call(table, tile_local)
    if paired:
        pieces = [gather_square(nodes)]
        (far,) = forward_call(*known, pieces[0], tile_local, ((0,),), rows)
        (near,) = forward_call(*known, pieces[0], tile_local, ((1,),), rows)
        pair, own = forward_call(*known, pieces[0], tile_local, ((2,), (3,)), rows)
        parts = [reduce_line(here, far, near, pair, own, (turned,))]
        kinds = [("all", "all", "inner")]
    else:
        pieces = [[lax.all_gather(nodes, "row", axis=0, tiled=True)]]
        (partial,) = forward_call(*known, pieces[0], tile_local, (tuple(range(n_col)),), rows)
        parts = [[lax.psum_scatter(partial, "col", scatter_dimension=0, tiled=True)]]
        kinds = [("all",)]
    vectors = [v.reshape(1, width) for v in (bias_in, ln_gain, ln_shift)]
    (updated, gpre_b, act, gproj, message, vec), gmsgs = mlp_call(
        here, nodes, cotangent, parts, kinds, w_in, vectors[0], w_out, vectors[1], vectors[2]
    )
    factor = float(rows * n_row * n_col) ** -0.5
    weight_args = (here, nodes, message, act, gpre_b, gproj, cotangent, w_in, vec)
    if paired:
        halves = ((14, 15, 6, 11), (2, 3, 7, 10), (0, 1, 4, 5, 8, 9, 12, 13))
        grads = [gather_line(gmsgs[0])]
        kept, sent, direct = weight_call(factor, n_row, *weight_args, (grads[0][1], grads[0][2]))
        near_grads, token = tile_grad_call(
            *known, [grads[0][:4]], pieces, tile_local.shape, rows, (3, 2, 1), after=(grads[0][4],)
        )
        row_weights = scatter_weights(here, kept, sent, (token,))
        urgent, rest, even = back_call(
            *known, grads[0], turned, total, gathered, halves, (row_weights,)
        )
        urgent, rest = swap(urgent, 1), swap(rest, 1)
        arrived, first = reduce_square(here, even, urgent, rest, rows)
        grad_tiles, token = tile_grad_call(
            *known, grads, pieces, tile_local.shape, rows, (0,), near_grads, first
        )
        row_weights = sum_call(here, row_weights.shape[0], [(row_weights, 0)], after=(rest, *first))
        all_weights = level_weights(here, row_weights, (token,))
        joint = jnp.concatenate([all_weights] + [swap(all_weights, bits) for bits in (2, 4, 6)], axis=0)
        weights = unpack_call(here, joint, swap(joint, 1), width)
        grad_nodes = sum_call(here, rows, [(direct, 0), (even, 0), (rest, 0)], split=arrived)
    else:
        grads = [[lax.all_gather(gmsgs[0], "col", axis=0, tiled=True)]]
        weight_terms, direct = weight_call(factor, 1, *weight_args)
        weight_sums = lax.psum(weight_terms, ("row", "col"))
        weights = (
            weight_sums[: 2 * width],
            weight_sums[2 * width : 3 * width],
            weight_sums[3 * width : 3 * width + 3],
        )
        (terms,) = back_call(*known, grads[0], turned, total, gathered, (tuple(range(n_row)),))
        back = lax.psum_scatter(terms, "row", scatter_dimension=0, tiled=True)
        grad_nodes = sum_call(here, rows, [(direct, 0), (back, 0)])
        grad_tiles, _ = tile_grad_call(
            *known, grads, pieces, tile_local.shape, rows, tuple(range(n_col))
        )
    grad_tiles = grad_tiles.reshape(tiles.shape)
    return (updated, grad_nodes, grad_tiles, *weights)


def solution(mesh):
    placed = (
        P(("row", "col"), None),
        P("row", "col", None, None, None),
        P("row", "col", None),
        P("row", "col"),
        P(),
        P(),
        P(),
        P(),
        P(),
        P(("row", "col"), None),
    )
    return jax.shard_map(
        functools.partial(body, mesh.shape["row"], mesh.shape["col"]),
        mesh=mesh,
        in_specs=placed,
        out_specs=(
            P(("row", "col"), None),
            P(("row", "col"), None),
            P("row", "col", None, None, None),
            P(),
            P(),
            P(),
        ),
        check_vma=False,
    )
```

```python
import functools

import jax
import jax.numpy as jnp
from jax import lax
from jax.experimental import pallas as pl
from jax.experimental.pallas import tpu as pltpu
from jax.sharding import PartitionSpec as P

F32 = jnp.float32
BF16 = jnp.bfloat16
ANY = pl.BlockSpec(memory_space=pl.ANY)
HBM = pl.BlockSpec(memory_space=pltpu.HBM)
SMEM = pl.BlockSpec(memory_space=pltpu.SMEM)
VMEM = pl.BlockSpec(memory_space=pltpu.VMEM)
MIB = 1 << 20
TN = (((0,), (0,)), ((), ()))
NT = (((1,), (1,)), ((), ()))
SMALL = pl.CostEstimate(flops=1 << 20, bytes_accessed=1 << 16, transcendentals=0)


LIVE_STEP = 4
GRAD_PLAN = ((3, 0, None), (2, 1, None), (1, 2, "inner"), (1, 3, "outer"), (0, 4, "inner"), (0, 5, "outer"))
SWAP_ORDER = (0, 4, 2, 6, 1, 5, 3, 7)


def params(mib):
    return pltpu.CompilerParams(vmem_limit_bytes=mib * MIB)


def mm(a, b, dims=(((1,), (0,)), ((), ()))):
    return lax.dot_general(a, b, dims, preferred_element_type=F32)


def block_at(index, block):
    return pl.ds(pl.multiple_of(index * block, block), block)


class Place:
    def __init__(self, ref, paired=True, blocks=1):
        self.mine, self.level = lax.shift_right_logical(ref[0], 2), ref[0] & 3
        self.paired, self.blocks = paired, blocks

    def inner(self):
        return (self.level == 1) | (self.level == 2)

    def group(self, pick):
        if not self.paired:
            return pick
        low = self.level < 2
        choices = (jnp.where(low, 3, 0), jnp.where(low, 2, 1), self.level ^ 1, self.level)
        return choices[pick]

    def source(self, col):
        if not self.paired:
            return col
        shift = self.blocks.bit_length() - 1
        if 1 << shift == self.blocks:
            return col ^ lax.shift_left(self.mine, jnp.int32(shift))
        return (lax.div(col, self.blocks) ^ self.mine) * self.blocks + lax.rem(col, self.blocks)


def load_pieces(pieces, dst, sem, first):
    copies = []
    offset = 0
    for index, piece in enumerate(pieces):
        copy = pltpu.make_async_copy(
            piece, dst.at[pl.ds(offset, piece.shape[0])], sem.at[first + index]
        )
        copy.start()
        copies.append(copy)
        offset += piece.shape[0]
    return copies


def masked_tile(tile, live):
    return jnp.where(live, tile, jnp.zeros_like(tile))


def forward_kernel(outputs, n_pieces, paired, here, cols, *refs):
    pieces, tiles = refs[:n_pieces], refs[n_pieces]
    outs = refs[n_pieces + 1 : n_pieces + 1 + len(outputs)]
    nodes_v, tiles_v, sem, tile_sem = refs[n_pieces + 1 + len(outputs) :]
    rows = outs[0].shape[0] // len(outputs[0])
    slots, block = tiles.shape[1], tiles.shape[2]
    blocks = rows // block
    here = Place(here, paired, blocks)
    copies = load_pieces(pieces, nodes_v, sem, 0)
    places = [(pick, out, index) for out, picks in zip(outs, outputs) for index, pick in enumerate(picks)]
    tile_copies = []
    for place, (pick, _, _) in enumerate(places):
        copy = pltpu.make_async_copy(
            tiles.at[pl.ds(here.group(pick) * blocks, blocks)],
            tiles_v.at[pl.ds(place * blocks, blocks)],
            tile_sem.at[place],
        )
        copy.start()
        tile_copies.append(copy)
    for copy in copies:
        copy.wait()
    for place, (pick, out, index) in enumerate(places):
        tile_copies[place].wait()
        first = here.group(pick) * blocks

        def step(i, carry, first=first, out=out, index=index, place=place):
            row = first + i
            count = cols[slots, row]
            parts = []
            for pair in range(slots // 2):
                both = (2 * pair, 2 * pair + 1)
                tile = jnp.concatenate(
                    [masked_tile(tiles_v[place * blocks + i, slot], slot < count) for slot in both], axis=1
                )
                node = jnp.concatenate(
                    [nodes_v[block_at(here.source(cols[slot, row]), block)] for slot in both], axis=0
                )
                parts.append(mm(tile, node))
            value = parts[0]
            for part in parts[1:]:
                value = value + part
            out[block_at(index * blocks + i, block)] = value.astype(BF16)
            return carry

        lax.fori_loop(0, blocks, step, 0, unroll=4)


def forward_call(paired, here, cols, pieces, tiles, outputs, rows):
    width = pieces[0].shape[1]
    gathered = sum(piece.shape[0] for piece in pieces)
    slots, block = tiles.shape[1], tiles.shape[2]
    n_picks = sum(len(picks) for picks in outputs)
    return pl.pallas_call(
        functools.partial(forward_kernel, outputs, len(pieces), paired),
        out_shape=[jax.ShapeDtypeStruct((len(picks) * rows, width), BF16) for picks in outputs],
        in_specs=[SMEM] * 2 + [ANY] * len(pieces) + [HBM],
        out_specs=[VMEM] * len(outputs),
        scratch_shapes=[
            pltpu.VMEM((gathered, width), BF16),
            pltpu.VMEM((n_picks * (rows // block),) + tiles.shape[1:], BF16),
            pltpu.SemaphoreType.DMA((len(pieces),)),
            pltpu.SemaphoreType.DMA((n_picks,)),
        ],
        compiler_params=params(48),
        cost_estimate=SMALL,
        name="partial_messages",
    )(here, cols, *pieces, tiles)


def mlp_kernel(kinds, step, here, nodes, cot, *refs):
    n_parts = sum(len(chunk) for chunk in kinds)
    parts = refs[:n_parts]
    w_in, bias, w_out, gain, shift, updated, gpre_o, act_o, gproj_o, msg_o, vec = refs[
        n_parts : n_parts + 11
    ]
    gmsgs = refs[n_parts + 11 :]
    rows, width = nodes.shape
    inner = Place(here).inner()
    vec[...] = jnp.zeros_like(vec)
    for first in range(0, rows, step):
        where = slice(first, first + step)
        messages = []
        place = 0
        for chunk in kinds:
            total = None
            for kind in chunk:
                term = parts[place][where].astype(F32)
                place += 1
                if kind == "inner":
                    term = jnp.where(inner, term, 0.0)
                total = term if total is None else total + term
            messages.append(total.astype(BF16))
        message = jnp.concatenate(messages, axis=1) if len(messages) > 1 else messages[0]
        node = nodes[where]
        pre = mm(node, w_in[:width]) + mm(message, w_in[width:]) + bias[...]
        sig = 0.5 + 0.5 * jnp.tanh(0.5 * pre)
        act = (pre * sig).astype(BF16)
        proj = mm(act, w_out[...])
        mean = jnp.mean(proj, axis=-1, keepdims=True)
        var = jnp.mean((proj - mean) ** 2, axis=-1, keepdims=True)
        rstd = 1.0 / jnp.sqrt(var + 1e-05)
        normed = (proj - mean) * rstd
        updated[where] = (node.astype(F32) + normed * gain[...] + shift[...]).astype(BF16)
        grad_out = cot[where].astype(F32)
        gscaled = grad_out * gain[...]
        gproj = (
            (
                gscaled
                - jnp.mean(gscaled, axis=-1, keepdims=True)
                - normed * jnp.mean(gscaled * normed, axis=-1, keepdims=True)
            )
            * rstd
        ).astype(BF16)
        gact = mm(gproj, w_out[...], NT)
        gpre = gact * sig * (1.0 + pre * (1.0 - sig))
        gpre_b = gpre.astype(BF16)
        gmsg = mm(gpre_b, w_in[width:], NT).astype(BF16)
        part = width // len(gmsgs)
        for index, out in enumerate(gmsgs):
            out[where] = gmsg[:, index * part : (index + 1) * part]
        gpre_o[where] = gpre_b
        act_o[where] = act
        gproj_o[where] = gproj
        msg_o[where] = message
        vec[0:1] += jnp.sum(gpre, axis=0, keepdims=True)
        vec[1:2] += jnp.sum(grad_out * normed, axis=0, keepdims=True)
        vec[2:3] += jnp.sum(grad_out, axis=0, keepdims=True)


def mlp_call(here, nodes, cot, parts, kinds, w_in, bias, w_out, gain, shift):
    rows, width = nodes.shape
    step = min(rows, 512)

    flat = [term for chunk in parts for term in chunk]
    row_like = jax.ShapeDtypeStruct((rows, width), BF16)
    chunk_like = jax.ShapeDtypeStruct((rows, width // len(parts)), BF16)
    outs = [row_like] * 5 + [jax.ShapeDtypeStruct((8, width), F32)] + [chunk_like] * len(parts)
    weights = (w_in, bias, w_out, gain, shift)
    result = pl.pallas_call(
        functools.partial(mlp_kernel, kinds, step),
        out_shape=outs,
        in_specs=[SMEM] + [VMEM] * (2 + len(flat) + len(weights)),
        out_specs=[VMEM] * len(outs),
        compiler_params=params(40),
        cost_estimate=SMALL,
        name="mlp",
    )(here, nodes, cot, *flat, *weights)
    return result[:6], result[6:]


def weight_kernel(factor, pieces, step, n_after, here, nodes, msg, act, gpre, gproj, cot, w_in, vec, *refs):
    *outs, direct, grads = refs[n_after:]
    rows, width = nodes.shape
    for first in range(0, rows, step):
        where = slice(first, first + step)
        gpre_b = gpre[where]
        terms = (mm(nodes[where], gpre_b, TN), mm(msg[where], gpre_b, TN), mm(act[where], gproj[where], TN))
        for index, term in enumerate(terms):
            own = slice(index * width, (index + 1) * width)
            grads[own] = term if first == 0 else grads[own] + term
        direct[where] = cot[where].astype(F32) + mm(gpre_b, w_in[:width], NT)
    grads[3 * width : 3 * width + 8] = vec[...]
    grads[3 * width + 8 :] = jnp.zeros((grads.shape[0] - 3 * width - 8, width), F32)
    if pieces == 1:
        outs[0][...] = grads[: outs[0].shape[0]] * factor
    else:
        rows = grads.shape[0] // pieces
        for place, member in enumerate(SWAP_ORDER):
            where = pl.ds(pl.multiple_of((Place(here).mine ^ member) * rows, 8), rows)
            out, index = outs[2 * place // pieces], place % (pieces // 2)
            out[index * rows : (index + 1) * rows] = grads[where] * factor


def weight_call(factor, pieces, here, nodes, msg, act, gpre, gproj, cot, w_in, vec, after=()):
    rows, width = nodes.shape
    step = min(rows, 256)
    padded = (3 * width + width // 2, width)
    if pieces == 1:
        outs = [jax.ShapeDtypeStruct((3 * width + 8, width), F32)]
    else:
        outs = [jax.ShapeDtypeStruct((padded[0] // 2, width), F32)] * 2
    return pl.pallas_call(
        functools.partial(weight_kernel, factor, pieces, step, len(after)),
        out_shape=[*outs, jax.ShapeDtypeStruct((rows, width), F32)],
        in_specs=[SMEM] + [VMEM] * 8 + [ANY] * len(after),
        out_specs=[VMEM] * (len(outs) + 1),
        scratch_shapes=[pltpu.VMEM(padded, F32)],
        compiler_params=params(40),
        cost_estimate=SMALL,
        name="weight_grads",
    )(here, nodes, msg, act, gpre, gproj, cot, w_in, vec, *after)


def unpack_kernel(here, even, odd, w_in, w_out, vectors, grads):
    width = w_in.shape[1]
    rows = grads.shape[0] // 8
    for member in range(8):
        part = (even, odd)[member % 2]
        first = member // 2 * rows
        where = pl.ds(pl.multiple_of((Place(here).mine ^ member) * rows, 8), rows)
        grads[where] = part[first : first + rows].astype(F32)
    w_in[...] = grads[: 2 * width]
    w_out[...] = grads[2 * width : 3 * width]
    vectors[...] = grads[3 * width : 3 * width + 3]


def unpack_call(here, even, odd, width):
    shapes = ((2 * width, width), (width, width), (3, width))
    return pl.pallas_call(
        unpack_kernel,
        out_shape=[jax.ShapeDtypeStruct(shape, F32) for shape in shapes],
        in_specs=[SMEM, VMEM, VMEM],
        out_specs=[VMEM] * 3,
        scratch_shapes=[pltpu.VMEM((3 * width + width // 2, width), F32)],
        compiler_params=params(16),
        cost_estimate=SMALL,
        name="weight_unpack",
    )(here, even, odd)


def grad_jobs(rows, refs, dst, sem, here, groups=None):
    if len(refs) == 1:
        return [(None, pltpu.make_async_copy(refs[0], dst, sem.at[0]))]
    inner = here.inner()
    conditions = {None: None, "inner": inner, "outer": jnp.logical_not(inner)}
    jobs = []
    for group, index, kind in GRAD_PLAN:
        if groups is None:
            where = block_at(here.group(group), rows)
        elif group in groups:
            where = pl.ds(groups.index(group) * rows, rows)
        else:
            continue
        copy = pltpu.make_async_copy(refs[index], dst.at[where], sem.at[index])
        jobs.append((conditions[kind], copy))
    return jobs


def run_jobs(jobs, verb):
    for condition, copy in jobs:
        if condition is None:
            getattr(copy, verb)()
        else:
            pl.when(condition)(getattr(copy, verb))


def for_live(first, last, entry):
    def several(i, carry):
        for index in range(LIVE_STEP):
            entry(first + i * LIVE_STEP + index)
        return carry

    def one(i, carry):
        entry(i)
        return carry

    full = jnp.maximum(last - first, 0) // LIVE_STEP
    lax.fori_loop(0, full, several, 0)
    lax.fori_loop(first + full * LIVE_STEP, last, one, 0)


def turn_kernel(slots, cols, tiles, out, tiles_v, live, sem):
    copy = pltpu.make_async_copy(tiles, tiles_v, sem.at[0])
    copy.start()

    def collect(row, found):
        count = cols[slots, row]
        for slot in range(slots):
            live[found] = row * slots + slot
            found = found + (slot < count).astype(jnp.int32)
        return found

    found = lax.fori_loop(0, tiles.shape[0] // slots, collect, jnp.int32(0))
    copy.wait()

    def entry(place):
        out[place] = tiles_v[live[place]].T

    for_live(0, found, entry)


def turn_call(cols, tiles):
    row_blocks, slots, block = tiles.shape[:3]
    shape = (row_blocks * slots, block, block)
    return pl.pallas_call(
        functools.partial(turn_kernel, slots),
        out_shape=jax.ShapeDtypeStruct(shape, BF16),
        in_specs=[SMEM, HBM],
        out_specs=VMEM,
        scratch_shapes=[
            pltpu.VMEM(shape, BF16),
            pltpu.SMEM((row_blocks * slots + 8,), jnp.int32),
            pltpu.SemaphoreType.DMA((1,)),
        ],
        compiler_params=params(16 if row_blocks <= 32 else 32),
        cost_estimate=SMALL,
        name="turned_tiles",
    )(cols, tiles.reshape(shape))


def back_kernel(rows, slots, n_grads, n_after, out_pieces, paired, here, cols, *refs):
    grads, tiles = refs[:n_grads], refs[n_grads]
    refs = refs[n_grads + 1 + n_after :]
    outs = refs[: len(out_pieces)]
    grad_v, acc, live, source, sem = refs[len(out_pieces) :]
    n_tiles, block = tiles.shape[:2]
    here = Place(here, paired, rows // block)
    jobs = grad_jobs(rows, grads, grad_v, sem, here)
    run_jobs(jobs, "start")

    def collect(row, found):
        count = cols[slots, row]
        for slot in range(slots):
            live[found] = row
            source[found] = here.source(cols[slot, row])
            found = found + (slot < count).astype(jnp.int32)
        return found

    found = lax.fori_loop(0, n_tiles // slots, collect, jnp.int32(0))
    acc[...] = jnp.zeros_like(acc)
    run_jobs(jobs, "wait")

    def entry(place):
        term = mm(tiles[place], grad_v[block_at(live[place], block)])
        acc[block_at(source[place], block)] += term

    for_live(0, found, entry)
    piece = acc.shape[0] // sum(len(members) for members in out_pieces)
    for out, members in zip(outs, out_pieces):
        for index, member in enumerate(members):
            out[pl.ds(index * piece, piece)] = acc[pl.ds(member * piece, piece)].astype(BF16)


def back_call(paired, here, cols, grads, tiles, total, gathered, out_pieces, after=()):
    rows, width = grads[0].shape
    rows = total if len(grads) == 1 else rows
    n_tiles, block = tiles.shape[:2]
    slots = cols.shape[0] - 1
    piece = gathered // sum(len(members) for members in out_pieces)
    return pl.pallas_call(
        functools.partial(back_kernel, rows, slots, len(grads), len(after), out_pieces, paired),
        out_shape=[jax.ShapeDtypeStruct((len(m) * piece, width), BF16) for m in out_pieces],
        in_specs=[SMEM] * 2 + [ANY] * len(grads) + [VMEM] + [ANY] * len(after),
        out_specs=[VMEM] * len(out_pieces),
        scratch_shapes=[
            pltpu.VMEM((total, width), BF16),
            pltpu.VMEM((gathered, width), F32),
            pltpu.SMEM((n_tiles + 8,), jnp.int32),
            pltpu.SMEM((n_tiles + 8,), jnp.int32),
            pltpu.SemaphoreType.DMA((len(grads),)),
        ],
        compiler_params=params(28 if gathered <= 8192 else 56),
        cost_estimate=SMALL,
        name="back_terms",
    )(here, cols, *grads, tiles, *after)


def tile_grad_kernel(
    rows, slots, n_grads, n_pieces, n_chunks, n_after, groups, paired, here, cols, *refs
):
    grads = refs[: n_grads * n_chunks]
    refs = refs[n_grads * n_chunks :]
    pieces = refs[: n_pieces * n_chunks]
    out, token, grad_v, nodes_v, tiles_v, live, source, sem, piece_sem, out_sem = refs[n_pieces * n_chunks + n_after :]
    token[...] = jnp.zeros_like(token)
    block = out.shape[1]
    width = nodes_v.shape[1]
    part = width // n_chunks
    scale = float(width) ** -0.5
    blocks = grad_v.shape[0] // (block * len(groups))
    here = Place(here, paired, blocks)
    jobs, copies = [], []
    for chunk in range(n_chunks):
        columns = pl.ds(chunk * part, part)
        jobs += grad_jobs(
            rows,
            grads[chunk * n_grads : (chunk + 1) * n_grads],
            grad_v.at[:, columns],
            sem.at[chunk],
            here,
            groups,
        )
        copies += load_pieces(
            pieces[chunk * n_pieces : (chunk + 1) * n_pieces],
            nodes_v.at[:, columns],
            piece_sem.at[chunk],
            0,
        )
    run_jobs(jobs, "start")
    tiles_v[...] = jnp.zeros_like(tiles_v)
    found = jnp.int32(0)
    for index, group in enumerate(groups):
        first = here.group(group) * blocks

        def collect(i, found, first=first, index=index):
            row = first + i
            count = cols[slots, row]
            for slot in range(slots):
                live[found] = (index * blocks + i) * slots + slot
                source[found] = here.source(cols[slot, row])
                found = found + (slot < count).astype(jnp.int32)
            return found

        found = lax.fori_loop(0, blocks, collect, found)
    run_jobs(jobs, "wait")
    for copy in copies:
        copy.wait()

    def entry(place):
        tile_index = live[place]
        grad = grad_v[block_at(tile_index // slots, block)]
        node = nodes_v[block_at(source[place], block)]
        tiles_v[tile_index] = (mm(grad, node, NT) * scale).astype(BF16)

    for_live(0, found, entry)
    size = blocks * slots
    copies = []
    for index, group in enumerate(groups):
        copy = pltpu.make_async_copy(
            tiles_v.at[pl.ds(index * size, size)],
            out.at[pl.ds(here.group(group) * size, size)],
            out_sem.at[index],
        )
        copy.start()
        copies.append(copy)
    for copy in copies:
        copy.wait()


def tile_grad_call(paired, here, cols, grads, pieces, shape, rows, groups, base=None, after=()):
    row_blocks, slots, block = shape[:3]
    chunks = len(grads)
    width = grads[0][0].shape[1] * chunks
    gathered = sum(piece.shape[0] for piece in pieces[0])
    flat = [a for chunk in grads for a in chunk] + [a for chunk in pieces for a in chunk]
    after = after if base is None else (base,) + tuple(after)
    entries = len(groups) * rows // block * slots
    return pl.pallas_call(
        functools.partial(
            tile_grad_kernel, rows, slots, len(grads[0]), len(pieces[0]), chunks, len(after), groups, paired
        ),
        out_shape=[
            jax.ShapeDtypeStruct((row_blocks * slots, block, block), BF16),
            jax.ShapeDtypeStruct((8, 128), F32),
        ],
        in_specs=[SMEM] * 2 + [ANY] * (len(flat) + len(after)),
        out_specs=[ANY, VMEM],
        input_output_aliases={} if base is None else {2 + len(flat): 0},
        scratch_shapes=[
            pltpu.VMEM((len(groups) * rows, width), BF16),
            pltpu.VMEM((gathered, width), BF16),
            pltpu.VMEM((entries, block, block), BF16),
            pltpu.SMEM((entries + 8,), jnp.int32),
            pltpu.SMEM((entries + 8,), jnp.int32),
            pltpu.SemaphoreType.DMA((chunks, len(grads[0]))),
            pltpu.SemaphoreType.DMA((chunks, len(pieces[0]))),
            pltpu.SemaphoreType.DMA((len(groups),)),
        ],
        compiler_params=params(16 if gathered <= 8192 else 40),
        cost_estimate=SMALL,
        name="tile_grads",
    )(here, cols, *flat, *after)


def swap(value, bit):
    return lax.ppermute(value, "row", [(i, i ^ bit) for i in range(8)])


def outer_swap(value):
    return lax.ppermute(value, "col", [(0, 1), (1, 0), (2, 3), (3, 2)])


def turn(value, by):
    return lax.ppermute(value, "col", [(i, (i + by) % 4) for i in range(4)])


def inner_swap(value):
    pairs = []
    for row in range(8):
        for col in range(4):
            partner = (row, 3 - col) if col in (1, 2) else (row ^ 1, col)
            pairs.append((row * 4 + col, partner[0] * 4 + partner[1]))
    return lax.ppermute(value, ("row", "col"), pairs)


def gather_square(nodes):
    half = nodes.shape[0] // 2
    lower, upper = nodes[:half], nodes[half:]
    y_lower, x_upper = swap(lower, 4), swap(upper, 2)
    x_lower, y_upper = swap(lower, 2), swap(upper, 4)
    d_lower, d_upper = swap(y_lower, 2), swap(x_upper, 4)
    pieces = [lower, upper, swap(nodes, 1)]
    for pair in ((x_lower, x_upper), (y_lower, y_upper), (d_lower, d_upper)):
        pieces += [*pair, *(swap(piece, 1) for piece in pair)]
    return pieces


def reduce_square(here, even, urgent, rest, rows):
    half = rows // 2
    first = [
        sum_call(here, rows, [(even, (6, 2)), (urgent, (0, 2))]),
        sum_call(here, rows, [(even, (7, 5)), (urgent, (1, 3))]),
    ]
    x_first, y_first = swap(first[0], 2), swap(first[1], 4)
    y_lower = swap(sum_call(here, half, [(even, 4), (rest, 3), (x_first, 0)]), 4)
    x_upper = swap(sum_call(here, half, [(even, 3), (rest, 2), (y_first, 0)]), 2)
    return [((x_first, 1), (x_upper, 0)), ((y_lower, 0), (y_first, 1))], first


def sum_kernel(n_terms, n_gated, n_split, *refs):
    inner, refs = Place(refs[0]).inner(), refs[1:]
    total = None
    for index, ref in enumerate(refs[: n_terms + n_gated]):
        term = ref[...].astype(F32)
        if index >= n_terms:
            term = jnp.where(inner, term, 0.0)
        total = term if total is None else total + term
    for index in range(n_split):
        first, second = refs[n_terms + n_gated + 2 * index :][:2]
        early = pl.program_id(0) < pl.num_programs(0) // 2
        total = total + jnp.where(early, first[...], second[...]).astype(F32)
    refs[-1][...] = total.astype(refs[-1].dtype)


def sum_call(here, rows, terms, gated=(), split=(), dtype=BF16, after=()):
    both = [*terms, *gated]
    width = both[0][0].shape[1]
    step = min(rows, 512)
    steps = rows // step
    half = steps // 2

    def spec(piece):
        if isinstance(piece, int):
            return pl.BlockSpec((step, width), lambda i: (piece * steps + i, 0))
        lower, upper = piece
        return pl.BlockSpec(
            (step, width), lambda i: (jnp.where(i < half, lower * half + i, (upper - 1) * half + i), 0)
        )

    def early(piece):
        return pl.BlockSpec((step, width), lambda i: (piece * half + jnp.minimum(i, half - 1), 0))

    def late(piece):
        return pl.BlockSpec((step, width), lambda i: (piece * half + jnp.maximum(i - half, 0), 0))

    return pl.pallas_call(
        functools.partial(sum_kernel, len(terms), len(gated), len(split)),
        grid=(steps,),
        out_shape=jax.ShapeDtypeStruct((rows, width), dtype),
        in_specs=[SMEM]
        + [spec(piece) for _, piece in both]
        + [spec_of(piece) for pair in split for spec_of, (_, piece) in zip((early, late), pair)]
        + [ANY] * len(after),
        out_specs=pl.BlockSpec((step, width), lambda i: (i, 0)),
        compiler_params=params(16),
        cost_estimate=SMALL,
        name="sum_terms",
    )(here, *(array for array, _ in both), *(array for pair in split for array, _ in pair), *after)


def scatter_weights(here, kept, sent, after):
    rows = kept.shape[0] // 4
    received = swap(sent, 1)
    pieces = [
        sum_call(here, rows, [(kept, place), (received, place)], dtype=F32) for place in range(4)
    ]
    terms = [pieces[0]] + [swap(piece, bits) for piece, bits in zip(pieces[1:], SWAP_ORDER[1:4])]
    return sum_call(here, rows, [(term, 0) for term in terms], after=after)


def level_weights(here, value, after):
    terms = [value] + [turn(value, by) for by in (1, 2, 3)]
    return sum_call(here, value.shape[0], [(term, 0) for term in terms], after=after)


def reduce_line(here, far, near, pair, own, after):
    rows = own.shape[0]
    far_sum = inner_swap(sum_call(here, rows, [(far, 0), (outer_swap(far), 0)], after=after))
    near_sum = inner_swap(sum_call(here, rows, [(near, 0), (outer_swap(near), 0)]))
    pair_in = outer_swap(sum_call(here, rows, [(pair, 0)], [(far_sum, 0)]))
    return own, pair_in, near_sum


def gather_line(own):
    pair = outer_swap(own)
    near_inner = inner_swap(own)
    far_inner = inner_swap(pair)
    near_outer = outer_swap(near_inner)
    far_outer = outer_swap(far_inner)
    return [own, pair, near_inner, near_outer, far_inner, far_outer]


def body(n_row, n_col, nodes, tiles, tile_col, tile_count, w_in, bias_in, w_out, ln_gain, ln_shift, cotangent):
    rows, width = nodes.shape
    row_blocks, _, slots, block = tiles.shape[:4]
    tile_local = tiles.reshape(row_blocks, slots, block, block)
    table = jnp.concatenate([tile_col.reshape(row_blocks, slots).T, tile_count.reshape(1, row_blocks)], axis=0)
    gathered, total = n_row * rows, n_col * rows
    paired = n_row == 8 and n_col == 4
    here = lax.axis_index(("row", "col")).astype(jnp.int32).reshape(1)
    known = (paired, here, table)
    turned = turn_call(table, tile_local)
    if paired:
        pieces = [gather_square(nodes)]
        (far,) = forward_call(*known, pieces[0], tile_local, ((0,),), rows)
        (near,) = forward_call(*known, pieces[0], tile_local, ((1,),), rows)
        pair, own = forward_call(*known, pieces[0], tile_local, ((2,), (3,)), rows)
        parts = [reduce_line(here, far, near, pair, own, (turned,))]
        kinds = [("all", "all", "inner")]
    else:
        pieces = [[lax.all_gather(nodes, "row", axis=0, tiled=True)]]
        (partial,) = forward_call(*known, pieces[0], tile_local, (tuple(range(n_col)),), rows)
        parts = [[lax.psum_scatter(partial, "col", scatter_dimension=0, tiled=True)]]
        kinds = [("all",)]
    vectors = [v.reshape(1, width) for v in (bias_in, ln_gain, ln_shift)]
    (updated, gpre_b, act, gproj, message, vec), gmsgs = mlp_call(
        here, nodes, cotangent, parts, kinds, w_in, vectors[0], w_out, vectors[1], vectors[2]
    )
    factor = float(rows * n_row * n_col) ** -0.5
    weight_args = (here, nodes, message, act, gpre_b, gproj, cotangent, w_in, vec)
    if paired:
        halves = ((14, 15, 6, 11), (2, 3, 7, 10), (0, 1, 4, 5, 8, 9, 12, 13))
        grads = [gather_line(gmsgs[0])]
        kept, sent, direct = weight_call(factor, n_row, *weight_args, (grads[0][1], grads[0][2]))
        near_grads, token = tile_grad_call(
            *known, [grads[0][:4]], pieces, tile_local.shape, rows, (3, 2, 1), after=(grads[0][4],)
        )
        row_weights = scatter_weights(here, kept, sent, (token,))
        urgent, rest, even = back_call(
            *known, grads[0], turned, total, gathered, halves, (row_weights,)
        )
        urgent, rest = swap(urgent, 1), swap(rest, 1)
        arrived, first = reduce_square(here, even, urgent, rest, rows)
        grad_tiles, _ = tile_grad_call(
            *known, grads, pieces, tile_local.shape, rows, (0,), near_grads, first
        )
        row_weights = sum_call(here, row_weights.shape[0], [(row_weights, 0)], after=(rest, *first))
        all_weights = level_weights(here, row_weights, first)
        joint = jnp.concatenate([all_weights] + [swap(all_weights, bits) for bits in (2, 4, 6)], axis=0)
        weights = unpack_call(here, joint, swap(joint, 1), width)
        grad_nodes = sum_call(here, rows, [(direct, 0), (even, 0), (rest, 0)], split=arrived)
    else:
        grads = [[lax.all_gather(gmsgs[0], "col", axis=0, tiled=True)]]
        weight_terms, direct = weight_call(factor, 1, *weight_args)
        weight_sums = lax.psum(weight_terms, ("row", "col"))
        weights = (
            weight_sums[: 2 * width],
            weight_sums[2 * width : 3 * width],
            weight_sums[3 * width : 3 * width + 3],
        )
        (terms,) = back_call(*known, grads[0], turned, total, gathered, (tuple(range(n_row)),))
        back = lax.psum_scatter(terms, "row", scatter_dimension=0, tiled=True)
        grad_nodes = sum_call(here, rows, [(direct, 0), (back, 0)])
        grad_tiles, _ = tile_grad_call(
            *known, grads, pieces, tile_local.shape, rows, tuple(range(n_col))
        )
    grad_tiles = grad_tiles.reshape(tiles.shape)
    return (updated, grad_nodes, grad_tiles, *weights)


def solution(mesh):
    placed = (
        P(("row", "col"), None),
        P("row", "col", None, None, None),
        P("row", "col", None),
        P("row", "col"),
        P(),
        P(),
        P(),
        P(),
        P(),
        P(("row", "col"), None),
    )
    return jax.shard_map(
        functools.partial(body, mesh.shape["row"], mesh.shape["col"]),
        mesh=mesh,
        in_specs=placed,
        out_specs=(
            P(("row", "col"), None),
            P(("row", "col"), None),
            P("row", "col", None, None, None),
            P(),
            P(),
            P(),
        ),
        check_vma=False,
    )
```

```python
import functools

import jax
import jax.numpy as jnp
from jax import lax
from jax.experimental import pallas as pl
from jax.experimental.pallas import tpu as pltpu
from jax.sharding import PartitionSpec as P

F32 = jnp.float32
BF16 = jnp.bfloat16
ANY = pl.BlockSpec(memory_space=pl.ANY)
HBM = pl.BlockSpec(memory_space=pltpu.HBM)
SMEM = pl.BlockSpec(memory_space=pltpu.SMEM)
VMEM = pl.BlockSpec(memory_space=pltpu.VMEM)
MIB = 1 << 20
TN = (((0,), (0,)), ((), ()))
NT = (((1,), (1,)), ((), ()))
SMALL = pl.CostEstimate(flops=1 << 20, bytes_accessed=1 << 16, transcendentals=0)


LIVE_STEPS = (8, 2, 1)
GRAD_PLAN = ((3, 0, None), (2, 1, None), (1, 2, "inner"), (1, 3, "outer"), (0, 4, "inner"), (0, 5, "outer"))
SWAP_ORDER = (0, 4, 2, 6, 1, 5, 3, 7)


def params(mib):
    return pltpu.CompilerParams(vmem_limit_bytes=mib * MIB)


def mm(a, b, dims=(((1,), (0,)), ((), ()))):
    return lax.dot_general(a, b, dims, preferred_element_type=F32)


def block_at(index, block):
    return pl.ds(pl.multiple_of(index * block, block), block)


class Place:
    def __init__(self, ref, paired=True, blocks=1):
        self.mine, self.level = lax.shift_right_logical(ref[0], 2), ref[0] & 3
        self.paired, self.blocks = paired, blocks

    def inner(self):
        return (self.level == 1) | (self.level == 2)

    def group(self, pick):
        if not self.paired:
            return pick
        low = self.level < 2
        choices = (jnp.where(low, 3, 0), jnp.where(low, 2, 1), self.level ^ 1, self.level)
        return choices[pick]

    def source(self, col):
        if not self.paired:
            return col
        shift = self.blocks.bit_length() - 1
        if 1 << shift == self.blocks:
            return col ^ lax.shift_left(self.mine, jnp.int32(shift))
        return (lax.div(col, self.blocks) ^ self.mine) * self.blocks + lax.rem(col, self.blocks)


def load_pieces(pieces, dst, sem, first):
    copies = []
    offset = 0
    for index, piece in enumerate(pieces):
        copy = pltpu.make_async_copy(
            piece, dst.at[pl.ds(offset, piece.shape[0])], sem.at[first + index]
        )
        copy.start()
        copies.append(copy)
        offset += piece.shape[0]
    return copies


def masked_tile(tile, live):
    return jnp.where(live, tile, jnp.zeros_like(tile))


def forward_kernel(outputs, n_pieces, paired, here, cols, *refs):
    pieces, tiles = refs[:n_pieces], refs[n_pieces]
    outs = refs[n_pieces + 1 : n_pieces + 1 + len(outputs)]
    nodes_v, tiles_v, sem, tile_sem = refs[n_pieces + 1 + len(outputs) :]
    rows = outs[0].shape[0] // len(outputs[0])
    slots, block = tiles.shape[1], tiles.shape[2]
    blocks = rows // block
    here = Place(here, paired, blocks)
    copies = load_pieces(pieces, nodes_v, sem, 0)
    places = [(pick, out, index) for out, picks in zip(outs, outputs) for index, pick in enumerate(picks)]
    tile_copies = []
    for place, (pick, _, _) in enumerate(places):
        copy = pltpu.make_async_copy(
            tiles.at[pl.ds(here.group(pick) * blocks, blocks)],
            tiles_v.at[pl.ds(place * blocks, blocks)],
            tile_sem.at[place],
        )
        copy.start()
        tile_copies.append(copy)
    for copy in copies:
        copy.wait()
    for place, (pick, out, index) in enumerate(places):
        tile_copies[place].wait()
        first = here.group(pick) * blocks

        def step(i, carry, first=first, out=out, index=index, place=place):
            row = first + i
            count = cols[slots, row]
            parts = []
            for pair in range(slots // 2):
                both = (2 * pair, 2 * pair + 1)
                tile = jnp.concatenate(
                    [masked_tile(tiles_v[place * blocks + i, slot], slot < count) for slot in both], axis=1
                )
                node = jnp.concatenate(
                    [nodes_v[block_at(here.source(cols[slot, row]), block)] for slot in both], axis=0
                )
                parts.append(mm(tile, node))
            value = parts[0]
            for part in parts[1:]:
                value = value + part
            out[block_at(index * blocks + i, block)] = value.astype(BF16)
            return carry

        lax.fori_loop(0, blocks, step, 0, unroll=4)


def forward_call(paired, here, cols, pieces, tiles, outputs, rows):
    width = pieces[0].shape[1]
    gathered = sum(piece.shape[0] for piece in pieces)
    slots, block = tiles.shape[1], tiles.shape[2]
    n_picks = sum(len(picks) for picks in outputs)
    return pl.pallas_call(
        functools.partial(forward_kernel, outputs, len(pieces), paired),
        out_shape=[jax.ShapeDtypeStruct((len(picks) * rows, width), BF16) for picks in outputs],
        in_specs=[SMEM] * 2 + [ANY] * len(pieces) + [HBM],
        out_specs=[VMEM] * len(outputs),
        scratch_shapes=[
            pltpu.VMEM((gathered, width), BF16),
            pltpu.VMEM((n_picks * (rows // block),) + tiles.shape[1:], BF16),
            pltpu.SemaphoreType.DMA((len(pieces),)),
            pltpu.SemaphoreType.DMA((n_picks,)),
        ],
        compiler_params=params(48),
        cost_estimate=SMALL,
        name="partial_messages",
    )(here, cols, *pieces, tiles)


def mlp_kernel(kinds, step, here, nodes, cot, *refs):
    n_parts = sum(len(chunk) for chunk in kinds)
    parts = refs[:n_parts]
    w_in, bias, w_out, gain, shift, updated, gpre_o, act_o, gproj_o, msg_o, vec = refs[
        n_parts : n_parts + 11
    ]
    gmsgs = refs[n_parts + 11 :]
    rows, width = nodes.shape
    inner = Place(here).inner()
    vec[...] = jnp.zeros_like(vec)
    for first in range(0, rows, step):
        where = slice(first, first + step)
        messages = []
        place = 0
        for chunk in kinds:
            total = None
            for kind in chunk:
                term = parts[place][where].astype(F32)
                place += 1
                if kind == "inner":
                    term = jnp.where(inner, term, 0.0)
                total = term if total is None else total + term
            messages.append(total.astype(BF16))
        message = jnp.concatenate(messages, axis=1) if len(messages) > 1 else messages[0]
        node = nodes[where]
        pre = mm(node, w_in[:width]) + mm(message, w_in[width:]) + bias[...]
        sig = 0.5 + 0.5 * jnp.tanh(0.5 * pre)
        act = (pre * sig).astype(BF16)
        proj = mm(act, w_out[...])
        mean = jnp.mean(proj, axis=-1, keepdims=True)
        var = jnp.mean((proj - mean) ** 2, axis=-1, keepdims=True)
        rstd = 1.0 / jnp.sqrt(var + 1e-05)
        normed = (proj - mean) * rstd
        updated[where] = (node.astype(F32) + normed * gain[...] + shift[...]).astype(BF16)
        grad_out = cot[where].astype(F32)
        gscaled = grad_out * gain[...]
        gproj = (
            (
                gscaled
                - jnp.mean(gscaled, axis=-1, keepdims=True)
                - normed * jnp.mean(gscaled * normed, axis=-1, keepdims=True)
            )
            * rstd
        ).astype(BF16)
        gact = mm(gproj, w_out[...], NT)
        gpre = gact * sig * (1.0 + pre * (1.0 - sig))
        gpre_b = gpre.astype(BF16)
        gmsg = mm(gpre_b, w_in[width:], NT).astype(BF16)
        part = width // len(gmsgs)
        for index, out in enumerate(gmsgs):
            out[where] = gmsg[:, index * part : (index + 1) * part]
        gpre_o[where] = gpre_b
        act_o[where] = act
        gproj_o[where] = gproj
        msg_o[where] = message
        vec[0:1] += jnp.sum(gpre, axis=0, keepdims=True)
        vec[1:2] += jnp.sum(grad_out * normed, axis=0, keepdims=True)
        vec[2:3] += jnp.sum(grad_out, axis=0, keepdims=True)


def mlp_call(here, nodes, cot, parts, kinds, w_in, bias, w_out, gain, shift):
    rows, width = nodes.shape
    step = min(rows, 512)

    flat = [term for chunk in parts for term in chunk]
    row_like = jax.ShapeDtypeStruct((rows, width), BF16)
    chunk_like = jax.ShapeDtypeStruct((rows, width // len(parts)), BF16)
    outs = [row_like] * 5 + [jax.ShapeDtypeStruct((8, width), F32)] + [chunk_like] * len(parts)
    weights = (w_in, bias, w_out, gain, shift)
    result = pl.pallas_call(
        functools.partial(mlp_kernel, kinds, step),
        out_shape=outs,
        in_specs=[SMEM] + [VMEM] * (2 + len(flat) + len(weights)),
        out_specs=[VMEM] * len(outs),
        compiler_params=params(40),
        cost_estimate=SMALL,
        name="mlp",
    )(here, nodes, cot, *flat, *weights)
    return result[:6], result[6:]


def weight_kernel(factor, pieces, step, n_after, here, nodes, msg, act, gpre, gproj, cot, w_in, vec, *refs):
    *outs, direct, grads = refs[n_after:]
    rows, width = nodes.shape
    for first in range(0, rows, step):
        where = slice(first, first + step)
        gpre_b = gpre[where]
        terms = (mm(nodes[where], gpre_b, TN), mm(msg[where], gpre_b, TN), mm(act[where], gproj[where], TN))
        for index, term in enumerate(terms):
            own = slice(index * width, (index + 1) * width)
            grads[own] = term if first == 0 else grads[own] + term
        direct[where] = cot[where].astype(F32) + mm(gpre_b, w_in[:width], NT)
    grads[3 * width : 3 * width + 8] = vec[...]
    grads[3 * width + 8 :] = jnp.zeros((grads.shape[0] - 3 * width - 8, width), F32)
    if pieces == 1:
        outs[0][...] = grads[: outs[0].shape[0]] * factor
    else:
        rows = grads.shape[0] // pieces
        for place, member in enumerate(SWAP_ORDER):
            where = pl.ds(pl.multiple_of((Place(here).mine ^ member) * rows, 8), rows)
            out, index = outs[2 * place // pieces], place % (pieces // 2)
            out[index * rows : (index + 1) * rows] = grads[where] * factor


def weight_call(factor, pieces, here, nodes, msg, act, gpre, gproj, cot, w_in, vec, after=()):
    rows, width = nodes.shape
    step = min(rows, 256)
    padded = (3 * width + width // 2, width)
    if pieces == 1:
        outs = [jax.ShapeDtypeStruct((3 * width + 8, width), F32)]
    else:
        outs = [jax.ShapeDtypeStruct((padded[0] // 2, width), F32)] * 2
    return pl.pallas_call(
        functools.partial(weight_kernel, factor, pieces, step, len(after)),
        out_shape=[*outs, jax.ShapeDtypeStruct((rows, width), F32)],
        in_specs=[SMEM] + [VMEM] * 8 + [ANY] * len(after),
        out_specs=[VMEM] * (len(outs) + 1),
        scratch_shapes=[pltpu.VMEM(padded, F32)],
        compiler_params=params(40),
        cost_estimate=SMALL,
        name="weight_grads",
    )(here, nodes, msg, act, gpre, gproj, cot, w_in, vec, *after)


def unpack_kernel(here, even, odd, w_in, w_out, vectors, grads):
    width = w_in.shape[1]
    rows = grads.shape[0] // 8
    for member in range(8):
        part = (even, odd)[member % 2]
        first = member // 2 * rows
        where = pl.ds(pl.multiple_of((Place(here).mine ^ member) * rows, 8), rows)
        grads[where] = part[first : first + rows].astype(F32)
    w_in[...] = grads[: 2 * width]
    w_out[...] = grads[2 * width : 3 * width]
    vectors[...] = grads[3 * width : 3 * width + 3]


def unpack_call(here, even, odd, width):
    shapes = ((2 * width, width), (width, width), (3, width))
    return pl.pallas_call(
        unpack_kernel,
        out_shape=[jax.ShapeDtypeStruct(shape, F32) for shape in shapes],
        in_specs=[SMEM, VMEM, VMEM],
        out_specs=[VMEM] * 3,
        scratch_shapes=[pltpu.VMEM((3 * width + width // 2, width), F32)],
        compiler_params=params(16),
        cost_estimate=SMALL,
        name="weight_unpack",
    )(here, even, odd)


def grad_jobs(rows, refs, dst, sem, here, groups=None):
    if len(refs) == 1:
        return [(None, pltpu.make_async_copy(refs[0], dst, sem.at[0]))]
    inner = here.inner()
    conditions = {None: None, "inner": inner, "outer": jnp.logical_not(inner)}
    jobs = []
    for group, index, kind in GRAD_PLAN:
        if groups is None:
            where = block_at(here.group(group), rows)
        elif group in groups:
            where = pl.ds(groups.index(group) * rows, rows)
        else:
            continue
        copy = pltpu.make_async_copy(refs[index], dst.at[where], sem.at[index])
        jobs.append((conditions[kind], copy))
    return jobs


def run_jobs(jobs, verb):
    for condition, copy in jobs:
        if condition is None:
            getattr(copy, verb)()
        else:
            pl.when(condition)(getattr(copy, verb))


def for_live(first, last, entry):
    def several(many, start):
        def run(i, carry):
            for index in range(many):
                entry(start + i * many + index)
            return carry

        return run

    for many in LIVE_STEPS:
        times = jnp.maximum(last - first, 0) // many
        lax.fori_loop(0, times, several(many, first), 0)
        first = first + times * many


def turn_kernel(slots, cols, tiles, out, tiles_v, live, sem):
    copy = pltpu.make_async_copy(tiles, tiles_v, sem.at[0])
    copy.start()

    def collect(row, found):
        count = cols[slots, row]
        for slot in range(slots):
            live[found] = row * slots + slot
            found = found + (slot < count).astype(jnp.int32)
        return found

    found = lax.fori_loop(0, tiles.shape[0] // slots, collect, jnp.int32(0))
    copy.wait()

    def entry(place):
        out[place] = tiles_v[live[place]].T

    for_live(0, found, entry)


def turn_call(cols, tiles):
    row_blocks, slots, block = tiles.shape[:3]
    shape = (row_blocks * slots, block, block)
    return pl.pallas_call(
        functools.partial(turn_kernel, slots),
        out_shape=jax.ShapeDtypeStruct(shape, BF16),
        in_specs=[SMEM, HBM],
        out_specs=VMEM,
        scratch_shapes=[
            pltpu.VMEM(shape, BF16),
            pltpu.SMEM((row_blocks * slots + 8,), jnp.int32),
            pltpu.SemaphoreType.DMA((1,)),
        ],
        compiler_params=params(16 if row_blocks <= 32 else 32),
        cost_estimate=SMALL,
        name="turned_tiles",
    )(cols, tiles.reshape(shape))


def back_kernel(rows, slots, n_grads, n_after, out_pieces, paired, here, cols, *refs):
    grads, tiles = refs[:n_grads], refs[n_grads]
    refs = refs[n_grads + 1 + n_after :]
    outs = refs[: len(out_pieces)]
    grad_v, acc, live, source, sem = refs[len(out_pieces) :]
    n_tiles, block = tiles.shape[:2]
    here = Place(here, paired, rows // block)
    jobs = grad_jobs(rows, grads, grad_v, sem, here)
    run_jobs(jobs, "start")

    def collect(row, found):
        count = cols[slots, row]
        for slot in range(slots):
            live[found] = row
            source[found] = here.source(cols[slot, row])
            found = found + (slot < count).astype(jnp.int32)
        return found

    found = lax.fori_loop(0, n_tiles // slots, collect, jnp.int32(0))
    acc[...] = jnp.zeros_like(acc)
    run_jobs(jobs, "wait")

    def entry(place):
        term = mm(tiles[place], grad_v[block_at(live[place], block)])
        acc[block_at(source[place], block)] += term

    for_live(0, found, entry)
    piece = acc.shape[0] // sum(len(members) for members in out_pieces)
    for out, members in zip(outs, out_pieces):
        for index, member in enumerate(members):
            out[pl.ds(index * piece, piece)] = acc[pl.ds(member * piece, piece)].astype(BF16)


def back_call(paired, here, cols, grads, tiles, total, gathered, out_pieces, after=()):
    rows, width = grads[0].shape
    rows = total if len(grads) == 1 else rows
    n_tiles, block = tiles.shape[:2]
    slots = cols.shape[0] - 1
    piece = gathered // sum(len(members) for members in out_pieces)
    return pl.pallas_call(
        functools.partial(back_kernel, rows, slots, len(grads), len(after), out_pieces, paired),
        out_shape=[jax.ShapeDtypeStruct((len(m) * piece, width), BF16) for m in out_pieces],
        in_specs=[SMEM] * 2 + [ANY] * len(grads) + [VMEM] + [ANY] * len(after),
        out_specs=[VMEM] * len(out_pieces),
        scratch_shapes=[
            pltpu.VMEM((total, width), BF16),
            pltpu.VMEM((gathered, width), F32),
            pltpu.SMEM((n_tiles + 8,), jnp.int32),
            pltpu.SMEM((n_tiles + 8,), jnp.int32),
            pltpu.SemaphoreType.DMA((len(grads),)),
        ],
        compiler_params=params(28 if gathered <= 8192 else 56),
        cost_estimate=SMALL,
        name="back_terms",
    )(here, cols, *grads, tiles, *after)


def tile_grad_kernel(
    rows, slots, n_grads, n_pieces, n_chunks, n_after, groups, paired, here, cols, *refs
):
    grads = refs[: n_grads * n_chunks]
    refs = refs[n_grads * n_chunks :]
    pieces = refs[: n_pieces * n_chunks]
    out, token, grad_v, nodes_v, tiles_v, live, source, sem, piece_sem, out_sem = refs[n_pieces * n_chunks + n_after :]
    token[...] = jnp.zeros_like(token)
    block = out.shape[1]
    width = nodes_v.shape[1]
    part = width // n_chunks
    scale = float(width) ** -0.5
    blocks = grad_v.shape[0] // (block * len(groups))
    here = Place(here, paired, blocks)
    jobs, copies = [], []
    for chunk in range(n_chunks):
        columns = pl.ds(chunk * part, part)
        jobs += grad_jobs(
            rows,
            grads[chunk * n_grads : (chunk + 1) * n_grads],
            grad_v.at[:, columns],
            sem.at[chunk],
            here,
            groups,
        )
        copies += load_pieces(
            pieces[chunk * n_pieces : (chunk + 1) * n_pieces],
            nodes_v.at[:, columns],
            piece_sem.at[chunk],
            0,
        )
    run_jobs(jobs, "start")
    tiles_v[...] = jnp.zeros_like(tiles_v)
    found = jnp.int32(0)
    for index, group in enumerate(groups):
        first = here.group(group) * blocks

        def collect(i, found, first=first, index=index):
            row = first + i
            count = cols[slots, row]
            for slot in range(slots):
                live[found] = (index * blocks + i) * slots + slot
                source[found] = here.source(cols[slot, row])
                found = found + (slot < count).astype(jnp.int32)
            return found

        found = lax.fori_loop(0, blocks, collect, found)
    run_jobs(jobs, "wait")
    for copy in copies:
        copy.wait()

    def entry(place):
        tile_index = live[place]
        grad = grad_v[block_at(tile_index // slots, block)]
        node = nodes_v[block_at(source[place], block)]
        tiles_v[tile_index] = (mm(grad, node, NT) * scale).astype(BF16)

    for_live(0, found, entry)
    size = blocks * slots
    copies = []
    for index, group in enumerate(groups):
        copy = pltpu.make_async_copy(
            tiles_v.at[pl.ds(index * size, size)],
            out.at[pl.ds(here.group(group) * size, size)],
            out_sem.at[index],
        )
        copy.start()
        copies.append(copy)
    for copy in copies:
        copy.wait()


def tile_grad_call(paired, here, cols, grads, pieces, shape, rows, groups, base=None, after=()):
    row_blocks, slots, block = shape[:3]
    chunks = len(grads)
    width = grads[0][0].shape[1] * chunks
    gathered = sum(piece.shape[0] for piece in pieces[0])
    flat = [a for chunk in grads for a in chunk] + [a for chunk in pieces for a in chunk]
    after = after if base is None else (base,) + tuple(after)
    entries = len(groups) * rows // block * slots
    return pl.pallas_call(
        functools.partial(
            tile_grad_kernel, rows, slots, len(grads[0]), len(pieces[0]), chunks, len(after), groups, paired
        ),
        out_shape=[
            jax.ShapeDtypeStruct((row_blocks * slots, block, block), BF16),
            jax.ShapeDtypeStruct((8, 128), F32),
        ],
        in_specs=[SMEM] * 2 + [ANY] * (len(flat) + len(after)),
        out_specs=[ANY, VMEM],
        input_output_aliases={} if base is None else {2 + len(flat): 0},
        scratch_shapes=[
            pltpu.VMEM((len(groups) * rows, width), BF16),
            pltpu.VMEM((gathered, width), BF16),
            pltpu.VMEM((entries, block, block), BF16),
            pltpu.SMEM((entries + 8,), jnp.int32),
            pltpu.SMEM((entries + 8,), jnp.int32),
            pltpu.SemaphoreType.DMA((chunks, len(grads[0]))),
            pltpu.SemaphoreType.DMA((chunks, len(pieces[0]))),
            pltpu.SemaphoreType.DMA((len(groups),)),
        ],
        compiler_params=params(16 if gathered <= 8192 else 40),
        cost_estimate=SMALL,
        name="tile_grads",
    )(here, cols, *flat, *after)


def swap(value, bit):
    return lax.ppermute(value, "row", [(i, i ^ bit) for i in range(8)])


def outer_swap(value):
    return lax.ppermute(value, "col", [(0, 1), (1, 0), (2, 3), (3, 2)])


def turn(value, by):
    return lax.ppermute(value, "col", [(i, (i + by) % 4) for i in range(4)])


def inner_swap(value):
    pairs = []
    for row in range(8):
        for col in range(4):
            partner = (row, 3 - col) if col in (1, 2) else (row ^ 1, col)
            pairs.append((row * 4 + col, partner[0] * 4 + partner[1]))
    return lax.ppermute(value, ("row", "col"), pairs)


def gather_square(nodes):
    half = nodes.shape[0] // 2
    lower, upper = nodes[:half], nodes[half:]
    y_lower, x_upper = swap(lower, 4), swap(upper, 2)
    x_lower, y_upper = swap(lower, 2), swap(upper, 4)
    d_lower, d_upper = swap(y_lower, 2), swap(x_upper, 4)
    pieces = [lower, upper, swap(nodes, 1)]
    for pair in ((x_lower, x_upper), (y_lower, y_upper), (d_lower, d_upper)):
        pieces += [*pair, *(swap(piece, 1) for piece in pair)]
    return pieces


def reduce_square(here, even, urgent, rest, rows):
    half = rows // 2
    first = [
        sum_call(here, rows, [(even, (6, 2)), (urgent, (0, 2))]),
        sum_call(here, rows, [(even, (7, 5)), (urgent, (1, 3))]),
    ]
    x_first, y_first = swap(first[0], 2), swap(first[1], 4)
    y_lower = swap(sum_call(here, half, [(even, 4), (rest, 3), (x_first, 0)]), 4)
    x_upper = swap(sum_call(here, half, [(even, 3), (rest, 2), (y_first, 0)]), 2)
    return [((x_first, 1), (x_upper, 0)), ((y_lower, 0), (y_first, 1))], first


def sum_kernel(n_terms, n_gated, n_split, *refs):
    inner, refs = Place(refs[0]).inner(), refs[1:]
    total = None
    for index, ref in enumerate(refs[: n_terms + n_gated]):
        term = ref[...].astype(F32)
        if index >= n_terms:
            term = jnp.where(inner, term, 0.0)
        total = term if total is None else total + term
    for index in range(n_split):
        first, second = refs[n_terms + n_gated + 2 * index :][:2]
        early = pl.program_id(0) < pl.num_programs(0) // 2
        total = total + jnp.where(early, first[...], second[...]).astype(F32)
    refs[-1][...] = total.astype(refs[-1].dtype)


def sum_call(here, rows, terms, gated=(), split=(), dtype=BF16, after=()):
    both = [*terms, *gated]
    width = both[0][0].shape[1]
    step = min(rows, 512)
    steps = rows // step
    half = steps // 2

    def spec(piece):
        if isinstance(piece, int):
            return pl.BlockSpec((step, width), lambda i: (piece * steps + i, 0))
        lower, upper = piece
        return pl.BlockSpec(
            (step, width), lambda i: (jnp.where(i < half, lower * half + i, (upper - 1) * half + i), 0)
        )

    def early(piece):
        return pl.BlockSpec((step, width), lambda i: (piece * half + jnp.minimum(i, half - 1), 0))

    def late(piece):
        return pl.BlockSpec((step, width), lambda i: (piece * half + jnp.maximum(i - half, 0), 0))

    return pl.pallas_call(
        functools.partial(sum_kernel, len(terms), len(gated), len(split)),
        grid=(steps,),
        out_shape=jax.ShapeDtypeStruct((rows, width), dtype),
        in_specs=[SMEM]
        + [spec(piece) for _, piece in both]
        + [spec_of(piece) for pair in split for spec_of, (_, piece) in zip((early, late), pair)]
        + [ANY] * len(after),
        out_specs=pl.BlockSpec((step, width), lambda i: (i, 0)),
        compiler_params=params(16),
        cost_estimate=SMALL,
        name="sum_terms",
    )(here, *(array for array, _ in both), *(array for pair in split for array, _ in pair), *after)


def scatter_weights(here, kept, sent, after):
    rows = kept.shape[0] // 4
    received = swap(sent, 1)
    pieces = [
        sum_call(here, rows, [(kept, place), (received, place)], dtype=F32) for place in range(4)
    ]
    terms = [pieces[0]] + [swap(piece, bits) for piece, bits in zip(pieces[1:], SWAP_ORDER[1:4])]
    return sum_call(here, rows, [(term, 0) for term in terms], after=after)


def level_weights(here, value, after):
    terms = [value] + [turn(value, by) for by in (1, 2, 3)]
    return sum_call(here, value.shape[0], [(term, 0) for term in terms], after=after)


def reduce_line(here, far, near, pair, own, after):
    rows = own.shape[0]
    far_sum = inner_swap(sum_call(here, rows, [(far, 0), (outer_swap(far), 0)], after=after))
    near_sum = inner_swap(sum_call(here, rows, [(near, 0), (outer_swap(near), 0)]))
    pair_in = outer_swap(sum_call(here, rows, [(pair, 0)], [(far_sum, 0)]))
    return own, pair_in, near_sum


def gather_line(own):
    pair = outer_swap(own)
    near_inner = inner_swap(own)
    far_inner = inner_swap(pair)
    near_outer = outer_swap(near_inner)
    far_outer = outer_swap(far_inner)
    return [own, pair, near_inner, near_outer, far_inner, far_outer]


def body(n_row, n_col, nodes, tiles, tile_col, tile_count, w_in, bias_in, w_out, ln_gain, ln_shift, cotangent):
    rows, width = nodes.shape
    row_blocks, _, slots, block = tiles.shape[:4]
    tile_local = tiles.reshape(row_blocks, slots, block, block)
    table = jnp.concatenate([tile_col.reshape(row_blocks, slots).T, tile_count.reshape(1, row_blocks)], axis=0)
    gathered, total = n_row * rows, n_col * rows
    paired = n_row == 8 and n_col == 4
    here = lax.axis_index(("row", "col")).astype(jnp.int32).reshape(1)
    known = (paired, here, table)
    turned = turn_call(table, tile_local)
    if paired:
        pieces = [gather_square(nodes)]
        (far,) = forward_call(*known, pieces[0], tile_local, ((0,),), rows)
        (near,) = forward_call(*known, pieces[0], tile_local, ((1,),), rows)
        pair, own = forward_call(*known, pieces[0], tile_local, ((2,), (3,)), rows)
        parts = [reduce_line(here, far, near, pair, own, (turned,))]
        kinds = [("all", "all", "inner")]
    else:
        pieces = [[lax.all_gather(nodes, "row", axis=0, tiled=True)]]
        (partial,) = forward_call(*known, pieces[0], tile_local, (tuple(range(n_col)),), rows)
        parts = [[lax.psum_scatter(partial, "col", scatter_dimension=0, tiled=True)]]
        kinds = [("all",)]
    vectors = [v.reshape(1, width) for v in (bias_in, ln_gain, ln_shift)]
    (updated, gpre_b, act, gproj, message, vec), gmsgs = mlp_call(
        here, nodes, cotangent, parts, kinds, w_in, vectors[0], w_out, vectors[1], vectors[2]
    )
    factor = float(rows * n_row * n_col) ** -0.5
    weight_args = (here, nodes, message, act, gpre_b, gproj, cotangent, w_in, vec)
    if paired:
        halves = ((14, 15, 6, 11), (2, 3, 7, 10), (0, 1, 4, 5, 8, 9, 12, 13))
        grads = [gather_line(gmsgs[0])]
        kept, sent, direct = weight_call(factor, n_row, *weight_args, (grads[0][1], grads[0][2]))
        near_grads, token = tile_grad_call(
            *known, [grads[0][:4]], pieces, tile_local.shape, rows, (3, 2, 1), after=(grads[0][4],)
        )
        row_weights = scatter_weights(here, kept, sent, (token,))
        urgent, rest, even = back_call(
            *known, grads[0], turned, total, gathered, halves, (row_weights,)
        )
        urgent, rest = swap(urgent, 1), swap(rest, 1)
        arrived, first = reduce_square(here, even, urgent, rest, rows)
        grad_tiles, token = tile_grad_call(
            *known, grads, pieces, tile_local.shape, rows, (0,), near_grads, first
        )
        row_weights = sum_call(here, row_weights.shape[0], [(row_weights, 0)], after=(rest, *first))
        all_weights = level_weights(here, row_weights, (token,))
        joint = jnp.concatenate([all_weights] + [swap(all_weights, bits) for bits in (2, 4, 6)], axis=0)
        weights = unpack_call(here, joint, swap(joint, 1), width)
        grad_nodes = sum_call(here, rows, [(direct, 0), (even, 0), (rest, 0)], split=arrived)
    else:
        grads = [[lax.all_gather(gmsgs[0], "col", axis=0, tiled=True)]]
        weight_terms, direct = weight_call(factor, 1, *weight_args)
        weight_sums = lax.psum(weight_terms, ("row", "col"))
        weights = (
            weight_sums[: 2 * width],
            weight_sums[2 * width : 3 * width],
            weight_sums[3 * width : 3 * width + 3],
        )
        (terms,) = back_call(*known, grads[0], turned, total, gathered, (tuple(range(n_row)),))
        back = lax.psum_scatter(terms, "row", scatter_dimension=0, tiled=True)
        grad_nodes = sum_call(here, rows, [(direct, 0), (back, 0)])
        grad_tiles, _ = tile_grad_call(
            *known, grads, pieces, tile_local.shape, rows, tuple(range(n_col))
        )
    grad_tiles = grad_tiles.reshape(tiles.shape)
    return (updated, grad_nodes, grad_tiles, *weights)


def solution(mesh):
    placed = (
        P(("row", "col"), None),
        P("row", "col", None, None, None),
        P("row", "col", None),
        P("row", "col"),
        P(),
        P(),
        P(),
        P(),
        P(),
        P(("row", "col"), None),
    )
    return jax.shard_map(
        functools.partial(body, mesh.shape["row"], mesh.shape["col"]),
        mesh=mesh,
        in_specs=placed,
        out_specs=(
            P(("row", "col"), None),
            P(("row", "col"), None),
            P("row", "col", None, None, None),
            P(),
            P(),
            P(),
        ),
        check_vma=False,
    )
```
